32 devices in a mesh: batch: 2 (over x), seq: 16 (over z, y, core).
Axes of the slice: x: 2, y: 2, z: 4, core: 2. Of those that a mesh axis runs over, the one named last changes fastest.
Arguments:
- hidden_in: bfloat16 [4096, 2048], P(('batch', 'seq')), may hold values from -6 to 6
- cotangent: bfloat16 [4096, 2048], P(('batch', 'seq')), may hold values from -6 to 6
- master: float32 [2048, 24579], P(('batch', 'seq'))
- first: float32 [2048, 24579], P(('batch', 'seq'))
- second: float32 [2048, 24579], P(('batch', 'seq'))
- average: float32 [2048, 24579], P(('batch', 'seq'))
- lengths: int32 [2, 4], P('batch'), may hold values from 50 to 1024, as said below
- prefix: int32 [2, 4], P('batch'), may hold values from 1 to 1023, as said below
- padding: int32 [2, 4], P('batch'), may hold values from 0 to 256, as said below
Outputs:
- output: bfloat16 [4096, 2048], P(('batch', 'seq'))
- input_grad: bfloat16 [4096, 2048], P(('batch', 'seq'))
- new_master: float32 [2048, 24579], P(('batch', 'seq'))
- new_first: float32 [2048, 24579], P(('batch', 'seq'))
- new_second: float32 [2048, 24579], P(('batch', 'seq'))
- new_average: float32 [2048, 24579], P(('batch', 'seq'))
The draws below stay inside these ranges and needn't reach their ends.
Inputs may be any that keep to these rules, and one draw needn't show every extreme that they name: The lengths of each group sum to 2048; one of them is 1024. Each prefix is below its chain's length. Each padding is at most a quarter of its chain's length, rounded down.
All inputs are finite; a program needn't handle non-finite values.
Results may differ from the reference program's by a relative error of at most 0.0087.
Values may be sent and summed in bfloat16 or wider, within the bound.
A program may use at most 320 MiB of HBM per device.

```python
import math
import jax
import jax.numpy as jnp
from jax import lax

D = 2048
H = 16
HD = 128
FF = 5461
CHAIN_MAX = 1024
CHAIN_MIN = 50
STEP = 10
G = 2048
TOKENS = 4096
CHAINS = 4
WCOLS = 24579
N_BATCH = 2


def column_block(block_values):
    column = jnp.arange(WCOLS)
    edge_list = [3 * D, 4 * D, 4 * D + 2 * FF, 4 * D + 3 * FF]
    result = jnp.full((WCOLS,), block_values[4], jnp.float32)
    for edge_col, entry_value in reversed(list(zip(edge_list, block_values[:4]))):
        result = jnp.where(column < edge_col, entry_value, result)
    return result


def master_like(seed_key):
    normal_part = jax.random.normal(jax.random.fold_in(seed_key, 1), (D, WCOLS), jnp.float32)
    spread_part = jax.random.uniform(jax.random.fold_in(seed_key, 2), (D, WCOLS), jnp.float32, -0.3, 0.3)
    scale_cols = column_block((D ** (-0.5), (16.0 / D) ** 0.5, D ** (-0.5), FF ** (-0.5), 0.2))
    column = jnp.arange(WCOLS)
    gain_col = (column == WCOLS - 4) | (column == WCOLS - 2)
    return jnp.where(gain_col[None, :], 1.0 + spread_part, normal_part * scale_cols[None, :])


def grad_scale():
    return column_block((0.25, 0.1, 0.3, 0.6, 7.0)) * math.sqrt(TOKENS)


def draw_master(key, part):
    return master_like(jax.random.fold_in(key, 101))


def draw_average(key, part):
    return master_like(jax.random.fold_in(key, 102))


def draw_first(key, part):
    normal_part = jax.random.normal(jax.random.fold_in(key, 103), (D, WCOLS), jnp.float32)
    return 0.1 / 0.9 * grad_scale()[None, :] * normal_part


def draw_second(key, part):
    factor = jnp.exp(jax.random.uniform(jax.random.fold_in(key, 104), (D, WCOLS), jnp.float32, 0.0, math.log(4.0)))
    scale_cols = grad_scale()
    return 0.05 / 0.95 * (scale_cols * scale_cols)[None, :] * factor


def chain_draw(key):
    base_key = jax.random.fold_in(key, 11)
    weights_int = jax.random.randint(jax.random.fold_in(base_key, 1), (N_BATCH, CHAINS - 1), 8, 17)
    spare = G - CHAIN_MAX - (CHAINS - 1) * CHAIN_MIN
    extra = spare * weights_int // jnp.sum(weights_int, axis=1, keepdims=True)
    remain = spare - jnp.sum(extra, axis=1, keepdims=True)
    slot_ids = jnp.arange(CHAINS - 1)[None, :]
    extra = extra + (slot_ids < remain).astype(jnp.int32)
    chain_len = jnp.concatenate([jnp.full((N_BATCH, 1), CHAIN_MAX, jnp.int32), CHAIN_MIN + extra], axis=1)
    order_keys = jax.random.split(jax.random.fold_in(base_key, 2), N_BATCH)
    order = jax.vmap(lambda one_key: jax.random.permutation(one_key, CHAINS))(order_keys)
    chain_len = jnp.take_along_axis(chain_len, order, axis=1).astype(jnp.int32)
    chain_prefix = 1 + jax.random.randint(jax.random.fold_in(base_key, 3), (N_BATCH, CHAINS), 0, chain_len - 1)
    chain_pad = jax.random.randint(jax.random.fold_in(base_key, 4), (N_BATCH, CHAINS), 0, chain_len // 4 + 1)
    group_ids = jnp.arange(N_BATCH)[:, None]
    longest = order == 0
    top_slot = longest & (group_ids == 0)
    low_slot = longest & (group_ids == 1)
    chain_prefix = jnp.where(top_slot, CHAIN_MAX - 1, jnp.where(low_slot, 1, chain_prefix))
    chain_pad = jnp.where(top_slot, CHAIN_MAX // 4, jnp.where(low_slot, 0, chain_pad))
    return (chain_len, chain_prefix.astype(jnp.int32), chain_pad.astype(jnp.int32))


def draw_lengths(key, part):
    return chain_draw(key)[0]


def draw_prefix(key, part):
    return chain_draw(key)[1]


def draw_padding(key, part):
    return chain_draw(key)[2]


def block_levels(rng, dims, pieces, low, high):
    level = 1.0
    for dim, shards_of in pieces:
        draws = jax.random.uniform(jax.random.fold_in(jax.random.fold_in(rng, 6), dim), (shards_of,), jnp.float32, low / len(pieces), high / len(pieces))
        level = level * jnp.repeat(jnp.exp(draws), dims[dim] // shards_of).reshape((-1,) + (1,) * (len(dims) - 1 - dim))
    return level


def bell_draw(key, dims, scale, limit, pieces=(), kind=jnp.bfloat16):
    drawn = jax.random.normal(key, dims, jnp.float32) * scale
    if len(pieces) > 0:
        drawn = block_levels(key, dims, pieces, -0.22, 0.18) * drawn
    return jnp.clip(drawn, min=-limit, max=limit).astype(kind)


def setup_inputs(seed: int = 0) -> dict:
    streams_of = jax.random.split(jax.random.key(seed), 10)
    hidden_in = bell_draw(streams_of[0], (TOKENS, D), 1.0, 6.0, ((0, 32),))
    cotangent = bell_draw(streams_of[1], (TOKENS, D), 1.0, 6.0, ((0, 32),))
    master = draw_master(jax.random.fold_in(streams_of[9], 71), 0)
    first = draw_first(jax.random.fold_in(streams_of[9], 71), 0)
    second = draw_second(jax.random.fold_in(streams_of[9], 71), 0)
    average = draw_average(jax.random.fold_in(streams_of[9], 71), 0)
    lengths = draw_lengths(jax.random.fold_in(streams_of[9], 71), 0)
    prefix = draw_prefix(jax.random.fold_in(streams_of[9], 71), 0)
    padding = draw_padding(jax.random.fold_in(streams_of[9], 71), 0)
    return {"hidden_in": hidden_in, "cotangent": cotangent, "master": master, "first": first, "second": second, "average": average, "lengths": lengths, "prefix": prefix, "padding": padding}


DEEP_ALPHA = math.sqrt(48.0)
ROPE_BASE = 10000.0
NEG_LARGE = -1e+30
LN_EPS = 1e-05
BETA_ONE = 0.9
BETA_TWO = 0.95
ADAM_EPS = 1e-08
LR_MAT = 0.01
LR_VEC = 0.2
DECAY_MAT = 0.1
EMA_RATE = 0.9
HIGHEST_MODE = lax.Precision.HIGHEST

@jax.custom_vjp
def low(v):
    return lax.optimization_barrier(v.astype(jnp.bfloat16)).astype(jnp.float32)

@jax.custom_vjp
def low_back(v):
    return v

def low_keep(v):
    return (low(v), None)

def low_pass(kept, grad):
    return (grad,)

def back_keep(v):
    return (v, None)

def back_low(kept, grad):
    return (low(grad),)
low.defvjp(low_keep, low_pass)
low_back.defvjp(back_keep, back_low)

def layer_norm(values, gain_vec, bias_vec):
    centre = values - lax.optimization_barrier(jnp.mean(values, axis=-1, keepdims=True))
    spread = lax.optimization_barrier(jnp.mean(centre * centre, axis=-1, keepdims=True))
    return centre * lax.rsqrt(spread + LN_EPS) * gain_vec + bias_vec

def chain_tables(chain_len, chain_prefix, chain_pad, total):
    ends_at = jnp.cumsum(chain_len, dtype=jnp.int32)
    starts_at = ends_at - chain_len
    tokens_at = jnp.arange(total, dtype=jnp.int32)
    member = ((tokens_at[:, None] >= starts_at[None, :]) & (tokens_at[:, None] < ends_at[None, :])).astype(jnp.int32)
    chain_ids = jnp.arange(chain_len.shape[0], dtype=jnp.int32)
    segment = lax.optimization_barrier(jnp.sum(member * chain_ids[None, :], axis=1, dtype=jnp.int32))
    position = tokens_at - lax.optimization_barrier(jnp.sum(member * starts_at[None, :], axis=1, dtype=jnp.int32))
    prefix_tok = lax.optimization_barrier(jnp.sum(member * chain_prefix[None, :], axis=1, dtype=jnp.int32))
    live_len = lax.optimization_barrier(jnp.sum(member * (chain_len - chain_pad)[None, :], axis=1, dtype=jnp.int32))
    return (segment, position, prefix_tok, position < live_len)

def visible(q_index, k_index, seg_q, seg_k, pos_k, pref_k, live_k):
    same = seg_q[:, None] == seg_k[None, :]
    order = (pos_k < pref_k)[None, :] | (k_index[None, :] <= q_index[:, None])
    return same & live_k[None, :] & order

def rotate(values, position, sign):
    half = values.shape[-1] // 2
    freq = ROPE_BASE ** (-jnp.arange(half, dtype=jnp.float32) / half)
    angles = position.astype(jnp.float32)[:, None] * freq[None, :]
    cosine = jnp.cos(angles)[:, None, :]
    sine = sign * jnp.sin(angles)[:, None, :]
    first_half = values[..., :half]
    second_half = values[..., half:]
    return jnp.concatenate([first_half * cosine - second_half * sine, first_half * sine + second_half * cosine], axis=-1)

def forward(states_in, weights, lengths, prefix, padding):
    rounded = low(weights)
    w_qkv = rounded[:, :3 * D]
    w_out = rounded[:, 3 * D:4 * D]
    w_up = rounded[:, 4 * D:4 * D + 2 * FF]
    w_down = rounded[:, 4 * D + 2 * FF:4 * D + 3 * FF]
    base_col = 4 * D + 3 * FF
    normed = layer_norm(states_in, rounded[:, base_col], rounded[:, base_col + 1])
    projected = low_back(jnp.dot(low(normed), w_qkv, precision=HIGHEST_MODE)).reshape(TOKENS, 3, H, HD)
    tables = jax.vmap(lambda one_len, one_pre, one_pad: chain_tables(one_len, one_pre, one_pad, G))(lengths, prefix, padding)
    position = tables[1].reshape(TOKENS)
    query = low_back(low(rotate(projected[:, 0], position, 1.0))).reshape(N_BATCH, G, H, HD)
    key_all = low_back(low(rotate(projected[:, 1], position, 1.0))).reshape(N_BATCH, G, H, HD)
    value_all = low_back(low(projected[:, 2])).reshape(N_BATCH, G, H, HD)

    def group_attention(group_args):
        q_grp, k_grp, v_grp, segment, position_g, prefix_tok, live_tok = group_args
        token_ids = jnp.arange(G, dtype=jnp.int32)
        mask_grp = visible(token_ids, token_ids, segment, segment, position_g, prefix_tok, live_tok)

        def head_attention(head_args):
            q_head, k_head, v_head = head_args
            scores = low_back(HD ** (-0.5) * jnp.dot(q_head, k_head.T, precision=HIGHEST_MODE))
            scores = jnp.where(mask_grp, scores, NEG_LARGE)
            probs = jnp.exp(scores - lax.optimization_barrier(jnp.max(scores, axis=-1, keepdims=True)))
            probs = probs / lax.optimization_barrier(jnp.sum(probs, axis=-1, keepdims=True))
            return jnp.dot(low(probs), v_head, precision=HIGHEST_MODE)
        heads_out = lax.map(jax.checkpoint(head_attention), (q_grp.transpose(1, 0, 2), k_grp.transpose(1, 0, 2), v_grp.transpose(1, 0, 2)))
        return heads_out.transpose(1, 0, 2)
    attended = lax.map(group_attention, (query, key_all, value_all, tables[0], tables[1], tables[2], tables[3]))
    attended = low_back(low(attended.reshape(TOKENS, D)))
    branch = low_back(jnp.dot(attended, w_out, precision=HIGHEST_MODE))
    residual = DEEP_ALPHA * normed + branch
    normed_two = layer_norm(residual, rounded[:, base_col + 2], rounded[:, base_col + 3])
    gate_up = low_back(jnp.dot(low(normed_two), w_up, precision=HIGHEST_MODE))
    hidden = low(jax.nn.gelu(gate_up[:, :FF]) * gate_up[:, FF:])
    return DEEP_ALPHA * normed_two + jnp.dot(hidden, w_down.T, precision=HIGHEST_MODE)

def reference(hidden_in, cotangent, master, first, second, average, lengths, prefix, padding):
    states_in = hidden_in.astype(jnp.float32)
    output_f, pull = jax.vjp(lambda xs, ws: forward(xs, ws, lengths, prefix, padding), states_in, master)
    input_grad, weight_grad = pull(cotangent.astype(jnp.float32))
    column = jnp.arange(WCOLS)
    matrix_col = column < WCOLS - 4
    rate = jnp.where(matrix_col, LR_MAT, LR_VEC).astype(jnp.float32)
    decay = jnp.where(matrix_col, DECAY_MAT, 0.0).astype(jnp.float32)
    new_first = BETA_ONE * first + (1.0 - BETA_ONE) * weight_grad
    new_second = BETA_TWO * second + (1.0 - BETA_TWO) * weight_grad * weight_grad
    corrected = new_first / (1.0 - BETA_ONE ** STEP) / (jnp.sqrt(new_second / (1.0 - BETA_TWO ** STEP)) + ADAM_EPS)
    new_master = master - rate[None, :] * (corrected + decay[None, :] * master)
    new_average = EMA_RATE * average + (1.0 - EMA_RATE) * new_master
    return (output_f.astype(jnp.bfloat16), input_grad.astype(jnp.bfloat16), new_master, new_first, new_second, new_average)
```

```python
import functools
import math

import jax
import jax.numpy as jnp
from jax import lax
from jax.experimental import pallas as pl
from jax.experimental.pallas import tpu as pltpu
from jax.sharding import PartitionSpec as P

D = 2048
H = 16
HD = 128
FF = 5461
STEP = 10

DEEP_ALPHA = math.sqrt(48.0)
ROPE_BASE = 10000.0
NEG_LARGE = -1e30
LN_EPS = 1e-05
BETA_ONE = 0.9
BETA_TWO = 0.95
ADAM_EPS = 1e-08
LR_MAT = 0.01
LR_VEC = 0.2
DECAY_MAT = 0.1
EMA_RATE = 0.9

BF = jnp.bfloat16
F32 = jnp.float32
MESH = pl.DeviceIdType.MESH
ROWS = 256
LANES = 128
SUBS = 4
VMEM_BIG = 56 * 1024 * 1024


def nt(left, right):
    return lax.dot_general(left, right, (((1,), (1,)), ((), ())), preferred_element_type=F32)


def tn(left, right):
    return lax.dot_general(left, right, (((0,), (0,)), ((), ())), preferred_element_type=F32)


def nn(left, right):
    return jnp.dot(left, right, preferred_element_type=F32)


def vmem(limit=VMEM_BIG, **more):
    return pltpu.CompilerParams(vmem_limit_bytes=limit, **more)


class Ring:
    def __init__(self, count):
        self.pairs = count // 2
        self.batch, self.me = lax.axis_index("batch"), lax.axis_index("seq")
        self.core = lax.rem(self.me, 2)
        y, z = lax.rem(self.me // 2, 2), self.me // 4
        self.place = jnp.where(y == 0, z, self.pairs - 1 - z)
        self.sibling = self.me + 1 - 2 * self.core

    def at(self, steps, core=None):
        place = lax.rem(self.place + (1 - 2 * self.core) * steps + 4 * self.pairs, self.pairs)
        half = self.pairs // 2
        pair = jnp.where(place < half, 2 * place, 2 * (self.pairs - 1 - place) + 1)
        return pair * 2 + (self.core if core is None else core)

    def greet(self):
        barrier = pltpu.get_barrier_semaphore()
        for device in (self.at(-1), self.sibling):
            pl.semaphore_signal(barrier, inc=1, device_id=(self.batch, device), device_id_type=MESH)
        pl.semaphore_wait(barrier, 2)

    def greet_all(self, count):
        barrier = pltpu.get_barrier_semaphore()
        groups = lax.axis_size("batch")
        for step in range(1, count):
            device = lax.rem(self.me + step, count)
            pl.semaphore_signal(barrier, inc=1, device_id=(self.batch, device), device_id_type=MESH)
        for shift in range(1, groups):
            group = lax.rem(self.batch + shift, groups)
            pl.semaphore_signal(barrier, inc=1, device_id=(group, self.me), device_id_type=MESH)
        pl.semaphore_wait(barrier, count + groups - 2)

    def copy(self, src, dst, send, recv, device):
        return pltpu.make_async_remote_copy(
            src_ref=src,
            dst_ref=dst,
            send_sem=send,
            recv_sem=recv,
            device_id=(self.batch, device),
            device_id_type=MESH,
        )


class Columns:
    def __init__(self, ring, count, src, out, sems):
        self.ring, self.count, self.src, self.out = ring, count, src, out
        self.send, self.recv, self.on_send, self.on_recv, self.own = sems
        self.groups = lax.axis_size("batch")

    def piece(self, device):
        return self.src.at[device] if self.src.shape[0] == self.count else self.src.at[0]

    def group(self, shift):
        return lax.rem(self.ring.batch + shift + self.groups, self.groups)

    def start(self):
        ring, sends = self.ring, []
        self.mine = pltpu.make_async_copy(
            self.piece(ring.me), self.out.at[ring.batch, ring.me], self.own
        )
        self.mine.start()
        for step in range(1, self.count):
            device = lax.rem(ring.me + step, self.count)
            go = ring.copy(
                self.piece(device),
                self.out.at[ring.batch, ring.me],
                self.send.at[step],
                self.recv.at[step],
                device,
            )
            go.start()
            sends.append(go)
        self.sends = sends + self.forward(0)

    def forward(self, step):
        ring, sends = self.ring, []
        device = lax.rem(ring.me - step + self.count, self.count)
        here = self.out.at[ring.batch, device]
        for shift in range(1, self.groups):
            go = pltpu.make_async_remote_copy(
                src_ref=self.piece(ring.me) if step == 0 else here,
                dst_ref=here,
                send_sem=self.on_send.at[shift - 1, step],
                recv_sem=self.on_recv.at[shift - 1, step],
                device_id=(self.group(shift), ring.me),
                device_id_type=MESH,
            )
            go.start()
            sends.append(go)
        return sends

    def pass_on(self, step):
        ring = self.ring
        device = lax.rem(ring.me - step + self.count, self.count)
        here = self.out.at[ring.batch, device]
        ring.copy(here, here, self.send.at[step], self.recv.at[step], device).wait_recv()
        self.sends += self.forward(step)

    def finish(self):
        ring = self.ring
        for step in range(self.count):
            device = lax.rem(ring.me - step + self.count, self.count)
            for shift in range(1, self.groups):
                here = self.out.at[self.group(-shift), device]
                pltpu.make_async_remote_copy(
                    src_ref=here,
                    dst_ref=here,
                    send_sem=self.on_send.at[shift - 1, step],
                    recv_sem=self.on_recv.at[shift - 1, step],
                    device_id=(self.group(shift), ring.me),
                    device_id_type=MESH,
                ).wait_recv()
        for go in self.sends:
            go.wait_send()
        self.mine.wait()


def gather_kernel(count, extra, x_ref, *refs):
    parts, (o_ref, *outs), sems = refs[:extra], refs[extra : 2 * extra + 1], refs[2 * extra + 1 :]
    ring_s, ring_r, sib_s, sib_r, own_sem = sems[:5]
    ring = Ring(count)
    piece = x_ref.shape[0] // SUBS
    own = pltpu.make_async_copy(x_ref, o_ref.at[ring.me], own_sem)
    own.start()
    columns = [
        Columns(ring, count, parts[i], outs[i], sems[5 + 5 * i : 10 + 5 * i]) for i in range(extra)
    ]
    ring.greet_all(count)
    following, sends = ring.at(1), []
    ahead = 1
    for step in range(ring.pairs):
        block = ring.at(-step)
        for sub in range(SUBS):
            rows = pl.ds(sub * piece, piece)
            dst = o_ref.at[block].at[rows]
            src = x_ref.at[rows] if step == 0 else dst
            if step > 0:
                ring.copy(
                    dst, dst, ring_s.at[step - 1, sub], ring_r.at[step - 1, sub], following
                ).wait_recv()
            if step < ring.pairs - 1:
                go = ring.copy(src, dst, ring_s.at[step, sub], ring_r.at[step, sub], following)
                go.start()
                sends.append(go)
            go = ring.copy(src, dst, sib_s.at[step, sub], sib_r.at[step, sub], ring.sibling)
            go.start()
            sends.append(go)
        if step == 0:
            for column in columns:
                column.start()
        elif 2 * step >= ring.pairs:
            upto = count if step == ring.pairs - 1 else count * (2 * step - ring.pairs + 1) // ring.pairs
            for passed in range(ahead, max(ahead, upto)):
                for column in columns:
                    column.pass_on(passed)
            ahead = max(ahead, upto)
    for step in range(ring.pairs):
        block = ring.at(step, 1 - ring.core)
        for sub in range(SUBS):
            dst = o_ref.at[block].at[pl.ds(sub * piece, piece)]
            ring.copy(
                dst, dst, sib_s.at[step, sub], sib_r.at[step, sub], ring.sibling
            ).wait_recv()
    for go in sends:
        go.wait_send()
    own.wait()
    for column in columns:
        column.finish()


def ring_gather(values, blocks, count, ident):
    pairs, groups = count // 2, lax.axis_size("batch")
    anywhere = pl.BlockSpec(memory_space=pl.ANY)
    column_sems = [
        pltpu.SemaphoreType.DMA((count,)),
        pltpu.SemaphoreType.DMA((count,)),
        pltpu.SemaphoreType.DMA((groups, count)),
        pltpu.SemaphoreType.DMA((groups, count)),
        pltpu.SemaphoreType.DMA,
    ]
    return pl.pallas_call(
        functools.partial(gather_kernel, count, len(blocks)),
        out_shape=[jax.ShapeDtypeStruct((count,) + values.shape, values.dtype)]
        + [jax.ShapeDtypeStruct((groups, count) + b.shape[1:], b.dtype) for b in blocks],
        in_specs=[anywhere] * (1 + len(blocks)),
        out_specs=[anywhere] * (1 + len(blocks)),
        scratch_shapes=[pltpu.SemaphoreType.DMA((pairs, SUBS)) for _ in range(4)]
        + [pltpu.SemaphoreType.DMA]
        + column_sems * len(blocks),
        compiler_params=pltpu.CompilerParams(collective_id=ident, has_side_effects=True),
        cost_estimate=pl.CostEstimate(flops=0, bytes_accessed=150_000_000, transcendentals=0),
        name=f"ring_gather_{ident}",
    )(values, *blocks)


def scatter_kernel(count, x_ref, o_ref, own, sib, got, ring_s, ring_r, sib_s, sib_r, load):
    ring = Ring(count)
    piece = x_ref.shape[1] // SUBS
    pairs = ring.pairs
    loads = []
    for step in range(pairs):
        go = pltpu.make_async_copy(x_ref.at[ring.at(-1 - step)], own.at[step], load.at[step])
        go.start()
        loads.append(go)
    ring.greet()
    following, sends = ring.at(1), []
    for step in range(pairs):
        block = ring.at(1 + step, 1 - ring.core)
        for sub in range(SUBS):
            rows = pl.ds(sub * piece, piece)
            go = ring.copy(
                x_ref.at[block].at[rows],
                sib.at[step].at[rows],
                sib_s.at[step, sub],
                sib_r.at[step, sub],
                ring.sibling,
            )
            go.start()
            sends.append(go)
    for step in range(pairs):
        loads[step].wait()
        for sub in range(SUBS):
            rows = pl.ds(sub * piece, piece)
            here = own.at[step].at[rows]
            other = sib.at[step].at[rows]
            ring.copy(
                other, other, sib_s.at[step, sub], sib_r.at[step, sub], ring.sibling
            ).wait_recv()
            total = here[...].astype(F32) + other[...].astype(F32)
            if step > 0:
                came = got.at[step - 1].at[rows]
                ring.copy(
                    came, came, ring_s.at[step - 1, sub], ring_r.at[step - 1, sub], following
                ).wait_recv()
                total = total + came[...].astype(F32)
            if step == pairs - 1:
                o_ref[rows, :] = total
            else:
                here[...] = total.astype(BF)
                go = ring.copy(
                    here,
                    got.at[step].at[rows],
                    ring_s.at[step, sub],
                    ring_r.at[step, sub],
                    following,
                )
                go.start()
                sends.append(go)
    for go in sends:
        go.wait_send()


def ring_scatter(terms, count, ident):
    pairs = count // 2
    shape = terms.shape[1:]
    return pl.pallas_call(
        functools.partial(scatter_kernel, count),
        out_shape=jax.ShapeDtypeStruct(shape, F32),
        in_specs=[pl.BlockSpec(memory_space=pl.ANY)],
        out_specs=pl.BlockSpec(memory_space=pltpu.VMEM),
        scratch_shapes=[pltpu.VMEM((pairs,) + shape, BF) for _ in range(3)]
        + [pltpu.SemaphoreType.DMA((pairs, SUBS)) for _ in range(4)]
        + [pltpu.SemaphoreType.DMA((pairs,))],
        compiler_params=vmem(collective_id=ident, has_side_effects=True),
        cost_estimate=pl.CostEstimate(flops=0, bytes_accessed=150_000_000, transcendentals=0),
        name=f"ring_scatter_{ident}",
    )(terms)


def norm_parts(values):
    centre = values - jnp.mean(values, axis=-1, keepdims=True)
    inverse = lax.rsqrt(jnp.mean(centre * centre, axis=-1, keepdims=True) + LN_EPS)
    return centre * inverse, inverse


def qkv_kernel(x_ref, w_ref, vec_ref, cos_ref, sin_ref, a_ref, q_ref, k_ref, v_ref):
    normal, _ = norm_parts(x_ref[...].astype(F32))
    low = (normal * vec_ref[0:1, :] + vec_ref[1:2, :]).astype(BF)
    a_ref[...] = low
    projected = nn(low, w_ref[...])
    for index, ref in enumerate((q_ref, k_ref)):
        part = projected[:, index * HD : (index + 1) * HD]
        turned = part * cos_ref[...] + pltpu.roll(part, HD // 2, 1) * sin_ref[...]
        ref[...] = turned.astype(BF)
    v_ref[...] = projected[:, 2 * HD :].astype(BF)


def norm_and_project(states, w_qkv, vectors, cosine, sine):
    tokens = states.shape[0]
    whole = lambda shape: pl.BlockSpec(shape, lambda i: (0, 0))
    rows = lambda width: pl.BlockSpec((ROWS, width), lambda i: (i, 0))
    return pl.pallas_call(
        qkv_kernel,
        grid=(tokens // ROWS,),
        in_specs=[rows(D), whole((D, 3 * HD)), whole(vectors.shape), rows(HD), rows(HD)],
        out_specs=[rows(D), rows(HD), rows(HD), rows(HD)],
        out_shape=[jax.ShapeDtypeStruct((tokens, D), BF)]
        + [jax.ShapeDtypeStruct((tokens, HD), BF) for _ in range(3)],
        compiler_params=vmem(),
        cost_estimate=pl.CostEstimate(
            flops=2 * tokens * D * 3 * HD, bytes_accessed=24_000_000, transcendentals=0
        ),
        name="norm_and_project",
    )(states, w_qkv, vectors, cosine, sine)


def seen(block, first_ref, last_ref, keys):
    query = block * ROWS + lax.broadcasted_iota(jnp.int32, (ROWS, ROWS), 0)
    return (query >= first_ref[keys]) & (query < last_ref[keys])


def attend_kernel(
    low_ref, high_ref, q_ref, k_ref, v_ref, first_ref, last_ref, o_ref, full_ref, log_ref, held
):
    block = pl.program_id(0)
    query = q_ref[...]
    scale = HD ** (-0.5)

    def score(keys, top):
        scores = nt(query, k_ref[keys]) * scale
        scores = jnp.where(seen(block, first_ref, last_ref, keys), scores, NEG_LARGE)
        held[keys] = scores
        return jnp.maximum(top, jnp.max(scores, axis=-1, keepdims=True))

    def add(keys, carry):
        total, out = carry
        weight = jnp.exp(held[keys] - top)
        total = total + jnp.sum(weight, axis=-1, keepdims=True)
        return total, out + nn(weight.astype(BF), v_ref[keys])

    low, high = low_ref[block], high_ref[block]
    top = lax.fori_loop(low, high, score, jnp.full((ROWS, 1), NEG_LARGE, F32))
    total, out = lax.fori_loop(
        low, high, add, (jnp.zeros((ROWS, 1), F32), jnp.zeros((ROWS, HD), F32))
    )
    out = out / total
    o_ref[...] = out.astype(BF)
    full_ref[...] = out
    log_ref[...] = jnp.broadcast_to(top + jnp.log(total), (ROWS, LANES))


def attend(query, key, value, spans):
    tokens = query.shape[0]
    blocks = tokens // ROWS
    first, last, low, high = spans
    rows = pl.BlockSpec((ROWS, HD), lambda i, *_: (i, 0))
    whole = lambda shape: pl.BlockSpec(shape, lambda i, *_: (0,) * len(shape))
    cut = lambda values: values.reshape(blocks, ROWS, HD)
    return pl.pallas_call(
        attend_kernel,
        grid_spec=pltpu.PrefetchScalarGridSpec(
            num_scalar_prefetch=2,
            grid=(blocks,),
            in_specs=[rows]
            + [whole((blocks, ROWS, HD)) for _ in range(2)]
            + [whole((blocks, 1, ROWS)) for _ in range(2)],
            out_specs=[rows, rows, rows],
            scratch_shapes=[pltpu.VMEM((blocks, ROWS, ROWS), F32)],
        ),
        out_shape=[
            jax.ShapeDtypeStruct((tokens, HD), BF),
            jax.ShapeDtypeStruct((tokens, HD), F32),
            jax.ShapeDtypeStruct((tokens, LANES), F32),
        ],
        compiler_params=vmem(),
        cost_estimate=pl.CostEstimate(
            flops=2 * tokens * tokens * HD, bytes_accessed=4_000_000, transcendentals=0
        ),
        name="attend",
    )(low, high, query, cut(key), cut(value), first, last)


def attend_back_kernel(
    low_ref,
    high_ref,
    q_ref,
    g_ref,
    full_ref,
    log_ref,
    k_ref,
    v_ref,
    first_ref,
    last_ref,
    cos_ref,
    sin_ref,
    o_ref,
    dk_ref,
    dv_ref,
):
    block = pl.program_id(0)
    blocks = pl.num_programs(0)
    scale = HD ** (-0.5)

    @pl.when(block == 0)
    def _():
        dk_ref[...] = jnp.zeros_like(dk_ref)
        dv_ref[...] = jnp.zeros_like(dv_ref)

    query, grad = q_ref[...], g_ref[...]
    inner = jnp.sum(grad.astype(F32) * full_ref[...], axis=-1, keepdims=True)
    log = log_ref[:, 0:1]

    def one(keys, total):
        scores = nt(query, k_ref[keys]) * scale
        scores = jnp.where(seen(block, first_ref, last_ref, keys), scores, NEG_LARGE)
        weight = jnp.exp(scores - log)
        slope = (weight * (nt(grad, v_ref[keys]) - inner)).astype(BF)
        dv_ref[keys] += tn(weight.astype(BF), grad)
        dk_ref[keys] += tn(slope, query)
        return total + nn(slope, k_ref[keys])

    total = lax.fori_loop(
        low_ref[block], high_ref[block], one, jnp.zeros((ROWS, HD), F32)
    )

    def turn_back(values, cosine, sine):
        values = (values * scale).astype(BF).astype(F32)
        return (values * cosine - pltpu.roll(values, HD // 2, 1) * sine).astype(BF)

    rows = pl.ds(pl.multiple_of(block * ROWS, ROWS), ROWS)
    o_ref[rows, 0:HD] = turn_back(total, cos_ref[rows, :], sin_ref[rows, :])

    @pl.when(block == blocks - 1)
    def _():
        for part in range(dk_ref.shape[0]):
            there = pl.ds(part * ROWS, ROWS)
            o_ref[there, HD : 2 * HD] = turn_back(
                dk_ref[part], cos_ref[there, :], sin_ref[there, :]
            )
            o_ref[there, 2 * HD :] = dv_ref[part].astype(BF)


def attend_back(query, key, value, grad, full, log, spans, cosine, sine):
    tokens = query.shape[0]
    blocks = tokens // ROWS
    first, last, low, high = spans
    rows = pl.BlockSpec((ROWS, HD), lambda i, *_: (i, 0))
    whole = lambda shape: pl.BlockSpec(shape, lambda i, *_: (0,) * len(shape))
    cut = lambda values: values.reshape(blocks, ROWS, HD)
    return pl.pallas_call(
        attend_back_kernel,
        grid_spec=pltpu.PrefetchScalarGridSpec(
            num_scalar_prefetch=2,
            grid=(blocks,),
            in_specs=[rows] * 4
            + [whole((blocks, ROWS, HD)) for _ in range(2)]
            + [whole((blocks, 1, ROWS)) for _ in range(2)]
            + [whole((tokens, HD)) for _ in range(2)],
            out_specs=whole((tokens, 3 * HD)),
            scratch_shapes=[pltpu.VMEM((blocks, ROWS, HD), F32) for _ in range(2)],
        ),
        out_shape=jax.ShapeDtypeStruct((tokens, 3 * HD), BF),
        compiler_params=vmem(),
        cost_estimate=pl.CostEstimate(
            flops=5 * tokens * tokens * HD, bytes_accessed=6_000_000, transcendentals=0
        ),
        name="attend_back",
    )(low, high, query, grad, full, log, cut(key), cut(value), first, last, cosine, sine)


def residual_kernel(x_ref, heads_ref, w_ref, vec_ref, b_ref, own_ref):
    tokens = own_ref.shape[0]
    block = pl.program_id(0)
    normal, _ = norm_parts(x_ref[...].astype(F32))
    attended = jnp.concatenate([heads_ref[h] for h in range(heads_ref.shape[0])], axis=1)
    residual = DEEP_ALPHA * (normal * vec_ref[0:1, :] + vec_ref[1:2, :]) + nn(
        attended, w_ref[...]
    )
    second, _ = norm_parts(residual)
    b_ref[...] = (second * vec_ref[2:3, :] + vec_ref[3:4, :]).astype(BF)
    me = lax.axis_index("seq")
    for part in range(ROWS // tokens):

        @pl.when(block * (ROWS // tokens) + part == me)
        def _():
            own_ref[...] = residual[part * tokens : (part + 1) * tokens, :]


def residual_norm(states, heads, w_out, vectors, own_rows):
    tokens = states.shape[0]
    whole = lambda shape: pl.BlockSpec(shape, lambda i: (0,) * len(shape))
    rows = pl.BlockSpec((ROWS, D), lambda i: (i, 0))
    return pl.pallas_call(
        residual_kernel,
        grid=(tokens // ROWS,),
        in_specs=[
            rows,
            pl.BlockSpec((heads.shape[0], ROWS, HD), lambda i: (0, i, 0)),
            whole((D, D)),
            whole(vectors.shape),
        ],
        out_specs=[rows, whole((own_rows, D))],
        out_shape=[
            jax.ShapeDtypeStruct((tokens, D), BF),
            jax.ShapeDtypeStruct((own_rows, D), F32),
        ],
        compiler_params=vmem(),
        cost_estimate=pl.CostEstimate(
            flops=2 * tokens * D * D, bytes_accessed=32_000_000, transcendentals=0
        ),
        name="residual_norm",
    )(states, heads, w_out, vectors)


def feed_kernel(b_ref, cot_ref, w_ref, h_ref, du_ref, out_ref, db_ref):
    span = h_ref.shape[1]
    b, cot = b_ref[...], cot_ref[...]
    gate = nn(b, w_ref[:, :span])
    up = nn(b, w_ref[:, span : 2 * span])
    slope = nn(cot, w_ref[:, 2 * span :])
    coef = math.sqrt(2.0 / math.pi)
    square = gate * gate
    tanh = jnp.tanh(coef * gate * (1.0 + 0.044715 * square))
    half = 0.5 * (1.0 + tanh)
    gelu = gate * half
    gelu_slope = half + 0.5 * gate * (1.0 - tanh * tanh) * (
        coef * (1.0 + 3 * 0.044715 * square)
    )
    hidden = (gelu * up).astype(BF)
    h_ref[...] = hidden
    du = jnp.concatenate([slope * up * gelu_slope, slope * gelu], axis=1).astype(BF)
    du_ref[...] = du
    out_ref[...] = nt(hidden, w_ref[:, 2 * span :]).astype(BF)
    db_ref[...] = nt(du, w_ref[:, : 2 * span]).astype(BF)


def feed_forward(b_low, cot, w_feed):
    tokens = b_low.shape[0]
    span = w_feed.shape[1] // 3
    rows = lambda width: pl.BlockSpec((ROWS, width), lambda i: (i, 0))
    return pl.pallas_call(
        feed_kernel,
        grid=(tokens // ROWS,),
        in_specs=[rows(D), rows(D), pl.BlockSpec(w_feed.shape, lambda i: (0, 0))],
        out_specs=[rows(span), rows(2 * span), rows(D), rows(D)],
        out_shape=[
            jax.ShapeDtypeStruct((tokens, width), BF) for width in (span, 2 * span, D, D)
        ],
        compiler_params=vmem(),
        cost_estimate=pl.CostEstimate(
            flops=12 * tokens * D * span, bytes_accessed=48_000_000, transcendentals=0
        ),
        name="feed_forward",
    )(b_low, cot, w_feed)


def windows(at, span, count):
    total = 4 * D + 3 * FF + 4
    result = []
    for index in range(count):
        width = max(0, min(span, FF - index * span))
        begin = at + index * span
        turn = begin % LANES
        window = -(-(turn + width) // LANES) * LANES if width else 0
        window = min(window, (total - begin + turn) // LANES * LANES)
        result.append((begin - turn, window, turn, width))
    return result


FEED_AT = (4 * D, 4 * D + FF, 4 * D + 2 * FF)


def lay_out_kernel(count, span, m_ref, qkv_ref, out_ref, feed_ref):
    rows = m_ref.shape[0]
    for index in range(count):
        for part in range(3):
            at = part * D + index * HD
            qkv_ref[index, :, part * HD : (part + 1) * HD] = m_ref[:, at : at + HD].astype(BF)
    out_ref[...] = m_ref[:, 3 * D : 4 * D].astype(BF)
    column = lax.broadcasted_iota(jnp.int32, (rows, span), 1)
    for part, at in enumerate(FEED_AT):
        for index, (begin, window, turn, width) in enumerate(windows(at, span, count)):
            if width == 0:
                piece = jnp.zeros((rows, span), F32)
            else:
                piece = m_ref[:, begin : begin + window]
                if window < span:
                    piece = jnp.concatenate(
                        [piece, jnp.zeros((rows, span - window), F32)], axis=1
                    )
                if turn:
                    piece = pltpu.roll(piece, piece.shape[1] - turn, 1)
                piece = piece[:, :span]
                if width < span:
                    piece = jnp.where(column < width, piece, 0.0)
            feed_ref[index, :, part * span : (part + 1) * span] = piece.astype(BF)


def lay_out(master, count, span):
    rows = master.shape[0]
    inside = pl.BlockSpec(memory_space=pltpu.VMEM)
    return pl.pallas_call(
        functools.partial(lay_out_kernel, count, span),
        out_shape=[
            jax.ShapeDtypeStruct((count, rows, 3 * HD), BF),
            jax.ShapeDtypeStruct((rows, D), BF),
            jax.ShapeDtypeStruct((count, rows, 3 * span), BF),
        ],
        in_specs=[inside],
        out_specs=[inside] * 3,
        compiler_params=vmem(),
        cost_estimate=pl.CostEstimate(flops=0, bytes_accessed=10_000_000, transcendentals=0),
        name="lay_out",
    )(master)


STEP_COLS = 3072


def update_kernel(
    count, span, attn_ref, feed_ref, vec_ref, m_ref, f_ref, s_ref, a_ref, nm_ref, nf_ref, ns_ref, na_ref, grad
):
    rows = m_ref.shape[0]
    step = pl.program_id(0)
    total = 4 * D + 3 * FF + 4

    @pl.when(step == 0)
    def _():
        for index in range(count):
            for part in range(4):
                at = part * D + index * HD
                grad[:, at : at + HD] = attn_ref[index, :, part * HD : (part + 1) * HD].astype(F32)
        lane = lax.broadcasted_iota(jnp.int32, (rows, LANES), 1)
        tiles = span // LANES
        last = None
        for part, at in enumerate(FEED_AT):
            turn = at % LANES
            for tile in range(-(-(FF + turn) // LANES)):
                begin = at - turn + tile * LANES
                index, inner = divmod(tile, tiles)
                here = feed_ref[index, :, part * span + inner * LANES : part * span + (inner + 1) * LANES]
                here = here.astype(F32)
                if turn:
                    here = pltpu.roll(here, turn, 1)
                    before = last if tile == 0 else previous
                    value = here if before is None else jnp.where(lane < turn, before, here)
                    previous = here
                else:
                    value = here
                if begin + LANES <= total:
                    grad[:, begin : begin + LANES] = value
                    last = value
        edge = (total - 4) // LANES * LANES
        shift = (total - 4) % LANES
        both = jnp.concatenate([last, jnp.zeros_like(last)], axis=1)
        vec = jnp.concatenate([vec_ref[...], jnp.zeros_like(last)], axis=1)
        vec = pltpu.roll(vec, shift, 1)
        wide = lax.broadcasted_iota(jnp.int32, (rows, 2 * LANES), 1)
        both = jnp.where(wide < shift, both, vec)
        grad[:, edge : edge + 2 * LANES] = both

    begin = pl.multiple_of(step * STEP_COLS, LANES)
    g = grad[:, pl.ds(begin, STEP_COLS)]
    vector = step * STEP_COLS + lax.broadcasted_iota(jnp.int32, (1, STEP_COLS), 1) >= total - 4
    rate = jnp.where(vector, LR_VEC, LR_MAT)
    decay = jnp.where(vector, 0.0, DECAY_MAT)
    new_first = BETA_ONE * f_ref[...] + (1.0 - BETA_ONE) * g
    new_second = BETA_TWO * s_ref[...] + (1.0 - BETA_TWO) * g * g
    nf_ref[...] = new_first
    ns_ref[...] = new_second
    root = jnp.sqrt(new_second * (1.0 / (1.0 - BETA_TWO**STEP))) + ADAM_EPS
    corrected = new_first * (1.0 / (1.0 - BETA_ONE**STEP)) / root
    master = m_ref[...]
    new_master = master - rate * (corrected + decay * master)
    nm_ref[...] = new_master
    na_ref[...] = EMA_RATE * a_ref[...] + (1.0 - EMA_RATE) * new_master


def update(attn, feed, vec, master, first, second, average, span):
    count, rows = feed.shape[:2]
    columns = master.shape[1]
    steps = -(-columns // STEP_COLS)
    whole = lambda values: pl.BlockSpec(values.shape, lambda i: (0,) * values.ndim)
    cols = pl.BlockSpec((rows, STEP_COLS), lambda i: (0, i))
    return pl.pallas_call(
        functools.partial(update_kernel, count, span),
        grid=(steps,),
        in_specs=[whole(attn), whole(feed), whole(vec)] + [cols] * 4,
        out_specs=[cols] * 4,
        out_shape=[jax.ShapeDtypeStruct(master.shape, F32) for _ in range(4)],
        scratch_shapes=[pltpu.VMEM((rows, steps * STEP_COLS), F32)],
        compiler_params=vmem(),
        cost_estimate=pl.CostEstimate(flops=0, bytes_accessed=56_000_000, transcendentals=0),
        name="update",
    )(attn, feed, vec, master, first, second, average)


def chain_spans(lengths, prefix, padding, total):
    ends = jnp.cumsum(lengths, dtype=jnp.int32)
    starts = ends - lengths
    token = jnp.arange(total, dtype=jnp.int32)
    member = (token[:, None] >= starts[None, :]) & (token[:, None] < ends[None, :])
    pick = lambda values: jnp.sum(jnp.where(member, values[None, :], 0), axis=1, dtype=jnp.int32)
    start, end, pre, live = pick(starts), pick(ends), pick(prefix), pick(lengths - padding)
    place = token - start
    first = jnp.where(place < pre, start, token)
    first = jnp.where(place < live, first, 2 * total)
    blocks = total // ROWS
    low = start[::ROWS] // ROWS
    high = (end[ROWS - 1 :: ROWS] + ROWS - 1) // ROWS
    cut = lambda values: values.reshape(blocks, 1, ROWS)
    return (cut(first), cut(end), low, high), place


def rotary_tables(place):
    half = HD // 2
    freq = ROPE_BASE ** (-jnp.arange(half, dtype=F32) / half)
    angles = place.astype(F32)[:, None] * freq[None, :]
    cosine, sine = jnp.cos(angles), jnp.sin(angles)
    return jnp.concatenate([cosine, cosine], axis=1), jnp.concatenate([-sine, sine], axis=1)


def over_batch(block_of, own):
    count = lax.axis_size("batch")
    me = lax.axis_index("batch")
    arrived = [
        lax.ppermute(
            block_of(lax.rem(me + shift, count)),
            "batch",
            [(i, (i + shift) % count) for i in range(count)],
        )
        for shift in range(1, count)
    ]
    return functools.reduce(lambda total, part: total + part.astype(F32), arrived, own())


def rows_of(grad_rows):
    seq = lax.axis_size("seq")
    total = over_batch(
        lambda there: grad_rows(there).astype(BF), lambda: grad_rows(lax.axis_index("batch"))
    )
    blocks = total.astype(BF).reshape(seq, -1, total.shape[1])
    return lax.all_to_all(blocks, "seq", split_axis=0, concat_axis=0, tiled=True)


def vector_rows(sums):
    batch, seq = lax.axis_size("batch"), lax.axis_size("seq")
    me = lax.axis_index("batch")
    kinds = sums.shape[0]
    cut = sums.reshape(kinds, batch, seq, -1).transpose(2, 1, 0, 3)
    came = lax.all_to_all(cut, "seq", split_axis=0, concat_axis=0, tiled=True)
    totals = jnp.sum(came, axis=0)
    part = lambda place: lax.dynamic_index_in_dim(totals, place, 0, keepdims=False)
    return over_batch(part, lambda: part(me)).T


def on_device(hidden_in, cotangent, master, first, second, average, lengths, prefix, padding):
    groups, seq = lax.axis_size("batch"), lax.axis_size("seq")
    own = hidden_in.shape[0]
    tokens = own * seq
    rows = master.shape[0]
    span = -(-FF // (seq * LANES)) * LANES
    vec_cut = master[:, 4 * D + 3 * FF :].astype(BF).astype(F32).T
    vec_cut = jnp.pad(vec_cut, ((0, 8 - vec_cut.shape[0]), (0, LANES - rows)))[None]
    qkv_cut, out_cut, feed_cut = lay_out(master, seq, span)
    states, w_qkv, vectors = ring_gather(hidden_in, [qkv_cut, vec_cut], seq, 1)
    states = states.reshape(tokens, D)
    w_qkv = w_qkv.reshape(D, 3 * HD)
    vectors = vectors[..., :rows].transpose(2, 0, 1, 3).reshape(8, D)
    w_out = lax.all_gather(out_cut, ("batch", "seq"), axis=0, tiled=True)
    cot_all = lax.all_gather(cotangent, "seq", axis=0, tiled=True)

    spans, place = chain_spans(lengths[0], prefix[0], padding[0], tokens)
    cosine, sine = rotary_tables(place)
    a_low, query, key, value = norm_and_project(states, w_qkv, vectors, cosine, sine)
    attended, full, log = attend(query, key, value, spans)
    heads, w_feed = ring_gather(attended, [feed_cut], seq, 2)
    w_feed = w_feed.reshape(D, 3 * span)
    b_low, residual = residual_norm(states, heads, w_out, vectors, own)
    hidden, du, out_terms, db_terms = feed_forward(b_low, cot_all, w_feed)

    db_sum = ring_scatter(db_terms.reshape(seq, own, D), seq, 3)
    out_sum = lax.psum_scatter(out_terms, "seq", scatter_dimension=0, tiled=True)
    gain_one, bias_one, gain_two, bias_two = (vectors[i][None, :] for i in range(4))

    def norm_back(normal, inverse, slope, gain):
        scaled = slope * gain
        back = inverse * (
            scaled
            - jnp.mean(scaled, axis=-1, keepdims=True)
            - normal * jnp.mean(scaled * normal, axis=-1, keepdims=True)
        )
        return back, jnp.stack([jnp.sum(slope * normal, axis=0), jnp.sum(slope, axis=0)])

    normal_two, inverse_two = norm_parts(residual)
    output = DEEP_ALPHA * (normal_two * gain_two + bias_two) + out_sum.astype(F32)
    db = DEEP_ALPHA * cotangent.astype(F32) + db_sum
    dr, sums_two = norm_back(normal_two, inverse_two, db, gain_two)
    dr_low = dr.astype(BF)
    do = nt(dr_low, w_out).astype(BF)
    to_heads = lambda values: lax.all_to_all(
        values.reshape(own, seq, HD).transpose(1, 0, 2), "seq", split_axis=0, concat_axis=0, tiled=True
    ).reshape(tokens, HD)
    do_head = to_heads(do)
    dr_cols = to_heads(dr_low)

    def row_part(values, place):
        return lax.dynamic_slice_in_dim(values, place * (D // groups), D // groups, 1)

    grad_feed = rows_of(
        lambda place: jnp.concatenate(
            [tn(row_part(b_low, place), du), tn(row_part(cot_all, place), hidden)], axis=1
        )
    )
    dp = attend_back(query, key, value, do_head, full, log, spans, cosine, sine)
    da_terms = nt(dp, w_qkv).astype(BF)
    da_sum = ring_scatter(da_terms.reshape(seq, own, D), seq, 5)
    grad_out = jnp.einsum("htd,tn->hdn", heads, dr_cols, preferred_element_type=F32).reshape(D, HD)
    grad_attn = rows_of(
        lambda place: jnp.concatenate(
            [
                tn(row_part(a_low, place), dp),
                lax.dynamic_slice_in_dim(grad_out, place * (D // groups), D // groups, 0),
            ],
            axis=1,
        )
    )
    normal_one, inverse_one = norm_parts(hidden_in.astype(F32))
    da = DEEP_ALPHA * dr + da_sum
    input_grad, sums_one = norm_back(normal_one, inverse_one, da, gain_one)
    vector_grad = vector_rows(jnp.concatenate([sums_one, sums_two]))

    vector_grad = jnp.pad(vector_grad, ((0, 0), (0, LANES - vector_grad.shape[1])))
    updated = update(grad_attn, grad_feed, vector_grad, master, first, second, average, span)
    return (
        output.astype(BF),
        input_grad.astype(BF),
        *updated,
    )


def solution(mesh):
    spread = P(("batch", "seq"), None)
    return jax.shard_map(
        on_device,
        mesh=mesh,
        in_specs=(spread,) * 6 + (P("batch", None),) * 3,
        out_specs=(spread,) * 6,
        check_vma=False,
    )
```

```python
import functools
import math

import jax
import jax.numpy as jnp
from jax import lax
from jax.experimental import pallas as pl
from jax.experimental.pallas import tpu as pltpu
from jax.sharding import PartitionSpec as P

D = 2048
H = 16
HD = 128
FF = 5461
STEP = 10

DEEP_ALPHA = math.sqrt(48.0)
ROPE_BASE = 10000.0
NEG_LARGE = -1e30
LN_EPS = 1e-05
BETA_ONE = 0.9
BETA_TWO = 0.95
ADAM_EPS = 1e-08
LR_MAT = 0.01
LR_VEC = 0.2
DECAY_MAT = 0.1
EMA_RATE = 0.9

BF = jnp.bfloat16
F32 = jnp.float32
MESH = pl.DeviceIdType.MESH
ROWS = 256
LANES = 128
SUBS = 4
VMEM_BIG = 56 * 1024 * 1024


def nt(left, right):
    return lax.dot_general(left, right, (((1,), (1,)), ((), ())), preferred_element_type=F32)


def tn(left, right):
    return lax.dot_general(left, right, (((0,), (0,)), ((), ())), preferred_element_type=F32)


def nn(left, right):
    return jnp.dot(left, right, preferred_element_type=F32)


def vmem(limit=VMEM_BIG, **more):
    return pltpu.CompilerParams(vmem_limit_bytes=limit, **more)


class Ring:
    def __init__(self, count):
        self.pairs = count // 2
        self.batch, self.me = lax.axis_index("batch"), lax.axis_index("seq")
        self.core = lax.rem(self.me, 2)
        y, z = lax.rem(self.me // 2, 2), self.me // 4
        self.place = jnp.where(y == 0, z, self.pairs - 1 - z)
        self.sibling = self.me + 1 - 2 * self.core

    def at(self, steps, core=None):
        place = lax.rem(self.place + (1 - 2 * self.core) * steps + 4 * self.pairs, self.pairs)
        half = self.pairs // 2
        pair = jnp.where(place < half, 2 * place, 2 * (self.pairs - 1 - place) + 1)
        return pair * 2 + (self.core if core is None else core)

    def greet_all(self, count):
        barrier = pltpu.get_barrier_semaphore()
        groups = lax.axis_size("batch")
        for step in range(1, count):
            device = lax.rem(self.me + step, count)
            pl.semaphore_signal(barrier, inc=1, device_id=(self.batch, device), device_id_type=MESH)
        for shift in range(1, groups):
            group = lax.rem(self.batch + shift, groups)
            pl.semaphore_signal(barrier, inc=1, device_id=(group, self.me), device_id_type=MESH)
        pl.semaphore_wait(barrier, count + groups - 2)

    def greet_groups(self, groups):
        barrier = pltpu.get_barrier_semaphore()
        for device in (self.at(-1), self.sibling):
            pl.semaphore_signal(barrier, inc=1, device_id=(self.batch, device), device_id_type=MESH)
        for shift in range(1, groups):
            group = lax.rem(self.batch + shift, groups)
            pl.semaphore_signal(barrier, inc=1, device_id=(group, self.me), device_id_type=MESH)
        pl.semaphore_wait(barrier, 1 + groups)

    def copy(self, src, dst, send, recv, device):
        return pltpu.make_async_remote_copy(
            src_ref=src,
            dst_ref=dst,
            send_sem=send,
            recv_sem=recv,
            device_id=(self.batch, device),
            device_id_type=MESH,
        )


class Columns:
    def __init__(self, ring, count, src, out, sems):
        self.ring, self.count, self.src, self.out = ring, count, src, out
        self.send, self.recv, self.on_send, self.on_recv, self.own = sems
        self.groups = lax.axis_size("batch")

    def piece(self, device):
        return self.src.at[device] if self.src.shape[0] == self.count else self.src.at[0]

    def group(self, shift):
        return lax.rem(self.ring.batch + shift + self.groups, self.groups)

    def start(self):
        ring, sends = self.ring, []
        self.mine = pltpu.make_async_copy(
            self.piece(ring.me), self.out.at[ring.batch, ring.me], self.own
        )
        self.mine.start()
        for step in range(1, self.count):
            device = lax.rem(ring.me + step, self.count)
            go = ring.copy(
                self.piece(device),
                self.out.at[ring.batch, ring.me],
                self.send.at[step],
                self.recv.at[step],
                device,
            )
            go.start()
            sends.append(go)
        self.sends = sends + self.forward(0)

    def forward(self, step):
        ring, sends = self.ring, []
        device = lax.rem(ring.me - step + self.count, self.count)
        here = self.out.at[ring.batch, device]
        for shift in range(1, self.groups):
            go = pltpu.make_async_remote_copy(
                src_ref=self.piece(ring.me) if step == 0 else here,
                dst_ref=here,
                send_sem=self.on_send.at[shift - 1, step],
                recv_sem=self.on_recv.at[shift - 1, step],
                device_id=(self.group(shift), ring.me),
                device_id_type=MESH,
            )
            go.start()
            sends.append(go)
        return sends

    def pass_on(self, step):
        ring = self.ring
        device = lax.rem(ring.me - step + self.count, self.count)
        here = self.out.at[ring.batch, device]
        ring.copy(here, here, self.send.at[step], self.recv.at[step], device).wait_recv()
        self.sends += self.forward(step)

    def finish(self):
        ring = self.ring
        for step in range(self.count):
            device = lax.rem(ring.me - step + self.count, self.count)
            for shift in range(1, self.groups):
                here = self.out.at[self.group(-shift), device]
                pltpu.make_async_remote_copy(
                    src_ref=here,
                    dst_ref=here,
                    send_sem=self.on_send.at[shift - 1, step],
                    recv_sem=self.on_recv.at[shift - 1, step],
                    device_id=(self.group(shift), ring.me),
                    device_id_type=MESH,
                ).wait_recv()
        for go in self.sends:
            go.wait_send()
        self.mine.wait()


def pass_round(ring, count, x_ref, o_ref, sems, columns, work):
    ring_s, ring_r, sib_s, sib_r, own_sem = sems
    piece = x_ref.shape[0] // SUBS
    own = pltpu.make_async_copy(x_ref, o_ref.at[ring.me], own_sem)
    own.start()
    ring.greet_all(count)
    following, sends = ring.at(1), []
    ahead = 1
    for step in range(ring.pairs):
        block = ring.at(-step)
        for sub in range(SUBS):
            rows = pl.ds(sub * piece, piece)
            dst = o_ref.at[block].at[rows]
            src = x_ref.at[rows] if step == 0 else dst
            if step > 0:
                ring.copy(
                    dst, dst, ring_s.at[step - 1, sub], ring_r.at[step - 1, sub], following
                ).wait_recv()
            if step < ring.pairs - 1:
                go = ring.copy(src, dst, ring_s.at[step, sub], ring_r.at[step, sub], following)
                go.start()
                sends.append(go)
            go = ring.copy(src, dst, sib_s.at[step, sub], sib_r.at[step, sub], ring.sibling)
            go.start()
            sends.append(go)
        if step == 0:
            for column in columns:
                column.start()
            own.wait()
        else:
            upto = count if step == ring.pairs - 1 else min(count, 1 + 2 * step)
            for passed in range(ahead, max(ahead, upto)):
                for column in columns:
                    column.pass_on(passed)
            ahead = max(ahead, upto)
        other = ring.at(step, 1 - ring.core)
        for sub in range(SUBS):
            dst = o_ref.at[other].at[pl.ds(sub * piece, piece)]
            ring.copy(
                dst, dst, sib_s.at[step, sub], sib_r.at[step, sub], ring.sibling
            ).wait_recv()
        work(step, block, other)
    return sends


def gather_kernel(count, extra, x_ref, *refs):
    parts, (o_ref, *outs), sems = refs[:extra], refs[extra : 2 * extra + 1], refs[2 * extra + 1 :]
    ring = Ring(count)
    columns = [
        Columns(ring, count, parts[i], outs[i], sems[5 + 5 * i : 10 + 5 * i]) for i in range(extra)
    ]
    sends = pass_round(ring, count, x_ref, o_ref, sems[:5], columns, lambda *_: None)
    for go in sends:
        go.wait_send()
    for column in columns:
        column.finish()


def ring_gather(values, blocks, count, ident):
    pairs, groups = count // 2, lax.axis_size("batch")
    anywhere = pl.BlockSpec(memory_space=pl.ANY)
    return pl.pallas_call(
        functools.partial(gather_kernel, count, len(blocks)),
        out_shape=[jax.ShapeDtypeStruct((count,) + values.shape, values.dtype)]
        + [jax.ShapeDtypeStruct((groups, count) + b.shape[1:], b.dtype) for b in blocks],
        in_specs=[anywhere] * (1 + len(blocks)),
        out_specs=[anywhere] * (1 + len(blocks)),
        scratch_shapes=ring_sems(pairs) + column_sems(count, groups) * len(blocks),
        compiler_params=pltpu.CompilerParams(collective_id=ident, has_side_effects=True),
        cost_estimate=pl.CostEstimate(flops=0, bytes_accessed=150_000_000, transcendentals=0),
        name=f"ring_gather_{ident}",
    )(values, *blocks)


def ring_sems(pairs):
    return [pltpu.SemaphoreType.DMA((pairs, SUBS)) for _ in range(4)] + [pltpu.SemaphoreType.DMA]


def column_sems(count, groups):
    return [
        pltpu.SemaphoreType.DMA((count,)),
        pltpu.SemaphoreType.DMA((count,)),
        pltpu.SemaphoreType.DMA((groups, count)),
        pltpu.SemaphoreType.DMA((groups, count)),
        pltpu.SemaphoreType.DMA,
    ]


def residual_kernel(
    count,
    x_ref,
    part_ref,
    states_ref,
    w_ref,
    vec_ref,
    heads_ref,
    feed_ref,
    b_ref,
    own_ref,
    heads,
    w_out,
    total,
    states,
    low,
    w_sem,
    load_sem,
    store_sem,
    heads_sem,
    *sems,
):
    ring = Ring(count)
    tokens, own = total.shape[0], own_ref.shape[0]
    blocks = tokens // ROWS
    weights = pltpu.make_async_copy(w_ref, w_out, w_sem)
    weights.start()
    columns = [Columns(ring, count, part_ref, feed_ref, sems[5:10])]

    def rows_of(block):
        return pl.ds(pl.multiple_of(block * ROWS, ROWS), ROWS)

    def load(block):
        slot = lax.rem(block, 2)
        return pltpu.make_async_copy(
            states_ref.at[rows_of(block)], states.at[slot], load_sem.at[slot]
        )

    def store(block):
        slot = lax.rem(block, 2)
        return pltpu.make_async_copy(low.at[slot], b_ref.at[rows_of(block)], store_sem.at[slot])

    load(0).start()

    def begin():
        @pl.loop(0, blocks)
        def _(block):
            @pl.when(block + 1 < blocks)
            def _():
                load(block + 1).start()

            load(block).wait()
            normal, _ = norm_parts(states[lax.rem(block, 2)].astype(F32))
            total[rows_of(block), :] = DEEP_ALPHA * (normal * vec_ref[0:1, :] + vec_ref[1:2, :])

        weights.wait()

    def saves(step, block, other):
        return [
            pltpu.make_async_copy(heads.at[head], heads_ref.at[head], heads_sem.at[step, part])
            for part, head in enumerate((block, other))
        ]

    kept = []

    def work(step, block, other):
        if step == 0:
            begin()
        for go in saves(step, block, other):
            go.start()
            kept.append(go)
        wide = 512

        @pl.loop(0, blocks)
        def _(part):
            rows = rows_of(part)
            left = jnp.concatenate([heads[block, rows, :], heads[other, rows, :]], axis=1)
            for at in range(0, D, wide):
                right = jnp.concatenate(
                    [
                        w_out[pl.ds(pl.multiple_of(head * HD, HD), HD), at : at + wide]
                        for head in (block, other)
                    ],
                    axis=0,
                )
                total[rows, at : at + wide] += nn(left, right)

    sends = pass_round(ring, count, x_ref, heads, sems[:5], columns, work)

    @pl.loop(0, blocks)
    def _(block):
        @pl.when(block >= 2)
        def _():
            store(block - 2).wait()

        normal, _ = norm_parts(total[rows_of(block), :])
        low[lax.rem(block, 2)] = (normal * vec_ref[2:3, :] + vec_ref[3:4, :]).astype(BF)
        store(block).start()

    own_ref[...] = total[pl.ds(pl.multiple_of(ring.me * own, own), own), :]
    for block in (blocks - 2, blocks - 1):
        store(block).wait()
    for go in kept:
        go.wait()
    for go in sends:
        go.wait_send()
    for column in columns:
        column.finish()


def gather_residual(attended, feed_cut, states, w_out, vectors, own, count, ident):
    tokens = attended.shape[0]
    pairs, groups = count // 2, lax.axis_size("batch")
    inside, anywhere = pl.BlockSpec(memory_space=pltpu.VMEM), pl.BlockSpec(memory_space=pl.ANY)
    return pl.pallas_call(
        functools.partial(residual_kernel, count),
        out_shape=[
            jax.ShapeDtypeStruct((count, tokens, HD), BF),
            jax.ShapeDtypeStruct((groups,) + feed_cut.shape, BF),
            jax.ShapeDtypeStruct((tokens, D), BF),
            jax.ShapeDtypeStruct((own, D), F32),
        ],
        in_specs=[anywhere] * 4 + [inside],
        out_specs=[anywhere] * 3 + [inside],
        scratch_shapes=[
            pltpu.VMEM((count, tokens, HD), BF),
            pltpu.VMEM((D, D), BF),
            pltpu.VMEM((tokens, D), F32),
            pltpu.VMEM((2, ROWS, D), BF),
            pltpu.VMEM((2, ROWS, D), BF),
            pltpu.SemaphoreType.DMA,
            pltpu.SemaphoreType.DMA((2,)),
            pltpu.SemaphoreType.DMA((2,)),
            pltpu.SemaphoreType.DMA((pairs, 2)),
        ]
        + ring_sems(pairs)
        + column_sems(count, groups),
        compiler_params=vmem(collective_id=ident, has_side_effects=True),
        cost_estimate=pl.CostEstimate(
            flops=2 * tokens * D * D, bytes_accessed=200_000_000, transcendentals=0
        ),
        name="gather_residual",
    )(attended, feed_cut, states, w_out, vectors)


class RingSum:
    def __init__(self, ring, own, sib, got, sems, out):
        self.ring, self.own, self.sib, self.got, self.out = ring, own, sib, got, out
        self.ring_s, self.ring_r, self.sib_s, self.sib_r = sems
        self.piece = own.shape[1] // SUBS

    def clear(self):
        self.got[0] = jnp.zeros_like(self.got[0])

    def given(self, step, src):
        return self.ring.copy(
            src, self.sib.at[step], self.sib_s.at[step], self.sib_r.at[step], self.ring.sibling
        )

    def passed(self, step, sub):
        rows = pl.ds(sub * self.piece, self.piece)
        return self.ring.copy(
            self.own.at[step].at[rows],
            self.got.at[step + 1].at[rows],
            self.ring_s.at[step, sub],
            self.ring_r.at[step, sub],
            self.ring.at(1),
        )

    def advance(self, step):
        last = self.ring.pairs - 1
        self.given(step, self.sib.at[step]).wait_recv()
        for sub in range(SUBS):
            rows = pl.ds(sub * self.piece, self.piece)

            @pl.when(step > 0)
            def _():
                self.passed(step - 1, sub).wait_recv()

            total = self.own[step, rows, :].astype(F32) + self.sib[step, rows, :].astype(F32)
            total = total + self.got[step, rows, :].astype(F32)

            @pl.when(step < last)
            def _():
                self.own[step, rows, :] = total.astype(BF)
                self.passed(step, sub).start()

            @pl.when(step == last)
            def _():
                self.out[rows, :] = total

    def finish(self):
        @pl.loop(0, self.ring.pairs - 1)
        def _(step):
            for sub in range(SUBS):
                self.passed(step, sub).wait_send()

    @staticmethod
    def scratch(pairs, rows):
        return [pltpu.VMEM((pairs, rows, D), BF) for _ in range(3)] + [
            pltpu.SemaphoreType.DMA((pairs, SUBS)),
            pltpu.SemaphoreType.DMA((pairs, SUBS)),
            pltpu.SemaphoreType.DMA((pairs,)),
            pltpu.SemaphoreType.DMA((pairs,)),
        ]


class Exchange:
    def __init__(self, ring, count, src, out, sems):
        self.ring, self.count, self.src, self.out = ring, count, src, out
        self.send, self.recv, self.own = sems

    def copies(self):
        ring = self.ring
        for step in range(1, self.count):
            device = lax.rem(ring.me + step, self.count)
            yield ring.copy(
                self.src.at[device],
                self.out.at[ring.me],
                self.send.at[step],
                self.recv.at[step],
                device,
            )

    def start(self):
        pltpu.make_async_copy(self.src.at[self.ring.me], self.out.at[self.ring.me], self.own).start()
        for go in self.copies():
            go.start()

    def finish(self):
        for go in self.copies():
            go.wait()
        pltpu.make_async_copy(self.src.at[self.ring.me], self.out.at[self.ring.me], self.own).wait()

    @staticmethod
    def scratch(count):
        return [pltpu.SemaphoreType.DMA((count,)) for _ in range(2)] + [pltpu.SemaphoreType.DMA]


class GroupSum:
    def __init__(self, ring, groups, sent, came, sems, out):
        self.ring, self.groups, self.sent, self.came, self.out = ring, groups, sent, came, out
        self.send, self.recv = sems
        self.tiles, self.each = D // ROWS, D // ROWS // groups

    def group(self, tile):
        return lax.rem(self.ring.batch + 1 + tile // self.each, self.groups)

    def column(self, tile):
        return (self.group(tile) * self.each + lax.rem(tile, self.each)) * ROWS

    def copy(self, tile):
        return pltpu.make_async_remote_copy(
            src_ref=self.sent.at[tile],
            dst_ref=self.came.at[tile],
            send_sem=self.send.at[tile],
            recv_sem=self.recv.at[tile],
            device_id=(self.group(tile), self.ring.me),
            device_id_type=MESH,
        )

    def put(self, tile, values):
        away = self.tiles - self.each

        @pl.when(tile < away)
        def _():
            self.sent[tile] = values.astype(BF)
            self.copy(tile).start()

        @pl.when(tile >= away)
        def _():
            self.out[tile - away] = values.astype(BF)

    def finish(self):
        @pl.loop(0, self.each)
        def _(tile):
            total = self.out[tile].astype(F32)
            for shift in range(self.groups - 1):
                self.copy(shift * self.each + tile).wait_recv()
                total = total + self.came[shift * self.each + tile].astype(F32)
            self.out[tile] = total.astype(BF)

        @pl.loop(0, self.tiles - self.each)
        def _(tile):
            self.copy(tile).wait_send()

    @staticmethod
    def scratch(groups, width):
        away = D // ROWS - D // ROWS // groups
        return [pltpu.VMEM((away, ROWS, width), BF) for _ in range(2)] + [
            pltpu.SemaphoreType.DMA((away,)) for _ in range(2)
        ]


def feed_kernel(
    count, groups, span, b_ref, cot_ref, w_ref, db_ref, out_ref, grad_ref, bs, cs, stage, h, du, tiles, *rest
):
    ring = Ring(count)
    own = db_ref.shape[0]
    sums = [
        RingSum(ring, *rest[7 * i : 7 * i + 3], rest[7 * i + 3 : 7 * i + 7], ref)
        for i, ref in enumerate((db_ref, out_ref))
    ]
    grads = GroupSum(ring, groups, rest[14], rest[15], rest[16:18], grad_ref)
    row_sem, tile_sem = rest[18:]
    pairs = ring.pairs

    def places(step):
        return ring.at(-1 - step) * own, ring.at(1 + step, 1 - ring.core) * own

    def row_loads(step):
        slot = lax.rem(step, 2)
        return [
            pltpu.make_async_copy(
                ref.at[pl.ds(pl.multiple_of(place, own), own)],
                held.at[slot, pl.ds(half * own, own)],
                row_sem.at[slot, 2 * which + half],
            )
            for which, (ref, held) in enumerate(((b_ref, bs), (cot_ref, cs)))
            for half, place in enumerate(places(step))
        ]

    def tile_loads(tile):
        slot = lax.rem(tile, 2)
        cols = pl.ds(pl.multiple_of(grads.column(tile), ROWS), ROWS)
        return [
            pltpu.make_async_copy(ref.at[:, cols], tiles.at[slot, which], tile_sem.at[slot, which])
            for which, ref in enumerate((b_ref, cot_ref))
        ]

    for go in row_loads(0):
        go.start()
    ring.greet_groups(groups)
    for each in sums:
        each.clear()

    def feed(step):
        slot = lax.rem(step, 2)

        @pl.when(step + 1 < pairs)
        def _():
            for go in row_loads(step + 1):
                go.start()

        for go in row_loads(step):
            go.wait()
        gate = nn(bs[slot], w_ref[:, :span])
        up = nn(bs[slot], w_ref[:, span : 2 * span])
        slope = nn(cs[slot], w_ref[:, 2 * span :])
        coef = math.sqrt(2.0 / math.pi)
        square = gate * gate
        tanh = jnp.tanh(coef * gate * (1.0 + 0.044715 * square))
        half = 0.5 * (1.0 + tanh)
        gelu = gate * half
        gelu_slope = half + 0.5 * gate * (1.0 - tanh * tanh) * (coef * (1.0 + 3 * 0.044715 * square))
        hidden = (gelu * up).astype(BF)
        both = jnp.concatenate([slope * up * gelu_slope, slope * gelu], axis=1).astype(BF)
        for part, place in enumerate(places(step)):
            rows = pl.ds(pl.multiple_of(place, own), own)
            h[rows, :] = hidden[part * own : (part + 1) * own]
            du[rows, :] = both[part * own : (part + 1) * own]

        @pl.when(step >= 2)
        def _():
            for which, each in enumerate(sums):
                each.given(step - 2, stage.at[slot, which]).wait_send()

        wide = 512
        for which, (each, left, low, high) in enumerate(
            ((sums[0], both, 0, 2 * span), (sums[1], hidden, 2 * span, 3 * span))
        ):
            for at in range(0, D, wide):
                terms = nt(left, w_ref[at : at + wide, low:high]).astype(BF)
                each.own[step, :, at : at + wide] = terms[:own]
                stage[slot, which, :, at : at + wide] = terms[own:]
            each.given(step, stage.at[slot, which]).start()

    @pl.loop(0, pairs)
    def _(step):
        feed(step)

        @pl.when(lax.rem(step, 2) == 0)
        def _():
            sums[0].advance(step // 2)

    for go in tile_loads(0):
        go.start()

    @pl.loop(0, grads.tiles)
    def _(tile):
        slot = lax.rem(tile, 2)

        @pl.when(tile + 1 < grads.tiles)
        def _():
            for go in tile_loads(tile + 1):
                go.start()

        for go in tile_loads(tile):
            go.wait()
        values = jnp.concatenate([tn(tiles[slot, 0], du[...]), tn(tiles[slot, 1], h[...])], axis=1)
        grads.put(tile, values)
        later = pairs // 2 + tile // 3

        @pl.when((lax.rem(tile, 3) == 1) & (later < pairs))
        def _():
            sums[0].advance(later)

    passed = pairs // 2 + len([t for t in range(grads.tiles) if t % 3 == 1])

    @pl.loop(min(passed, pairs), pairs)
    def _(step):
        sums[0].advance(step)

    @pl.loop(0, pairs)
    def _(step):
        sums[1].advance(step)

    grads.finish()
    for step in (pairs - 2, pairs - 1):
        for which, each in enumerate(sums):
            each.given(step, stage.at[step % 2, which]).wait_send()
    for each in sums:
        each.finish()


def feed_forward(b_low, cot, w_feed, own, count, groups, ident):
    tokens, span, pairs = b_low.shape[0], w_feed.shape[1] // 3, count // 2
    inside, anywhere = pl.BlockSpec(memory_space=pltpu.VMEM), pl.BlockSpec(memory_space=pl.ANY)
    return pl.pallas_call(
        functools.partial(feed_kernel, count, groups, span),
        in_specs=[anywhere, anywhere, inside],
        out_specs=[inside] * 3,
        out_shape=[
            jax.ShapeDtypeStruct((own, D), F32),
            jax.ShapeDtypeStruct((own, D), F32),
            jax.ShapeDtypeStruct((D // groups // ROWS, ROWS, 3 * span), BF),
        ],
        scratch_shapes=[
            pltpu.VMEM((2, 2 * own, D), BF),
            pltpu.VMEM((2, 2 * own, D), BF),
            pltpu.VMEM((2, 2, own, D), BF),
            pltpu.VMEM((tokens, span), BF),
            pltpu.VMEM((tokens, 2 * span), BF),
            pltpu.VMEM((2, 2, tokens, ROWS), BF),
        ]
        + RingSum.scratch(pairs, own) * 2
        + GroupSum.scratch(groups, 3 * span)
        + [pltpu.SemaphoreType.DMA((2, 4)), pltpu.SemaphoreType.DMA((2, 2))],
        compiler_params=vmem(60 * 1024 * 1024, collective_id=ident, has_side_effects=True),
        cost_estimate=pl.CostEstimate(
            flops=18 * tokens * D * span, bytes_accessed=250_000_000, transcendentals=0
        ),
        name="feed_forward",
    )(b_low, cot, w_feed)


def project_kernel(
    count,
    groups,
    dp_ref,
    w_ref,
    a_ref,
    heads_ref,
    dr_ref,
    feed_ref,
    da_ref,
    grad_ref,
    feed_out_ref,
    stage,
    tiles,
    *rest,
):
    ring = Ring(count)
    own = da_ref.shape[0]
    sums = RingSum(ring, *rest[:3], rest[3:7], da_ref)
    grads = GroupSum(ring, groups, rest[7], rest[8], rest[9:11], grad_ref)
    tile_sem = rest[11]
    feed = Exchange(ring, count, feed_ref, feed_out_ref, rest[12:15])
    pairs, width = ring.pairs, heads_ref.shape[2]

    def places(step):
        return ring.at(-1 - step) * own, ring.at(1 + step, 1 - ring.core) * own

    def tile_loads(tile):
        slot = lax.rem(tile, 2)
        begin = pl.multiple_of(grads.column(tile), ROWS)
        loads = [
            pltpu.make_async_copy(
                a_ref.at[:, pl.ds(begin, ROWS)], tiles.at[slot, 0], tile_sem.at[slot, 0]
            )
        ]
        for part in range(ROWS // width):
            loads.append(
                pltpu.make_async_copy(
                    heads_ref.at[begin // width + part],
                    tiles.at[slot, 1, :, pl.ds(part * width, width)],
                    tile_sem.at[slot, 1 + part],
                )
            )
        return loads

    for go in tile_loads(0):
        go.start()
    ring.greet_all(count)
    feed.start()
    sums.clear()

    def terms_of(step):
        slot = lax.rem(step, 2)

        @pl.when(step >= 2)
        def _():
            sums.given(step - 2, stage.at[slot]).wait_send()

        left = jnp.concatenate(
            [dp_ref[pl.ds(pl.multiple_of(place, own), own), :] for place in places(step)], axis=0
        )
        wide = 512
        for at in range(0, D, wide):
            terms = nt(left, w_ref[at : at + wide, :]).astype(BF)
            sums.own[step, :, at : at + wide] = terms[:own]
            stage[slot, :, at : at + wide] = terms[own:]
        sums.given(step, stage.at[slot]).start()

    terms_of(0)
    sums.advance(0)

    @pl.loop(0, grads.tiles)
    def _(tile):
        slot = lax.rem(tile, 2)

        @pl.when(tile + 1 < grads.tiles)
        def _():
            for go in tile_loads(tile + 1):
                go.start()

        for go in tile_loads(tile):
            go.wait()
        values = jnp.concatenate(
            [tn(tiles[slot, 0], dp_ref[...]), tn(tiles[slot, 1], dr_ref[...])], axis=1
        )
        grads.put(tile, values)

        @pl.when(tile + 1 < pairs)
        def _():
            terms_of(tile + 1)

        @pl.when((lax.rem(tile, 4) == 3) & (tile // 4 + 1 < pairs))
        def _():
            sums.advance(tile // 4 + 1)

    @pl.loop(1 + grads.tiles // 4, pairs)
    def _(step):
        sums.advance(step)

    grads.finish()
    for step in (pairs - 2, pairs - 1):
        sums.given(step, stage.at[step % 2]).wait_send()
    sums.finish()
    feed.finish()


def project_back(dp, w_qkv, a_low, heads, dr_cols, grad_feed, own, count, groups, ident):
    tokens, pairs = dp.shape[0], count // 2
    width = 3 * HD + dr_cols.shape[1]
    inside, anywhere = pl.BlockSpec(memory_space=pltpu.VMEM), pl.BlockSpec(memory_space=pl.ANY)
    return pl.pallas_call(
        functools.partial(project_kernel, count, groups),
        in_specs=[inside, inside, anywhere, anywhere, inside, anywhere],
        out_specs=[inside, inside, anywhere],
        out_shape=[
            jax.ShapeDtypeStruct((own, D), F32),
            jax.ShapeDtypeStruct((D // groups // ROWS, ROWS, width), BF),
            jax.ShapeDtypeStruct(grad_feed.shape, BF),
        ],
        scratch_shapes=[
            pltpu.VMEM((2, own, D), BF),
            pltpu.VMEM((2, 2, tokens, ROWS), BF),
        ]
        + RingSum.scratch(pairs, own)
        + GroupSum.scratch(groups, width)
        + [pltpu.SemaphoreType.DMA((2, 1 + ROWS // HD))]
        + Exchange.scratch(count),
        compiler_params=vmem(collective_id=ident, has_side_effects=True),
        cost_estimate=pl.CostEstimate(
            flops=4 * tokens * D * 3 * HD, bytes_accessed=200_000_000, transcendentals=0
        ),
        name="project_back",
    )(dp, w_qkv, a_low, heads, dr_cols, grad_feed)


def norm_parts(values):
    centre = values - jnp.mean(values, axis=-1, keepdims=True)
    inverse = lax.rsqrt(jnp.mean(centre * centre, axis=-1, keepdims=True) + LN_EPS)
    return centre * inverse, inverse


def qkv_kernel(x_ref, w_ref, vec_ref, cos_ref, sin_ref, a_ref, q_ref, k_ref, v_ref):
    normal, _ = norm_parts(x_ref[...].astype(F32))
    low = (normal * vec_ref[0:1, :] + vec_ref[1:2, :]).astype(BF)
    a_ref[...] = low
    projected = nn(low, w_ref[...])
    for index, ref in enumerate((q_ref, k_ref)):
        part = projected[:, index * HD : (index + 1) * HD]
        turned = part * cos_ref[...] + pltpu.roll(part, HD // 2, 1) * sin_ref[...]
        ref[...] = turned.astype(BF)
    v_ref[...] = projected[:, 2 * HD :].astype(BF)


def norm_and_project(states, w_qkv, vectors, cosine, sine):
    tokens = states.shape[0]
    whole = lambda shape: pl.BlockSpec(shape, lambda i: (0, 0))
    rows = lambda width: pl.BlockSpec((ROWS, width), lambda i: (i, 0))
    return pl.pallas_call(
        qkv_kernel,
        grid=(tokens // ROWS,),
        in_specs=[rows(D), whole((D, 3 * HD)), whole(vectors.shape), rows(HD), rows(HD)],
        out_specs=[rows(D), rows(HD), rows(HD), rows(HD)],
        out_shape=[jax.ShapeDtypeStruct((tokens, D), BF)]
        + [jax.ShapeDtypeStruct((tokens, HD), BF) for _ in range(3)],
        compiler_params=vmem(),
        cost_estimate=pl.CostEstimate(
            flops=2 * tokens * D * 3 * HD, bytes_accessed=24_000_000, transcendentals=0
        ),
        name="norm_and_project",
    )(states, w_qkv, vectors, cosine, sine)


def seen(block, first_ref, last_ref, keys):
    query = block * ROWS + lax.broadcasted_iota(jnp.int32, (ROWS, ROWS), 0)
    return (query >= first_ref[keys]) & (query < last_ref[keys])


def attend_kernel(
    low_ref, high_ref, q_ref, k_ref, v_ref, first_ref, last_ref, o_ref, full_ref, log_ref, held
):
    block = pl.program_id(0)
    query = q_ref[...]
    scale = HD ** (-0.5)

    def score(keys, top):
        scores = nt(query, k_ref[keys]) * scale
        scores = jnp.where(seen(block, first_ref, last_ref, keys), scores, NEG_LARGE)
        held[keys] = scores
        return jnp.maximum(top, jnp.max(scores, axis=-1, keepdims=True))

    def add(keys, carry):
        total, out = carry
        weight = jnp.exp(held[keys] - top)
        total = total + jnp.sum(weight, axis=-1, keepdims=True)
        return total, out + nn(weight.astype(BF), v_ref[keys])

    low, high = low_ref[block], high_ref[block]
    top = lax.fori_loop(low, high, score, jnp.full((ROWS, 1), NEG_LARGE, F32))
    total, out = lax.fori_loop(
        low, high, add, (jnp.zeros((ROWS, 1), F32), jnp.zeros((ROWS, HD), F32))
    )
    out = out / total
    o_ref[...] = out.astype(BF)
    full_ref[...] = out
    log_ref[...] = jnp.broadcast_to(top + jnp.log(total), (ROWS, LANES))


def attend(query, key, value, spans):
    tokens = query.shape[0]
    blocks = tokens // ROWS
    first, last, low, high = spans
    rows = pl.BlockSpec((ROWS, HD), lambda i, *_: (i, 0))
    whole = lambda shape: pl.BlockSpec(shape, lambda i, *_: (0,) * len(shape))
    cut = lambda values: values.reshape(blocks, ROWS, HD)
    return pl.pallas_call(
        attend_kernel,
        grid_spec=pltpu.PrefetchScalarGridSpec(
            num_scalar_prefetch=2,
            grid=(blocks,),
            in_specs=[rows]
            + [whole((blocks, ROWS, HD)) for _ in range(2)]
            + [whole((blocks, 1, ROWS)) for _ in range(2)],
            out_specs=[rows, rows, rows],
            scratch_shapes=[pltpu.VMEM((blocks, ROWS, ROWS), F32)],
        ),
        out_shape=[
            jax.ShapeDtypeStruct((tokens, HD), BF),
            jax.ShapeDtypeStruct((tokens, HD), F32),
            jax.ShapeDtypeStruct((tokens, LANES), F32),
        ],
        compiler_params=vmem(),
        cost_estimate=pl.CostEstimate(
            flops=2 * tokens * tokens * HD, bytes_accessed=4_000_000, transcendentals=0
        ),
        name="attend",
    )(low, high, query, cut(key), cut(value), first, last)


def attend_back_kernel(
    low_ref,
    high_ref,
    q_ref,
    g_ref,
    full_ref,
    log_ref,
    k_ref,
    v_ref,
    first_ref,
    last_ref,
    cos_ref,
    sin_ref,
    o_ref,
    dk_ref,
    dv_ref,
):
    block = pl.program_id(0)
    blocks = pl.num_programs(0)
    scale = HD ** (-0.5)

    @pl.when(block == 0)
    def _():
        dk_ref[...] = jnp.zeros_like(dk_ref)
        dv_ref[...] = jnp.zeros_like(dv_ref)

    query, grad = q_ref[...], g_ref[...]
    inner = jnp.sum(grad.astype(F32) * full_ref[...], axis=-1, keepdims=True)
    log = log_ref[:, 0:1]

    def one(keys, total):
        scores = nt(query, k_ref[keys]) * scale
        scores = jnp.where(seen(block, first_ref, last_ref, keys), scores, NEG_LARGE)
        weight = jnp.exp(scores - log)
        slope = (weight * (nt(grad, v_ref[keys]) - inner)).astype(BF)
        dv_ref[keys] += tn(weight.astype(BF), grad)
        dk_ref[keys] += tn(slope, query)
        return total + nn(slope, k_ref[keys])

    total = lax.fori_loop(
        low_ref[block], high_ref[block], one, jnp.zeros((ROWS, HD), F32)
    )

    def turn_back(values, cosine, sine):
        values = (values * scale).astype(BF).astype(F32)
        return (values * cosine - pltpu.roll(values, HD // 2, 1) * sine).astype(BF)

    rows = pl.ds(pl.multiple_of(block * ROWS, ROWS), ROWS)
    o_ref[rows, 0:HD] = turn_back(total, cos_ref[rows, :], sin_ref[rows, :])

    @pl.when(block == blocks - 1)
    def _():
        for part in range(dk_ref.shape[0]):
            there = pl.ds(part * ROWS, ROWS)
            o_ref[there, HD : 2 * HD] = turn_back(
                dk_ref[part], cos_ref[there, :], sin_ref[there, :]
            )
            o_ref[there, 2 * HD :] = dv_ref[part].astype(BF)


def attend_back(query, key, value, grad, full, log, spans, cosine, sine):
    tokens = query.shape[0]
    blocks = tokens // ROWS
    first, last, low, high = spans
    rows = pl.BlockSpec((ROWS, HD), lambda i, *_: (i, 0))
    whole = lambda shape: pl.BlockSpec(shape, lambda i, *_: (0,) * len(shape))
    cut = lambda values: values.reshape(blocks, ROWS, HD)
    return pl.pallas_call(
        attend_back_kernel,
        grid_spec=pltpu.PrefetchScalarGridSpec(
            num_scalar_prefetch=2,
            grid=(blocks,),
            in_specs=[rows] * 4
            + [whole((blocks, ROWS, HD)) for _ in range(2)]
            + [whole((blocks, 1, ROWS)) for _ in range(2)]
            + [whole((tokens, HD)) for _ in range(2)],
            out_specs=whole((tokens, 3 * HD)),
            scratch_shapes=[pltpu.VMEM((blocks, ROWS, HD), F32) for _ in range(2)],
        ),
        out_shape=jax.ShapeDtypeStruct((tokens, 3 * HD), BF),
        compiler_params=vmem(),
        cost_estimate=pl.CostEstimate(
            flops=5 * tokens * tokens * HD, bytes_accessed=6_000_000, transcendentals=0
        ),
        name="attend_back",
    )(low, high, query, grad, full, log, cut(key), cut(value), first, last, cosine, sine)


def windows(at, span, count):
    total = 4 * D + 3 * FF + 4
    result = []
    for index in range(count):
        width = max(0, min(span, FF - index * span))
        begin = at + index * span
        turn = begin % LANES
        window = -(-(turn + width) // LANES) * LANES if width else 0
        window = min(window, (total - begin + turn) // LANES * LANES)
        result.append((begin - turn, window, turn, width))
    return result


FEED_AT = (4 * D, 4 * D + FF, 4 * D + 2 * FF)


def lay_out_kernel(count, span, m_ref, qkv_ref, out_ref, feed_ref):
    rows = m_ref.shape[0]
    for index in range(count):
        for part in range(3):
            at = part * D + index * HD
            qkv_ref[index, :, part * HD : (part + 1) * HD] = m_ref[:, at : at + HD].astype(BF)
    out_ref[...] = m_ref[:, 3 * D : 4 * D].astype(BF)
    column = lax.broadcasted_iota(jnp.int32, (rows, span), 1)
    for part, at in enumerate(FEED_AT):
        for index, (begin, window, turn, width) in enumerate(windows(at, span, count)):
            if width == 0:
                piece = jnp.zeros((rows, span), F32)
            else:
                piece = m_ref[:, begin : begin + window]
                if window < span:
                    piece = jnp.concatenate(
                        [piece, jnp.zeros((rows, span - window), F32)], axis=1
                    )
                if turn:
                    piece = pltpu.roll(piece, piece.shape[1] - turn, 1)
                piece = piece[:, :span]
                if width < span:
                    piece = jnp.where(column < width, piece, 0.0)
            feed_ref[index, :, part * span : (part + 1) * span] = piece.astype(BF)


def lay_out(master, count, span):
    rows = master.shape[0]
    inside = pl.BlockSpec(memory_space=pltpu.VMEM)
    return pl.pallas_call(
        functools.partial(lay_out_kernel, count, span),
        out_shape=[
            jax.ShapeDtypeStruct((count, rows, 3 * HD), BF),
            jax.ShapeDtypeStruct((rows, D), BF),
            jax.ShapeDtypeStruct((count, rows, 3 * span), BF),
        ],
        in_specs=[inside],
        out_specs=[inside] * 3,
        compiler_params=vmem(),
        cost_estimate=pl.CostEstimate(flops=0, bytes_accessed=10_000_000, transcendentals=0),
        name="lay_out",
    )(master)


STEP_COLS = 3072


def update_kernel(
    count, span, attn_ref, feed_ref, vec_ref, m_ref, f_ref, s_ref, a_ref, nm_ref, nf_ref, ns_ref, na_ref, grad
):
    rows = m_ref.shape[0]
    step = pl.program_id(0)
    total = 4 * D + 3 * FF + 4

    @pl.when(step == 0)
    def _():
        for index in range(count):
            for part in range(4):
                at = part * D + index * HD
                grad[:, at : at + HD] = attn_ref[index, :, part * HD : (part + 1) * HD].astype(F32)
        lane = lax.broadcasted_iota(jnp.int32, (rows, LANES), 1)
        tiles = span // LANES
        last = None
        for part, at in enumerate(FEED_AT):
            turn = at % LANES
            for tile in range(-(-(FF + turn) // LANES)):
                begin = at - turn + tile * LANES
                index, inner = divmod(tile, tiles)
                here = feed_ref[index, :, part * span + inner * LANES : part * span + (inner + 1) * LANES]
                here = here.astype(F32)
                if turn:
                    here = pltpu.roll(here, turn, 1)
                    before = last if tile == 0 else previous
                    value = here if before is None else jnp.where(lane < turn, before, here)
                    previous = here
                else:
                    value = here
                if begin + LANES <= total:
                    grad[:, begin : begin + LANES] = value
                    last = value
        edge = (total - 4) // LANES * LANES
        shift = (total - 4) % LANES
        both = jnp.concatenate([last, jnp.zeros_like(last)], axis=1)
        vec = jnp.concatenate([vec_ref[...], jnp.zeros_like(last)], axis=1)
        vec = pltpu.roll(vec, shift, 1)
        wide = lax.broadcasted_iota(jnp.int32, (rows, 2 * LANES), 1)
        both = jnp.where(wide < shift, both, vec)
        grad[:, edge : edge + 2 * LANES] = both

    begin = pl.multiple_of(step * STEP_COLS, LANES)
    g = grad[:, pl.ds(begin, STEP_COLS)]
    vector = step * STEP_COLS + lax.broadcasted_iota(jnp.int32, (1, STEP_COLS), 1) >= total - 4
    rate = jnp.where(vector, LR_VEC, LR_MAT)
    decay = jnp.where(vector, 0.0, DECAY_MAT)
    new_first = BETA_ONE * f_ref[...] + (1.0 - BETA_ONE) * g
    new_second = BETA_TWO * s_ref[...] + (1.0 - BETA_TWO) * g * g
    nf_ref[...] = new_first
    ns_ref[...] = new_second
    root = jnp.sqrt(new_second * (1.0 / (1.0 - BETA_TWO**STEP))) + ADAM_EPS
    corrected = new_first * (1.0 / (1.0 - BETA_ONE**STEP)) / root
    master = m_ref[...]
    new_master = master - rate * (corrected + decay * master)
    nm_ref[...] = new_master
    na_ref[...] = EMA_RATE * a_ref[...] + (1.0 - EMA_RATE) * new_master


def update(attn, feed, vec, master, first, second, average, span):
    count, rows = feed.shape[:2]
    columns = master.shape[1]
    steps = -(-columns // STEP_COLS)
    whole = lambda values: pl.BlockSpec(values.shape, lambda i: (0,) * values.ndim)
    cols = pl.BlockSpec((rows, STEP_COLS), lambda i: (0, i))
    return pl.pallas_call(
        functools.partial(update_kernel, count, span),
        grid=(steps,),
        in_specs=[whole(attn), whole(feed), whole(vec)] + [cols] * 4,
        out_specs=[cols] * 4,
        out_shape=[jax.ShapeDtypeStruct(master.shape, F32) for _ in range(4)],
        scratch_shapes=[pltpu.VMEM((rows, steps * STEP_COLS), F32)],
        compiler_params=vmem(),
        cost_estimate=pl.CostEstimate(flops=0, bytes_accessed=56_000_000, transcendentals=0),
        name="update",
    )(attn, feed, vec, master, first, second, average)


def chain_spans(lengths, prefix, padding, total):
    ends = jnp.cumsum(lengths, dtype=jnp.int32)
    starts = ends - lengths
    token = jnp.arange(total, dtype=jnp.int32)
    member = (token[:, None] >= starts[None, :]) & (token[:, None] < ends[None, :])
    pick = lambda values: jnp.sum(jnp.where(member, values[None, :], 0), axis=1, dtype=jnp.int32)
    start, end, pre, live = pick(starts), pick(ends), pick(prefix), pick(lengths - padding)
    place = token - start
    first = jnp.where(place < pre, start, token)
    first = jnp.where(place < live, first, 2 * total)
    blocks = total // ROWS
    low = start[::ROWS] // ROWS
    high = (end[ROWS - 1 :: ROWS] + ROWS - 1) // ROWS
    cut = lambda values: values.reshape(blocks, 1, ROWS)
    return (cut(first), cut(end), low, high), place


def rotary_tables(place):
    half = HD // 2
    freq = ROPE_BASE ** (-jnp.arange(half, dtype=F32) / half)
    angles = place.astype(F32)[:, None] * freq[None, :]
    cosine, sine = jnp.cos(angles), jnp.sin(angles)
    return jnp.concatenate([cosine, cosine], axis=1), jnp.concatenate([-sine, sine], axis=1)


def over_batch(block_of, own):
    count = lax.axis_size("batch")
    me = lax.axis_index("batch")
    arrived = [
        lax.ppermute(
            block_of(lax.rem(me + shift, count)),
            "batch",
            [(i, (i + shift) % count) for i in range(count)],
        )
        for shift in range(1, count)
    ]
    return functools.reduce(lambda total, part: total + part.astype(F32), arrived, own())


def to_rows(grad):
    blocks = grad.reshape(lax.axis_size("seq"), -1, grad.shape[-1])
    return lax.all_to_all(blocks, "seq", split_axis=0, concat_axis=0, tiled=True)


def vector_rows(sums):
    batch, seq = lax.axis_size("batch"), lax.axis_size("seq")
    me = lax.axis_index("batch")
    kinds = sums.shape[0]
    cut = sums.reshape(kinds, batch, seq, -1).transpose(2, 1, 0, 3)
    came = lax.all_to_all(cut, "seq", split_axis=0, concat_axis=0, tiled=True)
    totals = jnp.sum(came, axis=0)
    part = lambda place: lax.dynamic_index_in_dim(totals, place, 0, keepdims=False)
    return over_batch(part, lambda: part(me)).T


def on_device(hidden_in, cotangent, master, first, second, average, lengths, prefix, padding):
    groups, seq = lax.axis_size("batch"), lax.axis_size("seq")
    own = hidden_in.shape[0]
    tokens = own * seq
    rows = master.shape[0]
    span = -(-FF // (seq * LANES)) * LANES
    vec_cut = master[:, 4 * D + 3 * FF :].astype(BF).astype(F32).T
    vec_cut = jnp.pad(vec_cut, ((0, 8 - vec_cut.shape[0]), (0, LANES - rows)))[None]
    qkv_cut, out_cut, feed_cut = lay_out(master, seq, span)
    states, w_qkv, vectors = ring_gather(hidden_in, [qkv_cut, vec_cut], seq, 1)
    states = states.reshape(tokens, D)
    w_qkv = w_qkv.reshape(D, 3 * HD)
    vectors = vectors[..., :rows].transpose(2, 0, 1, 3).reshape(8, D)
    w_out = lax.all_gather(out_cut, ("batch", "seq"), axis=0, tiled=True)
    cot_all = lax.all_gather(cotangent, "seq", axis=0, tiled=True)

    spans, place = chain_spans(lengths[0], prefix[0], padding[0], tokens)
    cosine, sine = rotary_tables(place)
    a_low, query, key, value = norm_and_project(states, w_qkv, vectors, cosine, sine)
    attended, full, log = attend(query, key, value, spans)
    heads, w_feed, b_low, residual = gather_residual(
        attended, feed_cut, states, w_out, vectors, own, seq, 2
    )
    w_feed = w_feed.reshape(D, 3 * span)
    db_sum, out_sum, grad_feed = feed_forward(b_low, cot_all, w_feed, own, seq, groups, 3)
    grad_feed = grad_feed.reshape(seq, rows, 3 * span)
    gain_one, bias_one, gain_two, bias_two = (vectors[i][None, :] for i in range(4))

    def norm_back(normal, inverse, slope, gain):
        scaled = slope * gain
        back = inverse * (
            scaled
            - jnp.mean(scaled, axis=-1, keepdims=True)
            - normal * jnp.mean(scaled * normal, axis=-1, keepdims=True)
        )
        return back, jnp.stack([jnp.sum(slope * normal, axis=0), jnp.sum(slope, axis=0)])

    normal_two, inverse_two = norm_parts(residual)
    output = DEEP_ALPHA * (normal_two * gain_two + bias_two) + out_sum
    db = DEEP_ALPHA * cotangent.astype(F32) + db_sum
    dr, sums_two = norm_back(normal_two, inverse_two, db, gain_two)
    dr_low = dr.astype(BF)
    do = nt(dr_low, w_out).astype(BF)
    to_heads = lambda values: lax.all_to_all(
        values.reshape(own, seq, HD).transpose(1, 0, 2), "seq", split_axis=0, concat_axis=0, tiled=True
    ).reshape(tokens, HD)
    do_head = to_heads(do)
    dr_cols = to_heads(dr_low)

    dp = attend_back(query, key, value, do_head, full, log, spans, cosine, sine)
    da_sum, grad_attn, grad_feed = project_back(
        dp, w_qkv, a_low, heads, dr_cols, grad_feed, own, seq, groups, 4
    )
    grad_attn = to_rows(grad_attn)

    normal_one, inverse_one = norm_parts(hidden_in.astype(F32))
    da = DEEP_ALPHA * dr + da_sum
    input_grad, sums_one = norm_back(normal_one, inverse_one, da, gain_one)
    vector_grad = vector_rows(jnp.concatenate([sums_one, sums_two]))

    vector_grad = jnp.pad(vector_grad, ((0, 0), (0, LANES - vector_grad.shape[1])))
    updated = update(grad_attn, grad_feed, vector_grad, master, first, second, average, span)
    return (
        output.astype(BF),
        input_grad.astype(BF),
        *updated,
    )


def solution(mesh):
    spread = P(("batch", "seq"), None)
    return jax.shard_map(
        on_device,
        mesh=mesh,
        in_specs=(spread,) * 6 + (P("batch", None),) * 3,
        out_specs=(spread,) * 6,
        check_vma=False,
    )
```

```python
import functools
import math

import jax
import jax.numpy as jnp
from jax import lax
from jax.experimental import pallas as pl
from jax.experimental.pallas import tpu as pltpu
from jax.sharding import PartitionSpec as P

D = 2048
H = 16
HD = 128
FF = 5461
STEP = 10

DEEP_ALPHA = math.sqrt(48.0)
ROPE_BASE = 10000.0
NEG_LARGE = -1e30
LN_EPS = 1e-05
BETA_ONE = 0.9
BETA_TWO = 0.95
ADAM_EPS = 1e-08
LR_MAT = 0.01
LR_VEC = 0.2
DECAY_MAT = 0.1
EMA_RATE = 0.9

BF = jnp.bfloat16
F32 = jnp.float32
MESH = pl.DeviceIdType.MESH
ROWS = 256
KEYS = 512
LANES = 128
SUBS = 4
VMEM_BIG = 56 * 1024 * 1024


def nt(left, right):
    return lax.dot_general(left, right, (((1,), (1,)), ((), ())), preferred_element_type=F32)


def tn(left, right):
    return lax.dot_general(left, right, (((0,), (0,)), ((), ())), preferred_element_type=F32)


def nn(left, right):
    return jnp.dot(left, right, preferred_element_type=F32)


def vmem(limit=VMEM_BIG, **more):
    return pltpu.CompilerParams(vmem_limit_bytes=limit, **more)


class Ring:
    def __init__(self, count):
        self.pairs = count // 2
        self.batch, self.me = lax.axis_index("batch"), lax.axis_index("seq")
        self.core = lax.rem(self.me, 2)
        y, z = lax.rem(self.me // 2, 2), self.me // 4
        self.place = jnp.where(y == 0, z, self.pairs - 1 - z)
        self.sibling = self.me + 1 - 2 * self.core

    def at(self, steps, core=None):
        place = lax.rem(self.place + (1 - 2 * self.core) * steps + 4 * self.pairs, self.pairs)
        half = self.pairs // 2
        pair = jnp.where(place < half, 2 * place, 2 * (self.pairs - 1 - place) + 1)
        return pair * 2 + (self.core if core is None else core)

    def greet_all(self, count):
        barrier = pltpu.get_barrier_semaphore()
        groups = lax.axis_size("batch")
        for step in range(1, count):
            device = lax.rem(self.me + step, count)
            pl.semaphore_signal(barrier, inc=1, device_id=(self.batch, device), device_id_type=MESH)
        for shift in range(1, groups):
            group = lax.rem(self.batch + shift, groups)
            pl.semaphore_signal(barrier, inc=1, device_id=(group, self.me), device_id_type=MESH)
        pl.semaphore_wait(barrier, count + groups - 2)

    def greet_groups(self, groups):
        barrier = pltpu.get_barrier_semaphore()
        for device in (self.at(-1), self.sibling):
            pl.semaphore_signal(barrier, inc=1, device_id=(self.batch, device), device_id_type=MESH)
        for shift in range(1, groups):
            group = lax.rem(self.batch + shift, groups)
            pl.semaphore_signal(barrier, inc=1, device_id=(group, self.me), device_id_type=MESH)
        pl.semaphore_wait(barrier, 1 + groups)

    def greet_whole(self, count):
        barrier = pltpu.get_barrier_semaphore()
        total = count * lax.axis_size("batch")
        for step in range(1, total):
            flat = lax.rem(self.batch * count + self.me + step, total)
            there = (flat // count, lax.rem(flat, count))
            pl.semaphore_signal(barrier, inc=1, device_id=there, device_id_type=MESH)
        pl.semaphore_wait(barrier, total - 1)

    def copy(self, src, dst, send, recv, device):
        return pltpu.make_async_remote_copy(
            src_ref=src,
            dst_ref=dst,
            send_sem=send,
            recv_sem=recv,
            device_id=(self.batch, device),
            device_id_type=MESH,
        )


class Columns:
    def __init__(self, ring, count, src, out, sems):
        self.ring, self.count, self.src, self.out = ring, count, src, out
        self.send, self.recv, self.on_send, self.on_recv, self.own = sems
        self.groups = lax.axis_size("batch")

    def piece(self, device):
        return self.src.at[device] if self.src.shape[0] == self.count else self.src.at[0]

    def group(self, shift):
        return lax.rem(self.ring.batch + shift + self.groups, self.groups)

    def start(self):
        ring, sends = self.ring, []
        self.mine = pltpu.make_async_copy(
            self.piece(ring.me), self.out.at[ring.batch, ring.me], self.own
        )
        self.mine.start()
        for step in range(1, self.count):
            device = lax.rem(ring.me + step, self.count)
            go = ring.copy(
                self.piece(device),
                self.out.at[ring.batch, ring.me],
                self.send.at[step],
                self.recv.at[step],
                device,
            )
            go.start()
            sends.append(go)
        self.sends = sends + self.forward(0)

    def forward(self, step):
        ring, sends = self.ring, []
        device = lax.rem(ring.me - step + self.count, self.count)
        here = self.out.at[ring.batch, device]
        for shift in range(1, self.groups):
            go = pltpu.make_async_remote_copy(
                src_ref=self.piece(ring.me) if step == 0 else here,
                dst_ref=here,
                send_sem=self.on_send.at[shift - 1, step],
                recv_sem=self.on_recv.at[shift - 1, step],
                device_id=(self.group(shift), ring.me),
                device_id_type=MESH,
            )
            go.start()
            sends.append(go)
        return sends

    def pass_on(self, step):
        ring = self.ring
        device = lax.rem(ring.me - step + self.count, self.count)
        here = self.out.at[ring.batch, device]
        ring.copy(here, here, self.send.at[step], self.recv.at[step], device).wait_recv()
        self.sends += self.forward(step)

    def finish(self):
        ring = self.ring
        for step in range(self.count):
            device = lax.rem(ring.me - step + self.count, self.count)
            for shift in range(1, self.groups):
                here = self.out.at[self.group(-shift), device]
                pltpu.make_async_remote_copy(
                    src_ref=here,
                    dst_ref=here,
                    send_sem=self.on_send.at[shift - 1, step],
                    recv_sem=self.on_recv.at[shift - 1, step],
                    device_id=(self.group(shift), ring.me),
                    device_id_type=MESH,
                ).wait_recv()
        for go in self.sends:
            go.wait_send()
        self.mine.wait()


def pass_round(ring, count, x_ref, o_ref, sems, columns, work):
    ring_s, ring_r, sib_s, sib_r, own_sem = sems
    piece = x_ref.shape[0] // SUBS
    own = pltpu.make_async_copy(x_ref, o_ref.at[ring.me], own_sem)
    own.start()
    ring.greet_all(count)
    following, sends = ring.at(1), []
    ahead = 1
    for step in range(ring.pairs):
        block = ring.at(-step)
        for sub in range(SUBS):
            rows = pl.ds(sub * piece, piece)
            dst = o_ref.at[block].at[rows]
            src = x_ref.at[rows] if step == 0 else dst
            if step > 0:
                ring.copy(
                    dst, dst, ring_s.at[step - 1, sub], ring_r.at[step - 1, sub], following
                ).wait_recv()
            if step < ring.pairs - 1:
                go = ring.copy(src, dst, ring_s.at[step, sub], ring_r.at[step, sub], following)
                go.start()
                sends.append(go)
            go = ring.copy(src, dst, sib_s.at[step, sub], sib_r.at[step, sub], ring.sibling)
            go.start()
            sends.append(go)
        if step == 0:
            for column in columns:
                column.start()
            own.wait()
        else:
            upto = count if step == ring.pairs - 1 else min(count, 1 + 2 * step)
            for passed in range(ahead, max(ahead, upto)):
                for column in columns:
                    column.pass_on(passed)
            ahead = max(ahead, upto)
        other = ring.at(step, 1 - ring.core)
        for sub in range(SUBS):
            dst = o_ref.at[other].at[pl.ds(sub * piece, piece)]
            ring.copy(
                dst, dst, sib_s.at[step, sub], sib_r.at[step, sub], ring.sibling
            ).wait_recv()
        work(step, block, other)
    return sends


def gather_kernel(count, extra, x_ref, *refs):
    parts, (o_ref, *outs), sems = refs[:extra], refs[extra : 2 * extra + 1], refs[2 * extra + 1 :]
    ring = Ring(count)
    columns = [
        Columns(ring, count, parts[i], outs[i], sems[5 + 5 * i : 10 + 5 * i]) for i in range(extra)
    ]
    sends = pass_round(ring, count, x_ref, o_ref, sems[:5], columns, lambda *_: None)
    for go in sends:
        go.wait_send()
    for column in columns:
        column.finish()


def ring_gather(values, blocks, count, ident):
    pairs, groups = count // 2, lax.axis_size("batch")
    anywhere = pl.BlockSpec(memory_space=pl.ANY)
    return pl.pallas_call(
        functools.partial(gather_kernel, count, len(blocks)),
        out_shape=[jax.ShapeDtypeStruct((count,) + values.shape, values.dtype)]
        + [jax.ShapeDtypeStruct((groups, count) + b.shape[1:], b.dtype) for b in blocks],
        in_specs=[anywhere] * (1 + len(blocks)),
        out_specs=[anywhere] * (1 + len(blocks)),
        scratch_shapes=ring_sems(pairs) + column_sems(count, groups) * len(blocks),
        compiler_params=pltpu.CompilerParams(collective_id=ident, has_side_effects=True),
        cost_estimate=pl.CostEstimate(flops=0, bytes_accessed=150_000_000, transcendentals=0),
        name=f"ring_gather_{ident}",
    )(values, *blocks)


def ring_sems(pairs):
    return [pltpu.SemaphoreType.DMA((pairs, SUBS)) for _ in range(4)] + [pltpu.SemaphoreType.DMA]


def column_sems(count, groups):
    return [
        pltpu.SemaphoreType.DMA((count,)),
        pltpu.SemaphoreType.DMA((count,)),
        pltpu.SemaphoreType.DMA((groups, count)),
        pltpu.SemaphoreType.DMA((groups, count)),
        pltpu.SemaphoreType.DMA,
    ]


def residual_kernel(
    count,
    x_ref,
    part_ref,
    states_ref,
    w_ref,
    vec_ref,
    heads_ref,
    feed_ref,
    b_ref,
    own_ref,
    heads,
    w_out,
    total,
    states,
    low,
    w_sem,
    load_sem,
    store_sem,
    heads_sem,
    *sems,
):
    ring = Ring(count)
    tokens, own = total.shape[0], own_ref.shape[0]
    blocks = tokens // ROWS
    weights = pltpu.make_async_copy(w_ref, w_out, w_sem)
    weights.start()
    columns = [Columns(ring, count, part_ref, feed_ref, sems[5:10])]

    def rows_of(block):
        return pl.ds(pl.multiple_of(block * ROWS, ROWS), ROWS)

    def load(block):
        slot = lax.rem(block, 2)
        return pltpu.make_async_copy(
            states_ref.at[rows_of(block)], states.at[slot], load_sem.at[slot]
        )

    def store(block):
        slot = lax.rem(block, 2)
        return pltpu.make_async_copy(low.at[slot], b_ref.at[rows_of(block)], store_sem.at[slot])

    load(0).start()

    def begin():
        @pl.loop(0, blocks)
        def _(block):
            @pl.when(block + 1 < blocks)
            def _():
                load(block + 1).start()

            load(block).wait()
            normal, _ = norm_parts(states[lax.rem(block, 2)].astype(F32))
            total[rows_of(block), :] = DEEP_ALPHA * (normal * vec_ref[0:1, :] + vec_ref[1:2, :])

        weights.wait()

    def saves(step, block, other):
        return [
            pltpu.make_async_copy(heads.at[head], heads_ref.at[head], heads_sem.at[step, part])
            for part, head in enumerate((block, other))
        ]

    kept = []

    def work(step, block, other):
        if step == 0:
            begin()
        for go in saves(step, block, other):
            go.start()
            kept.append(go)
        wide = 512

        @pl.loop(0, blocks)
        def _(part):
            rows = rows_of(part)
            left = jnp.concatenate([heads[block, rows, :], heads[other, rows, :]], axis=1)
            for at in range(0, D, wide):
                right = jnp.concatenate(
                    [
                        w_out[pl.ds(pl.multiple_of(head * HD, HD), HD), at : at + wide]
                        for head in (block, other)
                    ],
                    axis=0,
                )
                total[rows, at : at + wide] += nn(left, right)

    sends = pass_round(ring, count, x_ref, heads, sems[:5], columns, work)

    @pl.loop(0, blocks)
    def _(block):
        @pl.when(block >= 2)
        def _():
            store(block - 2).wait()

        normal, _ = norm_parts(total[rows_of(block), :])
        low[lax.rem(block, 2)] = (normal * vec_ref[2:3, :] + vec_ref[3:4, :]).astype(BF)
        store(block).start()

    own_ref[...] = total[pl.ds(pl.multiple_of(ring.me * own, own), own), :]
    for block in (blocks - 2, blocks - 1):
        store(block).wait()
    for go in kept:
        go.wait()
    for go in sends:
        go.wait_send()
    for column in columns:
        column.finish()


def gather_residual(attended, feed_cut, states, w_out, vectors, own, count, ident):
    tokens = attended.shape[0]
    pairs, groups = count // 2, lax.axis_size("batch")
    inside, anywhere = pl.BlockSpec(memory_space=pltpu.VMEM), pl.BlockSpec(memory_space=pl.ANY)
    return pl.pallas_call(
        functools.partial(residual_kernel, count),
        out_shape=[
            jax.ShapeDtypeStruct((count, tokens, HD), BF),
            jax.ShapeDtypeStruct((groups,) + feed_cut.shape, BF),
            jax.ShapeDtypeStruct((tokens, D), BF),
            jax.ShapeDtypeStruct((own, D), F32),
        ],
        in_specs=[anywhere] * 4 + [inside],
        out_specs=[anywhere] * 3 + [inside],
        scratch_shapes=[
            pltpu.VMEM((count, tokens, HD), BF),
            pltpu.VMEM((D, D), BF),
            pltpu.VMEM((tokens, D), F32),
            pltpu.VMEM((2, ROWS, D), BF),
            pltpu.VMEM((2, ROWS, D), BF),
            pltpu.SemaphoreType.DMA,
            pltpu.SemaphoreType.DMA((2,)),
            pltpu.SemaphoreType.DMA((2,)),
            pltpu.SemaphoreType.DMA((pairs, 2)),
        ]
        + ring_sems(pairs)
        + column_sems(count, groups),
        compiler_params=vmem(collective_id=ident, has_side_effects=True),
        cost_estimate=pl.CostEstimate(
            flops=2 * tokens * D * D, bytes_accessed=200_000_000, transcendentals=0
        ),
        name="gather_residual",
    )(attended, feed_cut, states, w_out, vectors)


class RingSum:
    def __init__(self, ring, own, sib, got, sems, out):
        self.ring, self.own, self.sib, self.got, self.out = ring, own, sib, got, out
        self.ring_s, self.ring_r, self.sib_s, self.sib_r = sems
        self.piece = own.shape[1] // SUBS

    def given(self, step, src):
        return self.ring.copy(
            src, self.sib.at[step], self.sib_s.at[step], self.sib_r.at[step], self.ring.sibling
        )

    def passed(self, step, sub):
        rows = pl.ds(sub * self.piece, self.piece)
        return self.ring.copy(
            self.own.at[step].at[rows],
            self.got.at[step].at[rows],
            self.ring_s.at[step, sub],
            self.ring_r.at[step, sub],
            self.ring.at(1),
        )

    def advance(self, step):
        last = self.ring.pairs - 1
        self.given(step, self.sib.at[step]).wait_recv()
        for sub in range(SUBS):
            rows = pl.ds(sub * self.piece, self.piece)

            total = self.own[step, rows, :].astype(F32) + self.sib[step, rows, :].astype(F32)

            @pl.when(step == 0)
            def _():
                self.own[step, rows, :] = total.astype(BF)

            @pl.when(step > 0)
            def _():
                self.passed(step - 1, sub).wait_recv()
                more = total + self.got[step - 1, rows, :].astype(F32)

                @pl.when(step < last)
                def _():
                    self.own[step, rows, :] = more.astype(BF)

                @pl.when(step == last)
                def _():
                    self.out[rows, :] = more

            @pl.when(step < last)
            def _():
                self.passed(step, sub).start()

    def finish(self):
        @pl.loop(0, self.ring.pairs - 1)
        def _(step):
            for sub in range(SUBS):
                self.passed(step, sub).wait_send()

    @staticmethod
    def scratch(pairs, rows):
        return [pltpu.VMEM((pairs - late, rows, D), BF) for late in (0, 0, 1)] + [
            pltpu.SemaphoreType.DMA((pairs, SUBS)),
            pltpu.SemaphoreType.DMA((pairs, SUBS)),
            pltpu.SemaphoreType.DMA((pairs,)),
            pltpu.SemaphoreType.DMA((pairs,)),
        ]


class Exchange:
    def __init__(self, ring, count, src, out, sems):
        self.ring, self.count, self.src, self.out = ring, count, src, out
        self.send, self.recv, self.own = sems

    def copies(self):
        ring = self.ring
        for step in range(1, self.count):
            device = lax.rem(ring.me + step, self.count)
            yield ring.copy(
                self.src.at[device],
                self.out.at[ring.me],
                self.send.at[step],
                self.recv.at[step],
                device,
            )

    def start(self):
        pltpu.make_async_copy(self.src.at[self.ring.me], self.out.at[self.ring.me], self.own).start()
        for go in self.copies():
            go.start()

    def finish(self):
        for go in self.copies():
            go.wait()
        pltpu.make_async_copy(self.src.at[self.ring.me], self.out.at[self.ring.me], self.own).wait()

    @staticmethod
    def scratch(count):
        return [pltpu.SemaphoreType.DMA((count,)) for _ in range(2)] + [pltpu.SemaphoreType.DMA]


class Spread:
    def __init__(self, ring, count, groups, src, came, sems):
        self.ring, self.count, self.groups, self.src, self.came = ring, count, groups, src, came
        self.send, self.recv = sems
        self.total = count * groups
        self.shared = self.total // src.shape[0]

    def copies(self):
        me = self.ring.batch * self.count + self.ring.me
        for step in range(1, self.total):
            flat = lax.rem(me + step, self.total)
            yield pltpu.make_async_remote_copy(
                src_ref=self.src.at[flat // self.shared],
                dst_ref=self.came.at[step],
                send_sem=self.send.at[step],
                recv_sem=self.recv.at[step],
                device_id=(flat // self.count, lax.rem(flat, self.count)),
                device_id_type=MESH,
            )

    def start(self):
        for go in self.copies():
            go.start()
        me = self.ring.batch * self.count + self.ring.me
        self.came[0] = self.src[me // self.shared]

    def finish(self):
        total = self.came[0]
        for step, go in enumerate(self.copies(), 1):
            go.wait()
            total = total + self.came[step]
        return total

    @staticmethod
    def scratch(total):
        return [pltpu.SemaphoreType.DMA((total,)) for _ in range(2)]


class GroupSum:
    def __init__(self, ring, groups, sent, came, sems, out):
        self.ring, self.groups, self.sent, self.came, self.out = ring, groups, sent, came, out
        self.send, self.recv = sems
        self.tiles, self.each = D // ROWS, D // ROWS // groups

    def group(self, tile):
        return lax.rem(self.ring.batch + 1 + tile // self.each, self.groups)

    def column(self, tile):
        return (self.group(tile) * self.each + lax.rem(tile, self.each)) * ROWS

    def copy(self, tile):
        return pltpu.make_async_remote_copy(
            src_ref=self.sent.at[tile],
            dst_ref=self.came.at[tile],
            send_sem=self.send.at[tile],
            recv_sem=self.recv.at[tile],
            device_id=(self.group(tile), self.ring.me),
            device_id_type=MESH,
        )

    def put(self, tile, values):
        away = self.tiles - self.each

        @pl.when(tile < away)
        def _():
            self.sent[tile] = values.astype(BF)
            self.copy(tile).start()

        @pl.when(tile >= away)
        def _():
            self.out[tile - away] = values.astype(BF)

    def finish(self):
        @pl.loop(0, self.each)
        def _(tile):
            total = self.out[tile].astype(F32)
            for shift in range(self.groups - 1):
                self.copy(shift * self.each + tile).wait_recv()
                total = total + self.came[shift * self.each + tile].astype(F32)
            self.out[tile] = total.astype(BF)

        @pl.loop(0, self.tiles - self.each)
        def _(tile):
            self.copy(tile).wait_send()

    @staticmethod
    def scratch(groups, width):
        away = D // ROWS - D // ROWS // groups
        return [pltpu.VMEM((away, ROWS, width), BF) for _ in range(2)] + [
            pltpu.SemaphoreType.DMA((away,)) for _ in range(2)
        ]


def norm_back(normal, inverse, slope, gain):
    scaled = slope * gain
    back = inverse * (
        scaled
        - jnp.mean(scaled, axis=-1, keepdims=True)
        - normal * jnp.mean(scaled * normal, axis=-1, keepdims=True)
    )
    return back, jnp.sum(slope * normal, axis=0, keepdims=True), jnp.sum(slope, axis=0, keepdims=True)


def feed_kernel(
    count,
    groups,
    span,
    b_ref,
    cot_ref,
    w_ref,
    w_out_ref,
    res_ref,
    cot_own_ref,
    vec_ref,
    out_ref,
    grad_ref,
    dr_ref,
    vec_sum_ref,
    do_ref,
    dr_send,
    bs,
    cs,
    stage,
    h,
    du,
    tiles,
    db_ref,
    do_send,
    *rest,
):
    ring = Ring(count)
    own = out_ref.shape[0]
    sums = [
        RingSum(ring, *rest[7 * i : 7 * i + 3], rest[7 * i + 3 : 7 * i + 7], ref)
        for i, ref in enumerate((db_ref, out_ref))
    ]
    grads = GroupSum(ring, groups, rest[14], rest[15], rest[16:18], grad_ref)
    row_sem, tile_sem, w_sem = rest[18:21]
    exchange = Exchange(ring, count, do_send, do_ref, rest[21:24])
    pairs = ring.pairs

    def weights(index):
        held = (bs, cs)[index // 2 % 2].at[index % 2]
        rows = pl.ds(index * 2 * own, 2 * own)
        return pltpu.make_async_copy(w_out_ref.at[rows], held, w_sem.at[index % 4])


    def places(step):
        return ring.at(-1 - step) * own, ring.at(1 + step, 1 - ring.core) * own

    def row_loads(step):
        slot = lax.rem(step, 2)
        return [
            pltpu.make_async_copy(
                ref.at[pl.ds(pl.multiple_of(place, own), own)],
                held.at[slot, pl.ds(half * own, own)],
                row_sem.at[slot, 2 * which + half],
            )
            for which, (ref, held) in enumerate(((b_ref, bs), (cot_ref, cs)))
            for half, place in enumerate(places(step))
        ]

    def tile_loads(tile):
        slot = lax.rem(tile, 2)
        cols = pl.ds(pl.multiple_of(grads.column(tile), ROWS), ROWS)
        return [
            pltpu.make_async_copy(ref.at[:, cols], tiles.at[slot, which], tile_sem.at[slot, which])
            for which, ref in enumerate((b_ref, cot_ref))
        ]

    for go in row_loads(0):
        go.start()
    ring.greet_all(count)

    def feed(step):
        slot = lax.rem(step, 2)

        @pl.when(step + 1 < pairs)
        def _():
            for go in row_loads(step + 1):
                go.start()

        for go in row_loads(step):
            go.wait()
        gate = nn(bs[slot], w_ref[:, :span])
        up = nn(bs[slot], w_ref[:, span : 2 * span])
        slope = nn(cs[slot], w_ref[:, 2 * span :])
        coef = math.sqrt(2.0 / math.pi)
        square = gate * gate
        tanh = jnp.tanh(coef * gate * (1.0 + 0.044715 * square))
        half = 0.5 * (1.0 + tanh)
        gelu = gate * half
        gelu_slope = half + 0.5 * gate * (1.0 - tanh * tanh) * (coef * (1.0 + 3 * 0.044715 * square))
        hidden = (gelu * up).astype(BF)
        both = jnp.concatenate([slope * up * gelu_slope, slope * gelu], axis=1).astype(BF)
        for part, place in enumerate(places(step)):
            rows = pl.ds(pl.multiple_of(place, own), own)
            h[rows, :] = hidden[part * own : (part + 1) * own]
            du[rows, :] = both[part * own : (part + 1) * own]

        @pl.when(step >= 2)
        def _():
            for which, each in enumerate(sums):
                each.given(step - 2, stage.at[slot, which]).wait_send()

        wide = 512
        for which, (each, left, low, high) in enumerate(
            ((sums[0], both, 0, 2 * span), (sums[1], hidden, 2 * span, 3 * span))
        ):
            for at in range(0, D, wide):
                terms = nt(left, w_ref[at : at + wide, low:high]).astype(BF)
                each.own[step, :, at : at + wide] = terms[:own]
                stage[slot, which, :, at : at + wide] = terms[own:]
            each.given(step, stage.at[slot, which]).start()

    @pl.loop(0, pairs)
    def _(step):
        feed(step)

        @pl.when(lax.rem(step, 2) == 0)
        def _():
            sums[0].advance(step // 2)

    for go in tile_loads(0):
        go.start()
    for index in range(4):
        weights(index).start()

    @pl.loop(0, grads.tiles)
    def _(tile):
        slot = lax.rem(tile, 2)

        @pl.when(tile + 1 < grads.tiles)
        def _():
            for go in tile_loads(tile + 1):
                go.start()

        for go in tile_loads(tile):
            go.wait()
        values = jnp.concatenate([tn(tiles[slot, 0], du[...]), tn(tiles[slot, 1], h[...])], axis=1)
        grads.put(tile, values)
        later = pairs // 2 + tile // 3

        @pl.when((lax.rem(tile, 3) == 1) & (later < pairs))
        def _():
            sums[0].advance(later)

    passed = pairs // 2 + len([t for t in range(grads.tiles) if t % 3 == 1])

    @pl.loop(min(passed, pairs), pairs)
    def _(step):
        sums[0].advance(step)

    normal, inverse = norm_parts(res_ref[...])
    slope = DEEP_ALPHA * cot_own_ref[...].astype(F32) + db_ref[...]
    dr, gain_sum, bias_sum = norm_back(normal, inverse, slope, vec_ref[2:3, :])
    dr_ref[...] = dr
    vec_sum_ref[...] = jnp.concatenate([gain_sum, bias_sum], axis=0)
    dr_low = dr.astype(BF)
    for index in range(D // (2 * own)):
        weights(index).wait()
        do = nt(dr_low, (bs, cs)[index // 2 % 2][index % 2]).astype(BF)
        if (index + 4) * 2 * own < D:
            weights(index + 4).start()
        for part in range(0, 2 * own, HD):
            at = index * 2 * own + part
            do_send[at // HD] = do[:, part : part + HD]
            dr_send[at // HD] = dr_low[:, at : at + HD]
    exchange.start()

    @pl.loop(0, pairs)
    def _(step):
        sums[1].advance(step)

    exchange.finish()
    grads.finish()
    for step in (pairs - 2, pairs - 1):
        for which, each in enumerate(sums):
            each.given(step, stage.at[step % 2, which]).wait_send()
    for each in sums:
        each.finish()


def feed_forward(b_low, cot, w_feed, w_out, residual, cot_own, vectors, count, groups, ident):
    tokens, span, pairs = b_low.shape[0], w_feed.shape[1] // 3, count // 2
    own = residual.shape[0]
    inside, anywhere = pl.BlockSpec(memory_space=pltpu.VMEM), pl.BlockSpec(memory_space=pl.ANY)
    return pl.pallas_call(
        functools.partial(feed_kernel, count, groups, span),
        in_specs=[anywhere, anywhere, inside, anywhere, inside, inside, inside],
        out_specs=[inside] * 4 + [anywhere, inside],
        out_shape=[
            jax.ShapeDtypeStruct((own, D), F32),
            jax.ShapeDtypeStruct((D // groups // ROWS, ROWS, 3 * span), BF),
            jax.ShapeDtypeStruct((own, D), F32),
            jax.ShapeDtypeStruct((2, D), F32),
            jax.ShapeDtypeStruct((count, own, HD), BF),
            jax.ShapeDtypeStruct((count, own, HD), BF),
        ],
        scratch_shapes=[
            pltpu.VMEM((2, 2 * own, D), BF),
            pltpu.VMEM((2, 2 * own, D), BF),
            pltpu.VMEM((2, 2, own, D), BF),
            pltpu.VMEM((tokens, span), BF),
            pltpu.VMEM((tokens, 2 * span), BF),
            pltpu.VMEM((2, 2, tokens, ROWS), BF),
            pltpu.VMEM((own, D), F32),
            pltpu.VMEM((count, own, HD), BF),
        ]
        + RingSum.scratch(pairs, own) * 2
        + GroupSum.scratch(groups, 3 * span)
        + [pltpu.SemaphoreType.DMA((2, 4)), pltpu.SemaphoreType.DMA((2, 2)), pltpu.SemaphoreType.DMA((4,))]
        + Exchange.scratch(count),
        compiler_params=vmem(62 * 1024 * 1024, collective_id=ident, has_side_effects=True),
        cost_estimate=pl.CostEstimate(
            flops=18 * tokens * D * span, bytes_accessed=250_000_000, transcendentals=0
        ),
        name="feed_forward",
    )(b_low, cot, w_feed, w_out, residual, cot_own, vectors)


def project_kernel(
    count,
    groups,
    dp_ref,
    w_ref,
    a_ref,
    heads_ref,
    dr_ref,
    feed_ref,
    x_ref,
    dr_own_ref,
    vec_ref,
    vec_sum_ref,
    back_ref,
    grad_ref,
    feed_out_ref,
    vec_out_ref,
    stage,
    tiles,
    da_ref,
    vec_send,
    vec_came,
    *rest,
):
    ring = Ring(count)
    own = da_ref.shape[0]
    sums = RingSum(ring, *rest[:3], rest[3:7], da_ref)
    grads = GroupSum(ring, groups, rest[7], rest[8], rest[9:11], grad_ref)
    tile_sem = rest[11]
    feed = Exchange(ring, count, feed_ref, feed_out_ref, rest[12:15])
    spread = Spread(ring, count, groups, vec_send, vec_came, rest[15:17])
    pairs, width = ring.pairs, heads_ref.shape[2]

    def places(step):
        return ring.at(-1 - step) * own, ring.at(1 + step, 1 - ring.core) * own

    def tile_loads(tile):
        slot = lax.rem(tile, 2)
        begin = pl.multiple_of(grads.column(tile), ROWS)
        loads = [
            pltpu.make_async_copy(
                a_ref.at[:, pl.ds(begin, ROWS)], tiles.at[slot, 0], tile_sem.at[slot, 0]
            )
        ]
        for part in range(ROWS // width):
            loads.append(
                pltpu.make_async_copy(
                    heads_ref.at[begin // width + part],
                    tiles.at[slot, 1, :, pl.ds(part * width, width)],
                    tile_sem.at[slot, 1 + part],
                )
            )
        return loads

    for go in tile_loads(0):
        go.start()
    ring.greet_whole(count)
    feed.start()

    def terms_of(step):
        slot = lax.rem(step, 2)

        @pl.when(step >= 2)
        def _():
            sums.given(step - 2, stage.at[slot]).wait_send()

        left = jnp.concatenate(
            [dp_ref[pl.ds(pl.multiple_of(place, own), own), :] for place in places(step)], axis=0
        )
        wide = 512
        for at in range(0, D, wide):
            terms = nt(left, w_ref[at : at + wide, :]).astype(BF)
            sums.own[step, :, at : at + wide] = terms[:own]
            stage[slot, :, at : at + wide] = terms[own:]
        sums.given(step, stage.at[slot]).start()

    terms_of(0)
    sums.advance(0)

    @pl.loop(0, grads.tiles)
    def _(tile):
        slot = lax.rem(tile, 2)

        @pl.when(tile + 1 < grads.tiles)
        def _():
            for go in tile_loads(tile + 1):
                go.start()

        for go in tile_loads(tile):
            go.wait()
        values = jnp.concatenate(
            [tn(tiles[slot, 0], dp_ref[...]), tn(tiles[slot, 1], dr_ref[...])], axis=1
        )
        grads.put(tile, values)

        @pl.when(tile + 1 < pairs)
        def _():
            terms_of(tile + 1)

        @pl.when((lax.rem(tile, 4) == 3) & (tile // 4 + 1 < pairs))
        def _():
            sums.advance(tile // 4 + 1)

    @pl.loop(1 + grads.tiles // 4, pairs)
    def _(step):
        sums.advance(step)

    normal, inverse = norm_parts(x_ref[...].astype(F32))
    slope = DEEP_ALPHA * dr_own_ref[...] + da_ref[...]
    back, gain_sum, bias_sum = norm_back(normal, inverse, slope, vec_ref[0:1, :])
    back_ref[...] = back.astype(BF)
    kinds = [gain_sum, bias_sum, vec_sum_ref[0:1, :], vec_sum_ref[1:2, :]]
    for tile in range(D // LANES):
        for kind, values in enumerate(kinds):
            vec_send[tile, kind : kind + 1, :] = values[:, tile * LANES : (tile + 1) * LANES]
    spread.start()
    grads.finish()
    for step in (pairs - 2, pairs - 1):
        sums.given(step, stage.at[step % 2]).wait_send()
    sums.finish()
    vec_out_ref[...] = spread.finish()
    feed.finish()


def project_back(
    dp, w_qkv, a_low, heads, dr_cols, grad_feed, states, dr, vectors, vec_sums, count, groups, ident
):
    tokens, pairs = dp.shape[0], count // 2
    own, width = dr.shape[0], 3 * HD + dr_cols.shape[1]
    inside, anywhere = pl.BlockSpec(memory_space=pltpu.VMEM), pl.BlockSpec(memory_space=pl.ANY)
    return pl.pallas_call(
        functools.partial(project_kernel, count, groups),
        in_specs=[inside, inside, anywhere, anywhere, inside, anywhere] + [inside] * 4,
        out_specs=[inside, inside, anywhere, inside],
        out_shape=[
            jax.ShapeDtypeStruct((own, D), BF),
            jax.ShapeDtypeStruct((D // groups // ROWS, ROWS, width), BF),
            jax.ShapeDtypeStruct(grad_feed.shape, BF),
            jax.ShapeDtypeStruct((8, LANES), F32),
        ],
        scratch_shapes=[
            pltpu.VMEM((2, own, D), BF),
            pltpu.VMEM((2, 2, tokens, ROWS), BF),
            pltpu.VMEM((own, D), F32),
            pltpu.VMEM((D // LANES, 8, LANES), F32),
            pltpu.VMEM((count * groups, 8, LANES), F32),
        ]
        + RingSum.scratch(pairs, own)
        + GroupSum.scratch(groups, width)
        + [pltpu.SemaphoreType.DMA((2, 1 + ROWS // HD))]
        + Exchange.scratch(count)
        + Spread.scratch(count * groups),
        compiler_params=vmem(collective_id=ident, has_side_effects=True),
        cost_estimate=pl.CostEstimate(
            flops=4 * tokens * D * 3 * HD, bytes_accessed=200_000_000, transcendentals=0
        ),
        name="project_back",
    )(dp, w_qkv, a_low, heads, dr_cols, grad_feed, states, dr, vectors, vec_sums)


def norm_parts(values):
    centre = values - jnp.mean(values, axis=-1, keepdims=True)
    inverse = lax.rsqrt(jnp.mean(centre * centre, axis=-1, keepdims=True) + LN_EPS)
    return centre * inverse, inverse


def qkv_kernel(x_ref, w_ref, vec_ref, cos_ref, sin_ref, a_ref, q_ref, k_ref, v_ref, kt_ref, vt_ref):
    normal, _ = norm_parts(x_ref[...].astype(F32))
    low = (normal * vec_ref[0:1, :] + vec_ref[1:2, :]).astype(BF)
    a_ref[...] = low
    projected = nn(low, w_ref[...])
    for index, ref in enumerate((q_ref, k_ref)):
        part = projected[:, index * HD : (index + 1) * HD]
        turned = part * cos_ref[...] + pltpu.roll(part, HD // 2, 1) * sin_ref[...]
        ref[...] = turned.astype(BF)
    kt_ref[...] = turned.T.astype(BF)[None]
    v_ref[...] = projected[:, 2 * HD :].astype(BF)
    vt_ref[...] = projected[:, 2 * HD :].T.astype(BF)[None]


def norm_and_project(states, w_qkv, vectors, cosine, sine):
    tokens = states.shape[0]
    whole = lambda shape: pl.BlockSpec(shape, lambda i: (0, 0))
    rows = lambda width: pl.BlockSpec((ROWS, width), lambda i: (i, 0))
    turned = pl.BlockSpec((1, HD, ROWS), lambda i: (i * ROWS // KEYS, 0, i % (KEYS // ROWS)))
    return pl.pallas_call(
        qkv_kernel,
        grid=(tokens // ROWS,),
        in_specs=[rows(D), whole((D, 3 * HD)), whole(vectors.shape), rows(HD), rows(HD)],
        out_specs=[rows(D), rows(HD), rows(HD), rows(HD), turned, turned],
        out_shape=[jax.ShapeDtypeStruct((tokens, D), BF)]
        + [jax.ShapeDtypeStruct((tokens, HD), BF) for _ in range(3)]
        + [jax.ShapeDtypeStruct((tokens // KEYS, HD, KEYS), BF) for _ in range(2)],
        compiler_params=vmem(),
        cost_estimate=pl.CostEstimate(
            flops=2 * tokens * D * 3 * HD, bytes_accessed=24_000_000, transcendentals=0
        ),
        name="norm_and_project",
    )(states, w_qkv, vectors, cosine, sine)


def masked_scores(block, query, k_ref, first_ref, last_ref, keys):
    place = block * ROWS + lax.broadcasted_iota(jnp.int32, (1, LANES), 1)
    scores = nt(k_ref[keys], query) * HD ** (-0.5)
    parts = []
    for at in range(0, ROWS, LANES):
        seen = (place + at >= first_ref[keys]) & (place + at < last_ref[keys])
        parts.append(jnp.where(seen, scores[:, at : at + LANES], NEG_LARGE))
    return jnp.concatenate(parts, axis=1)


def attend_kernel(
    low_ref, high_ref, q_ref, k_ref, vt_ref, first_ref, last_ref, o_ref, full_ref, log_ref, held
):
    block = pl.program_id(0)
    query = q_ref[...]

    def score(keys, top):
        scores = masked_scores(block, query, k_ref, first_ref, last_ref, keys)
        held[keys] = scores
        return jnp.maximum(top, jnp.max(scores, axis=0, keepdims=True))

    def add(keys, carry):
        total, out = carry
        weight = jnp.exp(held[keys] - top)
        total = total + jnp.sum(weight, axis=0, keepdims=True)
        return total, out + nn(vt_ref[keys], weight.astype(BF))

    low, high = low_ref[block], high_ref[block]
    top = lax.fori_loop(low, high, score, jnp.full((1, ROWS), NEG_LARGE, F32))
    total, out = lax.fori_loop(
        low, high, add, (jnp.zeros((1, ROWS), F32), jnp.zeros((HD, ROWS), F32))
    )
    out = out / total
    o_ref[...] = out.T.astype(BF)
    full_ref[...] = out[None]
    log_ref[...] = (top + jnp.log(total))[None]


def attend(query, key, value_t, spans):
    tokens = query.shape[0]
    blocks, span = tokens // ROWS, tokens // KEYS
    first, last, low, high = spans
    rows = pl.BlockSpec((ROWS, HD), lambda i, *_: (i, 0))
    one = lambda shape: pl.BlockSpec((1,) + shape, lambda i, *_: (i, 0, 0))
    whole = lambda shape: pl.BlockSpec(shape, lambda i, *_: (0,) * len(shape))
    return pl.pallas_call(
        attend_kernel,
        grid_spec=pltpu.PrefetchScalarGridSpec(
            num_scalar_prefetch=2,
            grid=(blocks,),
            in_specs=[
                rows,
                whole((span, KEYS, HD)),
                whole((span, HD, KEYS)),
                whole((span, KEYS, LANES)),
                whole((span, KEYS, LANES)),
            ],
            out_specs=[rows, one((HD, ROWS)), one((1, ROWS))],
            scratch_shapes=[pltpu.VMEM((span, KEYS, ROWS), F32)],
        ),
        out_shape=[
            jax.ShapeDtypeStruct((tokens, HD), BF),
            jax.ShapeDtypeStruct((blocks, HD, ROWS), F32),
            jax.ShapeDtypeStruct((blocks, 1, ROWS), F32),
        ],
        compiler_params=vmem(),
        cost_estimate=pl.CostEstimate(
            flops=2 * tokens * tokens * HD, bytes_accessed=4_000_000, transcendentals=0
        ),
        name="attend",
    )(low, high, query, key.reshape(span, KEYS, HD), value_t, first, last)


def attend_back_kernel(
    low_ref,
    high_ref,
    q_ref,
    g_ref,
    full_ref,
    log_ref,
    k_ref,
    kt_ref,
    v_ref,
    first_ref,
    last_ref,
    cos_ref,
    sin_ref,
    o_ref,
    dk_ref,
    dv_ref,
):
    block = pl.program_id(0)
    blocks = pl.num_programs(0)
    scale = HD ** (-0.5)

    @pl.when(block == 0)
    def _():
        dk_ref[...] = jnp.zeros_like(dk_ref)
        dv_ref[...] = jnp.zeros_like(dv_ref)

    query, grad = q_ref[...], g_ref[...]
    inner = jnp.sum(grad.astype(F32).T * full_ref[0], axis=0, keepdims=True)
    log = log_ref[0]

    def one(keys, total):
        scores = masked_scores(block, query, k_ref, first_ref, last_ref, keys)
        weight = jnp.exp(scores - log)
        slope = (weight * (nt(v_ref[keys], grad) - inner)).astype(BF)
        dv_ref[keys] += nn(weight.astype(BF), grad)
        dk_ref[keys] += nn(slope, query)
        return total + nn(kt_ref[keys], slope)

    total = lax.fori_loop(low_ref[block], high_ref[block], one, jnp.zeros((HD, ROWS), F32))

    def turn_back(values, cosine, sine):
        values = (values * scale).astype(BF).astype(F32)
        return (values * cosine - pltpu.roll(values, HD // 2, 1) * sine).astype(BF)

    rows = pl.ds(pl.multiple_of(block * ROWS, ROWS), ROWS)
    o_ref[rows, 0:HD] = turn_back(total.T, cos_ref[rows, :], sin_ref[rows, :])

    @pl.when(block == blocks - 1)
    def _():
        for part in range(dk_ref.shape[0]):
            there = pl.ds(part * KEYS, KEYS)
            o_ref[there, HD : 2 * HD] = turn_back(
                dk_ref[part], cos_ref[there, :], sin_ref[there, :]
            )
            o_ref[there, 2 * HD :] = dv_ref[part].astype(BF)


def attend_back(query, key, key_t, value, grad, full, log, spans, cosine, sine):
    tokens = query.shape[0]
    blocks, span = tokens // ROWS, tokens // KEYS
    first, last, low, high = spans
    rows = pl.BlockSpec((ROWS, HD), lambda i, *_: (i, 0))
    one = lambda shape: pl.BlockSpec((1,) + shape, lambda i, *_: (i, 0, 0))
    whole = lambda shape: pl.BlockSpec(shape, lambda i, *_: (0,) * len(shape))
    return pl.pallas_call(
        attend_back_kernel,
        grid_spec=pltpu.PrefetchScalarGridSpec(
            num_scalar_prefetch=2,
            grid=(blocks,),
            in_specs=[
                rows,
                rows,
                one((HD, ROWS)),
                one((1, ROWS)),
                whole((span, KEYS, HD)),
                whole((span, HD, KEYS)),
                whole((span, KEYS, HD)),
                whole((span, KEYS, LANES)),
                whole((span, KEYS, LANES)),
                whole((tokens, HD)),
                whole((tokens, HD)),
            ],
            out_specs=whole((tokens, 3 * HD)),
            scratch_shapes=[pltpu.VMEM((span, KEYS, HD), F32) for _ in range(2)],
        ),
        out_shape=jax.ShapeDtypeStruct((tokens, 3 * HD), BF),
        compiler_params=vmem(),
        cost_estimate=pl.CostEstimate(
            flops=5 * tokens * tokens * HD, bytes_accessed=6_000_000, transcendentals=0
        ),
        name="attend_back",
    )(
        low,
        high,
        query,
        grad,
        full,
        log,
        key.reshape(span, KEYS, HD),
        key_t,
        value.reshape(span, KEYS, HD),
        first,
        last,
        cosine,
        sine,
    )


def windows(at, span, count):
    total = 4 * D + 3 * FF + 4
    result = []
    for index in range(count):
        width = max(0, min(span, FF - index * span))
        begin = at + index * span
        turn = begin % LANES
        window = -(-(turn + width) // LANES) * LANES if width else 0
        window = min(window, (total - begin + turn) // LANES * LANES)
        result.append((begin - turn, window, turn, width))
    return result


FEED_AT = (4 * D, 4 * D + FF, 4 * D + 2 * FF)


def lay_out_kernel(count, span, m_ref, qkv_ref, out_ref, feed_ref):
    rows = m_ref.shape[0]
    for index in range(count):
        for part in range(3):
            at = part * D + index * HD
            qkv_ref[index, :, part * HD : (part + 1) * HD] = m_ref[:, at : at + HD].astype(BF)
    out_ref[...] = m_ref[:, 3 * D : 4 * D].astype(BF)
    column = lax.broadcasted_iota(jnp.int32, (rows, span), 1)
    for part, at in enumerate(FEED_AT):
        for index, (begin, window, turn, width) in enumerate(windows(at, span, count)):
            if width == 0:
                piece = jnp.zeros((rows, span), F32)
            else:
                piece = m_ref[:, begin : begin + window]
                if window < span:
                    piece = jnp.concatenate(
                        [piece, jnp.zeros((rows, span - window), F32)], axis=1
                    )
                if turn:
                    piece = pltpu.roll(piece, piece.shape[1] - turn, 1)
                piece = piece[:, :span]
                if width < span:
                    piece = jnp.where(column < width, piece, 0.0)
            feed_ref[index, :, part * span : (part + 1) * span] = piece.astype(BF)


def lay_out(master, count, span):
    rows = master.shape[0]
    inside = pl.BlockSpec(memory_space=pltpu.VMEM)
    return pl.pallas_call(
        functools.partial(lay_out_kernel, count, span),
        out_shape=[
            jax.ShapeDtypeStruct((count, rows, 3 * HD), BF),
            jax.ShapeDtypeStruct((rows, D), BF),
            jax.ShapeDtypeStruct((count, rows, 3 * span), BF),
        ],
        in_specs=[inside],
        out_specs=[inside] * 3,
        compiler_params=vmem(),
        cost_estimate=pl.CostEstimate(flops=0, bytes_accessed=10_000_000, transcendentals=0),
        name="lay_out",
    )(master)


STEP_COLS = 2048


def tile_of_part(ref, part, at, begin, rows, span):
    turn = at % LANES
    index = (begin - at + turn) // LANES
    tiles = span // LANES

    def piece(index):
        if index < 0 or index * LANES >= FF:
            return None
        device, inner = divmod(index, tiles)
        low = part * span + inner * LANES
        values = ref[device, :, low : low + LANES].astype(F32)
        return pltpu.roll(values, turn, 1) if turn else values

    lane = lax.broadcasted_iota(jnp.int32, (rows, LANES), 1)
    here, before = piece(index), piece(index - 1) if turn else None
    if here is None:
        return before
    return here if before is None else jnp.where(lane < turn, before, here)


def feed_tile(begin, feed_ref, vec_ref, rows, span):
    lane = lax.broadcasted_iota(jnp.int32, (rows, LANES), 1)
    total = 4 * D + 3 * FF + 4
    value = None
    for part, at in enumerate(FEED_AT):
        if at < begin + LANES and at + FF > begin:
            piece = tile_of_part(feed_ref, part, at, begin, rows, span)
            value = piece if value is None else jnp.where(lane < at - begin, value, piece)
    if begin + LANES > total - 4:
        vec = pltpu.roll(vec_ref[...], (total - 4) % LANES, 1)
        value = vec if value is None else jnp.where(lane < total - 4 - begin, value, vec)
    return value


def update_kernel(first_step, steps, tile_at, sources, *refs):
    grads, (m_ref, f_ref, s_ref, a_ref), outs = refs[:sources], refs[sources : sources + 4], refs[-4:]
    nm_ref, nf_ref, ns_ref, na_ref = outs
    rows = m_ref.shape[0]
    total = 4 * D + 3 * FF + 4

    def one(begin, cols):
        g = tile_at(begin, *grads)
        rate, decay = LR_MAT, DECAY_MAT
        if begin + LANES > total - 4:
            vector = begin + lax.broadcasted_iota(jnp.int32, (1, LANES), 1) >= total - 4
            rate, decay = jnp.where(vector, LR_VEC, LR_MAT), jnp.where(vector, 0.0, DECAY_MAT)
        new_first = BETA_ONE * f_ref[:, cols] + (1.0 - BETA_ONE) * g
        new_second = BETA_TWO * s_ref[:, cols] + (1.0 - BETA_TWO) * g * g
        nf_ref[:, cols] = new_first
        ns_ref[:, cols] = new_second
        root = jnp.sqrt(new_second * (1.0 / (1.0 - BETA_TWO**STEP))) + ADAM_EPS
        corrected = new_first * (1.0 / (1.0 - BETA_ONE**STEP)) / root
        master = m_ref[:, cols]
        new_master = master - rate * (corrected + decay * master)
        nm_ref[:, cols] = new_master
        na_ref[:, cols] = EMA_RATE * a_ref[:, cols] + (1.0 - EMA_RATE) * new_master

    for step in range(steps):

        @pl.when(pl.program_id(0) == step)
        def _():
            for at in range(0, STEP_COLS, LANES):
                begin = (first_step + step) * STEP_COLS + at
                if begin < total:
                    one(begin, slice(at, at + LANES))


def update(grads, tile_at, state, first_step, steps, done=()):
    rows, columns = state[0].shape
    whole = lambda values: pl.BlockSpec(values.shape, lambda i: (0,) * values.ndim)
    cols = pl.BlockSpec((rows, STEP_COLS), lambda i: (0, first_step + i))
    return pl.pallas_call(
        functools.partial(update_kernel, first_step, steps, tile_at, len(grads)),
        grid=(steps,),
        in_specs=[whole(g) for g in grads]
        + [cols] * 4
        + [pl.BlockSpec(memory_space=pl.ANY)] * len(done),
        out_specs=[cols] * 4,
        out_shape=[jax.ShapeDtypeStruct((rows, columns), F32) for _ in range(4)],
        input_output_aliases={len(grads) + 4 + i: i for i in range(len(done))},
        compiler_params=vmem(),
        cost_estimate=pl.CostEstimate(
            flops=0, bytes_accessed=36 * rows * steps * STEP_COLS, transcendentals=0
        ),
        name=f"update_{first_step}",
    )(*grads, *state, *done)


def chain_spans(lengths, prefix, padding, total):
    ends = jnp.cumsum(lengths, dtype=jnp.int32)
    starts = ends - lengths
    token = jnp.arange(total, dtype=jnp.int32)
    member = (token[:, None] >= starts[None, :]) & (token[:, None] < ends[None, :])
    pick = lambda values: jnp.sum(jnp.where(member, values[None, :], 0), axis=1, dtype=jnp.int32)
    start, end, pre, live = pick(starts), pick(ends), pick(prefix), pick(lengths - padding)
    place = token - start
    first = jnp.where(place < pre, start, token)
    first = jnp.where(place < live, first, 2 * total)
    low = start[::ROWS] // KEYS
    high = (end[ROWS - 1 :: ROWS] + KEYS - 1) // KEYS
    cut = lambda values: jnp.broadcast_to(values[:, None], (total, LANES)).reshape(-1, KEYS, LANES)
    return (cut(first), cut(end), low, high), place


def rotary_tables(place):
    half = HD // 2
    freq = ROPE_BASE ** (-jnp.arange(half, dtype=F32) / half)
    angles = place.astype(F32)[:, None] * freq[None, :]
    cosine, sine = jnp.cos(angles), jnp.sin(angles)
    return jnp.concatenate([cosine, cosine], axis=1), jnp.concatenate([-sine, sine], axis=1)


def to_rows(grad):
    blocks = grad.reshape(lax.axis_size("seq"), -1, grad.shape[-1])
    return lax.all_to_all(blocks, "seq", split_axis=0, concat_axis=0, tiled=True)


def on_device(hidden_in, cotangent, master, first, second, average, lengths, prefix, padding):
    groups, seq = lax.axis_size("batch"), lax.axis_size("seq")
    own = hidden_in.shape[0]
    tokens = own * seq
    rows = master.shape[0]
    span = -(-FF // (seq * LANES)) * LANES
    vec_cut = master[:, 4 * D + 3 * FF :].astype(BF).astype(F32).T
    vec_cut = jnp.pad(vec_cut, ((0, 8 - vec_cut.shape[0]), (0, LANES - rows)))[None]
    qkv_cut, out_cut, feed_cut = lay_out(master, seq, span)
    states, w_qkv, vectors = ring_gather(hidden_in, [qkv_cut, vec_cut], seq, 1)
    states = states.reshape(tokens, D)
    w_qkv = w_qkv.reshape(D, 3 * HD)
    vectors = vectors[..., :rows].transpose(2, 0, 1, 3).reshape(8, D)
    w_out = lax.all_gather(out_cut, ("batch", "seq"), axis=0, tiled=True)
    cot_all = lax.all_gather(cotangent, "seq", axis=0, tiled=True)

    spans, place = chain_spans(lengths[0], prefix[0], padding[0], tokens)
    cosine, sine = rotary_tables(place)
    a_low, query, key, value, key_t, value_t = norm_and_project(states, w_qkv, vectors, cosine, sine)
    attended, full, log = attend(query, key, value_t, spans)
    heads, w_feed, b_low, residual = gather_residual(
        attended, feed_cut, states, w_out, vectors, own, seq, 2
    )
    w_feed = w_feed.reshape(D, 3 * span)
    out_sum, grad_feed, dr, vec_sums, do, dr_cut = feed_forward(
        b_low, cot_all, w_feed, w_out, residual, cotangent, vectors, seq, groups, 3
    )
    dr_cols = lax.all_to_all(dr_cut, "seq", split_axis=0, concat_axis=0, tiled=True)
    normal_two, _ = norm_parts(residual)
    output = DEEP_ALPHA * (normal_two * vectors[2:3] + vectors[3:4]) + out_sum

    dp = attend_back(query, key, key_t, value, do.reshape(tokens, HD), full, log, spans, cosine, sine)
    input_grad, grad_attn, grad_feed, grad_vec = project_back(
        dp,
        w_qkv,
        a_low,
        heads,
        dr_cols.reshape(tokens, HD),
        grad_feed.reshape(seq, rows, 3 * span),
        hidden_in,
        dr,
        vectors,
        vec_sums,
        seq,
        groups,
        4,
    )
    grad_attn = to_rows(grad_attn)
    place = lax.rem(lax.axis_index("batch") * seq + lax.axis_index("seq"), LANES // rows) * rows
    grad_vec = lax.dynamic_slice_in_dim(grad_vec, place, rows, 1)[:4].T
    grad_vec = jnp.pad(grad_vec, ((0, 0), (0, LANES - 4)))

    def attn_tile(begin, ref):
        part, index = divmod(begin // HD, seq)
        return ref[index, :, part * HD : (part + 1) * HD].astype(F32)

    def other_tile(begin, feed_ref, vec_ref):
        return feed_tile(begin, feed_ref, vec_ref, rows, span)

    state = (master, first, second, average)
    steps, attn_steps = -(-master.shape[1] // STEP_COLS), 4 * D // STEP_COLS
    updated = update([grad_feed, grad_vec], other_tile, state, attn_steps, steps - attn_steps)
    updated = update([grad_attn], attn_tile, state, 0, attn_steps, updated)
    return (
        output.astype(BF),
        input_grad,
        *updated,
    )


def solution(mesh):
    spread = P(("batch", "seq"), None)
    return jax.shard_map(
        on_device,
        mesh=mesh,
        in_specs=(spread,) * 6 + (P("batch", None),) * 3,
        out_specs=(spread,) * 6,
        check_vma=False,
    )
```

```python
import functools
import math

import jax
import jax.numpy as jnp
from jax import lax
from jax.experimental import pallas as pl
from jax.experimental.pallas import tpu as pltpu
from jax.sharding import PartitionSpec as P

D = 2048
H = 16
HD = 128
FF = 5461
STEP = 10

DEEP_ALPHA = math.sqrt(48.0)
ROPE_BASE = 10000.0
NEG_LARGE = -1e30
LN_EPS = 1e-05
BETA_ONE = 0.9
BETA_TWO = 0.95
ADAM_EPS = 1e-08
LR_MAT = 0.01
LR_VEC = 0.2
DECAY_MAT = 0.1
EMA_RATE = 0.9

BF = jnp.bfloat16
F32 = jnp.float32
MESH = pl.DeviceIdType.MESH
ROWS = 256
KEYS = 512
LANES = 128
SUBS = 4
VMEM_BIG = 56 * 1024 * 1024


def nt(left, right):
    return lax.dot_general(left, right, (((1,), (1,)), ((), ())), preferred_element_type=F32)


def tn(left, right):
    return lax.dot_general(left, right, (((0,), (0,)), ((), ())), preferred_element_type=F32)


def nn(left, right):
    return jnp.dot(left, right, preferred_element_type=F32)


def vmem(limit=VMEM_BIG, **more):
    return pltpu.CompilerParams(vmem_limit_bytes=limit, **more)


class Ring:
    def __init__(self, count):
        self.pairs = count // 2
        self.batch, self.me = lax.axis_index("batch"), lax.axis_index("seq")
        self.core = lax.rem(self.me, 2)
        y, z = lax.rem(self.me // 2, 2), self.me // 4
        self.place = jnp.where(y == 0, z, self.pairs - 1 - z)
        self.sibling = self.me + 1 - 2 * self.core

    def at(self, steps, core=None):
        place = lax.rem(self.place + (1 - 2 * self.core) * steps + 4 * self.pairs, self.pairs)
        half = self.pairs // 2
        pair = jnp.where(place < half, 2 * place, 2 * (self.pairs - 1 - place) + 1)
        return pair * 2 + (self.core if core is None else core)

    def greet_all(self, count):
        barrier = pltpu.get_barrier_semaphore()
        groups = lax.axis_size("batch")
        for step in range(1, count):
            device = lax.rem(self.me + step, count)
            pl.semaphore_signal(barrier, inc=1, device_id=(self.batch, device), device_id_type=MESH)
        for shift in range(1, groups):
            group = lax.rem(self.batch + shift, groups)
            pl.semaphore_signal(barrier, inc=1, device_id=(group, self.me), device_id_type=MESH)
        pl.semaphore_wait(barrier, count + groups - 2)

    def greet_groups(self, groups):
        barrier = pltpu.get_barrier_semaphore()
        for device in (self.at(-1), self.sibling):
            pl.semaphore_signal(barrier, inc=1, device_id=(self.batch, device), device_id_type=MESH)
        for shift in range(1, groups):
            group = lax.rem(self.batch + shift, groups)
            pl.semaphore_signal(barrier, inc=1, device_id=(group, self.me), device_id_type=MESH)
        pl.semaphore_wait(barrier, 1 + groups)

    def greet_whole(self, count):
        barrier = pltpu.get_barrier_semaphore()
        total = count * lax.axis_size("batch")
        for step in range(1, total):
            flat = lax.rem(self.batch * count + self.me + step, total)
            there = (flat // count, lax.rem(flat, count))
            pl.semaphore_signal(barrier, inc=1, device_id=there, device_id_type=MESH)
        pl.semaphore_wait(barrier, total - 1)

    def copy(self, src, dst, send, recv, device):
        return pltpu.make_async_remote_copy(
            src_ref=src,
            dst_ref=dst,
            send_sem=send,
            recv_sem=recv,
            device_id=(self.batch, device),
            device_id_type=MESH,
        )


class Columns:
    def __init__(self, ring, count, src, out, sems):
        self.ring, self.count, self.src, self.out = ring, count, src, out
        self.send, self.recv, self.on_send, self.on_recv, self.own = sems
        self.groups = lax.axis_size("batch")

    def piece(self, device):
        return self.src.at[device] if self.src.shape[0] == self.count else self.src.at[0]

    def group(self, shift):
        return lax.rem(self.ring.batch + shift + self.groups, self.groups)

    def start(self):
        ring, sends = self.ring, []
        self.mine = pltpu.make_async_copy(
            self.piece(ring.me), self.out.at[ring.batch, ring.me], self.own
        )
        self.mine.start()
        for step in range(1, self.count):
            device = lax.rem(ring.me + step, self.count)
            go = ring.copy(
                self.piece(device),
                self.out.at[ring.batch, ring.me],
                self.send.at[step],
                self.recv.at[step],
                device,
            )
            go.start()
            sends.append(go)
        self.sends = sends + self.forward(0)

    def forward(self, step):
        ring, sends = self.ring, []
        device = lax.rem(ring.me - step + self.count, self.count)
        here = self.out.at[ring.batch, device]
        for shift in range(1, self.groups):
            go = pltpu.make_async_remote_copy(
                src_ref=self.piece(ring.me) if step == 0 else here,
                dst_ref=here,
                send_sem=self.on_send.at[shift - 1, step],
                recv_sem=self.on_recv.at[shift - 1, step],
                device_id=(self.group(shift), ring.me),
                device_id_type=MESH,
            )
            go.start()
            sends.append(go)
        return sends

    def pass_on(self, step):
        ring = self.ring
        device = lax.rem(ring.me - step + self.count, self.count)
        here = self.out.at[ring.batch, device]
        ring.copy(here, here, self.send.at[step], self.recv.at[step], device).wait_recv()
        self.sends += self.forward(step)

    def finish(self):
        ring = self.ring
        for step in range(self.count):
            device = lax.rem(ring.me - step + self.count, self.count)
            for shift in range(1, self.groups):
                here = self.out.at[self.group(-shift), device]
                pltpu.make_async_remote_copy(
                    src_ref=here,
                    dst_ref=here,
                    send_sem=self.on_send.at[shift - 1, step],
                    recv_sem=self.on_recv.at[shift - 1, step],
                    device_id=(self.group(shift), ring.me),
                    device_id_type=MESH,
                ).wait_recv()
        for go in self.sends:
            go.wait_send()
        self.mine.wait()


def pass_round(ring, count, lag, x_ref, o_ref, sems, columns, work):
    ring_s, ring_r, sib_s, sib_r, own_sem = sems
    piece = x_ref.shape[0] // SUBS
    own = pltpu.make_async_copy(x_ref, o_ref.at[ring.me], own_sem)
    own.start()
    ring.greet_all(count)
    following, sends = ring.at(1), []
    ahead = 1

    def complete(step):
        if step == 0:
            own.wait()
        other = ring.at(step, 1 - ring.core)
        for sub in range(SUBS):
            dst = o_ref.at[other].at[pl.ds(sub * piece, piece)]
            ring.copy(
                dst, dst, sib_s.at[step, sub], sib_r.at[step, sub], ring.sibling
            ).wait_recv()
        work(ring.at(-step), other)

    for step in range(ring.pairs):
        block = ring.at(-step)
        for sub in range(SUBS):
            rows = pl.ds(sub * piece, piece)
            dst = o_ref.at[block].at[rows]
            src = x_ref.at[rows] if step == 0 else dst
            if step > 0:
                ring.copy(
                    dst, dst, ring_s.at[step - 1, sub], ring_r.at[step - 1, sub], following
                ).wait_recv()
            if step < ring.pairs - 1:
                go = ring.copy(src, dst, ring_s.at[step, sub], ring_r.at[step, sub], following)
                go.start()
                sends.append(go)
            go = ring.copy(src, dst, sib_s.at[step, sub], sib_r.at[step, sub], ring.sibling)
            go.start()
            sends.append(go)
        if step == 0:
            for column in columns:
                column.start()
        else:
            upto = count if step == ring.pairs - 1 else min(count, 1 + 2 * step)
            for passed in range(ahead, max(ahead, upto)):
                for column in columns:
                    column.pass_on(passed)
            ahead = max(ahead, upto)
        if step >= lag:
            complete(step - lag)
    for step in range(max(0, ring.pairs - lag), ring.pairs):
        complete(step)
    return sends


class Line:
    def __init__(self, ring, count):
        self.ring, self.length = ring, count // 4
        self.y, self.z = lax.rem(ring.me // 2, 2), ring.me // 4

    def nearest(self, index):
        order = [sorted(range(self.length), key=lambda q: (abs(q - z), q)) for z in range(self.length)]
        place = order[0][index] + 0 * self.z
        for z in range(1, self.length):
            place = jnp.where(self.z == z, order[z][index], place)
        return place

    def device(self, z, row=0, core=0):
        y = self.y if row == 0 else 1 - self.y
        return (z * 2 + y) * 2 + (self.ring.core if core == 0 else 1 - self.ring.core)


def pass_along(ring, count, x_ref, o_ref, sems, columns):
    line_s, line_r, over_s, over_r, sib_s, sib_r, own_sem = sems
    line = Line(ring, count)
    piece = x_ref.shape[0] // SUBS
    own = pltpu.make_async_copy(x_ref, o_ref.at[ring.me], own_sem)
    own.start()
    ring.greet_all(count)
    across = line.device(line.z, 1)
    sends = []

    def send(condition, src, dst, send_sem, recv_sem, device):
        go = ring.copy(src, dst, send_sem, recv_sem, device)
        if condition is None:
            go.start()
        else:
            pl.when(condition)(go.start)
        sends.append((condition, go))

    order = sorted(((row, index) for row in (0, 1) for index in range(line.length)), key=lambda p: (p[0] + p[1], p[0]))
    ahead = 1
    for turn, (row, index) in enumerate(order):
        z = line.nearest(index)
        block = line.device(z, row)
        for sub in range(SUBS):
            rows = pl.ds(sub * piece, piece)
            dst = o_ref.at[block].at[rows]
            first = row == 0 and index == 0
            src = x_ref.at[rows] if first else dst
            if row == 1:
                ring.copy(dst, dst, over_s.at[z, sub], over_r.at[z, sub], across).wait_recv()
            elif not first:
                ring.copy(dst, dst, line_s.at[0, z, sub], line_r.at[z, sub], across).wait_recv()
            if row == 0:
                if first:
                    for side, step in enumerate((1, -1)):
                        there = line.z + step
                        go_on = (there >= 0) & (there < line.length)
                        there = jnp.where(go_on, there, line.z - step)
                        send(go_on, src, dst, line_s.at[side, z, sub], line_r.at[z, sub], line.device(there))
                else:
                    there = jnp.where(z < line.z, line.z + 1, line.z - 1)
                    go_on = (there >= 0) & (there < line.length)
                    there = jnp.where(go_on, there, jnp.where(z < line.z, line.z - 1, line.z + 1))
                    send(go_on, src, dst, line_s.at[0, z, sub], line_r.at[z, sub], line.device(there))
                send(None, src, dst, over_s.at[z, sub], over_r.at[z, sub], across)
            send(None, src, dst, sib_s.at[row, z, sub], sib_r.at[row, z, sub], ring.sibling)
        if turn == 0:
            for column in columns:
                column.start()
        else:
            upto = count if turn == len(order) - 1 else min(count, 1 + 2 * turn)
            for passed in range(ahead, max(ahead, upto)):
                for column in columns:
                    column.pass_on(passed)
            ahead = max(ahead, upto)
    for row, index in order:
        z = line.nearest(index)
        other = line.device(z, row, 1)
        for sub in range(SUBS):
            dst = o_ref.at[other].at[pl.ds(sub * piece, piece)]
            ring.copy(
                dst, dst, sib_s.at[row, z, sub], sib_r.at[row, z, sub], ring.sibling
            ).wait_recv()
    own.wait()
    return sends


def wait_sends(sends):
    for condition, go in sends:
        if condition is None:
            go.wait_send()
        else:
            pl.when(condition)(go.wait_send)


def gather_kernel(count, extra, x_ref, *refs):
    parts, (o_ref, *outs), sems = refs[:extra], refs[extra : 2 * extra + 1], refs[2 * extra + 1 :]
    ring = Ring(count)
    columns = [
        Columns(ring, count, parts[i], outs[i], sems[7 + 5 * i : 12 + 5 * i]) for i in range(extra)
    ]
    wait_sends(pass_along(ring, count, x_ref, o_ref, sems[:7], columns))
    for column in columns:
        column.finish()


def ring_gather(values, blocks, count, ident):
    pairs, groups = count // 2, lax.axis_size("batch")
    anywhere = pl.BlockSpec(memory_space=pl.ANY)
    return pl.pallas_call(
        functools.partial(gather_kernel, count, len(blocks)),
        out_shape=[jax.ShapeDtypeStruct((count,) + values.shape, values.dtype)]
        + [jax.ShapeDtypeStruct((groups, count) + b.shape[1:], b.dtype) for b in blocks],
        in_specs=[anywhere] * (1 + len(blocks)),
        out_specs=[anywhere] * (1 + len(blocks)),
        scratch_shapes=line_sems(count) + column_sems(count, groups) * len(blocks),
        compiler_params=pltpu.CompilerParams(collective_id=ident, has_side_effects=True),
        cost_estimate=pl.CostEstimate(flops=0, bytes_accessed=150_000_000, transcendentals=0),
        name=f"ring_gather_{ident}",
    )(values, *blocks)


def ring_sems(pairs):
    return [pltpu.SemaphoreType.DMA((pairs, SUBS)) for _ in range(4)] + [pltpu.SemaphoreType.DMA]


def line_sems(count):
    dma = pltpu.SemaphoreType.DMA
    shapes = [(2, count // 4, SUBS)] + [(count // 4, SUBS)] * 3 + [(2, count // 4, SUBS)] * 2
    return [dma(shape) for shape in shapes] + [dma]


def column_sems(count, groups):
    return [
        pltpu.SemaphoreType.DMA((count,)),
        pltpu.SemaphoreType.DMA((count,)),
        pltpu.SemaphoreType.DMA((groups, count)),
        pltpu.SemaphoreType.DMA((groups, count)),
        pltpu.SemaphoreType.DMA,
    ]


def residual_kernel(
    count,
    x_ref,
    feed_ref,
    states_ref,
    w_ref,
    vec_ref,
    heads_ref,
    feed_far_ref,
    b_ref,
    own_ref,
    heads,
    w_out,
    total,
    states,
    low,
    w_sem,
    load_sem,
    store_sem,
    heads_sem,
    *sems,
):
    ring = Ring(count)
    tokens, own = total.shape[0], own_ref.shape[0]
    blocks = tokens // ROWS
    weights = pltpu.make_async_copy(w_ref, w_out, w_sem)
    weights.start()
    groups = lax.axis_size("batch")

    def onward(shift):
        return pltpu.make_async_remote_copy(
            src_ref=feed_ref,
            dst_ref=feed_far_ref.at[shift - 1],
            send_sem=sems[5].at[shift - 1],
            recv_sem=sems[6].at[shift - 1],
            device_id=(lax.rem(ring.batch + shift, groups), ring.me),
            device_id_type=MESH,
        )

    def rows_of(block):
        return pl.ds(pl.multiple_of(block * ROWS, ROWS), ROWS)

    def load(block):
        slot = lax.rem(block, 2)
        return pltpu.make_async_copy(
            states_ref.at[rows_of(block)], states.at[slot], load_sem.at[slot]
        )

    def store(block):
        slot = lax.rem(block, 2)
        return pltpu.make_async_copy(low.at[slot], b_ref.at[rows_of(block)], store_sem.at[slot])

    load(0).start()

    kept, waiting = [], []

    def add(group, first, last):
        wide = 512

        @pl.loop(0, blocks)
        def _(block):
            rows = rows_of(block)
            left = jnp.concatenate([heads[head, rows, :] for head in group], axis=1)
            if first:

                @pl.when(block + 1 < blocks)
                def _():
                    load(block + 1).start()

                load(block).wait()
                normal, _ = norm_parts(states[lax.rem(block, 2)].astype(F32))
                total[rows, :] = DEEP_ALPHA * (normal * vec_ref[0:1, :] + vec_ref[1:2, :])
            for at in range(0, D, wide):
                right = [
                    w_out[pl.ds(pl.multiple_of(head * HD, HD), HD), at : at + wide]
                    for head in group
                ]
                total[rows, at : at + wide] += nn(left, jnp.concatenate(right, axis=0))
            if last:

                @pl.when(block >= 2)
                def _():
                    store(block - 2).wait()

                normal, _ = norm_parts(total[rows, :])
                low[lax.rem(block, 2)] = (normal * vec_ref[2:3, :] + vec_ref[3:4, :]).astype(BF)
                store(block).start()

    def work(block, other):
        turn, turns = len(kept) // 2, count // 2
        if turn == 0:
            for shift in range(1, groups):
                onward(shift).start()
        for part, head in enumerate((block, other)):
            go = pltpu.make_async_copy(heads.at[head], heads_ref.at[head], heads_sem.at[turn, part])
            go.start()
            kept.append(go)
            waiting.append(head)
        if turn == 1:
            weights.wait()
        if turn == turns - 1 or turn in (1, turns // 2, turns - 2):
            add(list(waiting), turn == 1, turn == turns - 1)
            waiting.clear()

    sends = pass_round(ring, count, 2, x_ref, heads, sems[:5], [], work)

    own_ref[...] = total[pl.ds(pl.multiple_of(ring.me * own, own), own), :]
    for block in (blocks - 2, blocks - 1):
        store(block).wait()
    for go in kept:
        go.wait()
    for go in sends:
        go.wait_send()
    for shift in range(1, groups):
        onward(shift).wait()


def gather_residual(attended, feed_own, states, w_out, vectors, own, count, ident):
    tokens = attended.shape[0]
    pairs, groups = count // 2, lax.axis_size("batch")
    inside, anywhere = pl.BlockSpec(memory_space=pltpu.VMEM), pl.BlockSpec(memory_space=pl.ANY)
    return pl.pallas_call(
        functools.partial(residual_kernel, count),
        out_shape=[
            jax.ShapeDtypeStruct((count, tokens, HD), BF),
            jax.ShapeDtypeStruct((groups - 1,) + feed_own.shape, BF),
            jax.ShapeDtypeStruct((tokens, D), BF),
            jax.ShapeDtypeStruct((own, D), F32),
        ],
        in_specs=[anywhere] * 4 + [inside],
        out_specs=[anywhere] * 3 + [inside],
        scratch_shapes=[
            pltpu.VMEM((count, tokens, HD), BF),
            pltpu.VMEM((D, D), BF),
            pltpu.VMEM((tokens, D), F32),
            pltpu.VMEM((2, ROWS, D), BF),
            pltpu.VMEM((2, ROWS, D), BF),
            pltpu.SemaphoreType.DMA,
            pltpu.SemaphoreType.DMA((2,)),
            pltpu.SemaphoreType.DMA((2,)),
            pltpu.SemaphoreType.DMA((pairs, 2)),
        ]
        + ring_sems(pairs)
        + [pltpu.SemaphoreType.DMA((max(1, groups - 1),)) for _ in range(2)],
        compiler_params=vmem(collective_id=ident, has_side_effects=True),
        cost_estimate=pl.CostEstimate(
            flops=2 * tokens * D * D, bytes_accessed=200_000_000, transcendentals=0
        ),
        name="gather_residual",
    )(attended, feed_own, states, w_out, vectors)


class RingSum:
    def __init__(self, ring, own, sib, got, sems, out):
        self.ring, self.own, self.sib, self.got, self.out = ring, own, sib, got, out
        self.ring_s, self.ring_r, self.sib_s, self.sib_r = sems
        self.piece = own.shape[1] // SUBS

    def given(self, step, src):
        return self.ring.copy(
            src, self.sib.at[step], self.sib_s.at[step], self.sib_r.at[step], self.ring.sibling
        )

    def passed(self, step, sub):
        rows = pl.ds(sub * self.piece, self.piece)
        return self.ring.copy(
            self.own.at[step].at[rows],
            self.got.at[step].at[rows],
            self.ring_s.at[step, sub],
            self.ring_r.at[step, sub],
            self.ring.at(1),
        )

    def advance(self, step):
        last = self.ring.pairs - 1
        self.given(step, self.sib.at[step]).wait_recv()
        for sub in range(SUBS):
            rows = pl.ds(sub * self.piece, self.piece)

            total = self.own[step, rows, :].astype(F32) + self.sib[step, rows, :].astype(F32)

            @pl.when(step == 0)
            def _():
                self.own[step, rows, :] = total.astype(BF)

            @pl.when(step > 0)
            def _():
                self.passed(step - 1, sub).wait_recv()
                more = total + self.got[step - 1, rows, :].astype(F32)

                @pl.when(step < last)
                def _():
                    self.own[step, rows, :] = more.astype(BF)

                @pl.when(step == last)
                def _():
                    self.out[rows, :] = more

            @pl.when(step < last)
            def _():
                self.passed(step, sub).start()

    def finish(self):
        @pl.loop(0, self.ring.pairs - 1)
        def _(step):
            for sub in range(SUBS):
                self.passed(step, sub).wait_send()

    @staticmethod
    def scratch(pairs, rows):
        return [pltpu.VMEM((pairs - late, rows, D), BF) for late in (0, 0, 1)] + [
            pltpu.SemaphoreType.DMA((pairs, SUBS)),
            pltpu.SemaphoreType.DMA((pairs, SUBS)),
            pltpu.SemaphoreType.DMA((pairs,)),
            pltpu.SemaphoreType.DMA((pairs,)),
        ]


class Exchange:
    def __init__(self, ring, count, src, out, sems):
        self.ring, self.count, self.src, self.out = ring, count, src, out
        self.send, self.recv, self.own = sems

    def copies(self):
        ring = self.ring
        for step in range(1, self.count):
            device = lax.rem(ring.me + step, self.count)
            yield ring.copy(
                self.src.at[device],
                self.out.at[ring.me],
                self.send.at[step],
                self.recv.at[step],
                device,
            )

    def start(self):
        pltpu.make_async_copy(self.src.at[self.ring.me], self.out.at[self.ring.me], self.own).start()
        for go in self.copies():
            go.start()

    def finish(self):
        for go in self.copies():
            go.wait()
        pltpu.make_async_copy(self.src.at[self.ring.me], self.out.at[self.ring.me], self.own).wait()

    @staticmethod
    def scratch(count):
        return [pltpu.SemaphoreType.DMA((count,)) for _ in range(2)] + [pltpu.SemaphoreType.DMA]


class Spread:
    def __init__(self, ring, count, groups, src, came, sems):
        self.ring, self.count, self.groups, self.src, self.came = ring, count, groups, src, came
        self.send, self.recv = sems
        self.total = count * groups
        self.shared = self.total // src.shape[0]

    def copies(self):
        me = self.ring.batch * self.count + self.ring.me
        for step in range(1, self.total):
            flat = lax.rem(me + step, self.total)
            yield pltpu.make_async_remote_copy(
                src_ref=self.src.at[flat // self.shared],
                dst_ref=self.came.at[step],
                send_sem=self.send.at[step],
                recv_sem=self.recv.at[step],
                device_id=(flat // self.count, lax.rem(flat, self.count)),
                device_id_type=MESH,
            )

    def start(self):
        for go in self.copies():
            go.start()
        me = self.ring.batch * self.count + self.ring.me
        self.came[0] = self.src[me // self.shared]

    def finish(self):
        total = self.came[0]
        for step, go in enumerate(self.copies(), 1):
            go.wait()
            total = total + self.came[step]
        return total

    @staticmethod
    def scratch(total):
        return [pltpu.SemaphoreType.DMA((total,)) for _ in range(2)]


class GroupSum:
    def __init__(self, ring, groups, sent, came, sems, out):
        self.ring, self.groups, self.sent, self.came, self.out = ring, groups, sent, came, out
        self.send, self.recv = sems
        self.tiles, self.each = D // ROWS, D // ROWS // groups

    def group(self, tile):
        return lax.rem(self.ring.batch + 1 + tile // self.each, self.groups)

    def column(self, tile):
        return (self.group(tile) * self.each + lax.rem(tile, self.each)) * ROWS

    def copy(self, tile):
        return pltpu.make_async_remote_copy(
            src_ref=self.sent.at[tile],
            dst_ref=self.came.at[tile],
            send_sem=self.send.at[tile],
            recv_sem=self.recv.at[tile],
            device_id=(self.group(tile), self.ring.me),
            device_id_type=MESH,
        )

    def put(self, tile, values):
        away = self.tiles - self.each

        @pl.when(tile < away)
        def _():
            self.sent[tile] = values.astype(BF)
            self.copy(tile).start()

        @pl.when(tile >= away)
        def _():
            self.out[tile - away] = values.astype(BF)

    def finish(self):
        @pl.loop(0, self.each)
        def _(tile):
            total = self.out[tile].astype(F32)
            for shift in range(self.groups - 1):
                self.copy(shift * self.each + tile).wait_recv()
                total = total + self.came[shift * self.each + tile].astype(F32)
            self.out[tile] = total.astype(BF)

        @pl.loop(0, self.tiles - self.each)
        def _(tile):
            self.copy(tile).wait_send()

    @staticmethod
    def scratch(groups, width):
        away = D // ROWS - D // ROWS // groups
        return [pltpu.VMEM((away, ROWS, width), BF) for _ in range(2)] + [
            pltpu.SemaphoreType.DMA((away,)) for _ in range(2)
        ]


def norm_back(normal, inverse, slope, gain):
    scaled = slope * gain
    back = inverse * (
        scaled
        - jnp.mean(scaled, axis=-1, keepdims=True)
        - normal * jnp.mean(scaled * normal, axis=-1, keepdims=True)
    )
    return back, jnp.sum(slope * normal, axis=0, keepdims=True), jnp.sum(slope, axis=0, keepdims=True)


def feed_kernel(
    count,
    groups,
    span,
    b_ref,
    cot_ref,
    feed_own_ref,
    feed_far_ref,
    w_out_ref,
    res_ref,
    cot_own_ref,
    vec_ref,
    out_ref,
    grad_ref,
    dr_ref,
    vec_sum_ref,
    do_ref,
    dr_send,
    bs,
    cs,
    stage,
    h,
    du,
    tiles,
    w_ref,
    db_ref,
    do_send,
    *rest,
):
    ring = Ring(count)
    own = out_ref.shape[0]
    sums = [
        RingSum(ring, *rest[7 * i : 7 * i + 3], rest[7 * i + 3 : 7 * i + 7], ref)
        for i, ref in enumerate((db_ref, out_ref))
    ]
    grads = GroupSum(ring, groups, rest[14], rest[15], rest[16:18], grad_ref)
    row_sem, tile_sem, w_sem = rest[18:21]
    exchange = Exchange(ring, count, do_send, do_ref, rest[21:24])
    pairs = ring.pairs

    def weights(index):
        held = (bs, cs)[index // 2 % 2].at[index % 2]
        rows = pl.ds(index * 2 * own, 2 * own)
        return pltpu.make_async_copy(w_out_ref.at[rows], held, w_sem.at[index % 4])


    def places(step):
        return ring.at(-1 - step) * own, ring.at(1 + step, 1 - ring.core) * own

    def row_loads(step):
        slot = lax.rem(step, 2)
        return [
            pltpu.make_async_copy(
                ref.at[pl.ds(pl.multiple_of(place, own), own)],
                held.at[slot, pl.ds(half * own, own)],
                row_sem.at[slot, 2 * which + half],
            )
            for which, (ref, held) in enumerate(((b_ref, bs), (cot_ref, cs)))
            for half, place in enumerate(places(step))
        ]

    def tile_loads(tile):
        slot = lax.rem(tile, 2)
        cols = pl.ds(pl.multiple_of(grads.column(tile), ROWS), ROWS)
        return [
            pltpu.make_async_copy(ref.at[:, cols], tiles.at[slot, which], tile_sem.at[slot, which])
            for which, ref in enumerate((b_ref, cot_ref))
        ]

    def feed_rows(shift):
        part = D // groups
        begin = lax.rem(ring.batch - shift + groups, groups) * part
        src = feed_own_ref if shift == 0 else feed_far_ref.at[shift - 1]
        return pltpu.make_async_copy(
            src, w_ref.at[pl.ds(pl.multiple_of(begin, part), part)], rest[24].at[shift]
        )

    for go in row_loads(0):
        go.start()
    for shift in range(groups):
        feed_rows(shift).start()
    ring.greet_all(count)
    for shift in range(groups):
        feed_rows(shift).wait()

    def feed(step):
        slot = lax.rem(step, 2)

        @pl.when(step + 1 < pairs)
        def _():
            for go in row_loads(step + 1):
                go.start()

        for go in row_loads(step):
            go.wait()
        gate = nn(bs[slot], w_ref[:, :span])
        up = nn(bs[slot], w_ref[:, span : 2 * span])
        slope = nn(cs[slot], w_ref[:, 2 * span :])
        coef = math.sqrt(2.0 / math.pi)
        square = gate * gate
        tanh = jnp.tanh(coef * gate * (1.0 + 0.044715 * square))
        half = 0.5 * (1.0 + tanh)
        gelu = gate * half
        gelu_slope = half + 0.5 * gate * (1.0 - tanh * tanh) * (coef * (1.0 + 3 * 0.044715 * square))
        hidden = (gelu * up).astype(BF)
        both = jnp.concatenate([slope * up * gelu_slope, slope * gelu], axis=1).astype(BF)
        for part, place in enumerate(places(step)):
            rows = pl.ds(pl.multiple_of(place, own), own)
            h[rows, :] = hidden[part * own : (part + 1) * own]
            du[rows, :] = both[part * own : (part + 1) * own]

        @pl.when(step >= 2)
        def _():
            for which, each in enumerate(sums):
                each.given(step - 2, stage.at[slot, which]).wait_send()

        wide = 512
        for which, (each, left, low, high) in enumerate(
            ((sums[0], both, 0, 2 * span), (sums[1], hidden, 2 * span, 3 * span))
        ):
            for at in range(0, D, wide):
                terms = nt(left, w_ref[at : at + wide, low:high]).astype(BF)
                each.own[step, :, at : at + wide] = terms[:own]
                stage[slot, which, :, at : at + wide] = terms[own:]
            each.given(step, stage.at[slot, which]).start()

    @pl.loop(0, pairs)
    def _(step):
        feed(step)

        @pl.when(lax.rem(step, 2) == 0)
        def _():
            sums[0].advance(step // 2)

    for go in tile_loads(0):
        go.start()
    for index in range(4):
        weights(index).start()

    @pl.loop(0, grads.tiles)
    def _(tile):
        slot = lax.rem(tile, 2)

        @pl.when(tile + 1 < grads.tiles)
        def _():
            for go in tile_loads(tile + 1):
                go.start()

        for go in tile_loads(tile):
            go.wait()
        values = jnp.concatenate([tn(tiles[slot, 0], du[...]), tn(tiles[slot, 1], h[...])], axis=1)
        grads.put(tile, values)
        later = pairs // 2 + tile // 2

        @pl.when((lax.rem(tile, 2) == 1) & (later < pairs))
        def _():
            sums[0].advance(later)

    passed = pairs // 2 + grads.tiles // 2

    @pl.loop(min(passed, pairs), pairs)
    def _(step):
        sums[0].advance(step)

    sums[1].advance(0)
    normal, inverse = norm_parts(res_ref[...])
    slope = DEEP_ALPHA * cot_own_ref[...].astype(F32) + db_ref[...]
    dr, gain_sum, bias_sum = norm_back(normal, inverse, slope, vec_ref[2:3, :])
    dr_ref[...] = dr
    vec_sum_ref[...] = jnp.concatenate([gain_sum, bias_sum], axis=0)
    dr_low = dr.astype(BF)
    for index in range(D // (2 * own)):
        weights(index).wait()
        do = nt(dr_low, (bs, cs)[index // 2 % 2][index % 2]).astype(BF)
        if (index + 4) * 2 * own < D:
            weights(index + 4).start()
        for part in range(0, 2 * own, HD):
            at = index * 2 * own + part
            do_send[at // HD] = do[:, part : part + HD]
            dr_send[at // HD] = dr_low[:, at : at + HD]
    exchange.start()

    @pl.loop(1, pairs)
    def _(step):
        sums[1].advance(step)

    exchange.finish()
    grads.finish()
    for step in (pairs - 2, pairs - 1):
        for which, each in enumerate(sums):
            each.given(step, stage.at[step % 2, which]).wait_send()
    for each in sums:
        each.finish()


def feed_forward(
    b_low, cot, feed_own, feed_far, w_out, residual, cot_own, vectors, count, groups, ident
):
    tokens, span, pairs = b_low.shape[0], feed_own.shape[1] // 3, count // 2
    own = residual.shape[0]
    inside, anywhere = pl.BlockSpec(memory_space=pltpu.VMEM), pl.BlockSpec(memory_space=pl.ANY)
    return pl.pallas_call(
        functools.partial(feed_kernel, count, groups, span),
        in_specs=[anywhere] * 5 + [inside] * 3,
        out_specs=[inside] * 4 + [anywhere, inside],
        out_shape=[
            jax.ShapeDtypeStruct((own, D), F32),
            jax.ShapeDtypeStruct((D // groups // ROWS, ROWS, 3 * span), BF),
            jax.ShapeDtypeStruct((own, D), F32),
            jax.ShapeDtypeStruct((2, D), F32),
            jax.ShapeDtypeStruct((count, own, HD), BF),
            jax.ShapeDtypeStruct((count, own, HD), BF),
        ],
        scratch_shapes=[
            pltpu.VMEM((2, 2 * own, D), BF),
            pltpu.VMEM((2, 2 * own, D), BF),
            pltpu.VMEM((2, 2, own, D), BF),
            pltpu.VMEM((tokens, span), BF),
            pltpu.VMEM((tokens, 2 * span), BF),
            pltpu.VMEM((2, 2, tokens, ROWS), BF),
            pltpu.VMEM((D, 3 * span), BF),
            pltpu.VMEM((own, D), F32),
            pltpu.VMEM((count, own, HD), BF),
        ]
        + RingSum.scratch(pairs, own) * 2
        + GroupSum.scratch(groups, 3 * span)
        + [pltpu.SemaphoreType.DMA((2, 4)), pltpu.SemaphoreType.DMA((2, 2)), pltpu.SemaphoreType.DMA((4,))]
        + Exchange.scratch(count)
        + [pltpu.SemaphoreType.DMA((groups,))],
        compiler_params=vmem(62 * 1024 * 1024, collective_id=ident, has_side_effects=True),
        cost_estimate=pl.CostEstimate(
            flops=18 * tokens * D * span, bytes_accessed=250_000_000, transcendentals=0
        ),
        name="feed_forward",
    )(b_low, cot, feed_own, feed_far, w_out, residual, cot_own, vectors)


def project_kernel(
    count,
    groups,
    dp_ref,
    w_ref,
    a_ref,
    heads_ref,
    dr_ref,
    feed_ref,
    x_ref,
    dr_own_ref,
    vec_ref,
    vec_sum_ref,
    back_ref,
    grad_ref,
    feed_out_ref,
    vec_out_ref,
    stage,
    tiles,
    da_ref,
    vec_send,
    vec_came,
    *rest,
):
    ring = Ring(count)
    own = da_ref.shape[0]
    sums = RingSum(ring, *rest[:3], rest[3:7], da_ref)
    grads = GroupSum(ring, groups, rest[7], rest[8], rest[9:11], grad_ref)
    tile_sem = rest[11]
    feed = Exchange(ring, count, feed_ref, feed_out_ref, rest[12:15])
    spread = Spread(ring, count, groups, vec_send, vec_came, rest[15:17])
    pairs, width = ring.pairs, heads_ref.shape[2]

    def places(step):
        return ring.at(-1 - step) * own, ring.at(1 + step, 1 - ring.core) * own

    def tile_loads(tile):
        slot = lax.rem(tile, 2)
        begin = pl.multiple_of(grads.column(tile), ROWS)
        loads = [
            pltpu.make_async_copy(
                a_ref.at[:, pl.ds(begin, ROWS)], tiles.at[slot, 0], tile_sem.at[slot, 0]
            )
        ]
        for part in range(ROWS // width):
            loads.append(
                pltpu.make_async_copy(
                    heads_ref.at[begin // width + part],
                    tiles.at[slot, 1, :, pl.ds(part * width, width)],
                    tile_sem.at[slot, 1 + part],
                )
            )
        return loads

    for go in tile_loads(0):
        go.start()
    ring.greet_whole(count)
    feed.start()

    def terms_of(step):
        slot = lax.rem(step, 2)

        @pl.when(step >= 2)
        def _():
            sums.given(step - 2, stage.at[slot]).wait_send()

        left = jnp.concatenate(
            [dp_ref[pl.ds(pl.multiple_of(place, own), own), :] for place in places(step)], axis=0
        )
        wide = 512
        for at in range(0, D, wide):
            terms = nt(left, w_ref[at : at + wide, :]).astype(BF)
            sums.own[step, :, at : at + wide] = terms[:own]
            stage[slot, :, at : at + wide] = terms[own:]
        sums.given(step, stage.at[slot]).start()

    terms_of(0)
    sums.advance(0)

    @pl.loop(0, grads.tiles)
    def _(tile):
        slot = lax.rem(tile, 2)

        @pl.when(tile + 1 < grads.tiles)
        def _():
            for go in tile_loads(tile + 1):
                go.start()

        for go in tile_loads(tile):
            go.wait()
        values = jnp.concatenate(
            [tn(tiles[slot, 0], dp_ref[...]), tn(tiles[slot, 1], dr_ref[...])], axis=1
        )
        grads.put(tile, values)

        @pl.when(tile + 1 < pairs)
        def _():
            terms_of(tile + 1)

        @pl.when((lax.rem(tile, 2) == 1) & (tile // 2 + 1 < pairs))
        def _():
            sums.advance(tile // 2 + 1)

    @pl.loop(1 + grads.tiles // 2, pairs)
    def _(step):
        sums.advance(step)

    normal, inverse = norm_parts(x_ref[...].astype(F32))
    slope = DEEP_ALPHA * dr_own_ref[...] + da_ref[...]
    back, gain_sum, bias_sum = norm_back(normal, inverse, slope, vec_ref[0:1, :])
    back_ref[...] = back.astype(BF)
    kinds = [gain_sum, bias_sum, vec_sum_ref[0:1, :], vec_sum_ref[1:2, :]]
    for tile in range(D // LANES):
        for kind, values in enumerate(kinds):
            vec_send[tile, kind : kind + 1, :] = values[:, tile * LANES : (tile + 1) * LANES]
    spread.start()
    grads.finish()
    for step in (pairs - 2, pairs - 1):
        sums.given(step, stage.at[step % 2]).wait_send()
    sums.finish()
    vec_out_ref[...] = spread.finish()
    feed.finish()


def project_back(
    dp, w_qkv, a_low, heads, dr_cols, grad_feed, states, dr, vectors, vec_sums, count, groups, ident
):
    tokens, pairs = dp.shape[0], count // 2
    own, width = dr.shape[0], 3 * HD + dr_cols.shape[1]
    inside, anywhere = pl.BlockSpec(memory_space=pltpu.VMEM), pl.BlockSpec(memory_space=pl.ANY)
    return pl.pallas_call(
        functools.partial(project_kernel, count, groups),
        in_specs=[inside, inside, anywhere, anywhere, inside, anywhere] + [inside] * 4,
        out_specs=[inside, inside, anywhere, inside],
        out_shape=[
            jax.ShapeDtypeStruct((own, D), BF),
            jax.ShapeDtypeStruct((D // groups // ROWS, ROWS, width), BF),
            jax.ShapeDtypeStruct(grad_feed.shape, BF),
            jax.ShapeDtypeStruct((8, LANES), F32),
        ],
        scratch_shapes=[
            pltpu.VMEM((2, own, D), BF),
            pltpu.VMEM((2, 2, tokens, ROWS), BF),
            pltpu.VMEM((own, D), F32),
            pltpu.VMEM((D // LANES, 8, LANES), F32),
            pltpu.VMEM((count * groups, 8, LANES), F32),
        ]
        + RingSum.scratch(pairs, own)
        + GroupSum.scratch(groups, width)
        + [pltpu.SemaphoreType.DMA((2, 1 + ROWS // HD))]
        + Exchange.scratch(count)
        + Spread.scratch(count * groups),
        compiler_params=vmem(collective_id=ident, has_side_effects=True),
        cost_estimate=pl.CostEstimate(
            flops=4 * tokens * D * 3 * HD, bytes_accessed=200_000_000, transcendentals=0
        ),
        name="project_back",
    )(dp, w_qkv, a_low, heads, dr_cols, grad_feed, states, dr, vectors, vec_sums)


def norm_parts(values):
    centre = values - jnp.mean(values, axis=-1, keepdims=True)
    inverse = lax.rsqrt(jnp.mean(centre * centre, axis=-1, keepdims=True) + LN_EPS)
    return centre * inverse, inverse


def qkv_kernel(x_ref, w_ref, vec_ref, cos_ref, sin_ref, a_ref, q_ref, k_ref, v_ref, kt_ref, vt_ref):
    normal, _ = norm_parts(x_ref[...].astype(F32))
    low = (normal * vec_ref[0:1, :] + vec_ref[1:2, :]).astype(BF)
    a_ref[...] = low
    projected = nn(low, w_ref[...])
    for index, ref in enumerate((q_ref, k_ref)):
        part = projected[:, index * HD : (index + 1) * HD]
        turned = part * cos_ref[...] + pltpu.roll(part, HD // 2, 1) * sin_ref[...]
        ref[...] = turned.astype(BF)
    kt_ref[...] = turned.T.astype(BF)[None]
    v_ref[...] = projected[:, 2 * HD :].astype(BF)
    vt_ref[...] = projected[:, 2 * HD :].T.astype(BF)[None]


def norm_and_project(states, w_qkv, vectors, cosine, sine):
    tokens = states.shape[0]
    whole = lambda shape: pl.BlockSpec(shape, lambda i: (0, 0))
    rows = lambda width: pl.BlockSpec((ROWS, width), lambda i: (i, 0))
    turned = pl.BlockSpec((1, HD, ROWS), lambda i: (i * ROWS // KEYS, 0, i % (KEYS // ROWS)))
    return pl.pallas_call(
        qkv_kernel,
        grid=(tokens // ROWS,),
        in_specs=[rows(D), whole((D, 3 * HD)), whole(vectors.shape), rows(HD), rows(HD)],
        out_specs=[rows(D), rows(HD), rows(HD), rows(HD), turned, turned],
        out_shape=[jax.ShapeDtypeStruct((tokens, D), BF)]
        + [jax.ShapeDtypeStruct((tokens, HD), BF) for _ in range(3)]
        + [jax.ShapeDtypeStruct((tokens // KEYS, HD, KEYS), BF) for _ in range(2)],
        compiler_params=vmem(),
        cost_estimate=pl.CostEstimate(
            flops=2 * tokens * D * 3 * HD, bytes_accessed=24_000_000, transcendentals=0
        ),
        name="norm_and_project",
    )(states, w_qkv, vectors, cosine, sine)


def masked_scores(block, query, k_ref, first_ref, last_ref, keys):
    place = block * ROWS + lax.broadcasted_iota(jnp.int32, (1, LANES), 1)
    scores = nt(k_ref[keys], query) * HD ** (-0.5)
    parts = []
    for at in range(0, ROWS, LANES):
        seen = (place + at >= first_ref[keys]) & (place + at < last_ref[keys])
        parts.append(jnp.where(seen, scores[:, at : at + LANES], NEG_LARGE))
    return jnp.concatenate(parts, axis=1)


def attend_kernel(
    low_ref, high_ref, q_ref, k_ref, vt_ref, first_ref, last_ref, o_ref, full_ref, log_ref, held
):
    block = pl.program_id(0)
    query = q_ref[...]

    def score(keys, top):
        scores = masked_scores(block, query, k_ref, first_ref, last_ref, keys)
        held[keys] = scores
        return jnp.maximum(top, jnp.max(scores, axis=0, keepdims=True))

    def add(keys, carry):
        total, out = carry
        weight = jnp.exp(held[keys] - top)
        total = total + jnp.sum(weight, axis=0, keepdims=True)
        return total, out + nn(vt_ref[keys], weight.astype(BF))

    low, high = low_ref[block], high_ref[block]
    top = lax.fori_loop(low, high, score, jnp.full((1, ROWS), NEG_LARGE, F32))
    total, out = lax.fori_loop(
        low, high, add, (jnp.zeros((1, ROWS), F32), jnp.zeros((HD, ROWS), F32))
    )
    out = out / total
    o_ref[...] = out.T.astype(BF)
    full_ref[...] = out[None]
    log_ref[...] = (top + jnp.log(total))[None]


def attend(query, key, value_t, spans):
    tokens = query.shape[0]
    blocks, span = tokens // ROWS, tokens // KEYS
    first, last, low, high = spans
    rows = pl.BlockSpec((ROWS, HD), lambda i, *_: (i, 0))
    one = lambda shape: pl.BlockSpec((1,) + shape, lambda i, *_: (i, 0, 0))
    whole = lambda shape: pl.BlockSpec(shape, lambda i, *_: (0,) * len(shape))
    return pl.pallas_call(
        attend_kernel,
        grid_spec=pltpu.PrefetchScalarGridSpec(
            num_scalar_prefetch=2,
            grid=(blocks,),
            in_specs=[
                rows,
                whole((span, KEYS, HD)),
                whole((span, HD, KEYS)),
                whole((span, KEYS, LANES)),
                whole((span, KEYS, LANES)),
            ],
            out_specs=[rows, one((HD, ROWS)), one((1, ROWS))],
            scratch_shapes=[pltpu.VMEM((span, KEYS, ROWS), F32)],
        ),
        out_shape=[
            jax.ShapeDtypeStruct((tokens, HD), BF),
            jax.ShapeDtypeStruct((blocks, HD, ROWS), F32),
            jax.ShapeDtypeStruct((blocks, 1, ROWS), F32),
        ],
        compiler_params=vmem(),
        cost_estimate=pl.CostEstimate(
            flops=2 * tokens * tokens * HD, bytes_accessed=4_000_000, transcendentals=0
        ),
        name="attend",
    )(low, high, query, key.reshape(span, KEYS, HD), value_t, first, last)


def attend_back_kernel(
    low_ref,
    high_ref,
    q_ref,
    g_ref,
    full_ref,
    log_ref,
    k_ref,
    kt_ref,
    v_ref,
    first_ref,
    last_ref,
    cos_ref,
    sin_ref,
    o_ref,
    dk_ref,
    dv_ref,
):
    block = pl.program_id(0)
    blocks = pl.num_programs(0)
    scale = HD ** (-0.5)

    @pl.when(block == 0)
    def _():
        dk_ref[...] = jnp.zeros_like(dk_ref)
        dv_ref[...] = jnp.zeros_like(dv_ref)

    query, grad = q_ref[...], g_ref[...]
    inner = jnp.sum(grad.astype(F32).T * full_ref[0], axis=0, keepdims=True)
    log = log_ref[0]

    def one(keys, total):
        scores = masked_scores(block, query, k_ref, first_ref, last_ref, keys)
        weight = jnp.exp(scores - log)
        slope = (weight * (nt(v_ref[keys], grad) - inner)).astype(BF)
        dv_ref[keys] += nn(weight.astype(BF), grad)
        dk_ref[keys] += nn(slope, query)
        return total + nn(kt_ref[keys], slope)

    total = lax.fori_loop(low_ref[block], high_ref[block], one, jnp.zeros((HD, ROWS), F32))

    def turn_back(values, cosine, sine):
        values = (values * scale).astype(BF).astype(F32)
        return (values * cosine - pltpu.roll(values, HD // 2, 1) * sine).astype(BF)

    rows = pl.ds(pl.multiple_of(block * ROWS, ROWS), ROWS)
    o_ref[rows, 0:HD] = turn_back(total.T, cos_ref[rows, :], sin_ref[rows, :])

    @pl.when(block == blocks - 1)
    def _():
        for part in range(dk_ref.shape[0]):
            there = pl.ds(part * KEYS, KEYS)
            o_ref[there, HD : 2 * HD] = turn_back(
                dk_ref[part], cos_ref[there, :], sin_ref[there, :]
            )
            o_ref[there, 2 * HD :] = dv_ref[part].astype(BF)


def attend_back(query, key, key_t, value, grad, full, log, spans, cosine, sine):
    tokens = query.shape[0]
    blocks, span = tokens // ROWS, tokens // KEYS
    first, last, low, high = spans
    rows = pl.BlockSpec((ROWS, HD), lambda i, *_: (i, 0))
    one = lambda shape: pl.BlockSpec((1,) + shape, lambda i, *_: (i, 0, 0))
    whole = lambda shape: pl.BlockSpec(shape, lambda i, *_: (0,) * len(shape))
    return pl.pallas_call(
        attend_back_kernel,
        grid_spec=pltpu.PrefetchScalarGridSpec(
            num_scalar_prefetch=2,
            grid=(blocks,),
            in_specs=[
                rows,
                rows,
                one((HD, ROWS)),
                one((1, ROWS)),
                whole((span, KEYS, HD)),
                whole((span, HD, KEYS)),
                whole((span, KEYS, HD)),
                whole((span, KEYS, LANES)),
                whole((span, KEYS, LANES)),
                whole((tokens, HD)),
                whole((tokens, HD)),
            ],
            out_specs=whole((tokens, 3 * HD)),
            scratch_shapes=[pltpu.VMEM((span, KEYS, HD), F32) for _ in range(2)],
        ),
        out_shape=jax.ShapeDtypeStruct((tokens, 3 * HD), BF),
        compiler_params=vmem(),
        cost_estimate=pl.CostEstimate(
            flops=5 * tokens * tokens * HD, bytes_accessed=6_000_000, transcendentals=0
        ),
        name="attend_back",
    )(
        low,
        high,
        query,
        grad,
        full,
        log,
        key.reshape(span, KEYS, HD),
        key_t,
        value.reshape(span, KEYS, HD),
        first,
        last,
        cosine,
        sine,
    )


def windows(at, span, count):
    total = 4 * D + 3 * FF + 4
    result = []
    for index in range(count):
        width = max(0, min(span, FF - index * span))
        begin = at + index * span
        turn = begin % LANES
        window = -(-(turn + width) // LANES) * LANES if width else 0
        window = min(window, (total - begin + turn) // LANES * LANES)
        result.append((begin - turn, window, turn, width))
    return result


FEED_AT = (4 * D, 4 * D + FF, 4 * D + 2 * FF)


def lay_out_kernel(count, span, m_ref, qkv_ref, out_ref, feed_ref):
    rows = m_ref.shape[0]
    for index in range(count):
        for part in range(3):
            at = part * D + index * HD
            qkv_ref[index, :, part * HD : (part + 1) * HD] = m_ref[:, at : at + HD].astype(BF)
    out_ref[...] = m_ref[:, 3 * D : 4 * D].astype(BF)
    column = lax.broadcasted_iota(jnp.int32, (rows, span), 1)
    for part, at in enumerate(FEED_AT):
        for index, (begin, window, turn, width) in enumerate(windows(at, span, count)):
            if width == 0:
                piece = jnp.zeros((rows, span), F32)
            else:
                piece = m_ref[:, begin : begin + window]
                if window < span:
                    piece = jnp.concatenate(
                        [piece, jnp.zeros((rows, span - window), F32)], axis=1
                    )
                if turn:
                    piece = pltpu.roll(piece, piece.shape[1] - turn, 1)
                piece = piece[:, :span]
                if width < span:
                    piece = jnp.where(column < width, piece, 0.0)
            feed_ref[index, :, part * span : (part + 1) * span] = piece.astype(BF)


def lay_out(master, count, span):
    rows = master.shape[0]
    inside = pl.BlockSpec(memory_space=pltpu.VMEM)
    return pl.pallas_call(
        functools.partial(lay_out_kernel, count, span),
        out_shape=[
            jax.ShapeDtypeStruct((count, rows, 3 * HD), BF),
            jax.ShapeDtypeStruct((rows, D), BF),
            jax.ShapeDtypeStruct((count, rows, 3 * span), BF),
        ],
        in_specs=[inside],
        out_specs=[inside] * 3,
        compiler_params=vmem(),
        cost_estimate=pl.CostEstimate(flops=0, bytes_accessed=10_000_000, transcendentals=0),
        name="lay_out",
    )(master)


STEP_COLS = 2048


def tile_of_part(ref, part, at, begin, rows, span):
    turn = at % LANES
    index = (begin - at + turn) // LANES
    tiles = span // LANES

    def piece(index):
        if index < 0 or index * LANES >= FF:
            return None
        device, inner = divmod(index, tiles)
        low = part * span + inner * LANES
        values = ref[device, :, low : low + LANES].astype(F32)
        return pltpu.roll(values, turn, 1) if turn else values

    lane = lax.broadcasted_iota(jnp.int32, (rows, LANES), 1)
    here, before = piece(index), piece(index - 1) if turn else None
    if here is None:
        return before
    return here if before is None else jnp.where(lane < turn, before, here)


def feed_tile(begin, feed_ref, vec_ref, rows, span):
    lane = lax.broadcasted_iota(jnp.int32, (rows, LANES), 1)
    total = 4 * D + 3 * FF + 4
    value = None
    for part, at in enumerate(FEED_AT):
        if at < begin + LANES and at + FF > begin:
            piece = tile_of_part(feed_ref, part, at, begin, rows, span)
            value = piece if value is None else jnp.where(lane < at - begin, value, piece)
    if begin + LANES > total - 4:
        vec = pltpu.roll(vec_ref[...], (total - 4) % LANES, 1)
        value = vec if value is None else jnp.where(lane < total - 4 - begin, value, vec)
    return value


def update_kernel(first_step, steps, tile_at, sources, *refs):
    grads, (m_ref, f_ref, s_ref, a_ref), outs = refs[:sources], refs[sources : sources + 4], refs[-4:]
    nm_ref, nf_ref, ns_ref, na_ref = outs
    rows = m_ref.shape[0]
    total = 4 * D + 3 * FF + 4

    def one(begin, cols):
        g = tile_at(begin, *grads)
        rate, decay = LR_MAT, DECAY_MAT
        if begin + LANES > total - 4:
            vector = begin + lax.broadcasted_iota(jnp.int32, (1, LANES), 1) >= total - 4
            rate, decay = jnp.where(vector, LR_VEC, LR_MAT), jnp.where(vector, 0.0, DECAY_MAT)
        new_first = BETA_ONE * f_ref[:, cols] + (1.0 - BETA_ONE) * g
        new_second = BETA_TWO * s_ref[:, cols] + (1.0 - BETA_TWO) * g * g
        nf_ref[:, cols] = new_first
        ns_ref[:, cols] = new_second
        root = jnp.sqrt(new_second * (1.0 / (1.0 - BETA_TWO**STEP))) + ADAM_EPS
        corrected = new_first * (1.0 / (1.0 - BETA_ONE**STEP)) / root
        master = m_ref[:, cols]
        new_master = master - rate * (corrected + decay * master)
        nm_ref[:, cols] = new_master
        na_ref[:, cols] = EMA_RATE * a_ref[:, cols] + (1.0 - EMA_RATE) * new_master

    for step in range(steps):

        @pl.when(pl.program_id(0) == step)
        def _():
            for at in range(0, STEP_COLS, LANES):
                begin = (first_step + step) * STEP_COLS + at
                if begin < total:
                    one(begin, slice(at, at + LANES))


def update(grads, tile_at, state, first_step, steps, done=()):
    rows, columns = state[0].shape
    whole = lambda values: pl.BlockSpec(values.shape, lambda i: (0,) * values.ndim)
    cols = pl.BlockSpec((rows, STEP_COLS), lambda i: (0, first_step + i))
    return pl.pallas_call(
        functools.partial(update_kernel, first_step, steps, tile_at, len(grads)),
        grid=(steps,),
        in_specs=[whole(g) for g in grads]
        + [cols] * 4
        + [pl.BlockSpec(memory_space=pl.ANY)] * len(done),
        out_specs=[cols] * 4,
        out_shape=[jax.ShapeDtypeStruct((rows, columns), F32) for _ in range(4)],
        input_output_aliases={len(grads) + 4 + i: i for i in range(len(done))},
        compiler_params=vmem(),
        cost_estimate=pl.CostEstimate(
            flops=0, bytes_accessed=36 * rows * steps * STEP_COLS, transcendentals=0
        ),
        name=f"update_{first_step}",
    )(*grads, *state, *done)


def chain_spans(lengths, prefix, padding, total):
    ends = jnp.cumsum(lengths, dtype=jnp.int32)
    starts = ends - lengths
    token = jnp.arange(total, dtype=jnp.int32)
    member = (token[:, None] >= starts[None, :]) & (token[:, None] < ends[None, :])
    pick = lambda values: jnp.sum(jnp.where(member, values[None, :], 0), axis=1, dtype=jnp.int32)
    start, end, pre, live = pick(starts), pick(ends), pick(prefix), pick(lengths - padding)
    place = token - start
    first = jnp.where(place < pre, start, token)
    first = jnp.where(place < live, first, 2 * total)
    low = start[::ROWS] // KEYS
    high = (end[ROWS - 1 :: ROWS] + KEYS - 1) // KEYS
    cut = lambda values: jnp.broadcast_to(values[:, None], (total, LANES)).reshape(-1, KEYS, LANES)
    return (cut(first), cut(end), low, high), place


def rotary_tables(place):
    half = HD // 2
    freq = ROPE_BASE ** (-jnp.arange(half, dtype=F32) / half)
    angles = place.astype(F32)[:, None] * freq[None, :]
    cosine, sine = jnp.cos(angles), jnp.sin(angles)
    return jnp.concatenate([cosine, cosine], axis=1), jnp.concatenate([-sine, sine], axis=1)


def to_rows(grad):
    blocks = grad.reshape(lax.axis_size("seq"), -1, grad.shape[-1])
    return lax.all_to_all(blocks, "seq", split_axis=0, concat_axis=0, tiled=True)


def on_device(hidden_in, cotangent, master, first, second, average, lengths, prefix, padding):
    groups, seq = lax.axis_size("batch"), lax.axis_size("seq")
    own = hidden_in.shape[0]
    tokens = own * seq
    rows = master.shape[0]
    span = -(-FF // (seq * LANES)) * LANES
    vec_cut = master[:, 4 * D + 3 * FF :].astype(BF).astype(F32).T
    vec_cut = jnp.pad(vec_cut, ((0, 8 - vec_cut.shape[0]), (0, LANES - rows)))[None]
    qkv_cut, out_cut, feed_cut = lay_out(master, seq, span)
    states, w_qkv, vectors = ring_gather(hidden_in, [qkv_cut, vec_cut], seq, 1)
    states = states.reshape(tokens, D)
    w_qkv = w_qkv.reshape(D, 3 * HD)
    vectors = vectors[..., :rows].transpose(2, 0, 1, 3).reshape(8, D)
    w_out = lax.all_gather(out_cut, ("batch", "seq"), axis=0, tiled=True)
    feed_cut, w_qkv = lax.optimization_barrier((feed_cut, w_qkv))
    feed_own = lax.all_to_all(feed_cut, "seq", split_axis=0, concat_axis=0, tiled=True)
    feed_own = feed_own.reshape(D // groups, 3 * span)
    cot_all = lax.all_gather(cotangent, "seq", axis=0, tiled=True)

    spans, place = chain_spans(lengths[0], prefix[0], padding[0], tokens)
    cosine, sine = rotary_tables(place)
    a_low, query, key, value, key_t, value_t = norm_and_project(states, w_qkv, vectors, cosine, sine)
    attended, full, log = attend(query, key, value_t, spans)
    heads, feed_far, b_low, residual = gather_residual(
        attended, feed_own, states, w_out, vectors, own, seq, 2
    )
    out_sum, grad_feed, dr, vec_sums, do, dr_cut = feed_forward(
        b_low, cot_all, feed_own, feed_far, w_out, residual, cotangent, vectors, seq, groups, 3
    )
    dr_cols = lax.all_to_all(dr_cut, "seq", split_axis=0, concat_axis=0, tiled=True)
    normal_two, _ = norm_parts(residual)
    output = DEEP_ALPHA * (normal_two * vectors[2:3] + vectors[3:4]) + out_sum

    dp = attend_back(query, key, key_t, value, do.reshape(tokens, HD), full, log, spans, cosine, sine)
    input_grad, grad_attn, grad_feed, grad_vec = project_back(
        dp,
        w_qkv,
        a_low,
        heads,
        dr_cols.reshape(tokens, HD),
        grad_feed.reshape(seq, rows, 3 * span),
        hidden_in,
        dr,
        vectors,
        vec_sums,
        seq,
        groups,
        4,
    )
    grad_attn = to_rows(grad_attn)
    place = lax.rem(lax.axis_index("batch") * seq + lax.axis_index("seq"), LANES // rows) * rows
    grad_vec = lax.dynamic_slice_in_dim(grad_vec, place, rows, 1)[:4].T
    grad_vec = jnp.pad(grad_vec, ((0, 0), (0, LANES - 4)))

    def attn_tile(begin, ref):
        part, index = divmod(begin // HD, seq)
        return ref[index, :, part * HD : (part + 1) * HD].astype(F32)

    def other_tile(begin, feed_ref, vec_ref):
        return feed_tile(begin, feed_ref, vec_ref, rows, span)

    state = (master, first, second, average)
    steps, attn_steps = -(-master.shape[1] // STEP_COLS), 4 * D // STEP_COLS
    updated = update([grad_feed, grad_vec], other_tile, state, attn_steps, steps - attn_steps)
    updated = update([grad_attn], attn_tile, state, 0, attn_steps, updated)
    return (
        output.astype(BF),
        input_grad,
        *updated,
    )


def solution(mesh):
    spread = P(("batch", "seq"), None)
    return jax.shard_map(
        on_device,
        mesh=mesh,
        in_specs=(spread,) * 6 + (P("batch", None),) * 3,
        out_specs=(spread,) * 6,
        check_vma=False,
    )
```

```python
import functools
import math

import jax
import jax.numpy as jnp
from jax import lax
from jax.experimental import pallas as pl
from jax.experimental.pallas import tpu as pltpu
from jax.sharding import PartitionSpec as P

D = 2048
H = 16
HD = 128
FF = 5461
STEP = 10

DEEP_ALPHA = math.sqrt(48.0)
ROPE_BASE = 10000.0
NEG_LARGE = -1e30
LN_EPS = 1e-05
BETA_ONE = 0.9
BETA_TWO = 0.95
ADAM_EPS = 1e-08
LR_MAT = 0.01
LR_VEC = 0.2
DECAY_MAT = 0.1
EMA_RATE = 0.9

BF = jnp.bfloat16
F32 = jnp.float32
MESH = pl.DeviceIdType.MESH
ROWS = 256
KEYS = 512
LANES = 128
SUBS = 4
VMEM_BIG = 56 * 1024 * 1024


def nt(left, right):
    return lax.dot_general(left, right, (((1,), (1,)), ((), ())), preferred_element_type=F32)


def tn(left, right):
    return lax.dot_general(left, right, (((0,), (0,)), ((), ())), preferred_element_type=F32)


def nn(left, right):
    return jnp.dot(left, right, preferred_element_type=F32)


def vmem(limit=VMEM_BIG, **more):
    return pltpu.CompilerParams(vmem_limit_bytes=limit, **more)


class Ring:
    def __init__(self, count):
        self.pairs = count // 2
        self.batch, self.me = lax.axis_index("batch"), lax.axis_index("seq")
        self.core = lax.rem(self.me, 2)
        y, z = lax.rem(self.me // 2, 2), self.me // 4
        self.place = jnp.where(y == 0, z, self.pairs - 1 - z)
        self.sibling = self.me + 1 - 2 * self.core

    def at(self, steps, core=None):
        place = lax.rem(self.place + (1 - 2 * self.core) * steps + 4 * self.pairs, self.pairs)
        half = self.pairs // 2
        pair = jnp.where(place < half, 2 * place, 2 * (self.pairs - 1 - place) + 1)
        return pair * 2 + (self.core if core is None else core)

    def greet_all(self, count):
        barrier = pltpu.get_barrier_semaphore()
        groups = lax.axis_size("batch")
        for step in range(1, count):
            device = lax.rem(self.me + step, count)
            pl.semaphore_signal(barrier, inc=1, device_id=(self.batch, device), device_id_type=MESH)
        for shift in range(1, groups):
            group = lax.rem(self.batch + shift, groups)
            pl.semaphore_signal(barrier, inc=1, device_id=(group, self.me), device_id_type=MESH)
        pl.semaphore_wait(barrier, count + groups - 2)

    def greet_groups(self, groups):
        barrier = pltpu.get_barrier_semaphore()
        for device in (self.at(-1), self.sibling):
            pl.semaphore_signal(barrier, inc=1, device_id=(self.batch, device), device_id_type=MESH)
        for shift in range(1, groups):
            group = lax.rem(self.batch + shift, groups)
            pl.semaphore_signal(barrier, inc=1, device_id=(group, self.me), device_id_type=MESH)
        pl.semaphore_wait(barrier, 1 + groups)

    def greet_whole(self, count):
        barrier = pltpu.get_barrier_semaphore()
        total = count * lax.axis_size("batch")
        for step in range(1, total):
            flat = lax.rem(self.batch * count + self.me + step, total)
            there = (flat // count, lax.rem(flat, count))
            pl.semaphore_signal(barrier, inc=1, device_id=there, device_id_type=MESH)
        pl.semaphore_wait(barrier, total - 1)

    def copy(self, src, dst, send, recv, device):
        return pltpu.make_async_remote_copy(
            src_ref=src,
            dst_ref=dst,
            send_sem=send,
            recv_sem=recv,
            device_id=(self.batch, device),
            device_id_type=MESH,
        )


class Columns:
    def __init__(self, ring, count, src, out, sems):
        self.ring, self.count, self.src, self.out = ring, count, src, out
        self.send, self.recv, self.on_send, self.on_recv, self.own = sems
        self.groups = lax.axis_size("batch")

    def piece(self, device):
        return self.src.at[device] if self.src.shape[0] == self.count else self.src.at[0]

    def group(self, shift):
        return lax.rem(self.ring.batch + shift + self.groups, self.groups)

    def start(self):
        ring, sends = self.ring, []
        self.mine = pltpu.make_async_copy(
            self.piece(ring.me), self.out.at[ring.batch, ring.me], self.own
        )
        self.mine.start()
        for step in range(1, self.count):
            device = lax.rem(ring.me + step, self.count)
            go = ring.copy(
                self.piece(device),
                self.out.at[ring.batch, ring.me],
                self.send.at[step],
                self.recv.at[step],
                device,
            )
            go.start()
            sends.append(go)
        self.sends = sends + self.forward(0)

    def forward(self, step):
        ring, sends = self.ring, []
        device = lax.rem(ring.me - step + self.count, self.count)
        here = self.out.at[ring.batch, device]
        for shift in range(1, self.groups):
            go = pltpu.make_async_remote_copy(
                src_ref=self.piece(ring.me) if step == 0 else here,
                dst_ref=here,
                send_sem=self.on_send.at[shift - 1, step],
                recv_sem=self.on_recv.at[shift - 1, step],
                device_id=(self.group(shift), ring.me),
                device_id_type=MESH,
            )
            go.start()
            sends.append(go)
        return sends

    def pass_on(self, step):
        ring = self.ring
        device = lax.rem(ring.me - step + self.count, self.count)
        here = self.out.at[ring.batch, device]
        ring.copy(here, here, self.send.at[step], self.recv.at[step], device).wait_recv()
        self.sends += self.forward(step)

    def finish(self):
        ring = self.ring
        for step in range(self.count):
            device = lax.rem(ring.me - step + self.count, self.count)
            for shift in range(1, self.groups):
                here = self.out.at[self.group(-shift), device]
                pltpu.make_async_remote_copy(
                    src_ref=here,
                    dst_ref=here,
                    send_sem=self.on_send.at[shift - 1, step],
                    recv_sem=self.on_recv.at[shift - 1, step],
                    device_id=(self.group(shift), ring.me),
                    device_id_type=MESH,
                ).wait_recv()
        for go in self.sends:
            go.wait_send()
        self.mine.wait()


def pass_round(ring, count, lag, x_ref, o_ref, sems, columns, work):
    ring_s, ring_r, sib_s, sib_r, own_sem = sems
    piece = x_ref.shape[0] // SUBS
    own = pltpu.make_async_copy(x_ref, o_ref.at[ring.me], own_sem)
    own.start()
    ring.greet_all(count)
    following, sends = ring.at(1), []
    ahead = 1

    def complete(step):
        if step == 0:
            own.wait()
        other = ring.at(step, 1 - ring.core)
        for sub in range(SUBS):
            dst = o_ref.at[other].at[pl.ds(sub * piece, piece)]
            ring.copy(
                dst, dst, sib_s.at[step, sub], sib_r.at[step, sub], ring.sibling
            ).wait_recv()
        work(ring.at(-step), other)

    for step in range(ring.pairs):
        block = ring.at(-step)
        for sub in range(SUBS):
            rows = pl.ds(sub * piece, piece)
            dst = o_ref.at[block].at[rows]
            src = x_ref.at[rows] if step == 0 else dst
            if step > 0:
                ring.copy(
                    dst, dst, ring_s.at[step - 1, sub], ring_r.at[step - 1, sub], following
                ).wait_recv()
            if step < ring.pairs - 1:
                go = ring.copy(src, dst, ring_s.at[step, sub], ring_r.at[step, sub], following)
                go.start()
                sends.append(go)
            go = ring.copy(src, dst, sib_s.at[step, sub], sib_r.at[step, sub], ring.sibling)
            go.start()
            sends.append(go)
        if step == 0:
            for column in columns:
                column.start()
        else:
            upto = count if step == ring.pairs - 1 else min(count, 1 + 2 * step)
            for passed in range(ahead, max(ahead, upto)):
                for column in columns:
                    column.pass_on(passed)
            ahead = max(ahead, upto)
        if step >= lag:
            complete(step - lag)
    for step in range(max(0, ring.pairs - lag), ring.pairs):
        complete(step)
    return sends


class Line:
    def __init__(self, ring, count):
        self.ring, self.length = ring, count // 4
        self.y, self.z = lax.rem(ring.me // 2, 2), ring.me // 4

    def nearest(self, index):
        order = [sorted(range(self.length), key=lambda q: (abs(q - z), q)) for z in range(self.length)]
        place = order[0][index] + 0 * self.z
        for z in range(1, self.length):
            place = jnp.where(self.z == z, order[z][index], place)
        return place

    def device(self, z, row=0, core=0):
        y = self.y if row == 0 else 1 - self.y
        return (z * 2 + y) * 2 + (self.ring.core if core == 0 else 1 - self.ring.core)


def pass_along(ring, count, x_ref, o_ref, sems, columns):
    line_s, line_r, over_s, over_r, sib_s, sib_r, own_sem = sems
    line = Line(ring, count)
    piece = x_ref.shape[0] // SUBS
    own = pltpu.make_async_copy(x_ref, o_ref.at[ring.me], own_sem)
    own.start()
    ring.greet_all(count)
    across = line.device(line.z, 1)
    sends = []

    def send(condition, src, dst, send_sem, recv_sem, device):
        go = ring.copy(src, dst, send_sem, recv_sem, device)
        if condition is None:
            go.start()
        else:
            pl.when(condition)(go.start)
        sends.append((condition, go))

    order = sorted(((row, index) for row in (0, 1) for index in range(line.length)), key=lambda p: (p[0] + p[1], p[0]))
    ahead = 1
    for turn, (row, index) in enumerate(order):
        z = line.nearest(index)
        block = line.device(z, row)
        for sub in range(SUBS):
            rows = pl.ds(sub * piece, piece)
            dst = o_ref.at[block].at[rows]
            first = row == 0 and index == 0
            src = x_ref.at[rows] if first else dst
            if row == 1:
                ring.copy(dst, dst, over_s.at[z, sub], over_r.at[z, sub], across).wait_recv()
            elif not first:
                ring.copy(dst, dst, line_s.at[0, z, sub], line_r.at[z, sub], across).wait_recv()
            if row == 0:
                if first:
                    for side, step in enumerate((1, -1)):
                        there = line.z + step
                        go_on = (there >= 0) & (there < line.length)
                        there = jnp.where(go_on, there, line.z - step)
                        send(go_on, src, dst, line_s.at[side, z, sub], line_r.at[z, sub], line.device(there))
                else:
                    there = jnp.where(z < line.z, line.z + 1, line.z - 1)
                    go_on = (there >= 0) & (there < line.length)
                    there = jnp.where(go_on, there, jnp.where(z < line.z, line.z - 1, line.z + 1))
                    send(go_on, src, dst, line_s.at[0, z, sub], line_r.at[z, sub], line.device(there))
                send(None, src, dst, over_s.at[z, sub], over_r.at[z, sub], across)
            send(None, src, dst, sib_s.at[row, z, sub], sib_r.at[row, z, sub], ring.sibling)
        if turn == 0:
            for column in columns:
                column.start()
        else:
            upto = count if turn == len(order) - 1 else min(count, 1 + 2 * turn)
            for passed in range(ahead, max(ahead, upto)):
                for column in columns:
                    column.pass_on(passed)
            ahead = max(ahead, upto)
    for row, index in order:
        z = line.nearest(index)
        other = line.device(z, row, 1)
        for sub in range(SUBS):
            dst = o_ref.at[other].at[pl.ds(sub * piece, piece)]
            ring.copy(
                dst, dst, sib_s.at[row, z, sub], sib_r.at[row, z, sub], ring.sibling
            ).wait_recv()
    own.wait()
    return sends


def wait_sends(sends):
    for condition, go in sends:
        if condition is None:
            go.wait_send()
        else:
            pl.when(condition)(go.wait_send)


def gather_kernel(count, extra, x_ref, *refs):
    parts, (o_ref, *outs), sems = refs[:extra], refs[extra : 2 * extra + 1], refs[2 * extra + 1 :]
    ring = Ring(count)
    columns = [
        Columns(ring, count, parts[i], outs[i], sems[7 + 5 * i : 12 + 5 * i]) for i in range(extra)
    ]
    wait_sends(pass_along(ring, count, x_ref, o_ref, sems[:7], columns))
    for column in columns:
        column.finish()


def ring_gather(values, blocks, count, ident):
    pairs, groups = count // 2, lax.axis_size("batch")
    anywhere = pl.BlockSpec(memory_space=pl.ANY)
    return pl.pallas_call(
        functools.partial(gather_kernel, count, len(blocks)),
        out_shape=[jax.ShapeDtypeStruct((count,) + values.shape, values.dtype)]
        + [jax.ShapeDtypeStruct((groups, count) + b.shape[1:], b.dtype) for b in blocks],
        in_specs=[anywhere] * (1 + len(blocks)),
        out_specs=[anywhere] * (1 + len(blocks)),
        scratch_shapes=line_sems(count) + column_sems(count, groups) * len(blocks),
        compiler_params=pltpu.CompilerParams(collective_id=ident, has_side_effects=True),
        cost_estimate=pl.CostEstimate(flops=0, bytes_accessed=150_000_000, transcendentals=0),
        name=f"ring_gather_{ident}",
    )(values, *blocks)


def ring_sems(pairs):
    return [pltpu.SemaphoreType.DMA((pairs, SUBS)) for _ in range(4)] + [pltpu.SemaphoreType.DMA]


def line_sems(count):
    dma = pltpu.SemaphoreType.DMA
    shapes = [(2, count // 4, SUBS)] + [(count // 4, SUBS)] * 3 + [(2, count // 4, SUBS)] * 2
    return [dma(shape) for shape in shapes] + [dma]


def column_sems(count, groups):
    return [
        pltpu.SemaphoreType.DMA((count,)),
        pltpu.SemaphoreType.DMA((count,)),
        pltpu.SemaphoreType.DMA((groups, count)),
        pltpu.SemaphoreType.DMA((groups, count)),
        pltpu.SemaphoreType.DMA,
    ]


def residual_kernel(count, groups, x_ref, feed_ref, states_ref, vec_ref, plane_ref, *refs):
    far_refs, refs = refs[: groups - 1], refs[groups - 1 :]
    heads_ref, feed_far_ref, b_ref, w_ref, own_ref, heads, w_out, total, states, low = refs[:10]
    w_sem, load_sem, store_sem, heads_sem, *sems = refs[10:]
    ring = Ring(count)
    tokens, own = total.shape[0], own_ref.shape[0]
    blocks = tokens // ROWS
    part = D // groups
    half = part // 2

    def held_rows(shift):
        begin = lax.rem(ring.batch - shift + groups, groups) * part
        if shift == 0:
            return w_out.at[pl.ds(pl.multiple_of(begin, part), part)]
        return w_out.at[pl.ds(pl.multiple_of(begin + ring.core * half, half), half)]

    weights = [
        pltpu.make_async_copy(ref, held_rows(shift), w_sem.at[shift])
        for shift, ref in enumerate((plane_ref,) + far_refs)
    ]
    for go in weights:
        go.start()

    def handed(shift):
        return ring.copy(
            far_refs[shift - 1],
            held_rows(shift),
            sems[7].at[shift - 1],
            sems[8].at[shift - 1],
            ring.sibling,
        )

    keep = pltpu.make_async_copy(w_out, w_ref, w_sem.at[groups])

    def onward(shift):
        return pltpu.make_async_remote_copy(
            src_ref=feed_ref,
            dst_ref=feed_far_ref.at[shift - 1],
            send_sem=sems[5].at[shift - 1],
            recv_sem=sems[6].at[shift - 1],
            device_id=(lax.rem(ring.batch + shift, groups), ring.me),
            device_id_type=MESH,
        )

    def rows_of(block):
        return pl.ds(pl.multiple_of(block * ROWS, ROWS), ROWS)

    def load(block):
        slot = lax.rem(block, 2)
        return pltpu.make_async_copy(
            states_ref.at[rows_of(block)], states.at[slot], load_sem.at[slot]
        )

    def store(block):
        slot = lax.rem(block, 2)
        return pltpu.make_async_copy(low.at[slot], b_ref.at[rows_of(block)], store_sem.at[slot])

    load(0).start()

    kept, waiting = [], []

    def add(group, first, last):
        wide = 512

        @pl.loop(0, blocks)
        def _(block):
            rows = rows_of(block)
            left = jnp.concatenate([heads[head, rows, :] for head in group], axis=1)
            if first:

                @pl.when(block + 1 < blocks)
                def _():
                    load(block + 1).start()

                load(block).wait()
                normal, _ = norm_parts(states[lax.rem(block, 2)].astype(F32))
                total[rows, :] = DEEP_ALPHA * (normal * vec_ref[0:1, :] + vec_ref[1:2, :])
            for at in range(0, D, wide):
                right = [
                    w_out[pl.ds(pl.multiple_of(head * HD, HD), HD), at : at + wide]
                    for head in group
                ]
                total[rows, at : at + wide] += nn(left, jnp.concatenate(right, axis=0))
            if last:

                @pl.when(block >= 2)
                def _():
                    store(block - 2).wait()

                normal, _ = norm_parts(total[rows, :])
                low[lax.rem(block, 2)] = (normal * vec_ref[2:3, :] + vec_ref[3:4, :]).astype(BF)
                store(block).start()

    def work(block, other):
        turn, turns = len(kept) // 2, count // 2
        if turn == 0:
            for shift in range(1, groups):
                handed(shift).start()
                onward(shift).start()
        for part, head in enumerate((block, other)):
            go = pltpu.make_async_copy(heads.at[head], heads_ref.at[head], heads_sem.at[turn, part])
            go.start()
            kept.append(go)
            waiting.append(head)
        if turn == 1:
            for go in weights:
                go.wait()
            for shift in range(1, groups):
                handed(shift).wait()
            keep.start()
        if turn == turns - 1 or turn in (1, turns // 2, turns - 2):
            add(list(waiting), turn == 1, turn == turns - 1)
            waiting.clear()

    sends = pass_round(ring, count, 2, x_ref, heads, sems[:5], [], work)

    own_ref[...] = total[pl.ds(pl.multiple_of(ring.me * own, own), own), :]
    for block in (blocks - 2, blocks - 1):
        store(block).wait()
    for go in kept:
        go.wait()
    for go in sends:
        go.wait_send()
    for shift in range(1, groups):
        onward(shift).wait()
    keep.wait()


def gather_residual(attended, feed_own, states, vectors, w_plane, w_far, own, count, ident):
    tokens = attended.shape[0]
    pairs, groups = count // 2, lax.axis_size("batch")
    inside, anywhere = pl.BlockSpec(memory_space=pltpu.VMEM), pl.BlockSpec(memory_space=pl.ANY)
    return pl.pallas_call(
        functools.partial(residual_kernel, count, groups),
        out_shape=[
            jax.ShapeDtypeStruct((count, tokens, HD), BF),
            jax.ShapeDtypeStruct((groups - 1,) + feed_own.shape, BF),
            jax.ShapeDtypeStruct((tokens, D), BF),
            jax.ShapeDtypeStruct((D, D), BF),
            jax.ShapeDtypeStruct((own, D), F32),
        ],
        in_specs=[anywhere] * 3 + [inside] + [anywhere] * (1 + len(w_far)),
        out_specs=[anywhere] * 4 + [inside],
        scratch_shapes=[
            pltpu.VMEM((count, tokens, HD), BF),
            pltpu.VMEM((D, D), BF),
            pltpu.VMEM((tokens, D), F32),
            pltpu.VMEM((2, ROWS, D), BF),
            pltpu.VMEM((2, ROWS, D), BF),
            pltpu.SemaphoreType.DMA((groups + 1,)),
            pltpu.SemaphoreType.DMA((2,)),
            pltpu.SemaphoreType.DMA((2,)),
            pltpu.SemaphoreType.DMA((pairs, 2)),
        ]
        + ring_sems(pairs)
        + [pltpu.SemaphoreType.DMA((max(1, groups - 1),)) for _ in range(4)],
        compiler_params=vmem(collective_id=ident, has_side_effects=True),
        cost_estimate=pl.CostEstimate(
            flops=2 * tokens * D * D, bytes_accessed=200_000_000, transcendentals=0
        ),
        name="gather_residual",
    )(attended, feed_own, states, vectors, w_plane, *w_far)


class RingSum:
    def __init__(self, ring, own, sib, got, sems, out):
        self.ring, self.own, self.sib, self.got, self.out = ring, own, sib, got, out
        self.ring_s, self.ring_r, self.sib_s, self.sib_r = sems
        self.piece = own.shape[1] // SUBS

    def given(self, step, src):
        return self.ring.copy(
            src, self.sib.at[step], self.sib_s.at[step], self.sib_r.at[step], self.ring.sibling
        )

    def passed(self, step, sub):
        rows = pl.ds(sub * self.piece, self.piece)
        return self.ring.copy(
            self.own.at[step].at[rows],
            self.got.at[step].at[rows],
            self.ring_s.at[step, sub],
            self.ring_r.at[step, sub],
            self.ring.at(1),
        )

    def advance(self, step):
        last = self.ring.pairs - 1
        self.given(step, self.sib.at[step]).wait_recv()
        for sub in range(SUBS):
            rows = pl.ds(sub * self.piece, self.piece)

            total = self.own[step, rows, :].astype(F32) + self.sib[step, rows, :].astype(F32)

            @pl.when(step == 0)
            def _():
                self.own[step, rows, :] = total.astype(BF)

            @pl.when(step > 0)
            def _():
                self.passed(step - 1, sub).wait_recv()
                more = total + self.got[step - 1, rows, :].astype(F32)

                @pl.when(step < last)
                def _():
                    self.own[step, rows, :] = more.astype(BF)

                @pl.when(step == last)
                def _():
                    self.out[rows, :] = more

            @pl.when(step < last)
            def _():
                self.passed(step, sub).start()

    def finish(self):
        @pl.loop(0, self.ring.pairs - 1)
        def _(step):
            for sub in range(SUBS):
                self.passed(step, sub).wait_send()

    @staticmethod
    def scratch(pairs, rows):
        return [pltpu.VMEM((pairs - late, rows, D), BF) for late in (0, 0, 1)] + [
            pltpu.SemaphoreType.DMA((pairs, SUBS)),
            pltpu.SemaphoreType.DMA((pairs, SUBS)),
            pltpu.SemaphoreType.DMA((pairs,)),
            pltpu.SemaphoreType.DMA((pairs,)),
        ]


class Exchange:
    def __init__(self, ring, count, src, out, sems):
        self.ring, self.count, self.src, self.out = ring, count, src, out
        self.send, self.recv, self.own = sems

    def copies(self):
        ring = self.ring
        for step in range(1, self.count):
            device = lax.rem(ring.me + step, self.count)
            yield ring.copy(
                self.src.at[device],
                self.out.at[ring.me],
                self.send.at[step],
                self.recv.at[step],
                device,
            )

    def start(self):
        pltpu.make_async_copy(self.src.at[self.ring.me], self.out.at[self.ring.me], self.own).start()
        for go in self.copies():
            go.start()

    def finish(self):
        for go in self.copies():
            go.wait()
        pltpu.make_async_copy(self.src.at[self.ring.me], self.out.at[self.ring.me], self.own).wait()

    @staticmethod
    def scratch(count):
        return [pltpu.SemaphoreType.DMA((count,)) for _ in range(2)] + [pltpu.SemaphoreType.DMA]


class Spread:
    def __init__(self, ring, count, groups, src, came, sems):
        self.ring, self.count, self.groups, self.src, self.came = ring, count, groups, src, came
        self.send, self.recv = sems
        self.total = count * groups
        self.shared = self.total // src.shape[0]

    def copies(self):
        me = self.ring.batch * self.count + self.ring.me
        for step in range(1, self.total):
            flat = lax.rem(me + step, self.total)
            yield pltpu.make_async_remote_copy(
                src_ref=self.src.at[flat // self.shared],
                dst_ref=self.came.at[step],
                send_sem=self.send.at[step],
                recv_sem=self.recv.at[step],
                device_id=(flat // self.count, lax.rem(flat, self.count)),
                device_id_type=MESH,
            )

    def start(self):
        for go in self.copies():
            go.start()
        me = self.ring.batch * self.count + self.ring.me
        self.came[0] = self.src[me // self.shared]

    def finish(self):
        total = self.came[0]
        for step, go in enumerate(self.copies(), 1):
            go.wait()
            total = total + self.came[step]
        return total

    @staticmethod
    def scratch(total):
        return [pltpu.SemaphoreType.DMA((total,)) for _ in range(2)]


class GroupSum:
    def __init__(self, ring, groups, sent, came, sems, out):
        self.ring, self.groups, self.sent, self.came, self.out = ring, groups, sent, came, out
        self.send, self.recv = sems
        self.tiles, self.each = D // ROWS, D // ROWS // groups

    def group(self, tile):
        return lax.rem(self.ring.batch + 1 + tile // self.each, self.groups)

    def column(self, tile):
        return (self.group(tile) * self.each + lax.rem(tile, self.each)) * ROWS

    def copy(self, tile):
        return pltpu.make_async_remote_copy(
            src_ref=self.sent.at[tile],
            dst_ref=self.came.at[tile],
            send_sem=self.send.at[tile],
            recv_sem=self.recv.at[tile],
            device_id=(self.group(tile), self.ring.me),
            device_id_type=MESH,
        )

    def put(self, tile, values):
        away = self.tiles - self.each

        @pl.when(tile < away)
        def _():
            self.sent[tile] = values.astype(BF)
            self.copy(tile).start()

        @pl.when(tile >= away)
        def _():
            self.out[tile - away] = values.astype(BF)

    def finish(self):
        @pl.loop(0, self.each)
        def _(tile):
            total = self.out[tile].astype(F32)
            for shift in range(self.groups - 1):
                self.copy(shift * self.each + tile).wait_recv()
                total = total + self.came[shift * self.each + tile].astype(F32)
            self.out[tile] = total.astype(BF)

        @pl.loop(0, self.tiles - self.each)
        def _(tile):
            self.copy(tile).wait_send()

    @staticmethod
    def scratch(groups, width):
        away = D // ROWS - D // ROWS // groups
        return [pltpu.VMEM((away, ROWS, width), BF) for _ in range(2)] + [
            pltpu.SemaphoreType.DMA((away,)) for _ in range(2)
        ]


def norm_back(normal, inverse, slope, gain):
    scaled = slope * gain
    back = inverse * (
        scaled
        - jnp.mean(scaled, axis=-1, keepdims=True)
        - normal * jnp.mean(scaled * normal, axis=-1, keepdims=True)
    )
    return back, jnp.sum(slope * normal, axis=0, keepdims=True), jnp.sum(slope, axis=0, keepdims=True)


def feed_kernel(
    count,
    groups,
    span,
    b_ref,
    cot_ref,
    feed_own_ref,
    feed_far_ref,
    w_out_ref,
    res_ref,
    cot_own_ref,
    vec_ref,
    out_ref,
    grad_ref,
    dr_ref,
    vec_sum_ref,
    do_ref,
    dr_send,
    bs,
    cs,
    stage,
    h,
    du,
    tiles,
    w_ref,
    db_ref,
    do_send,
    *rest,
):
    ring = Ring(count)
    own = out_ref.shape[0]
    sums = [
        RingSum(ring, *rest[7 * i : 7 * i + 3], rest[7 * i + 3 : 7 * i + 7], ref)
        for i, ref in enumerate((db_ref, out_ref))
    ]
    grads = GroupSum(ring, groups, rest[14], rest[15], rest[16:18], grad_ref)
    row_sem, tile_sem, w_sem = rest[18:21]
    exchange = Exchange(ring, count, do_send, do_ref, rest[21:24])
    pairs = ring.pairs

    def weights(index):
        held = (bs, cs)[index // 2 % 2].at[index % 2]
        rows = pl.ds(index * 2 * own, 2 * own)
        return pltpu.make_async_copy(w_out_ref.at[rows], held, w_sem.at[index % 4])


    def places(step):
        return ring.at(-1 - step) * own, ring.at(1 + step, 1 - ring.core) * own

    def row_loads(step):
        slot = lax.rem(step, 2)
        return [
            pltpu.make_async_copy(
                ref.at[pl.ds(pl.multiple_of(place, own), own)],
                held.at[slot, pl.ds(half * own, own)],
                row_sem.at[slot, 2 * which + half],
            )
            for which, (ref, held) in enumerate(((b_ref, bs), (cot_ref, cs)))
            for half, place in enumerate(places(step))
        ]

    def tile_loads(tile):
        slot = lax.rem(tile, 2)
        cols = pl.ds(pl.multiple_of(grads.column(tile), ROWS), ROWS)
        return [
            pltpu.make_async_copy(ref.at[:, cols], tiles.at[slot, which], tile_sem.at[slot, which])
            for which, ref in enumerate((b_ref, cot_ref))
        ]

    def feed_rows(shift):
        part = D // groups
        begin = lax.rem(ring.batch - shift + groups, groups) * part
        src = feed_own_ref if shift == 0 else feed_far_ref.at[shift - 1]
        return pltpu.make_async_copy(
            src, w_ref.at[pl.ds(pl.multiple_of(begin, part), part)], rest[24].at[shift]
        )

    for go in row_loads(0):
        go.start()
    for shift in range(groups):
        feed_rows(shift).start()
    ring.greet_all(count)
    for shift in range(groups):
        feed_rows(shift).wait()

    def feed(step):
        slot = lax.rem(step, 2)

        @pl.when(step + 1 < pairs)
        def _():
            for go in row_loads(step + 1):
                go.start()

        for go in row_loads(step):
            go.wait()
        gate = nn(bs[slot], w_ref[:, :span])
        up = nn(bs[slot], w_ref[:, span : 2 * span])
        slope = nn(cs[slot], w_ref[:, 2 * span :])
        coef = math.sqrt(2.0 / math.pi)
        square = gate * gate
        tanh = jnp.tanh(coef * gate * (1.0 + 0.044715 * square))
        half = 0.5 * (1.0 + tanh)
        gelu = gate * half
        gelu_slope = half + 0.5 * gate * (1.0 - tanh * tanh) * (coef * (1.0 + 3 * 0.044715 * square))
        hidden = (gelu * up).astype(BF)
        both = jnp.concatenate([slope * up * gelu_slope, slope * gelu], axis=1).astype(BF)
        for part, place in enumerate(places(step)):
            rows = pl.ds(pl.multiple_of(place, own), own)
            h[rows, :] = hidden[part * own : (part + 1) * own]
            du[rows, :] = both[part * own : (part + 1) * own]

        @pl.when(step >= 2)
        def _():
            for which, each in enumerate(sums):
                each.given(step - 2, stage.at[slot, which]).wait_send()

        wide = 512
        for which, (each, left, low, high) in enumerate(
            ((sums[0], both, 0, 2 * span), (sums[1], hidden, 2 * span, 3 * span))
        ):
            for at in range(0, D, wide):
                terms = nt(left, w_ref[at : at + wide, low:high]).astype(BF)
                each.own[step, :, at : at + wide] = terms[:own]
                stage[slot, which, :, at : at + wide] = terms[own:]
            each.given(step, stage.at[slot, which]).start()

    @pl.loop(0, pairs)
    def _(step):
        feed(step)

        @pl.when(lax.rem(step, 2) == 0)
        def _():
            sums[0].advance(step // 2)

    for go in tile_loads(0):
        go.start()
    for index in range(4):
        weights(index).start()

    @pl.loop(0, grads.tiles)
    def _(tile):
        slot = lax.rem(tile, 2)

        @pl.when(tile + 1 < grads.tiles)
        def _():
            for go in tile_loads(tile + 1):
                go.start()

        for go in tile_loads(tile):
            go.wait()
        values = jnp.concatenate([tn(tiles[slot, 0], du[...]), tn(tiles[slot, 1], h[...])], axis=1)
        grads.put(tile, values)
        later = pairs // 2 + tile // 2

        @pl.when((lax.rem(tile, 2) == 1) & (later < pairs))
        def _():
            sums[0].advance(later)

    passed = pairs // 2 + grads.tiles // 2

    @pl.loop(min(passed, pairs), pairs)
    def _(step):
        sums[0].advance(step)

    sums[1].advance(0)
    normal, inverse = norm_parts(res_ref[...])
    slope = DEEP_ALPHA * cot_own_ref[...].astype(F32) + db_ref[...]
    dr, gain_sum, bias_sum = norm_back(normal, inverse, slope, vec_ref[2:3, :])
    dr_ref[...] = dr
    vec_sum_ref[...] = jnp.concatenate([gain_sum, bias_sum], axis=0)
    dr_low = dr.astype(BF)
    for index in range(D // (2 * own)):
        weights(index).wait()
        do = nt(dr_low, (bs, cs)[index // 2 % 2][index % 2]).astype(BF)
        if (index + 4) * 2 * own < D:
            weights(index + 4).start()
        for part in range(0, 2 * own, HD):
            at = index * 2 * own + part
            do_send[at // HD] = do[:, part : part + HD]
            dr_send[at // HD] = dr_low[:, at : at + HD]
    exchange.start()

    @pl.loop(1, pairs)
    def _(step):
        sums[1].advance(step)

    exchange.finish()
    grads.finish()
    for step in (pairs - 2, pairs - 1):
        for which, each in enumerate(sums):
            each.given(step, stage.at[step % 2, which]).wait_send()
    for each in sums:
        each.finish()


def feed_forward(
    b_low, cot, feed_own, feed_far, w_out, residual, cot_own, vectors, count, groups, ident
):
    tokens, span, pairs = b_low.shape[0], feed_own.shape[1] // 3, count // 2
    own = residual.shape[0]
    inside, anywhere = pl.BlockSpec(memory_space=pltpu.VMEM), pl.BlockSpec(memory_space=pl.ANY)
    return pl.pallas_call(
        functools.partial(feed_kernel, count, groups, span),
        in_specs=[anywhere] * 5 + [inside] * 3,
        out_specs=[inside] * 4 + [anywhere, inside],
        out_shape=[
            jax.ShapeDtypeStruct((own, D), F32),
            jax.ShapeDtypeStruct((D // groups // ROWS, ROWS, 3 * span), BF),
            jax.ShapeDtypeStruct((own, D), F32),
            jax.ShapeDtypeStruct((2, D), F32),
            jax.ShapeDtypeStruct((count, own, HD), BF),
            jax.ShapeDtypeStruct((count, own, HD), BF),
        ],
        scratch_shapes=[
            pltpu.VMEM((2, 2 * own, D), BF),
            pltpu.VMEM((2, 2 * own, D), BF),
            pltpu.VMEM((2, 2, own, D), BF),
            pltpu.VMEM((tokens, span), BF),
            pltpu.VMEM((tokens, 2 * span), BF),
            pltpu.VMEM((2, 2, tokens, ROWS), BF),
            pltpu.VMEM((D, 3 * span), BF),
            pltpu.VMEM((own, D), F32),
            pltpu.VMEM((count, own, HD), BF),
        ]
        + RingSum.scratch(pairs, own) * 2
        + GroupSum.scratch(groups, 3 * span)
        + [pltpu.SemaphoreType.DMA((2, 4)), pltpu.SemaphoreType.DMA((2, 2)), pltpu.SemaphoreType.DMA((4,))]
        + Exchange.scratch(count)
        + [pltpu.SemaphoreType.DMA((groups,))],
        compiler_params=vmem(62 * 1024 * 1024, collective_id=ident, has_side_effects=True),
        cost_estimate=pl.CostEstimate(
            flops=18 * tokens * D * span, bytes_accessed=250_000_000, transcendentals=0
        ),
        name="feed_forward",
    )(b_low, cot, feed_own, feed_far, w_out, residual, cot_own, vectors)


def project_kernel(
    count,
    groups,
    dp_ref,
    w_ref,
    a_ref,
    heads_ref,
    dr_ref,
    feed_ref,
    x_ref,
    dr_own_ref,
    vec_ref,
    vec_sum_ref,
    back_ref,
    grad_ref,
    feed_out_ref,
    vec_out_ref,
    stage,
    tiles,
    da_ref,
    vec_send,
    vec_came,
    *rest,
):
    ring = Ring(count)
    own = da_ref.shape[0]
    sums = RingSum(ring, *rest[:3], rest[3:7], da_ref)
    grads = GroupSum(ring, groups, rest[7], rest[8], rest[9:11], grad_ref)
    tile_sem = rest[11]
    feed = Exchange(ring, count, feed_ref, feed_out_ref, rest[12:15])
    spread = Spread(ring, count, groups, vec_send, vec_came, rest[15:17])
    pairs, width = ring.pairs, heads_ref.shape[2]

    def places(step):
        return ring.at(-1 - step) * own, ring.at(1 + step, 1 - ring.core) * own

    def tile_loads(tile):
        slot = lax.rem(tile, 2)
        begin = pl.multiple_of(grads.column(tile), ROWS)
        loads = [
            pltpu.make_async_copy(
                a_ref.at[:, pl.ds(begin, ROWS)], tiles.at[slot, 0], tile_sem.at[slot, 0]
            )
        ]
        for part in range(ROWS // width):
            loads.append(
                pltpu.make_async_copy(
                    heads_ref.at[begin // width + part],
                    tiles.at[slot, 1, :, pl.ds(part * width, width)],
                    tile_sem.at[slot, 1 + part],
                )
            )
        return loads

    for go in tile_loads(0):
        go.start()
    ring.greet_whole(count)
    feed.start()

    def terms_of(step):
        slot = lax.rem(step, 2)

        @pl.when(step >= 2)
        def _():
            sums.given(step - 2, stage.at[slot]).wait_send()

        left = jnp.concatenate(
            [dp_ref[pl.ds(pl.multiple_of(place, own), own), :] for place in places(step)], axis=0
        )
        wide = 512
        for at in range(0, D, wide):
            terms = nt(left, w_ref[at : at + wide, :]).astype(BF)
            sums.own[step, :, at : at + wide] = terms[:own]
            stage[slot, :, at : at + wide] = terms[own:]
        sums.given(step, stage.at[slot]).start()

    terms_of(0)
    sums.advance(0)

    @pl.loop(0, grads.tiles)
    def _(tile):
        slot = lax.rem(tile, 2)

        @pl.when(tile + 1 < grads.tiles)
        def _():
            for go in tile_loads(tile + 1):
                go.start()

        for go in tile_loads(tile):
            go.wait()
        values = jnp.concatenate(
            [tn(tiles[slot, 0], dp_ref[...]), tn(tiles[slot, 1], dr_ref[...])], axis=1
        )
        grads.put(tile, values)

        @pl.when(tile + 1 < pairs)
        def _():
            terms_of(tile + 1)

        @pl.when((lax.rem(tile, 2) == 1) & (tile // 2 + 1 < pairs))
        def _():
            sums.advance(tile // 2 + 1)

    @pl.loop(1 + grads.tiles // 2, pairs)
    def _(step):
        sums.advance(step)

    normal, inverse = norm_parts(x_ref[...].astype(F32))
    slope = DEEP_ALPHA * dr_own_ref[...] + da_ref[...]
    back, gain_sum, bias_sum = norm_back(normal, inverse, slope, vec_ref[0:1, :])
    back_ref[...] = back.astype(BF)
    kinds = [gain_sum, bias_sum, vec_sum_ref[0:1, :], vec_sum_ref[1:2, :]]
    for tile in range(D // LANES):
        for kind, values in enumerate(kinds):
            vec_send[tile, kind : kind + 1, :] = values[:, tile * LANES : (tile + 1) * LANES]
    spread.start()
    grads.finish()
    for step in (pairs - 2, pairs - 1):
        sums.given(step, stage.at[step % 2]).wait_send()
    sums.finish()
    vec_out_ref[...] = spread.finish()
    feed.finish()


def project_back(
    dp, w_qkv, a_low, heads, dr_cols, grad_feed, states, dr, vectors, vec_sums, count, groups, ident
):
    tokens, pairs = dp.shape[0], count // 2
    own, width = dr.shape[0], 3 * HD + dr_cols.shape[1]
    inside, anywhere = pl.BlockSpec(memory_space=pltpu.VMEM), pl.BlockSpec(memory_space=pl.ANY)
    return pl.pallas_call(
        functools.partial(project_kernel, count, groups),
        in_specs=[inside, inside, anywhere, anywhere, inside, anywhere] + [inside] * 4,
        out_specs=[inside, inside, anywhere, inside],
        out_shape=[
            jax.ShapeDtypeStruct((own, D), BF),
            jax.ShapeDtypeStruct((D // groups // ROWS, ROWS, width), BF),
            jax.ShapeDtypeStruct(grad_feed.shape, BF),
            jax.ShapeDtypeStruct((8, LANES), F32),
        ],
        scratch_shapes=[
            pltpu.VMEM((2, own, D), BF),
            pltpu.VMEM((2, 2, tokens, ROWS), BF),
            pltpu.VMEM((own, D), F32),
            pltpu.VMEM((D // LANES, 8, LANES), F32),
            pltpu.VMEM((count * groups, 8, LANES), F32),
        ]
        + RingSum.scratch(pairs, own)
        + GroupSum.scratch(groups, width)
        + [pltpu.SemaphoreType.DMA((2, 1 + ROWS // HD))]
        + Exchange.scratch(count)
        + Spread.scratch(count * groups),
        compiler_params=vmem(collective_id=ident, has_side_effects=True),
        cost_estimate=pl.CostEstimate(
            flops=4 * tokens * D * 3 * HD, bytes_accessed=200_000_000, transcendentals=0
        ),
        name="project_back",
    )(dp, w_qkv, a_low, heads, dr_cols, grad_feed, states, dr, vectors, vec_sums)


def norm_parts(values):
    centre = values - jnp.mean(values, axis=-1, keepdims=True)
    inverse = lax.rsqrt(jnp.mean(centre * centre, axis=-1, keepdims=True) + LN_EPS)
    return centre * inverse, inverse


def qkv_kernel(x_ref, w_ref, vec_ref, cos_ref, sin_ref, a_ref, q_ref, k_ref, v_ref, kt_ref, vt_ref):
    normal, _ = norm_parts(x_ref[...].astype(F32))
    low = (normal * vec_ref[0:1, :] + vec_ref[1:2, :]).astype(BF)
    a_ref[...] = low
    projected = nn(low, w_ref[...])
    for index, ref in enumerate((q_ref, k_ref)):
        part = projected[:, index * HD : (index + 1) * HD]
        turned = part * cos_ref[...] + pltpu.roll(part, HD // 2, 1) * sin_ref[...]
        ref[...] = turned.astype(BF)
    kt_ref[...] = turned.T.astype(BF)[None]
    v_ref[...] = projected[:, 2 * HD :].astype(BF)
    vt_ref[...] = projected[:, 2 * HD :].T.astype(BF)[None]


def norm_and_project(states, w_qkv, vectors, cosine, sine):
    tokens = states.shape[0]
    whole = lambda shape: pl.BlockSpec(shape, lambda i: (0, 0))
    rows = lambda width: pl.BlockSpec((ROWS, width), lambda i: (i, 0))
    turned = pl.BlockSpec((1, HD, ROWS), lambda i: (i * ROWS // KEYS, 0, i % (KEYS // ROWS)))
    return pl.pallas_call(
        qkv_kernel,
        grid=(tokens // ROWS,),
        in_specs=[rows(D), whole((D, 3 * HD)), whole(vectors.shape), rows(HD), rows(HD)],
        out_specs=[rows(D), rows(HD), rows(HD), rows(HD), turned, turned],
        out_shape=[jax.ShapeDtypeStruct((tokens, D), BF)]
        + [jax.ShapeDtypeStruct((tokens, HD), BF) for _ in range(3)]
        + [jax.ShapeDtypeStruct((tokens // KEYS, HD, KEYS), BF) for _ in range(2)],
        compiler_params=vmem(),
        cost_estimate=pl.CostEstimate(
            flops=2 * tokens * D * 3 * HD, bytes_accessed=24_000_000, transcendentals=0
        ),
        name="norm_and_project",
    )(states, w_qkv, vectors, cosine, sine)


def masked_scores(block, query, k_ref, first_ref, last_ref, keys):
    place = block * ROWS + lax.broadcasted_iota(jnp.int32, (1, LANES), 1)
    scores = nt(k_ref[keys], query) * HD ** (-0.5)
    parts = []
    for at in range(0, ROWS, LANES):
        seen = (place + at >= first_ref[keys]) & (place + at < last_ref[keys])
        parts.append(jnp.where(seen, scores[:, at : at + LANES], NEG_LARGE))
    return jnp.concatenate(parts, axis=1)


def attend_kernel(
    low_ref, high_ref, q_ref, k_ref, vt_ref, first_ref, last_ref, o_ref, full_ref, log_ref, held
):
    block = pl.program_id(0)
    query = q_ref[...]

    def score(keys, top):
        scores = masked_scores(block, query, k_ref, first_ref, last_ref, keys)
        held[keys] = scores
        return jnp.maximum(top, jnp.max(scores, axis=0, keepdims=True))

    def add(keys, carry):
        total, out = carry
        weight = jnp.exp(held[keys] - top)
        total = total + jnp.sum(weight, axis=0, keepdims=True)
        return total, out + nn(vt_ref[keys], weight.astype(BF))

    low, high = low_ref[block], high_ref[block]
    top = lax.fori_loop(low, high, score, jnp.full((1, ROWS), NEG_LARGE, F32))
    total, out = lax.fori_loop(
        low, high, add, (jnp.zeros((1, ROWS), F32), jnp.zeros((HD, ROWS), F32))
    )
    out = out / total
    o_ref[...] = out.T.astype(BF)
    full_ref[...] = out[None]
    log_ref[...] = (top + jnp.log(total))[None]


def attend(query, key, value_t, spans):
    tokens = query.shape[0]
    blocks, span = tokens // ROWS, tokens // KEYS
    first, last, low, high = spans
    rows = pl.BlockSpec((ROWS, HD), lambda i, *_: (i, 0))
    one = lambda shape: pl.BlockSpec((1,) + shape, lambda i, *_: (i, 0, 0))
    whole = lambda shape: pl.BlockSpec(shape, lambda i, *_: (0,) * len(shape))
    return pl.pallas_call(
        attend_kernel,
        grid_spec=pltpu.PrefetchScalarGridSpec(
            num_scalar_prefetch=2,
            grid=(blocks,),
            in_specs=[
                rows,
                whole((span, KEYS, HD)),
                whole((span, HD, KEYS)),
                whole((span, KEYS, LANES)),
                whole((span, KEYS, LANES)),
            ],
            out_specs=[rows, one((HD, ROWS)), one((1, ROWS))],
            scratch_shapes=[pltpu.VMEM((span, KEYS, ROWS), F32)],
        ),
        out_shape=[
            jax.ShapeDtypeStruct((tokens, HD), BF),
            jax.ShapeDtypeStruct((blocks, HD, ROWS), F32),
            jax.ShapeDtypeStruct((blocks, 1, ROWS), F32),
        ],
        compiler_params=vmem(),
        cost_estimate=pl.CostEstimate(
            flops=2 * tokens * tokens * HD, bytes_accessed=4_000_000, transcendentals=0
        ),
        name="attend",
    )(low, high, query, key.reshape(span, KEYS, HD), value_t, first, last)


def attend_back_kernel(
    low_ref,
    high_ref,
    q_ref,
    g_ref,
    full_ref,
    log_ref,
    k_ref,
    kt_ref,
    v_ref,
    first_ref,
    last_ref,
    cos_ref,
    sin_ref,
    o_ref,
    dk_ref,
    dv_ref,
):
    block = pl.program_id(0)
    blocks = pl.num_programs(0)
    scale = HD ** (-0.5)

    @pl.when(block == 0)
    def _():
        dk_ref[...] = jnp.zeros_like(dk_ref)
        dv_ref[...] = jnp.zeros_like(dv_ref)

    query, grad = q_ref[...], g_ref[...]
    inner = jnp.sum(grad.astype(F32).T * full_ref[0], axis=0, keepdims=True)
    log = log_ref[0]

    def one(keys, total):
        scores = masked_scores(block, query, k_ref, first_ref, last_ref, keys)
        weight = jnp.exp(scores - log)
        slope = (weight * (nt(v_ref[keys], grad) - inner)).astype(BF)
        dv_ref[keys] += nn(weight.astype(BF), grad)
        dk_ref[keys] += nn(slope, query)
        return total + nn(kt_ref[keys], slope)

    total = lax.fori_loop(low_ref[block], high_ref[block], one, jnp.zeros((HD, ROWS), F32))

    def turn_back(values, cosine, sine):
        values = (values * scale).astype(BF).astype(F32)
        return (values * cosine - pltpu.roll(values, HD // 2, 1) * sine).astype(BF)

    rows = pl.ds(pl.multiple_of(block * ROWS, ROWS), ROWS)
    o_ref[rows, 0:HD] = turn_back(total.T, cos_ref[rows, :], sin_ref[rows, :])

    @pl.when(block == blocks - 1)
    def _():
        for part in range(dk_ref.shape[0]):
            there = pl.ds(part * KEYS, KEYS)
            o_ref[there, HD : 2 * HD] = turn_back(
                dk_ref[part], cos_ref[there, :], sin_ref[there, :]
            )
            o_ref[there, 2 * HD :] = dv_ref[part].astype(BF)


def attend_back(query, key, key_t, value, grad, full, log, spans, cosine, sine):
    tokens = query.shape[0]
    blocks, span = tokens // ROWS, tokens // KEYS
    first, last, low, high = spans
    rows = pl.BlockSpec((ROWS, HD), lambda i, *_: (i, 0))
    one = lambda shape: pl.BlockSpec((1,) + shape, lambda i, *_: (i, 0, 0))
    whole = lambda shape: pl.BlockSpec(shape, lambda i, *_: (0,) * len(shape))
    return pl.pallas_call(
        attend_back_kernel,
        grid_spec=pltpu.PrefetchScalarGridSpec(
            num_scalar_prefetch=2,
            grid=(blocks,),
            in_specs=[
                rows,
                rows,
                one((HD, ROWS)),
                one((1, ROWS)),
                whole((span, KEYS, HD)),
                whole((span, HD, KEYS)),
                whole((span, KEYS, HD)),
                whole((span, KEYS, LANES)),
                whole((span, KEYS, LANES)),
                whole((tokens, HD)),
                whole((tokens, HD)),
            ],
            out_specs=whole((tokens, 3 * HD)),
            scratch_shapes=[pltpu.VMEM((span, KEYS, HD), F32) for _ in range(2)],
        ),
        out_shape=jax.ShapeDtypeStruct((tokens, 3 * HD), BF),
        compiler_params=vmem(),
        cost_estimate=pl.CostEstimate(
            flops=5 * tokens * tokens * HD, bytes_accessed=6_000_000, transcendentals=0
        ),
        name="attend_back",
    )(
        low,
        high,
        query,
        grad,
        full,
        log,
        key.reshape(span, KEYS, HD),
        key_t,
        value.reshape(span, KEYS, HD),
        first,
        last,
        cosine,
        sine,
    )


def windows(at, span, count):
    total = 4 * D + 3 * FF + 4
    result = []
    for index in range(count):
        width = max(0, min(span, FF - index * span))
        begin = at + index * span
        turn = begin % LANES
        window = -(-(turn + width) // LANES) * LANES if width else 0
        window = min(window, (total - begin + turn) // LANES * LANES)
        result.append((begin - turn, window, turn, width))
    return result


FEED_AT = (4 * D, 4 * D + FF, 4 * D + 2 * FF)


def lay_out_kernel(count, span, m_ref, qkv_ref, out_ref, feed_ref):
    rows = m_ref.shape[0]
    for index in range(count):
        for part in range(3):
            at = part * D + index * HD
            qkv_ref[index, :, part * HD : (part + 1) * HD] = m_ref[:, at : at + HD].astype(BF)
    out_ref[...] = m_ref[:, 3 * D : 4 * D].astype(BF)
    column = lax.broadcasted_iota(jnp.int32, (rows, span), 1)
    for part, at in enumerate(FEED_AT):
        for index, (begin, window, turn, width) in enumerate(windows(at, span, count)):
            if width == 0:
                piece = jnp.zeros((rows, span), F32)
            else:
                piece = m_ref[:, begin : begin + window]
                if window < span:
                    piece = jnp.concatenate(
                        [piece, jnp.zeros((rows, span - window), F32)], axis=1
                    )
                if turn:
                    piece = pltpu.roll(piece, piece.shape[1] - turn, 1)
                piece = piece[:, :span]
                if width < span:
                    piece = jnp.where(column < width, piece, 0.0)
            feed_ref[index, :, part * span : (part + 1) * span] = piece.astype(BF)


def lay_out(master, count, span):
    rows = master.shape[0]
    inside = pl.BlockSpec(memory_space=pltpu.VMEM)
    return pl.pallas_call(
        functools.partial(lay_out_kernel, count, span),
        out_shape=[
            jax.ShapeDtypeStruct((count, rows, 3 * HD), BF),
            jax.ShapeDtypeStruct((rows, D), BF),
            jax.ShapeDtypeStruct((count, rows, 3 * span), BF),
        ],
        in_specs=[inside],
        out_specs=[inside] * 3,
        compiler_params=vmem(),
        cost_estimate=pl.CostEstimate(flops=0, bytes_accessed=10_000_000, transcendentals=0),
        name="lay_out",
    )(master)


STEP_COLS = 2048


def tile_of_part(ref, part, at, begin, rows, span):
    turn = at % LANES
    index = (begin - at + turn) // LANES
    tiles = span // LANES

    def piece(index):
        if index < 0 or index * LANES >= FF:
            return None
        device, inner = divmod(index, tiles)
        low = part * span + inner * LANES
        values = ref[device, :, low : low + LANES].astype(F32)
        return pltpu.roll(values, turn, 1) if turn else values

    lane = lax.broadcasted_iota(jnp.int32, (rows, LANES), 1)
    here, before = piece(index), piece(index - 1) if turn else None
    if here is None:
        return before
    return here if before is None else jnp.where(lane < turn, before, here)


def feed_tile(begin, feed_ref, vec_ref, rows, span):
    lane = lax.broadcasted_iota(jnp.int32, (rows, LANES), 1)
    total = 4 * D + 3 * FF + 4
    value = None
    for part, at in enumerate(FEED_AT):
        if at < begin + LANES and at + FF > begin:
            piece = tile_of_part(feed_ref, part, at, begin, rows, span)
            value = piece if value is None else jnp.where(lane < at - begin, value, piece)
    if begin + LANES > total - 4:
        vec = pltpu.roll(vec_ref[...], (total - 4) % LANES, 1)
        value = vec if value is None else jnp.where(lane < total - 4 - begin, value, vec)
    return value


def update_kernel(first_step, steps, tile_at, sources, *refs):
    grads, (m_ref, f_ref, s_ref, a_ref), outs = refs[:sources], refs[sources : sources + 4], refs[-4:]
    nm_ref, nf_ref, ns_ref, na_ref = outs
    rows = m_ref.shape[0]
    total = 4 * D + 3 * FF + 4

    def one(begin, cols):
        g = tile_at(begin, *grads)
        rate, decay = LR_MAT, DECAY_MAT
        if begin + LANES > total - 4:
            vector = begin + lax.broadcasted_iota(jnp.int32, (1, LANES), 1) >= total - 4
            rate, decay = jnp.where(vector, LR_VEC, LR_MAT), jnp.where(vector, 0.0, DECAY_MAT)
        new_first = BETA_ONE * f_ref[:, cols] + (1.0 - BETA_ONE) * g
        new_second = BETA_TWO * s_ref[:, cols] + (1.0 - BETA_TWO) * g * g
        nf_ref[:, cols] = new_first
        ns_ref[:, cols] = new_second
        root = jnp.sqrt(new_second * (1.0 / (1.0 - BETA_TWO**STEP))) + ADAM_EPS
        corrected = new_first * (1.0 / (1.0 - BETA_ONE**STEP)) / root
        master = m_ref[:, cols]
        new_master = master - rate * (corrected + decay * master)
        nm_ref[:, cols] = new_master
        na_ref[:, cols] = EMA_RATE * a_ref[:, cols] + (1.0 - EMA_RATE) * new_master

    for step in range(steps):

        @pl.when(pl.program_id(0) == step)
        def _():
            for at in range(0, STEP_COLS, LANES):
                begin = (first_step + step) * STEP_COLS + at
                if begin < total:
                    one(begin, slice(at, at + LANES))


def update(grads, tile_at, state, first_step, steps, done=()):
    rows, columns = state[0].shape
    whole = lambda values: pl.BlockSpec(values.shape, lambda i: (0,) * values.ndim)
    cols = pl.BlockSpec((rows, STEP_COLS), lambda i: (0, first_step + i))
    return pl.pallas_call(
        functools.partial(update_kernel, first_step, steps, tile_at, len(grads)),
        grid=(steps,),
        in_specs=[whole(g) for g in grads]
        + [cols] * 4
        + [pl.BlockSpec(memory_space=pl.ANY)] * len(done),
        out_specs=[cols] * 4,
        out_shape=[jax.ShapeDtypeStruct((rows, columns), F32) for _ in range(4)],
        input_output_aliases={len(grads) + 4 + i: i for i in range(len(done))},
        compiler_params=vmem(),
        cost_estimate=pl.CostEstimate(
            flops=0, bytes_accessed=36 * rows * steps * STEP_COLS, transcendentals=0
        ),
        name=f"update_{first_step}",
    )(*grads, *state, *done)


def chain_spans(lengths, prefix, padding, total):
    ends = jnp.cumsum(lengths, dtype=jnp.int32)
    starts = ends - lengths
    token = jnp.arange(total, dtype=jnp.int32)
    member = (token[:, None] >= starts[None, :]) & (token[:, None] < ends[None, :])
    pick = lambda values: jnp.sum(jnp.where(member, values[None, :], 0), axis=1, dtype=jnp.int32)
    start, end, pre, live = pick(starts), pick(ends), pick(prefix), pick(lengths - padding)
    place = token - start
    first = jnp.where(place < pre, start, token)
    first = jnp.where(place < live, first, 2 * total)
    low = start[::ROWS] // KEYS
    high = (end[ROWS - 1 :: ROWS] + KEYS - 1) // KEYS
    cut = lambda values: jnp.broadcast_to(values[:, None], (total, LANES)).reshape(-1, KEYS, LANES)
    return (cut(first), cut(end), low, high), place


def rotary_tables(place):
    half = HD // 2
    freq = ROPE_BASE ** (-jnp.arange(half, dtype=F32) / half)
    angles = place.astype(F32)[:, None] * freq[None, :]
    cosine, sine = jnp.cos(angles), jnp.sin(angles)
    return jnp.concatenate([cosine, cosine], axis=1), jnp.concatenate([-sine, sine], axis=1)


def to_rows(grad):
    blocks = grad.reshape(lax.axis_size("seq"), -1, grad.shape[-1])
    return lax.all_to_all(blocks, "seq", split_axis=0, concat_axis=0, tiled=True)


def on_device(hidden_in, cotangent, master, first, second, average, lengths, prefix, padding):
    groups, seq = lax.axis_size("batch"), lax.axis_size("seq")
    own = hidden_in.shape[0]
    tokens = own * seq
    rows = master.shape[0]
    span = -(-FF // (seq * LANES)) * LANES
    vec_cut = master[:, 4 * D + 3 * FF :].astype(BF).astype(F32).T
    vec_cut = jnp.pad(vec_cut, ((0, 8 - vec_cut.shape[0]), (0, LANES - rows)))[None]
    qkv_cut, out_cut, feed_cut = lay_out(master, seq, span)
    states, w_qkv, vectors = ring_gather(hidden_in, [qkv_cut, vec_cut], seq, 1)
    states = states.reshape(tokens, D)
    w_qkv = w_qkv.reshape(D, 3 * HD)
    vectors = vectors[..., :rows].transpose(2, 0, 1, 3).reshape(8, D)
    w_plane = lax.all_gather(out_cut, "seq", axis=0, tiled=True)
    feed_cut, w_plane, w_qkv = lax.optimization_barrier((feed_cut, w_plane, w_qkv))
    half = w_plane.shape[0] // 2
    half_mine = lax.dynamic_slice_in_dim(w_plane, lax.rem(lax.axis_index("seq"), 2) * half, half, 0)
    w_far = []
    for shift in range(1, groups):
        far = [(index, (index + shift) % groups) for index in range(groups)]
        w_far.append(lax.ppermute(half_mine, "batch", far))
    feed_own = lax.all_to_all(feed_cut, "seq", split_axis=0, concat_axis=0, tiled=True)
    feed_own = feed_own.reshape(D // groups, 3 * span)
    cot_all = lax.all_gather(cotangent, "seq", axis=0, tiled=True)

    spans, place = chain_spans(lengths[0], prefix[0], padding[0], tokens)
    cosine, sine = rotary_tables(place)
    a_low, query, key, value, key_t, value_t = norm_and_project(states, w_qkv, vectors, cosine, sine)
    attended, full, log = attend(query, key, value_t, spans)
    heads, feed_far, b_low, w_out, residual = gather_residual(
        attended, feed_own, states, vectors, w_plane, w_far, own, seq, 2
    )
    out_sum, grad_feed, dr, vec_sums, do, dr_cut = feed_forward(
        b_low, cot_all, feed_own, feed_far, w_out, residual, cotangent, vectors, seq, groups, 3
    )
    dr_cols = lax.all_to_all(dr_cut, "seq", split_axis=0, concat_axis=0, tiled=True)
    normal_two, _ = norm_parts(residual)
    output = DEEP_ALPHA * (normal_two * vectors[2:3] + vectors[3:4]) + out_sum

    dp = attend_back(query, key, key_t, value, do.reshape(tokens, HD), full, log, spans, cosine, sine)
    input_grad, grad_attn, grad_feed, grad_vec = project_back(
        dp,
        w_qkv,
        a_low,
        heads,
        dr_cols.reshape(tokens, HD),
        grad_feed.reshape(seq, rows, 3 * span),
        hidden_in,
        dr,
        vectors,
        vec_sums,
        seq,
        groups,
        4,
    )
    grad_attn = to_rows(grad_attn)
    place = lax.rem(lax.axis_index("batch") * seq + lax.axis_index("seq"), LANES // rows) * rows
    grad_vec = lax.dynamic_slice_in_dim(grad_vec, place, rows, 1)[:4].T
    grad_vec = jnp.pad(grad_vec, ((0, 0), (0, LANES - 4)))

    def attn_tile(begin, ref):
        part, index = divmod(begin // HD, seq)
        return ref[index, :, part * HD : (part + 1) * HD].astype(F32)

    def other_tile(begin, feed_ref, vec_ref):
        return feed_tile(begin, feed_ref, vec_ref, rows, span)

    state = (master, first, second, average)
    steps, attn_steps = -(-master.shape[1] // STEP_COLS), 4 * D // STEP_COLS
    updated = update([grad_feed, grad_vec], other_tile, state, attn_steps, steps - attn_steps)
    updated = update([grad_attn], attn_tile, state, 0, attn_steps, updated)
    return (
        output.astype(BF),
        input_grad,
        *updated,
    )


def solution(mesh):
    spread = P(("batch", "seq"), None)
    return jax.shard_map(
        on_device,
        mesh=mesh,
        in_specs=(spread,) * 6 + (P("batch", None),) * 3,
        out_specs=(spread,) * 6,
        check_vma=False,
    )
```

```python
import functools
import math

import jax
import jax.numpy as jnp
from jax import lax
from jax.experimental import pallas as pl
from jax.experimental.pallas import tpu as pltpu
from jax.sharding import PartitionSpec as P

D = 2048
H = 16
HD = 128
FF = 5461
STEP = 10

DEEP_ALPHA = math.sqrt(48.0)
ROPE_BASE = 10000.0
NEG_LARGE = -1e30
LN_EPS = 1e-05
BETA_ONE = 0.9
BETA_TWO = 0.95
ADAM_EPS = 1e-08
LR_MAT = 0.01
LR_VEC = 0.2
DECAY_MAT = 0.1
EMA_RATE = 0.9

BF = jnp.bfloat16
F32 = jnp.float32
MESH = pl.DeviceIdType.MESH
ROWS = 256
KEYS = 512
LANES = 128
SUBS = 4
VMEM_BIG = 56 * 1024 * 1024


def nt(left, right):
    return lax.dot_general(left, right, (((1,), (1,)), ((), ())), preferred_element_type=F32)


def tn(left, right):
    return lax.dot_general(left, right, (((0,), (0,)), ((), ())), preferred_element_type=F32)


def nn(left, right):
    return jnp.dot(left, right, preferred_element_type=F32)


def vmem(limit=VMEM_BIG, **more):
    return pltpu.CompilerParams(vmem_limit_bytes=limit, **more)


class Ring:
    def __init__(self, count):
        self.pairs = count // 2
        self.batch, self.me = lax.axis_index("batch"), lax.axis_index("seq")
        self.core = lax.rem(self.me, 2)
        y, z = lax.rem(self.me // 2, 2), self.me // 4
        self.place = jnp.where(y == 0, z, self.pairs - 1 - z)
        self.sibling = self.me + 1 - 2 * self.core

    def at(self, steps, core=None):
        place = lax.rem(self.place + (1 - 2 * self.core) * steps + 4 * self.pairs, self.pairs)
        half = self.pairs // 2
        pair = jnp.where(place < half, 2 * place, 2 * (self.pairs - 1 - place) + 1)
        return pair * 2 + (self.core if core is None else core)

    def greet_all(self, count):
        barrier = pltpu.get_barrier_semaphore()
        groups = lax.axis_size("batch")
        for step in range(1, count):
            device = lax.rem(self.me + step, count)
            pl.semaphore_signal(barrier, inc=1, device_id=(self.batch, device), device_id_type=MESH)
        for shift in range(1, groups):
            group = lax.rem(self.batch + shift, groups)
            pl.semaphore_signal(barrier, inc=1, device_id=(group, self.me), device_id_type=MESH)
        pl.semaphore_wait(barrier, count + groups - 2)

    def greet_groups(self, groups):
        barrier = pltpu.get_barrier_semaphore()
        for device in (self.at(-1), self.sibling):
            pl.semaphore_signal(barrier, inc=1, device_id=(self.batch, device), device_id_type=MESH)
        for shift in range(1, groups):
            group = lax.rem(self.batch + shift, groups)
            pl.semaphore_signal(barrier, inc=1, device_id=(group, self.me), device_id_type=MESH)
        pl.semaphore_wait(barrier, 1 + groups)

    def greet_whole(self, count):
        barrier = pltpu.get_barrier_semaphore()
        total = count * lax.axis_size("batch")
        for step in range(1, total):
            flat = lax.rem(self.batch * count + self.me + step, total)
            there = (flat // count, lax.rem(flat, count))
            pl.semaphore_signal(barrier, inc=1, device_id=there, device_id_type=MESH)
        pl.semaphore_wait(barrier, total - 1)

    def copy(self, src, dst, send, recv, device):
        return pltpu.make_async_remote_copy(
            src_ref=src,
            dst_ref=dst,
            send_sem=send,
            recv_sem=recv,
            device_id=(self.batch, device),
            device_id_type=MESH,
        )


class Columns:
    def __init__(self, ring, count, src, out, sems):
        self.ring, self.count, self.src, self.out = ring, count, src, out
        self.send, self.recv, self.on_send, self.on_recv, self.own = sems
        self.groups = lax.axis_size("batch")

    def piece(self, device):
        return self.src.at[device] if self.src.shape[0] == self.count else self.src.at[0]

    def group(self, shift):
        return lax.rem(self.ring.batch + shift + self.groups, self.groups)

    def start(self):
        ring, sends = self.ring, []
        self.mine = pltpu.make_async_copy(
            self.piece(ring.me), self.out.at[ring.batch, ring.me], self.own
        )
        self.mine.start()
        for step in range(1, self.count):
            device = lax.rem(ring.me + step, self.count)
            go = ring.copy(
                self.piece(device),
                self.out.at[ring.batch, ring.me],
                self.send.at[step],
                self.recv.at[step],
                device,
            )
            go.start()
            sends.append(go)
        self.sends = sends + self.forward(0)

    def forward(self, step):
        ring, sends = self.ring, []
        device = lax.rem(ring.me - step + self.count, self.count)
        here = self.out.at[ring.batch, device]
        for shift in range(1, self.groups):
            go = pltpu.make_async_remote_copy(
                src_ref=self.piece(ring.me) if step == 0 else here,
                dst_ref=here,
                send_sem=self.on_send.at[shift - 1, step],
                recv_sem=self.on_recv.at[shift - 1, step],
                device_id=(self.group(shift), ring.me),
                device_id_type=MESH,
            )
            go.start()
            sends.append(go)
        return sends

    def pass_on(self, step):
        ring = self.ring
        device = lax.rem(ring.me - step + self.count, self.count)
        here = self.out.at[ring.batch, device]
        ring.copy(here, here, self.send.at[step], self.recv.at[step], device).wait_recv()
        self.sends += self.forward(step)

    def finish(self):
        ring = self.ring
        for step in range(self.count):
            device = lax.rem(ring.me - step + self.count, self.count)
            for shift in range(1, self.groups):
                here = self.out.at[self.group(-shift), device]
                pltpu.make_async_remote_copy(
                    src_ref=here,
                    dst_ref=here,
                    send_sem=self.on_send.at[shift - 1, step],
                    recv_sem=self.on_recv.at[shift - 1, step],
                    device_id=(self.group(shift), ring.me),
                    device_id_type=MESH,
                ).wait_recv()
        for go in self.sends:
            go.wait_send()
        self.mine.wait()


class Lap:
    def __init__(self, ring, x_ref, o_ref, sems):
        self.ring, self.x_ref, self.o_ref = ring, x_ref, o_ref
        self.ring_s, self.ring_r, self.sib_s, self.sib_r, own_sem = sems
        self.piece = x_ref.shape[0] // SUBS
        self.own = pltpu.make_async_copy(x_ref, o_ref.at[ring.me], own_sem)
        self.sends = []

    def step(self, step):
        ring = self.ring
        if step == 0:
            self.own.start()
        for sub in range(SUBS):
            rows = pl.ds(sub * self.piece, self.piece)
            dst = self.o_ref.at[ring.at(-step)].at[rows]
            src = self.x_ref.at[rows] if step == 0 else dst
            if step > 0:
                before = self.ring_s.at[step - 1, sub], self.ring_r.at[step - 1, sub]
                ring.copy(dst, dst, *before, ring.at(1)).wait_recv()
            if step < ring.pairs - 1:
                now = self.ring_s.at[step, sub], self.ring_r.at[step, sub]
                self.sends.append(ring.copy(src, dst, *now, ring.at(1)))
                self.sends[-1].start()
            across = self.sib_s.at[step, sub], self.sib_r.at[step, sub]
            self.sends.append(ring.copy(src, dst, *across, ring.sibling))
            self.sends[-1].start()

    def finish(self):
        ring = self.ring
        for step in range(ring.pairs):
            other = ring.at(step, 1 - ring.core)
            for sub in range(SUBS):
                dst = self.o_ref.at[other].at[pl.ds(sub * self.piece, self.piece)]
                across = self.sib_s.at[step, sub], self.sib_r.at[step, sub]
                ring.copy(dst, dst, *across, ring.sibling).wait_recv()
        for go in self.sends:
            go.wait_send()
        self.own.wait()


def pass_round(ring, count, lag, x_ref, o_ref, sems, columns, work, lap):
    ring_s, ring_r, sib_s, sib_r, own_sem = sems
    piece = x_ref.shape[0] // SUBS
    own = pltpu.make_async_copy(x_ref, o_ref.at[ring.me], own_sem)
    own.start()
    ring.greet_all(count)
    following, sends = ring.at(1), []
    ahead = 1

    def complete(step):
        if step == 0:
            own.wait()
        other = ring.at(step, 1 - ring.core)
        for sub in range(SUBS):
            dst = o_ref.at[other].at[pl.ds(sub * piece, piece)]
            ring.copy(
                dst, dst, sib_s.at[step, sub], sib_r.at[step, sub], ring.sibling
            ).wait_recv()
        work(ring.at(-step), other)

    for step in range(ring.pairs):
        block = ring.at(-step)
        for sub in range(SUBS):
            rows = pl.ds(sub * piece, piece)
            dst = o_ref.at[block].at[rows]
            src = x_ref.at[rows] if step == 0 else dst
            if step > 0:
                ring.copy(
                    dst, dst, ring_s.at[step - 1, sub], ring_r.at[step - 1, sub], following
                ).wait_recv()
            if step < ring.pairs - 1:
                go = ring.copy(src, dst, ring_s.at[step, sub], ring_r.at[step, sub], following)
                go.start()
                sends.append(go)
            go = ring.copy(src, dst, sib_s.at[step, sub], sib_r.at[step, sub], ring.sibling)
            go.start()
            sends.append(go)
        if step == 0:
            for column in columns:
                column.start()
        else:
            upto = count if step == ring.pairs - 1 else min(count, 1 + 2 * step)
            for passed in range(ahead, max(ahead, upto)):
                for column in columns:
                    column.pass_on(passed)
            ahead = max(ahead, upto)
        lap.step(step)
        if step >= lag:
            complete(step - lag)
    for step in range(max(0, ring.pairs - lag), ring.pairs):
        complete(step)
    return sends


class Line:
    def __init__(self, ring, count):
        self.ring, self.length = ring, count // 4
        self.y, self.z = lax.rem(ring.me // 2, 2), ring.me // 4

    def nearest(self, index):
        order = [sorted(range(self.length), key=lambda q: (abs(q - z), q)) for z in range(self.length)]
        place = order[0][index] + 0 * self.z
        for z in range(1, self.length):
            place = jnp.where(self.z == z, order[z][index], place)
        return place

    def device(self, z, row=0, core=0):
        y = self.y if row == 0 else 1 - self.y
        return (z * 2 + y) * 2 + (self.ring.core if core == 0 else 1 - self.ring.core)


def pass_along(ring, count, x_ref, o_ref, sems, columns):
    line_s, line_r, over_s, over_r, sib_s, sib_r, own_sem = sems
    line = Line(ring, count)
    piece = x_ref.shape[0] // SUBS
    own = pltpu.make_async_copy(x_ref, o_ref.at[ring.me], own_sem)
    own.start()
    ring.greet_all(count)
    across = line.device(line.z, 1)
    sends = []

    def send(condition, src, dst, send_sem, recv_sem, device):
        go = ring.copy(src, dst, send_sem, recv_sem, device)
        if condition is None:
            go.start()
        else:
            pl.when(condition)(go.start)
        sends.append((condition, go))

    order = sorted(((row, index) for row in (0, 1) for index in range(line.length)), key=lambda p: (p[0] + p[1], p[0]))
    ahead = 1
    for turn, (row, index) in enumerate(order):
        z = line.nearest(index)
        block = line.device(z, row)
        for sub in range(SUBS):
            rows = pl.ds(sub * piece, piece)
            dst = o_ref.at[block].at[rows]
            first = row == 0 and index == 0
            src = x_ref.at[rows] if first else dst
            if row == 1:
                ring.copy(dst, dst, over_s.at[z, sub], over_r.at[z, sub], across).wait_recv()
            elif not first:
                ring.copy(dst, dst, line_s.at[0, z, sub], line_r.at[z, sub], across).wait_recv()
            if row == 0:
                if first:
                    for side, step in enumerate((1, -1)):
                        there = line.z + step
                        go_on = (there >= 0) & (there < line.length)
                        there = jnp.where(go_on, there, line.z - step)
                        send(go_on, src, dst, line_s.at[side, z, sub], line_r.at[z, sub], line.device(there))
                else:
                    there = jnp.where(z < line.z, line.z + 1, line.z - 1)
                    go_on = (there >= 0) & (there < line.length)
                    there = jnp.where(go_on, there, jnp.where(z < line.z, line.z - 1, line.z + 1))
                    send(go_on, src, dst, line_s.at[0, z, sub], line_r.at[z, sub], line.device(there))
                send(None, src, dst, over_s.at[z, sub], over_r.at[z, sub], across)
            send(None, src, dst, sib_s.at[row, z, sub], sib_r.at[row, z, sub], ring.sibling)
        if turn == 0:
            for column in columns:
                column.start()
        else:
            upto = count if turn == len(order) - 1 else min(count, 1 + 2 * turn)
            for passed in range(ahead, max(ahead, upto)):
                for column in columns:
                    column.pass_on(passed)
            ahead = max(ahead, upto)
    for row, index in order:
        z = line.nearest(index)
        other = line.device(z, row, 1)
        for sub in range(SUBS):
            dst = o_ref.at[other].at[pl.ds(sub * piece, piece)]
            ring.copy(
                dst, dst, sib_s.at[row, z, sub], sib_r.at[row, z, sub], ring.sibling
            ).wait_recv()
    own.wait()
    return sends


def wait_sends(sends):
    for condition, go in sends:
        if condition is None:
            go.wait_send()
        else:
            pl.when(condition)(go.wait_send)


def gather_kernel(count, extra, x_ref, *refs):
    parts, (o_ref, *outs), sems = refs[:extra], refs[extra : 2 * extra + 1], refs[2 * extra + 1 :]
    ring = Ring(count)
    columns = [
        Columns(ring, count, parts[i], outs[i], sems[7 + 5 * i : 12 + 5 * i]) for i in range(extra)
    ]
    wait_sends(pass_along(ring, count, x_ref, o_ref, sems[:7], columns))
    for column in columns:
        column.finish()


def ring_gather(values, blocks, count, ident):
    pairs, groups = count // 2, lax.axis_size("batch")
    anywhere = pl.BlockSpec(memory_space=pl.ANY)
    return pl.pallas_call(
        functools.partial(gather_kernel, count, len(blocks)),
        out_shape=[jax.ShapeDtypeStruct((count,) + values.shape, values.dtype)]
        + [jax.ShapeDtypeStruct((groups, count) + b.shape[1:], b.dtype) for b in blocks],
        in_specs=[anywhere] * (1 + len(blocks)),
        out_specs=[anywhere] * (1 + len(blocks)),
        scratch_shapes=line_sems(count) + column_sems(count, groups) * len(blocks),
        compiler_params=pltpu.CompilerParams(collective_id=ident, has_side_effects=True),
        cost_estimate=pl.CostEstimate(flops=0, bytes_accessed=150_000_000, transcendentals=0),
        name=f"ring_gather_{ident}",
    )(values, *blocks)


def ring_sems(pairs):
    return [pltpu.SemaphoreType.DMA((pairs, SUBS)) for _ in range(4)] + [pltpu.SemaphoreType.DMA]


def line_sems(count):
    dma = pltpu.SemaphoreType.DMA
    shapes = [(2, count // 4, SUBS)] + [(count // 4, SUBS)] * 3 + [(2, count // 4, SUBS)] * 2
    return [dma(shape) for shape in shapes] + [dma]


def column_sems(count, groups):
    return [
        pltpu.SemaphoreType.DMA((count,)),
        pltpu.SemaphoreType.DMA((count,)),
        pltpu.SemaphoreType.DMA((groups, count)),
        pltpu.SemaphoreType.DMA((groups, count)),
        pltpu.SemaphoreType.DMA,
    ]


def residual_kernel(count, groups, x_ref, feed_ref, states_ref, vec_ref, cot_ref, plane_ref, *refs):
    far_refs, refs = refs[: groups - 1], refs[groups - 1 :]
    heads_ref, feed_far_ref, b_ref, w_ref, cot_all_ref, own_ref = refs[:6]
    heads, w_out, total, states, low, w_sem, load_sem, store_sem, heads_sem, *sems = refs[6:]
    ring = Ring(count)
    lap = Lap(ring, cot_ref, cot_all_ref, sems[9:14])
    tokens, own = total.shape[0], own_ref.shape[0]
    blocks = tokens // ROWS
    part = D // groups
    half = part // 2

    def held_rows(shift):
        begin = lax.rem(ring.batch - shift + groups, groups) * part
        if shift == 0:
            return w_out.at[pl.ds(pl.multiple_of(begin, part), part)]
        return w_out.at[pl.ds(pl.multiple_of(begin + ring.core * half, half), half)]

    weights = [
        pltpu.make_async_copy(ref, held_rows(shift), w_sem.at[shift])
        for shift, ref in enumerate((plane_ref,) + far_refs)
    ]
    for go in weights:
        go.start()

    def handed(shift):
        return ring.copy(
            far_refs[shift - 1],
            held_rows(shift),
            sems[7].at[shift - 1],
            sems[8].at[shift - 1],
            ring.sibling,
        )

    keep = pltpu.make_async_copy(w_out, w_ref, w_sem.at[groups])

    def onward(shift):
        return pltpu.make_async_remote_copy(
            src_ref=feed_ref,
            dst_ref=feed_far_ref.at[shift - 1],
            send_sem=sems[5].at[shift - 1],
            recv_sem=sems[6].at[shift - 1],
            device_id=(lax.rem(ring.batch + shift, groups), ring.me),
            device_id_type=MESH,
        )

    def rows_of(block):
        return pl.ds(pl.multiple_of(block * ROWS, ROWS), ROWS)

    def load(block):
        slot = lax.rem(block, 2)
        return pltpu.make_async_copy(
            states_ref.at[rows_of(block)], states.at[slot], load_sem.at[slot]
        )

    def store(block):
        slot = lax.rem(block, 2)
        return pltpu.make_async_copy(low.at[slot], b_ref.at[rows_of(block)], store_sem.at[slot])

    load(0).start()

    kept, waiting = [], []

    def add(group, first, last):
        wide = 512

        @pl.loop(0, blocks)
        def _(block):
            rows = rows_of(block)
            left = jnp.concatenate([heads[head, rows, :] for head in group], axis=1)
            if first:

                @pl.when(block + 1 < blocks)
                def _():
                    load(block + 1).start()

                load(block).wait()
                normal, _ = norm_parts(states[lax.rem(block, 2)].astype(F32))
                total[rows, :] = DEEP_ALPHA * (normal * vec_ref[0:1, :] + vec_ref[1:2, :])
            for at in range(0, D, wide):
                right = [
                    w_out[pl.ds(pl.multiple_of(head * HD, HD), HD), at : at + wide]
                    for head in group
                ]
                total[rows, at : at + wide] += nn(left, jnp.concatenate(right, axis=0))
            if last:

                @pl.when(block >= 2)
                def _():
                    store(block - 2).wait()

                normal, _ = norm_parts(total[rows, :])
                low[lax.rem(block, 2)] = (normal * vec_ref[2:3, :] + vec_ref[3:4, :]).astype(BF)
                store(block).start()

    def work(block, other):
        turn, turns = len(kept) // 2, count // 2
        if turn == 0:
            for shift in range(1, groups):
                handed(shift).start()
                onward(shift).start()
        for part, head in enumerate((block, other)):
            go = pltpu.make_async_copy(heads.at[head], heads_ref.at[head], heads_sem.at[turn, part])
            go.start()
            kept.append(go)
            waiting.append(head)
        if turn == 1:
            for go in weights:
                go.wait()
            for shift in range(1, groups):
                handed(shift).wait()
            keep.start()
        if turn == turns - 1 or turn in (1, turns // 2, turns - 2):
            add(list(waiting), turn == 1, turn == turns - 1)
            waiting.clear()

    sends = pass_round(ring, count, 2, x_ref, heads, sems[:5], [], work, lap)

    own_ref[...] = total[pl.ds(pl.multiple_of(ring.me * own, own), own), :]
    for block in (blocks - 2, blocks - 1):
        store(block).wait()
    for go in kept:
        go.wait()
    for go in sends:
        go.wait_send()
    for shift in range(1, groups):
        onward(shift).wait()
    keep.wait()
    lap.finish()


def gather_residual(attended, feed_own, states, vectors, cot, w_plane, w_far, own, count, ident):
    tokens = attended.shape[0]
    pairs, groups = count // 2, lax.axis_size("batch")
    inside, anywhere = pl.BlockSpec(memory_space=pltpu.VMEM), pl.BlockSpec(memory_space=pl.ANY)
    return pl.pallas_call(
        functools.partial(residual_kernel, count, groups),
        out_shape=[
            jax.ShapeDtypeStruct((count, tokens, HD), BF),
            jax.ShapeDtypeStruct((groups - 1,) + feed_own.shape, BF),
            jax.ShapeDtypeStruct((tokens, D), BF),
            jax.ShapeDtypeStruct((D, D), BF),
            jax.ShapeDtypeStruct((count,) + cot.shape, BF),
            jax.ShapeDtypeStruct((own, D), F32),
        ],
        in_specs=[anywhere] * 3 + [inside] + [anywhere] * (2 + len(w_far)),
        out_specs=[anywhere] * 5 + [inside],
        scratch_shapes=[
            pltpu.VMEM((count, tokens, HD), BF),
            pltpu.VMEM((D, D), BF),
            pltpu.VMEM((tokens, D), F32),
            pltpu.VMEM((2, ROWS, D), BF),
            pltpu.VMEM((2, ROWS, D), BF),
            pltpu.SemaphoreType.DMA((groups + 1,)),
            pltpu.SemaphoreType.DMA((2,)),
            pltpu.SemaphoreType.DMA((2,)),
            pltpu.SemaphoreType.DMA((pairs, 2)),
        ]
        + ring_sems(pairs)
        + [pltpu.SemaphoreType.DMA((max(1, groups - 1),)) for _ in range(4)]
        + ring_sems(pairs),
        compiler_params=vmem(collective_id=ident, has_side_effects=True),
        cost_estimate=pl.CostEstimate(
            flops=2 * tokens * D * D, bytes_accessed=200_000_000, transcendentals=0
        ),
        name="gather_residual",
    )(attended, feed_own, states, vectors, cot, w_plane, *w_far)


class RingSum:
    def __init__(self, ring, own, sib, got, sems, out):
        self.ring, self.own, self.sib, self.got, self.out = ring, own, sib, got, out
        self.ring_s, self.ring_r, self.sib_s, self.sib_r = sems
        self.piece = own.shape[1] // SUBS

    def given(self, step, src):
        return self.ring.copy(
            src, self.sib.at[step], self.sib_s.at[step], self.sib_r.at[step], self.ring.sibling
        )

    def passed(self, step, sub):
        rows = pl.ds(sub * self.piece, self.piece)
        return self.ring.copy(
            self.own.at[step].at[rows],
            self.got.at[step].at[rows],
            self.ring_s.at[step, sub],
            self.ring_r.at[step, sub],
            self.ring.at(1),
        )

    def advance(self, step):
        last = self.ring.pairs - 1
        self.given(step, self.sib.at[step]).wait_recv()
        for sub in range(SUBS):
            rows = pl.ds(sub * self.piece, self.piece)

            total = self.own[step, rows, :].astype(F32) + self.sib[step, rows, :].astype(F32)

            @pl.when(step == 0)
            def _():
                self.own[step, rows, :] = total.astype(BF)

            @pl.when(step > 0)
            def _():
                self.passed(step - 1, sub).wait_recv()
                more = total + self.got[step - 1, rows, :].astype(F32)

                @pl.when(step < last)
                def _():
                    self.own[step, rows, :] = more.astype(BF)

                @pl.when(step == last)
                def _():
                    self.out[rows, :] = more

            @pl.when(step < last)
            def _():
                self.passed(step, sub).start()

    def finish(self):
        @pl.loop(0, self.ring.pairs - 1)
        def _(step):
            for sub in range(SUBS):
                self.passed(step, sub).wait_send()

    @staticmethod
    def scratch(pairs, rows):
        return [pltpu.VMEM((pairs - late, rows, D), BF) for late in (0, 0, 1)] + [
            pltpu.SemaphoreType.DMA((pairs, SUBS)),
            pltpu.SemaphoreType.DMA((pairs, SUBS)),
            pltpu.SemaphoreType.DMA((pairs,)),
            pltpu.SemaphoreType.DMA((pairs,)),
        ]


class Exchange:
    def __init__(self, ring, count, src, out, sems):
        self.ring, self.count, self.src, self.out = ring, count, src, out
        self.send, self.recv, self.own = sems

    def copies(self):
        ring = self.ring
        for step in range(1, self.count):
            device = lax.rem(ring.me + step, self.count)
            yield ring.copy(
                self.src.at[device],
                self.out.at[ring.me],
                self.send.at[step],
                self.recv.at[step],
                device,
            )

    def start(self):
        pltpu.make_async_copy(self.src.at[self.ring.me], self.out.at[self.ring.me], self.own).start()
        for go in self.copies():
            go.start()

    def finish(self):
        for go in self.copies():
            go.wait()
        pltpu.make_async_copy(self.src.at[self.ring.me], self.out.at[self.ring.me], self.own).wait()

    @staticmethod
    def scratch(count):
        return [pltpu.SemaphoreType.DMA((count,)) for _ in range(2)] + [pltpu.SemaphoreType.DMA]


class Spread:
    def __init__(self, ring, count, groups, src, came, sems):
        self.ring, self.count, self.groups, self.src, self.came = ring, count, groups, src, came
        self.send, self.recv = sems
        self.total = count * groups
        self.shared = self.total // src.shape[0]

    def copies(self):
        me = self.ring.batch * self.count + self.ring.me
        for step in range(1, self.total):
            flat = lax.rem(me + step, self.total)
            yield pltpu.make_async_remote_copy(
                src_ref=self.src.at[flat // self.shared],
                dst_ref=self.came.at[step],
                send_sem=self.send.at[step],
                recv_sem=self.recv.at[step],
                device_id=(flat // self.count, lax.rem(flat, self.count)),
                device_id_type=MESH,
            )

    def start(self):
        for go in self.copies():
            go.start()
        me = self.ring.batch * self.count + self.ring.me
        self.came[0] = self.src[me // self.shared]

    def finish(self):
        total = self.came[0]
        for step, go in enumerate(self.copies(), 1):
            go.wait()
            total = total + self.came[step]
        return total

    @staticmethod
    def scratch(total):
        return [pltpu.SemaphoreType.DMA((total,)) for _ in range(2)]


class GroupSum:
    def __init__(self, ring, groups, sent, came, sems, out):
        self.ring, self.groups, self.sent, self.came, self.out = ring, groups, sent, came, out
        self.send, self.recv = sems
        self.tiles, self.each = D // ROWS, D // ROWS // groups

    def group(self, tile):
        return lax.rem(self.ring.batch + 1 + tile // self.each, self.groups)

    def column(self, tile):
        return (self.group(tile) * self.each + lax.rem(tile, self.each)) * ROWS

    def copy(self, tile):
        return pltpu.make_async_remote_copy(
            src_ref=self.sent.at[tile],
            dst_ref=self.came.at[tile],
            send_sem=self.send.at[tile],
            recv_sem=self.recv.at[tile],
            device_id=(self.group(tile), self.ring.me),
            device_id_type=MESH,
        )

    def put(self, tile, values):
        away = self.tiles - self.each

        @pl.when(tile < away)
        def _():
            self.sent[tile] = values.astype(BF)
            self.copy(tile).start()

        @pl.when(tile >= away)
        def _():
            self.out[tile - away] = values.astype(BF)

    def finish(self):
        @pl.loop(0, self.each)
        def _(tile):
            total = self.out[tile].astype(F32)
            for shift in range(self.groups - 1):
                self.copy(shift * self.each + tile).wait_recv()
                total = total + self.came[shift * self.each + tile].astype(F32)
            self.out[tile] = total.astype(BF)

        @pl.loop(0, self.tiles - self.each)
        def _(tile):
            self.copy(tile).wait_send()

    @staticmethod
    def scratch(groups, width):
        away = D // ROWS - D // ROWS // groups
        return [pltpu.VMEM((away, ROWS, width), BF) for _ in range(2)] + [
            pltpu.SemaphoreType.DMA((away,)) for _ in range(2)
        ]


def norm_back(normal, inverse, slope, gain):
    scaled = slope * gain
    back = inverse * (
        scaled
        - jnp.mean(scaled, axis=-1, keepdims=True)
        - normal * jnp.mean(scaled * normal, axis=-1, keepdims=True)
    )
    return back, jnp.sum(slope * normal, axis=0, keepdims=True), jnp.sum(slope, axis=0, keepdims=True)


def feed_kernel(
    count,
    groups,
    span,
    b_ref,
    cot_ref,
    feed_own_ref,
    feed_far_ref,
    w_out_ref,
    res_ref,
    cot_own_ref,
    vec_ref,
    out_ref,
    grad_ref,
    dr_ref,
    vec_sum_ref,
    do_ref,
    dr_send,
    bs,
    cs,
    stage,
    h,
    du,
    tiles,
    w_ref,
    db_ref,
    do_send,
    *rest,
):
    ring = Ring(count)
    own = out_ref.shape[0]
    sums = [
        RingSum(ring, *rest[7 * i : 7 * i + 3], rest[7 * i + 3 : 7 * i + 7], ref)
        for i, ref in enumerate((db_ref, out_ref))
    ]
    grads = GroupSum(ring, groups, rest[14], rest[15], rest[16:18], grad_ref)
    row_sem, tile_sem, w_sem = rest[18:21]
    exchange = Exchange(ring, count, do_send, do_ref, rest[21:24])
    pairs = ring.pairs

    def weights(index):
        held = (bs, cs)[index // 2 % 2].at[index % 2]
        rows = pl.ds(index * 2 * own, 2 * own)
        return pltpu.make_async_copy(w_out_ref.at[rows], held, w_sem.at[index % 4])


    def places(step):
        return ring.at(-1 - step) * own, ring.at(1 + step, 1 - ring.core) * own

    def row_loads(step):
        slot = lax.rem(step, 2)
        return [
            pltpu.make_async_copy(
                ref.at[pl.ds(pl.multiple_of(place, own), own)],
                held.at[slot, pl.ds(half * own, own)],
                row_sem.at[slot, 2 * which + half],
            )
            for which, (ref, held) in enumerate(((b_ref, bs), (cot_ref, cs)))
            for half, place in enumerate(places(step))
        ]

    def tile_loads(tile):
        slot = lax.rem(tile, 2)
        cols = pl.ds(pl.multiple_of(grads.column(tile), ROWS), ROWS)
        return [
            pltpu.make_async_copy(ref.at[:, cols], tiles.at[slot, which], tile_sem.at[slot, which])
            for which, ref in enumerate((b_ref, cot_ref))
        ]

    def feed_rows(shift):
        part = D // groups
        begin = lax.rem(ring.batch - shift + groups, groups) * part
        src = feed_own_ref if shift == 0 else feed_far_ref.at[shift - 1]
        return pltpu.make_async_copy(
            src, w_ref.at[pl.ds(pl.multiple_of(begin, part), part)], rest[24].at[shift]
        )

    for go in row_loads(0):
        go.start()
    for shift in range(groups):
        feed_rows(shift).start()
    ring.greet_all(count)
    for shift in range(groups):
        feed_rows(shift).wait()

    def feed(step):
        slot = lax.rem(step, 2)

        @pl.when(step + 1 < pairs)
        def _():
            for go in row_loads(step + 1):
                go.start()

        for go in row_loads(step):
            go.wait()
        gate = nn(bs[slot], w_ref[:, :span])
        up = nn(bs[slot], w_ref[:, span : 2 * span])
        slope = nn(cs[slot], w_ref[:, 2 * span :])
        coef = math.sqrt(2.0 / math.pi)
        square = gate * gate
        tanh = jnp.tanh(coef * gate * (1.0 + 0.044715 * square))
        half = 0.5 * (1.0 + tanh)
        gelu = gate * half
        gelu_slope = half + 0.5 * gate * (1.0 - tanh * tanh) * (coef * (1.0 + 3 * 0.044715 * square))
        hidden = (gelu * up).astype(BF)
        both = jnp.concatenate([slope * up * gelu_slope, slope * gelu], axis=1).astype(BF)
        for part, place in enumerate(places(step)):
            rows = pl.ds(pl.multiple_of(place, own), own)
            h[rows, :] = hidden[part * own : (part + 1) * own]
            du[rows, :] = both[part * own : (part + 1) * own]

        @pl.when(step >= 2)
        def _():
            for which, each in enumerate(sums):
                each.given(step - 2, stage.at[slot, which]).wait_send()

        wide = 512
        for which, (each, left, low, high) in enumerate(
            ((sums[0], both, 0, 2 * span), (sums[1], hidden, 2 * span, 3 * span))
        ):
            for at in range(0, D, wide):
                terms = nt(left, w_ref[at : at + wide, low:high]).astype(BF)
                each.own[step, :, at : at + wide] = terms[:own]
                stage[slot, which, :, at : at + wide] = terms[own:]
            each.given(step, stage.at[slot, which]).start()

    @pl.loop(0, pairs)
    def _(step):
        feed(step)

        @pl.when(lax.rem(step, 2) == 0)
        def _():
            sums[0].advance(step // 2)

    for go in tile_loads(0):
        go.start()
    for index in range(4):
        weights(index).start()

    @pl.loop(0, grads.tiles)
    def _(tile):
        slot = lax.rem(tile, 2)

        @pl.when(tile + 1 < grads.tiles)
        def _():
            for go in tile_loads(tile + 1):
                go.start()

        for go in tile_loads(tile):
            go.wait()
        values = jnp.concatenate([tn(tiles[slot, 0], du[...]), tn(tiles[slot, 1], h[...])], axis=1)
        grads.put(tile, values)
        later = pairs // 2 + tile // 2

        @pl.when((lax.rem(tile, 2) == 1) & (later < pairs))
        def _():
            sums[0].advance(later)

    passed = pairs // 2 + grads.tiles // 2

    @pl.loop(min(passed, pairs), pairs)
    def _(step):
        sums[0].advance(step)

    sums[1].advance(0)
    normal, inverse = norm_parts(res_ref[...])
    slope = DEEP_ALPHA * cot_own_ref[...].astype(F32) + db_ref[...]
    dr, gain_sum, bias_sum = norm_back(normal, inverse, slope, vec_ref[2:3, :])
    dr_ref[...] = dr
    vec_sum_ref[...] = jnp.concatenate([gain_sum, bias_sum], axis=0)
    dr_low = dr.astype(BF)
    for index in range(D // (2 * own)):
        weights(index).wait()
        do = nt(dr_low, (bs, cs)[index // 2 % 2][index % 2]).astype(BF)
        if (index + 4) * 2 * own < D:
            weights(index + 4).start()
        for part in range(0, 2 * own, HD):
            at = index * 2 * own + part
            do_send[at // HD] = do[:, part : part + HD]
            dr_send[at // HD] = dr_low[:, at : at + HD]
    exchange.start()

    @pl.loop(1, pairs)
    def _(step):
        sums[1].advance(step)

    exchange.finish()
    grads.finish()
    for step in (pairs - 2, pairs - 1):
        for which, each in enumerate(sums):
            each.given(step, stage.at[step % 2, which]).wait_send()
    for each in sums:
        each.finish()


def feed_forward(
    b_low, cot, feed_own, feed_far, w_out, residual, cot_own, vectors, count, groups, ident
):
    tokens, span, pairs = b_low.shape[0], feed_own.shape[1] // 3, count // 2
    own = residual.shape[0]
    inside, anywhere = pl.BlockSpec(memory_space=pltpu.VMEM), pl.BlockSpec(memory_space=pl.ANY)
    return pl.pallas_call(
        functools.partial(feed_kernel, count, groups, span),
        in_specs=[anywhere] * 5 + [inside] * 3,
        out_specs=[inside] * 4 + [anywhere, inside],
        out_shape=[
            jax.ShapeDtypeStruct((own, D), F32),
            jax.ShapeDtypeStruct((D // groups // ROWS, ROWS, 3 * span), BF),
            jax.ShapeDtypeStruct((own, D), F32),
            jax.ShapeDtypeStruct((2, D), F32),
            jax.ShapeDtypeStruct((count, own, HD), BF),
            jax.ShapeDtypeStruct((count, own, HD), BF),
        ],
        scratch_shapes=[
            pltpu.VMEM((2, 2 * own, D), BF),
            pltpu.VMEM((2, 2 * own, D), BF),
            pltpu.VMEM((2, 2, own, D), BF),
            pltpu.VMEM((tokens, span), BF),
            pltpu.VMEM((tokens, 2 * span), BF),
            pltpu.VMEM((2, 2, tokens, ROWS), BF),
            pltpu.VMEM((D, 3 * span), BF),
            pltpu.VMEM((own, D), F32),
            pltpu.VMEM((count, own, HD), BF),
        ]
        + RingSum.scratch(pairs, own) * 2
        + GroupSum.scratch(groups, 3 * span)
        + [pltpu.SemaphoreType.DMA((2, 4)), pltpu.SemaphoreType.DMA((2, 2)), pltpu.SemaphoreType.DMA((4,))]
        + Exchange.scratch(count)
        + [pltpu.SemaphoreType.DMA((groups,))],
        compiler_params=vmem(62 * 1024 * 1024, collective_id=ident, has_side_effects=True),
        cost_estimate=pl.CostEstimate(
            flops=18 * tokens * D * span, bytes_accessed=250_000_000, transcendentals=0
        ),
        name="feed_forward",
    )(b_low, cot, feed_own, feed_far, w_out, residual, cot_own, vectors)


def project_kernel(
    count,
    groups,
    dp_ref,
    w_ref,
    a_ref,
    heads_ref,
    dr_ref,
    feed_ref,
    x_ref,
    dr_own_ref,
    vec_ref,
    vec_sum_ref,
    back_ref,
    grad_ref,
    feed_out_ref,
    vec_out_ref,
    stage,
    tiles,
    da_ref,
    vec_send,
    vec_came,
    *rest,
):
    ring = Ring(count)
    own = da_ref.shape[0]
    sums = RingSum(ring, *rest[:3], rest[3:7], da_ref)
    grads = GroupSum(ring, groups, rest[7], rest[8], rest[9:11], grad_ref)
    tile_sem = rest[11]
    feed = Exchange(ring, count, feed_ref, feed_out_ref, rest[12:15])
    spread = Spread(ring, count, groups, vec_send, vec_came, rest[15:17])
    pairs, width = ring.pairs, heads_ref.shape[2]

    def places(step):
        return ring.at(-1 - step) * own, ring.at(1 + step, 1 - ring.core) * own

    def tile_loads(tile):
        slot = lax.rem(tile, 2)
        begin = pl.multiple_of(grads.column(tile), ROWS)
        loads = [
            pltpu.make_async_copy(
                a_ref.at[:, pl.ds(begin, ROWS)], tiles.at[slot, 0], tile_sem.at[slot, 0]
            )
        ]
        for part in range(ROWS // width):
            loads.append(
                pltpu.make_async_copy(
                    heads_ref.at[begin // width + part],
                    tiles.at[slot, 1, :, pl.ds(part * width, width)],
                    tile_sem.at[slot, 1 + part],
                )
            )
        return loads

    for go in tile_loads(0):
        go.start()
    ring.greet_whole(count)
    feed.start()

    def terms_of(step):
        slot = lax.rem(step, 2)

        @pl.when(step >= 2)
        def _():
            sums.given(step - 2, stage.at[slot]).wait_send()

        left = jnp.concatenate(
            [dp_ref[pl.ds(pl.multiple_of(place, own), own), :] for place in places(step)], axis=0
        )
        wide = 512
        for at in range(0, D, wide):
            terms = nt(left, w_ref[at : at + wide, :]).astype(BF)
            sums.own[step, :, at : at + wide] = terms[:own]
            stage[slot, :, at : at + wide] = terms[own:]
        sums.given(step, stage.at[slot]).start()

    terms_of(0)
    sums.advance(0)

    @pl.loop(0, grads.tiles)
    def _(tile):
        slot = lax.rem(tile, 2)

        @pl.when(tile + 1 < grads.tiles)
        def _():
            for go in tile_loads(tile + 1):
                go.start()

        for go in tile_loads(tile):
            go.wait()
        values = jnp.concatenate(
            [tn(tiles[slot, 0], dp_ref[...]), tn(tiles[slot, 1], dr_ref[...])], axis=1
        )
        grads.put(tile, values)

        @pl.when(tile + 1 < pairs)
        def _():
            terms_of(tile + 1)

        @pl.when((lax.rem(tile, 2) == 1) & (tile // 2 + 1 < pairs))
        def _():
            sums.advance(tile // 2 + 1)

    @pl.loop(1 + grads.tiles // 2, pairs)
    def _(step):
        sums.advance(step)

    normal, inverse = norm_parts(x_ref[...].astype(F32))
    slope = DEEP_ALPHA * dr_own_ref[...] + da_ref[...]
    back, gain_sum, bias_sum = norm_back(normal, inverse, slope, vec_ref[0:1, :])
    back_ref[...] = back.astype(BF)
    kinds = [gain_sum, bias_sum, vec_sum_ref[0:1, :], vec_sum_ref[1:2, :]]
    for tile in range(D // LANES):
        for kind, values in enumerate(kinds):
            vec_send[tile, kind : kind + 1, :] = values[:, tile * LANES : (tile + 1) * LANES]
    spread.start()
    grads.finish()
    for step in (pairs - 2, pairs - 1):
        sums.given(step, stage.at[step % 2]).wait_send()
    sums.finish()
    vec_out_ref[...] = spread.finish()
    feed.finish()


def project_back(
    dp, w_qkv, a_low, heads, dr_cols, grad_feed, states, dr, vectors, vec_sums, count, groups, ident
):
    tokens, pairs = dp.shape[0], count // 2
    own, width = dr.shape[0], 3 * HD + dr_cols.shape[1]
    inside, anywhere = pl.BlockSpec(memory_space=pltpu.VMEM), pl.BlockSpec(memory_space=pl.ANY)
    return pl.pallas_call(
        functools.partial(project_kernel, count, groups),
        in_specs=[inside, inside, anywhere, anywhere, inside, anywhere] + [inside] * 4,
        out_specs=[inside, inside, anywhere, inside],
        out_shape=[
            jax.ShapeDtypeStruct((own, D), BF),
            jax.ShapeDtypeStruct((D // groups // ROWS, ROWS, width), BF),
            jax.ShapeDtypeStruct(grad_feed.shape, BF),
            jax.ShapeDtypeStruct((8, LANES), F32),
        ],
        scratch_shapes=[
            pltpu.VMEM((2, own, D), BF),
            pltpu.VMEM((2, 2, tokens, ROWS), BF),
            pltpu.VMEM((own, D), F32),
            pltpu.VMEM((D // LANES, 8, LANES), F32),
            pltpu.VMEM((count * groups, 8, LANES), F32),
        ]
        + RingSum.scratch(pairs, own)
        + GroupSum.scratch(groups, width)
        + [pltpu.SemaphoreType.DMA((2, 1 + ROWS // HD))]
        + Exchange.scratch(count)
        + Spread.scratch(count * groups),
        compiler_params=vmem(collective_id=ident, has_side_effects=True),
        cost_estimate=pl.CostEstimate(
            flops=4 * tokens * D * 3 * HD, bytes_accessed=200_000_000, transcendentals=0
        ),
        name="project_back",
    )(dp, w_qkv, a_low, heads, dr_cols, grad_feed, states, dr, vectors, vec_sums)


def norm_parts(values):
    centre = values - jnp.mean(values, axis=-1, keepdims=True)
    inverse = lax.rsqrt(jnp.mean(centre * centre, axis=-1, keepdims=True) + LN_EPS)
    return centre * inverse, inverse


def qkv_kernel(x_ref, w_ref, vec_ref, cos_ref, sin_ref, a_ref, q_ref, k_ref, v_ref, kt_ref, vt_ref):
    normal, _ = norm_parts(x_ref[...].astype(F32))
    low = (normal * vec_ref[0:1, :] + vec_ref[1:2, :]).astype(BF)
    a_ref[...] = low
    projected = nn(low, w_ref[...])
    for index, ref in enumerate((q_ref, k_ref)):
        part = projected[:, index * HD : (index + 1) * HD]
        turned = part * cos_ref[...] + pltpu.roll(part, HD // 2, 1) * sin_ref[...]
        ref[...] = turned.astype(BF)
    kt_ref[...] = turned.T.astype(BF)[None]
    v_ref[...] = projected[:, 2 * HD :].astype(BF)
    vt_ref[...] = projected[:, 2 * HD :].T.astype(BF)[None]


def norm_and_project(states, w_qkv, vectors, cosine, sine):
    tokens = states.shape[0]
    whole = lambda shape: pl.BlockSpec(shape, lambda i: (0, 0))
    rows = lambda width: pl.BlockSpec((ROWS, width), lambda i: (i, 0))
    turned = pl.BlockSpec((1, HD, ROWS), lambda i: (i * ROWS // KEYS, 0, i % (KEYS // ROWS)))
    return pl.pallas_call(
        qkv_kernel,
        grid=(tokens // ROWS,),
        in_specs=[rows(D), whole((D, 3 * HD)), whole(vectors.shape), rows(HD), rows(HD)],
        out_specs=[rows(D), rows(HD), rows(HD), rows(HD), turned, turned],
        out_shape=[jax.ShapeDtypeStruct((tokens, D), BF)]
        + [jax.ShapeDtypeStruct((tokens, HD), BF) for _ in range(3)]
        + [jax.ShapeDtypeStruct((tokens // KEYS, HD, KEYS), BF) for _ in range(2)],
        compiler_params=vmem(),
        cost_estimate=pl.CostEstimate(
            flops=2 * tokens * D * 3 * HD, bytes_accessed=24_000_000, transcendentals=0
        ),
        name="norm_and_project",
    )(states, w_qkv, vectors, cosine, sine)


def masked_scores(block, query, k_ref, first_ref, last_ref, keys):
    place = block * ROWS + lax.broadcasted_iota(jnp.int32, (1, LANES), 1)
    scores = nt(k_ref[keys], query) * HD ** (-0.5)
    parts = []
    for at in range(0, ROWS, LANES):
        seen = (place + at >= first_ref[keys]) & (place + at < last_ref[keys])
        parts.append(jnp.where(seen, scores[:, at : at + LANES], NEG_LARGE))
    return jnp.concatenate(parts, axis=1)


def attend_kernel(
    low_ref, high_ref, q_ref, k_ref, vt_ref, first_ref, last_ref, o_ref, full_ref, log_ref, held
):
    block = pl.program_id(0)
    query = q_ref[...]

    def score(keys, top):
        scores = masked_scores(block, query, k_ref, first_ref, last_ref, keys)
        held[keys] = scores
        return jnp.maximum(top, jnp.max(scores, axis=0, keepdims=True))

    def add(keys, carry):
        total, out = carry
        weight = jnp.exp(held[keys] - top)
        total = total + jnp.sum(weight, axis=0, keepdims=True)
        return total, out + nn(vt_ref[keys], weight.astype(BF))

    low, high = low_ref[block], high_ref[block]
    top = lax.fori_loop(low, high, score, jnp.full((1, ROWS), NEG_LARGE, F32))
    total, out = lax.fori_loop(
        low, high, add, (jnp.zeros((1, ROWS), F32), jnp.zeros((HD, ROWS), F32))
    )
    out = out / total
    o_ref[...] = out.T.astype(BF)
    full_ref[...] = out[None]
    log_ref[...] = (top + jnp.log(total))[None]


def attend(query, key, value_t, spans):
    tokens = query.shape[0]
    blocks, span = tokens // ROWS, tokens // KEYS
    first, last, low, high = spans
    rows = pl.BlockSpec((ROWS, HD), lambda i, *_: (i, 0))
    one = lambda shape: pl.BlockSpec((1,) + shape, lambda i, *_: (i, 0, 0))
    whole = lambda shape: pl.BlockSpec(shape, lambda i, *_: (0,) * len(shape))
    return pl.pallas_call(
        attend_kernel,
        grid_spec=pltpu.PrefetchScalarGridSpec(
            num_scalar_prefetch=2,
            grid=(blocks,),
            in_specs=[
                rows,
                whole((span, KEYS, HD)),
                whole((span, HD, KEYS)),
                whole((span, KEYS, LANES)),
                whole((span, KEYS, LANES)),
            ],
            out_specs=[rows, one((HD, ROWS)), one((1, ROWS))],
            scratch_shapes=[pltpu.VMEM((span, KEYS, ROWS), F32)],
        ),
        out_shape=[
            jax.ShapeDtypeStruct((tokens, HD), BF),
            jax.ShapeDtypeStruct((blocks, HD, ROWS), F32),
            jax.ShapeDtypeStruct((blocks, 1, ROWS), F32),
        ],
        compiler_params=vmem(),
        cost_estimate=pl.CostEstimate(
            flops=2 * tokens * tokens * HD, bytes_accessed=4_000_000, transcendentals=0
        ),
        name="attend",
    )(low, high, query, key.reshape(span, KEYS, HD), value_t, first, last)


def attend_back_kernel(
    low_ref,
    high_ref,
    q_ref,
    g_ref,
    full_ref,
    log_ref,
    k_ref,
    kt_ref,
    v_ref,
    first_ref,
    last_ref,
    cos_ref,
    sin_ref,
    o_ref,
    dk_ref,
    dv_ref,
):
    block = pl.program_id(0)
    blocks = pl.num_programs(0)
    scale = HD ** (-0.5)

    @pl.when(block == 0)
    def _():
        dk_ref[...] = jnp.zeros_like(dk_ref)
        dv_ref[...] = jnp.zeros_like(dv_ref)

    query, grad = q_ref[...], g_ref[...]
    inner = jnp.sum(grad.astype(F32).T * full_ref[0], axis=0, keepdims=True)
    log = log_ref[0]

    def one(keys, total):
        scores = masked_scores(block, query, k_ref, first_ref, last_ref, keys)
        weight = jnp.exp(scores - log)
        slope = (weight * (nt(v_ref[keys], grad) - inner)).astype(BF)
        dv_ref[keys] += nn(weight.astype(BF), grad)
        dk_ref[keys] += nn(slope, query)
        return total + nn(kt_ref[keys], slope)

    total = lax.fori_loop(low_ref[block], high_ref[block], one, jnp.zeros((HD, ROWS), F32))

    def turn_back(values, cosine, sine):
        values = (values * scale).astype(BF).astype(F32)
        return (values * cosine - pltpu.roll(values, HD // 2, 1) * sine).astype(BF)

    rows = pl.ds(pl.multiple_of(block * ROWS, ROWS), ROWS)
    o_ref[rows, 0:HD] = turn_back(total.T, cos_ref[rows, :], sin_ref[rows, :])

    @pl.when(block == blocks - 1)
    def _():
        for part in range(dk_ref.shape[0]):
            there = pl.ds(part * KEYS, KEYS)
            o_ref[there, HD : 2 * HD] = turn_back(
                dk_ref[part], cos_ref[there, :], sin_ref[there, :]
            )
            o_ref[there, 2 * HD :] = dv_ref[part].astype(BF)


def attend_back(query, key, key_t, value, grad, full, log, spans, cosine, sine):
    tokens = query.shape[0]
    blocks, span = tokens // ROWS, tokens // KEYS
    first, last, low, high = spans
    rows = pl.BlockSpec((ROWS, HD), lambda i, *_: (i, 0))
    one = lambda shape: pl.BlockSpec((1,) + shape, lambda i, *_: (i, 0, 0))
    whole = lambda shape: pl.BlockSpec(shape, lambda i, *_: (0,) * len(shape))
    return pl.pallas_call(
        attend_back_kernel,
        grid_spec=pltpu.PrefetchScalarGridSpec(
            num_scalar_prefetch=2,
            grid=(blocks,),
            in_specs=[
                rows,
                rows,
                one((HD, ROWS)),
                one((1, ROWS)),
                whole((span, KEYS, HD)),
                whole((span, HD, KEYS)),
                whole((span, KEYS, HD)),
                whole((span, KEYS, LANES)),
                whole((span, KEYS, LANES)),
                whole((tokens, HD)),
                whole((tokens, HD)),
            ],
            out_specs=whole((tokens, 3 * HD)),
            scratch_shapes=[pltpu.VMEM((span, KEYS, HD), F32) for _ in range(2)],
        ),
        out_shape=jax.ShapeDtypeStruct((tokens, 3 * HD), BF),
        compiler_params=vmem(),
        cost_estimate=pl.CostEstimate(
            flops=5 * tokens * tokens * HD, bytes_accessed=6_000_000, transcendentals=0
        ),
        name="attend_back",
    )(
        low,
        high,
        query,
        grad,
        full,
        log,
        key.reshape(span, KEYS, HD),
        key_t,
        value.reshape(span, KEYS, HD),
        first,
        last,
        cosine,
        sine,
    )


def windows(at, span, count):
    total = 4 * D + 3 * FF + 4
    result = []
    for index in range(count):
        width = max(0, min(span, FF - index * span))
        begin = at + index * span
        turn = begin % LANES
        window = -(-(turn + width) // LANES) * LANES if width else 0
        window = min(window, (total - begin + turn) // LANES * LANES)
        result.append((begin - turn, window, turn, width))
    return result


FEED_AT = (4 * D, 4 * D + FF, 4 * D + 2 * FF)


def lay_out_kernel(count, span, m_ref, qkv_ref, out_ref, feed_ref):
    rows = m_ref.shape[0]
    for index in range(count):
        for part in range(3):
            at = part * D + index * HD
            qkv_ref[index, :, part * HD : (part + 1) * HD] = m_ref[:, at : at + HD].astype(BF)
    out_ref[...] = m_ref[:, 3 * D : 4 * D].astype(BF)
    column = lax.broadcasted_iota(jnp.int32, (rows, span), 1)
    for part, at in enumerate(FEED_AT):
        for index, (begin, window, turn, width) in enumerate(windows(at, span, count)):
            if width == 0:
                piece = jnp.zeros((rows, span), F32)
            else:
                piece = m_ref[:, begin : begin + window]
                if window < span:
                    piece = jnp.concatenate(
                        [piece, jnp.zeros((rows, span - window), F32)], axis=1
                    )
                if turn:
                    piece = pltpu.roll(piece, piece.shape[1] - turn, 1)
                piece = piece[:, :span]
                if width < span:
                    piece = jnp.where(column < width, piece, 0.0)
            feed_ref[index, :, part * span : (part + 1) * span] = piece.astype(BF)


def lay_out(master, count, span):
    rows = master.shape[0]
    inside = pl.BlockSpec(memory_space=pltpu.VMEM)
    return pl.pallas_call(
        functools.partial(lay_out_kernel, count, span),
        out_shape=[
            jax.ShapeDtypeStruct((count, rows, 3 * HD), BF),
            jax.ShapeDtypeStruct((rows, D), BF),
            jax.ShapeDtypeStruct((count, rows, 3 * span), BF),
        ],
        in_specs=[inside],
        out_specs=[inside] * 3,
        compiler_params=vmem(),
        cost_estimate=pl.CostEstimate(flops=0, bytes_accessed=10_000_000, transcendentals=0),
        name="lay_out",
    )(master)


STEP_COLS = 4096


def tile_of_part(ref, part, at, begin, rows, span):
    turn = at % LANES
    index = (begin - at + turn) // LANES
    tiles = span // LANES

    def piece(index):
        if index < 0 or index * LANES >= FF:
            return None
        device, inner = divmod(index, tiles)
        low = part * span + inner * LANES
        values = ref[device, :, low : low + LANES].astype(F32)
        return pltpu.roll(values, turn, 1) if turn else values

    lane = lax.broadcasted_iota(jnp.int32, (rows, LANES), 1)
    here, before = piece(index), piece(index - 1) if turn else None
    if here is None:
        return before
    return here if before is None else jnp.where(lane < turn, before, here)


def feed_tile(begin, feed_ref, vec_ref, rows, span):
    lane = lax.broadcasted_iota(jnp.int32, (rows, LANES), 1)
    total = 4 * D + 3 * FF + 4
    value = None
    for part, at in enumerate(FEED_AT):
        if at < begin + LANES and at + FF > begin:
            piece = tile_of_part(feed_ref, part, at, begin, rows, span)
            value = piece if value is None else jnp.where(lane < at - begin, value, piece)
    if begin + LANES > total - 4:
        vec = pltpu.roll(vec_ref[...], (total - 4) % LANES, 1)
        value = vec if value is None else jnp.where(lane < total - 4 - begin, value, vec)
    return value


def update_kernel(first_step, steps, tile_at, sources, *refs):
    grads, (m_ref, f_ref, s_ref, a_ref), outs = refs[:sources], refs[sources : sources + 4], refs[-4:]
    nm_ref, nf_ref, ns_ref, na_ref = outs
    rows = m_ref.shape[0]
    total = 4 * D + 3 * FF + 4

    def one(begin, cols):
        g = tile_at(begin, *grads)
        rate, decay = LR_MAT, DECAY_MAT
        if begin + LANES > total - 4:
            vector = begin + lax.broadcasted_iota(jnp.int32, (1, LANES), 1) >= total - 4
            rate, decay = jnp.where(vector, LR_VEC, LR_MAT), jnp.where(vector, 0.0, DECAY_MAT)
        new_first = BETA_ONE * f_ref[:, cols] + (1.0 - BETA_ONE) * g
        new_second = BETA_TWO * s_ref[:, cols] + (1.0 - BETA_TWO) * g * g
        nf_ref[:, cols] = new_first
        ns_ref[:, cols] = new_second
        root = jnp.sqrt(new_second * (1.0 / (1.0 - BETA_TWO**STEP))) + ADAM_EPS
        corrected = new_first * (1.0 / (1.0 - BETA_ONE**STEP)) / root
        master = m_ref[:, cols]
        new_master = master - rate * (corrected + decay * master)
        nm_ref[:, cols] = new_master
        na_ref[:, cols] = EMA_RATE * a_ref[:, cols] + (1.0 - EMA_RATE) * new_master

    for step in range(steps):

        @pl.when(pl.program_id(0) == step)
        def _():
            for at in range(0, STEP_COLS, LANES):
                begin = (first_step + step) * STEP_COLS + at
                if begin < total:
                    one(begin, slice(at, at + LANES))


def update(grads, tile_at, state, first_step, steps, done=()):
    rows, columns = state[0].shape
    whole = lambda values: pl.BlockSpec(values.shape, lambda i: (0,) * values.ndim)
    cols = pl.BlockSpec((rows, STEP_COLS), lambda i: (0, first_step + i))
    return pl.pallas_call(
        functools.partial(update_kernel, first_step, steps, tile_at, len(grads)),
        grid=(steps,),
        in_specs=[whole(g) for g in grads]
        + [cols] * 4
        + [pl.BlockSpec(memory_space=pl.ANY)] * len(done),
        out_specs=[cols] * 4,
        out_shape=[jax.ShapeDtypeStruct((rows, columns), F32) for _ in range(4)],
        input_output_aliases={len(grads) + 4 + i: i for i in range(len(done))},
        compiler_params=vmem(),
        cost_estimate=pl.CostEstimate(
            flops=0, bytes_accessed=36 * rows * steps * STEP_COLS, transcendentals=0
        ),
        name=f"update_{first_step}",
    )(*grads, *state, *done)


def chain_spans(lengths, prefix, padding, total):
    ends = jnp.cumsum(lengths, dtype=jnp.int32)
    starts = ends - lengths
    token = jnp.arange(total, dtype=jnp.int32)
    member = (token[:, None] >= starts[None, :]) & (token[:, None] < ends[None, :])
    pick = lambda values: jnp.sum(jnp.where(member, values[None, :], 0), axis=1, dtype=jnp.int32)
    start, end, pre, live = pick(starts), pick(ends), pick(prefix), pick(lengths - padding)
    place = token - start
    first = jnp.where(place < pre, start, token)
    first = jnp.where(place < live, first, 2 * total)
    low = start[::ROWS] // KEYS
    high = (end[ROWS - 1 :: ROWS] + KEYS - 1) // KEYS
    cut = lambda values: jnp.broadcast_to(values[:, None], (total, LANES)).reshape(-1, KEYS, LANES)
    return (cut(first), cut(end), low, high), place


def rotary_tables(place):
    half = HD // 2
    freq = ROPE_BASE ** (-jnp.arange(half, dtype=F32) / half)
    angles = place.astype(F32)[:, None] * freq[None, :]
    cosine, sine = jnp.cos(angles), jnp.sin(angles)
    return jnp.concatenate([cosine, cosine], axis=1), jnp.concatenate([-sine, sine], axis=1)


def to_rows(grad):
    blocks = grad.reshape(lax.axis_size("seq"), -1, grad.shape[-1])
    return lax.all_to_all(blocks, "seq", split_axis=0, concat_axis=0, tiled=True)


def on_device(hidden_in, cotangent, master, first, second, average, lengths, prefix, padding):
    groups, seq = lax.axis_size("batch"), lax.axis_size("seq")
    own = hidden_in.shape[0]
    tokens = own * seq
    rows = master.shape[0]
    span = -(-FF // (seq * LANES)) * LANES
    vec_cut = master[:, 4 * D + 3 * FF :].astype(BF).astype(F32).T
    vec_cut = jnp.pad(vec_cut, ((0, 8 - vec_cut.shape[0]), (0, LANES - rows)))[None]
    qkv_cut, out_cut, feed_cut = lay_out(master, seq, span)
    states, w_qkv, vectors = ring_gather(hidden_in, [qkv_cut, vec_cut], seq, 1)
    states = states.reshape(tokens, D)
    w_qkv = w_qkv.reshape(D, 3 * HD)
    vectors = vectors[..., :rows].transpose(2, 0, 1, 3).reshape(8, D)
    w_plane = lax.all_gather(out_cut, "seq", axis=0, tiled=True)
    feed_cut, w_plane, w_qkv = lax.optimization_barrier((feed_cut, w_plane, w_qkv))
    half = w_plane.shape[0] // 2
    half_mine = lax.dynamic_slice_in_dim(w_plane, lax.rem(lax.axis_index("seq"), 2) * half, half, 0)
    w_far = []
    for shift in range(1, groups):
        far = [(index, (index + shift) % groups) for index in range(groups)]
        w_far.append(lax.ppermute(half_mine, "batch", far))
    feed_own = lax.all_to_all(feed_cut, "seq", split_axis=0, concat_axis=0, tiled=True)
    feed_own = feed_own.reshape(D // groups, 3 * span)

    spans, place = chain_spans(lengths[0], prefix[0], padding[0], tokens)
    cosine, sine = rotary_tables(place)
    a_low, query, key, value, key_t, value_t = norm_and_project(states, w_qkv, vectors, cosine, sine)
    attended, full, log = attend(query, key, value_t, spans)
    heads, feed_far, b_low, w_out, cot_all, residual = gather_residual(
        attended, feed_own, states, vectors, cotangent, w_plane, w_far, own, seq, 2
    )
    cot_all = cot_all.reshape(tokens, D)
    out_sum, grad_feed, dr, vec_sums, do, dr_cut = feed_forward(
        b_low, cot_all, feed_own, feed_far, w_out, residual, cotangent, vectors, seq, groups, 3
    )
    dr_cols = lax.all_to_all(dr_cut, "seq", split_axis=0, concat_axis=0, tiled=True)
    normal_two, _ = norm_parts(residual)
    output = DEEP_ALPHA * (normal_two * vectors[2:3] + vectors[3:4]) + out_sum

    dp = attend_back(query, key, key_t, value, do.reshape(tokens, HD), full, log, spans, cosine, sine)
    input_grad, grad_attn, grad_feed, grad_vec = project_back(
        dp,
        w_qkv,
        a_low,
        heads,
        dr_cols.reshape(tokens, HD),
        grad_feed.reshape(seq, rows, 3 * span),
        hidden_in,
        dr,
        vectors,
        vec_sums,
        seq,
        groups,
        4,
    )
    grad_attn = to_rows(grad_attn)
    place = lax.rem(lax.axis_index("batch") * seq + lax.axis_index("seq"), LANES // rows) * rows
    grad_vec = lax.dynamic_slice_in_dim(grad_vec, place, rows, 1)[:4].T
    grad_vec = jnp.pad(grad_vec, ((0, 0), (0, LANES - 4)))

    def attn_tile(begin, ref):
        part, index = divmod(begin // HD, seq)
        return ref[index, :, part * HD : (part + 1) * HD].astype(F32)

    def other_tile(begin, feed_ref, vec_ref):
        return feed_tile(begin, feed_ref, vec_ref, rows, span)

    state = (master, first, second, average)
    steps, attn_steps = -(-master.shape[1] // STEP_COLS), 4 * D // STEP_COLS
    updated = update([grad_feed, grad_vec], other_tile, state, attn_steps, steps - attn_steps)
    updated = update([grad_attn], attn_tile, state, 0, attn_steps, updated)
    return (
        output.astype(BF),
        input_grad,
        *updated,
    )


def solution(mesh):
    spread = P(("batch", "seq"), None)
    return jax.shard_map(
        on_device,
        mesh=mesh,
        in_specs=(spread,) * 6 + (P("batch", None),) * 3,
        out_specs=(spread,) * 6,
        check_vma=False,
    )
```

```python
import functools
import math

import jax
import jax.numpy as jnp
from jax import lax
from jax.experimental import pallas as pl
from jax.experimental.pallas import tpu as pltpu
from jax.sharding import PartitionSpec as P

D = 2048
H = 16
HD = 128
FF = 5461
STEP = 10

DEEP_ALPHA = math.sqrt(48.0)
ROPE_BASE = 10000.0
NEG_LARGE = -1e30
LN_EPS = 1e-05
BETA_ONE = 0.9
BETA_TWO = 0.95
ADAM_EPS = 1e-08
LR_MAT = 0.01
LR_VEC = 0.2
DECAY_MAT = 0.1
EMA_RATE = 0.9

BF = jnp.bfloat16
F32 = jnp.float32
MESH = pl.DeviceIdType.MESH
ROWS = 256
KEYS = 512
LANES = 128
SUBS = 4
VMEM_BIG = 56 * 1024 * 1024


def nt(left, right):
    return lax.dot_general(left, right, (((1,), (1,)), ((), ())), preferred_element_type=F32)


def tn(left, right):
    return lax.dot_general(left, right, (((0,), (0,)), ((), ())), preferred_element_type=F32)


def nn(left, right):
    return jnp.dot(left, right, preferred_element_type=F32)


def vmem(limit=VMEM_BIG, **more):
    return pltpu.CompilerParams(vmem_limit_bytes=limit, **more)


class Ring:
    def __init__(self, count):
        self.pairs = count // 2
        self.batch, self.me = lax.axis_index("batch"), lax.axis_index("seq")
        self.core = lax.rem(self.me, 2)
        y, z = lax.rem(self.me // 2, 2), self.me // 4
        self.place = jnp.where(y == 0, z, self.pairs - 1 - z)
        self.sibling = self.me + 1 - 2 * self.core

    def at(self, steps, core=None):
        place = lax.rem(self.place + (1 - 2 * self.core) * steps + 4 * self.pairs, self.pairs)
        half = self.pairs // 2
        pair = jnp.where(place < half, 2 * place, 2 * (self.pairs - 1 - place) + 1)
        return pair * 2 + (self.core if core is None else core)

    def greet_all(self, count):
        barrier = pltpu.get_barrier_semaphore()
        groups = lax.axis_size("batch")
        for step in range(1, count):
            device = lax.rem(self.me + step, count)
            pl.semaphore_signal(barrier, inc=1, device_id=(self.batch, device), device_id_type=MESH)
        for shift in range(1, groups):
            group = lax.rem(self.batch + shift, groups)
            pl.semaphore_signal(barrier, inc=1, device_id=(group, self.me), device_id_type=MESH)
        pl.semaphore_wait(barrier, count + groups - 2)

    def greet_groups(self, groups):
        barrier = pltpu.get_barrier_semaphore()
        for device in (self.at(-1), self.sibling):
            pl.semaphore_signal(barrier, inc=1, device_id=(self.batch, device), device_id_type=MESH)
        for shift in range(1, groups):
            group = lax.rem(self.batch + shift, groups)
            pl.semaphore_signal(barrier, inc=1, device_id=(group, self.me), device_id_type=MESH)
        pl.semaphore_wait(barrier, 1 + groups)

    def greet_whole(self, count):
        barrier = pltpu.get_barrier_semaphore()
        total = count * lax.axis_size("batch")
        for step in range(1, total):
            flat = lax.rem(self.batch * count + self.me + step, total)
            there = (flat // count, lax.rem(flat, count))
            pl.semaphore_signal(barrier, inc=1, device_id=there, device_id_type=MESH)
        pl.semaphore_wait(barrier, total - 1)

    def copy(self, src, dst, send, recv, device):
        return pltpu.make_async_remote_copy(
            src_ref=src,
            dst_ref=dst,
            send_sem=send,
            recv_sem=recv,
            device_id=(self.batch, device),
            device_id_type=MESH,
        )


class Columns:
    def __init__(self, ring, count, src, out, sems):
        self.ring, self.count, self.src, self.out = ring, count, src, out
        self.send, self.recv, self.on_send, self.on_recv, self.own = sems
        self.groups = lax.axis_size("batch")

    def piece(self, device):
        return self.src.at[device] if self.src.shape[0] == self.count else self.src.at[0]

    def group(self, shift):
        return lax.rem(self.ring.batch + shift + self.groups, self.groups)

    def start(self):
        ring, sends = self.ring, []
        self.mine = pltpu.make_async_copy(
            self.piece(ring.me), self.out.at[ring.batch, ring.me], self.own
        )
        self.mine.start()
        for step in range(1, self.count):
            device = lax.rem(ring.me + step, self.count)
            go = ring.copy(
                self.piece(device),
                self.out.at[ring.batch, ring.me],
                self.send.at[step],
                self.recv.at[step],
                device,
            )
            go.start()
            sends.append(go)
        self.sends = sends + self.forward(0)

    def forward(self, step):
        ring, sends = self.ring, []
        device = lax.rem(ring.me - step + self.count, self.count)
        here = self.out.at[ring.batch, device]
        for shift in range(1, self.groups):
            go = pltpu.make_async_remote_copy(
                src_ref=self.piece(ring.me) if step == 0 else here,
                dst_ref=here,
                send_sem=self.on_send.at[shift - 1, step],
                recv_sem=self.on_recv.at[shift - 1, step],
                device_id=(self.group(shift), ring.me),
                device_id_type=MESH,
            )
            go.start()
            sends.append(go)
        return sends

    def pass_on(self, step):
        ring = self.ring
        device = lax.rem(ring.me - step + self.count, self.count)
        here = self.out.at[ring.batch, device]
        ring.copy(here, here, self.send.at[step], self.recv.at[step], device).wait_recv()
        self.sends += self.forward(step)

    def finish(self):
        ring = self.ring
        for step in range(self.count):
            device = lax.rem(ring.me - step + self.count, self.count)
            for shift in range(1, self.groups):
                here = self.out.at[self.group(-shift), device]
                pltpu.make_async_remote_copy(
                    src_ref=here,
                    dst_ref=here,
                    send_sem=self.on_send.at[shift - 1, step],
                    recv_sem=self.on_recv.at[shift - 1, step],
                    device_id=(self.group(shift), ring.me),
                    device_id_type=MESH,
                ).wait_recv()
        for go in self.sends:
            go.wait_send()
        self.mine.wait()


class Lap:
    def __init__(self, ring, x_ref, o_ref, sems):
        self.ring, self.x_ref, self.o_ref = ring, x_ref, o_ref
        self.ring_s, self.ring_r, self.sib_s, self.sib_r, own_sem = sems
        self.piece = x_ref.shape[0] // SUBS
        self.own = pltpu.make_async_copy(x_ref, o_ref.at[ring.me], own_sem)
        self.sends = []

    def step(self, step):
        ring = self.ring
        if step == 0:
            self.own.start()
        for sub in range(SUBS):
            rows = pl.ds(sub * self.piece, self.piece)
            dst = self.o_ref.at[ring.at(-step)].at[rows]
            src = self.x_ref.at[rows] if step == 0 else dst
            if step > 0:
                before = self.ring_s.at[step - 1, sub], self.ring_r.at[step - 1, sub]
                ring.copy(dst, dst, *before, ring.at(1)).wait_recv()
            if step < ring.pairs - 1:
                now = self.ring_s.at[step, sub], self.ring_r.at[step, sub]
                self.sends.append(ring.copy(src, dst, *now, ring.at(1)))
                self.sends[-1].start()
            across = self.sib_s.at[step, sub], self.sib_r.at[step, sub]
            self.sends.append(ring.copy(src, dst, *across, ring.sibling))
            self.sends[-1].start()

    def finish(self):
        ring = self.ring
        for step in range(ring.pairs):
            other = ring.at(step, 1 - ring.core)
            for sub in range(SUBS):
                dst = self.o_ref.at[other].at[pl.ds(sub * self.piece, self.piece)]
                across = self.sib_s.at[step, sub], self.sib_r.at[step, sub]
                ring.copy(dst, dst, *across, ring.sibling).wait_recv()
        for go in self.sends:
            go.wait_send()
        self.own.wait()


def pass_round(ring, count, lag, x_ref, o_ref, sems, columns, work, lap):
    ring_s, ring_r, sib_s, sib_r, own_sem = sems
    piece = x_ref.shape[0] // SUBS
    own = pltpu.make_async_copy(x_ref, o_ref.at[ring.me], own_sem)
    own.start()
    ring.greet_all(count)
    following, sends = ring.at(1), []
    ahead = 1

    def complete(step):
        if step == 0:
            own.wait()
        other = ring.at(step, 1 - ring.core)
        for sub in range(SUBS):
            dst = o_ref.at[other].at[pl.ds(sub * piece, piece)]
            ring.copy(
                dst, dst, sib_s.at[step, sub], sib_r.at[step, sub], ring.sibling
            ).wait_recv()
        work(ring.at(-step), other)

    for step in range(ring.pairs):
        block = ring.at(-step)
        for sub in range(SUBS):
            rows = pl.ds(sub * piece, piece)
            dst = o_ref.at[block].at[rows]
            src = x_ref.at[rows] if step == 0 else dst
            if step > 0:
                ring.copy(
                    dst, dst, ring_s.at[step - 1, sub], ring_r.at[step - 1, sub], following
                ).wait_recv()
            if step < ring.pairs - 1:
                go = ring.copy(src, dst, ring_s.at[step, sub], ring_r.at[step, sub], following)
                go.start()
                sends.append(go)
            go = ring.copy(src, dst, sib_s.at[step, sub], sib_r.at[step, sub], ring.sibling)
            go.start()
            sends.append(go)
        if step == 0:
            for column in columns:
                column.start()
        else:
            upto = count if step == ring.pairs - 1 else min(count, 1 + 2 * step)
            for passed in range(ahead, max(ahead, upto)):
                for column in columns:
                    column.pass_on(passed)
            ahead = max(ahead, upto)
        if step < ring.pairs - 1:
            lap.step(step)
        if step >= lag:
            complete(step - lag)
    for step in range(max(0, ring.pairs - lag), ring.pairs):
        complete(step)
    lap.step(ring.pairs - 1)
    return sends


class Line:
    def __init__(self, ring, count):
        self.ring, self.length = ring, count // 4
        self.y, self.z = lax.rem(ring.me // 2, 2), ring.me // 4

    def nearest(self, index):
        order = [sorted(range(self.length), key=lambda q: (abs(q - z), q)) for z in range(self.length)]
        place = order[0][index] + 0 * self.z
        for z in range(1, self.length):
            place = jnp.where(self.z == z, order[z][index], place)
        return place

    def device(self, z, row=0, core=0):
        y = self.y if row == 0 else 1 - self.y
        return (z * 2 + y) * 2 + (self.ring.core if core == 0 else 1 - self.ring.core)


def pass_along(ring, count, x_ref, o_ref, sems, columns):
    line_s, line_r, over_s, over_r, sib_s, sib_r, own_sem = sems
    line = Line(ring, count)
    piece = x_ref.shape[0] // SUBS
    own = pltpu.make_async_copy(x_ref, o_ref.at[ring.me], own_sem)
    own.start()
    ring.greet_all(count)
    across = line.device(line.z, 1)
    sends = []

    def send(condition, src, dst, send_sem, recv_sem, device):
        go = ring.copy(src, dst, send_sem, recv_sem, device)
        if condition is None:
            go.start()
        else:
            pl.when(condition)(go.start)
        sends.append((condition, go))

    order = sorted(((row, index) for row in (0, 1) for index in range(line.length)), key=lambda p: (p[0] + p[1], p[0]))
    ahead = 1
    for turn, (row, index) in enumerate(order):
        z = line.nearest(index)
        block = line.device(z, row)
        for sub in range(SUBS):
            rows = pl.ds(sub * piece, piece)
            dst = o_ref.at[block].at[rows]
            first = row == 0 and index == 0
            src = x_ref.at[rows] if first else dst
            if row == 1:
                ring.copy(dst, dst, over_s.at[z, sub], over_r.at[z, sub], across).wait_recv()
            elif not first:
                ring.copy(dst, dst, line_s.at[0, z, sub], line_r.at[z, sub], across).wait_recv()
            if row == 0:
                if first:
                    for side, step in enumerate((1, -1)):
                        there = line.z + step
                        go_on = (there >= 0) & (there < line.length)
                        there = jnp.where(go_on, there, line.z - step)
                        send(go_on, src, dst, line_s.at[side, z, sub], line_r.at[z, sub], line.device(there))
                else:
                    there = jnp.where(z < line.z, line.z + 1, line.z - 1)
                    go_on = (there >= 0) & (there < line.length)
                    there = jnp.where(go_on, there, jnp.where(z < line.z, line.z - 1, line.z + 1))
                    send(go_on, src, dst, line_s.at[0, z, sub], line_r.at[z, sub], line.device(there))
                send(None, src, dst, over_s.at[z, sub], over_r.at[z, sub], across)
            send(None, src, dst, sib_s.at[row, z, sub], sib_r.at[row, z, sub], ring.sibling)
        if turn == 0:
            for column in columns:
                column.start()
        else:
            upto = count if turn == len(order) - 1 else min(count, 1 + 2 * turn)
            for passed in range(ahead, max(ahead, upto)):
                for column in columns:
                    column.pass_on(passed)
            ahead = max(ahead, upto)
    for row, index in order:
        z = line.nearest(index)
        other = line.device(z, row, 1)
        for sub in range(SUBS):
            dst = o_ref.at[other].at[pl.ds(sub * piece, piece)]
            ring.copy(
                dst, dst, sib_s.at[row, z, sub], sib_r.at[row, z, sub], ring.sibling
            ).wait_recv()
    own.wait()
    return sends


def wait_sends(sends):
    for condition, go in sends:
        if condition is None:
            go.wait_send()
        else:
            pl.when(condition)(go.wait_send)


def gather_kernel(count, extra, x_ref, *refs):
    parts, (o_ref, *outs), sems = refs[:extra], refs[extra : 2 * extra + 1], refs[2 * extra + 1 :]
    ring = Ring(count)
    columns = [
        Columns(ring, count, parts[i], outs[i], sems[7 + 5 * i : 12 + 5 * i]) for i in range(extra)
    ]
    wait_sends(pass_along(ring, count, x_ref, o_ref, sems[:7], columns))
    for column in columns:
        column.finish()


def ring_gather(values, blocks, count, ident):
    pairs, groups = count // 2, lax.axis_size("batch")
    anywhere = pl.BlockSpec(memory_space=pl.ANY)
    return pl.pallas_call(
        functools.partial(gather_kernel, count, len(blocks)),
        out_shape=[jax.ShapeDtypeStruct((count,) + values.shape, values.dtype)]
        + [jax.ShapeDtypeStruct((groups, count) + b.shape[1:], b.dtype) for b in blocks],
        in_specs=[anywhere] * (1 + len(blocks)),
        out_specs=[anywhere] * (1 + len(blocks)),
        scratch_shapes=line_sems(count) + column_sems(count, groups) * len(blocks),
        compiler_params=pltpu.CompilerParams(collective_id=ident, has_side_effects=True),
        cost_estimate=pl.CostEstimate(flops=0, bytes_accessed=150_000_000, transcendentals=0),
        name=f"ring_gather_{ident}",
    )(values, *blocks)


def ring_sems(pairs):
    return [pltpu.SemaphoreType.DMA((pairs, SUBS)) for _ in range(4)] + [pltpu.SemaphoreType.DMA]


def line_sems(count):
    dma = pltpu.SemaphoreType.DMA
    shapes = [(2, count // 4, SUBS)] + [(count // 4, SUBS)] * 3 + [(2, count // 4, SUBS)] * 2
    return [dma(shape) for shape in shapes] + [dma]


def column_sems(count, groups):
    return [
        pltpu.SemaphoreType.DMA((count,)),
        pltpu.SemaphoreType.DMA((count,)),
        pltpu.SemaphoreType.DMA((groups, count)),
        pltpu.SemaphoreType.DMA((groups, count)),
        pltpu.SemaphoreType.DMA,
    ]


def residual_kernel(count, groups, x_ref, feed_ref, states_ref, vec_ref, cot_ref, plane_ref, *refs):
    far_refs, refs = refs[: groups - 1], refs[groups - 1 :]
    heads_ref, feed_far_ref, b_ref, w_ref, cot_all_ref, own_ref = refs[:6]
    heads, w_out, total, states, low, w_sem, load_sem, store_sem, heads_sem, *sems = refs[6:]
    ring = Ring(count)
    lap = Lap(ring, cot_ref, cot_all_ref, sems[9:14])
    tokens, own = total.shape[0], own_ref.shape[0]
    blocks = tokens // ROWS
    part = D // groups
    half = part // 2

    def held_rows(shift):
        begin = lax.rem(ring.batch - shift + groups, groups) * part
        if shift == 0:
            return w_out.at[pl.ds(pl.multiple_of(begin, part), part)]
        return w_out.at[pl.ds(pl.multiple_of(begin + ring.core * half, half), half)]

    weights = [
        pltpu.make_async_copy(ref, held_rows(shift), w_sem.at[shift])
        for shift, ref in enumerate((plane_ref,) + far_refs)
    ]
    for go in weights:
        go.start()

    def handed(shift):
        return ring.copy(
            far_refs[shift - 1],
            held_rows(shift),
            sems[7].at[shift - 1],
            sems[8].at[shift - 1],
            ring.sibling,
        )

    keep = pltpu.make_async_copy(w_out, w_ref, w_sem.at[groups])

    def onward(shift):
        return pltpu.make_async_remote_copy(
            src_ref=feed_ref,
            dst_ref=feed_far_ref.at[shift - 1],
            send_sem=sems[5].at[shift - 1],
            recv_sem=sems[6].at[shift - 1],
            device_id=(lax.rem(ring.batch + shift, groups), ring.me),
            device_id_type=MESH,
        )

    def rows_of(block):
        return pl.ds(pl.multiple_of(block * ROWS, ROWS), ROWS)

    def load(block):
        slot = lax.rem(block, 2)
        return pltpu.make_async_copy(
            states_ref.at[rows_of(block)], states.at[slot], load_sem.at[slot]
        )

    def store(block):
        slot = lax.rem(block, 2)
        return pltpu.make_async_copy(low.at[slot], b_ref.at[rows_of(block)], store_sem.at[slot])

    load(0).start()

    kept, waiting = [], []

    def add(group, first, last):
        wide = 512

        @pl.loop(0, blocks)
        def _(block):
            rows = rows_of(block)
            left = jnp.concatenate([heads[head, rows, :] for head in group], axis=1)
            if first:

                @pl.when(block + 1 < blocks)
                def _():
                    load(block + 1).start()

                load(block).wait()
                normal, _ = norm_parts(states[lax.rem(block, 2)].astype(F32))
                total[rows, :] = DEEP_ALPHA * (normal * vec_ref[0:1, :] + vec_ref[1:2, :])
            for at in range(0, D, wide):
                right = [
                    w_out[pl.ds(pl.multiple_of(head * HD, HD), HD), at : at + wide]
                    for head in group
                ]
                total[rows, at : at + wide] += nn(left, jnp.concatenate(right, axis=0))
            if last:

                @pl.when(block >= 2)
                def _():
                    store(block - 2).wait()

                normal, _ = norm_parts(total[rows, :])
                low[lax.rem(block, 2)] = (normal * vec_ref[2:3, :] + vec_ref[3:4, :]).astype(BF)
                store(block).start()

    def work(block, other):
        turn, turns = len(kept) // 2, count // 2
        if turn == 0:
            for shift in range(1, groups):
                handed(shift).start()
                onward(shift).start()
        for part, head in enumerate((block, other)):
            go = pltpu.make_async_copy(heads.at[head], heads_ref.at[head], heads_sem.at[turn, part])
            go.start()
            kept.append(go)
            waiting.append(head)
        if turn == 1:
            for go in weights:
                go.wait()
            for shift in range(1, groups):
                handed(shift).wait()
            keep.start()
        if turn == turns - 1 or turn in (1, turns // 2, turns - 2):
            add(list(waiting), turn == 1, turn == turns - 1)
            waiting.clear()

    sends = pass_round(ring, count, 2, x_ref, heads, sems[:5], [], work, lap)

    own_ref[...] = total[pl.ds(pl.multiple_of(ring.me * own, own), own), :]
    for block in (blocks - 2, blocks - 1):
        store(block).wait()
    for go in kept:
        go.wait()
    for go in sends:
        go.wait_send()
    for shift in range(1, groups):
        onward(shift).wait()
    keep.wait()
    lap.finish()


def gather_residual(attended, feed_own, states, vectors, cot, w_plane, w_far, own, count, ident):
    tokens = attended.shape[0]
    pairs, groups = count // 2, lax.axis_size("batch")
    inside, anywhere = pl.BlockSpec(memory_space=pltpu.VMEM), pl.BlockSpec(memory_space=pl.ANY)
    return pl.pallas_call(
        functools.partial(residual_kernel, count, groups),
        out_shape=[
            jax.ShapeDtypeStruct((count, tokens, HD), BF),
            jax.ShapeDtypeStruct((groups - 1,) + feed_own.shape, BF),
            jax.ShapeDtypeStruct((tokens, D), BF),
            jax.ShapeDtypeStruct((D, D), BF),
            jax.ShapeDtypeStruct((count,) + cot.shape, BF),
            jax.ShapeDtypeStruct((own, D), F32),
        ],
        in_specs=[anywhere] * 3 + [inside] + [anywhere] * (2 + len(w_far)),
        out_specs=[anywhere] * 5 + [inside],
        scratch_shapes=[
            pltpu.VMEM((count, tokens, HD), BF),
            pltpu.VMEM((D, D), BF),
            pltpu.VMEM((tokens, D), F32),
            pltpu.VMEM((2, ROWS, D), BF),
            pltpu.VMEM((2, ROWS, D), BF),
            pltpu.SemaphoreType.DMA((groups + 1,)),
            pltpu.SemaphoreType.DMA((2,)),
            pltpu.SemaphoreType.DMA((2,)),
            pltpu.SemaphoreType.DMA((pairs, 2)),
        ]
        + ring_sems(pairs)
        + [pltpu.SemaphoreType.DMA((max(1, groups - 1),)) for _ in range(4)]
        + ring_sems(pairs),
        compiler_params=vmem(collective_id=ident, has_side_effects=True),
        cost_estimate=pl.CostEstimate(
            flops=2 * tokens * D * D, bytes_accessed=200_000_000, transcendentals=0
        ),
        name="gather_residual",
    )(attended, feed_own, states, vectors, cot, w_plane, *w_far)


class RingSum:
    def __init__(self, ring, own, sib, got, sems, out):
        self.ring, self.own, self.sib, self.got, self.out = ring, own, sib, got, out
        self.ring_s, self.ring_r, self.sib_s, self.sib_r = sems
        self.piece = own.shape[1] // SUBS

    def given(self, step, src):
        return self.ring.copy(
            src, self.sib.at[step], self.sib_s.at[step], self.sib_r.at[step], self.ring.sibling
        )

    def passed(self, step, sub):
        rows = pl.ds(sub * self.piece, self.piece)
        return self.ring.copy(
            self.own.at[step].at[rows],
            self.got.at[step].at[rows],
            self.ring_s.at[step, sub],
            self.ring_r.at[step, sub],
            self.ring.at(1),
        )

    def advance(self, step):
        last = self.ring.pairs - 1
        self.given(step, self.sib.at[step]).wait_recv()
        for sub in range(SUBS):
            rows = pl.ds(sub * self.piece, self.piece)

            total = self.own[step, rows, :].astype(F32) + self.sib[step, rows, :].astype(F32)

            @pl.when(step == 0)
            def _():
                self.own[step, rows, :] = total.astype(BF)

            @pl.when(step > 0)
            def _():
                self.passed(step - 1, sub).wait_recv()
                more = total + self.got[step - 1, rows, :].astype(F32)

                @pl.when(step < last)
                def _():
                    self.own[step, rows, :] = more.astype(BF)

                @pl.when(step == last)
                def _():
                    self.out[rows, :] = more

            @pl.when(step < last)
            def _():
                self.passed(step, sub).start()

    def finish(self):
        @pl.loop(0, self.ring.pairs - 1)
        def _(step):
            for sub in range(SUBS):
                self.passed(step, sub).wait_send()

    @staticmethod
    def scratch(pairs, rows):
        return [pltpu.VMEM((pairs - late, rows, D), BF) for late in (0, 0, 1)] + [
            pltpu.SemaphoreType.DMA((pairs, SUBS)),
            pltpu.SemaphoreType.DMA((pairs, SUBS)),
            pltpu.SemaphoreType.DMA((pairs,)),
            pltpu.SemaphoreType.DMA((pairs,)),
        ]


class Exchange:
    def __init__(self, ring, count, src, out, sems):
        self.ring, self.count, self.src, self.out = ring, count, src, out
        self.send, self.recv, self.own = sems

    def copies(self):
        ring = self.ring
        for step in range(1, self.count):
            device = lax.rem(ring.me + step, self.count)
            yield ring.copy(
                self.src.at[device],
                self.out.at[ring.me],
                self.send.at[step],
                self.recv.at[step],
                device,
            )

    def start(self):
        pltpu.make_async_copy(self.src.at[self.ring.me], self.out.at[self.ring.me], self.own).start()
        for go in self.copies():
            go.start()

    def finish(self):
        for go in self.copies():
            go.wait()
        pltpu.make_async_copy(self.src.at[self.ring.me], self.out.at[self.ring.me], self.own).wait()

    @staticmethod
    def scratch(count):
        return [pltpu.SemaphoreType.DMA((count,)) for _ in range(2)] + [pltpu.SemaphoreType.DMA]


class Spread:
    def __init__(self, ring, count, groups, src, came, sems):
        self.ring, self.count, self.groups, self.src, self.came = ring, count, groups, src, came
        self.send, self.recv = sems
        self.total = count * groups
        self.shared = self.total // src.shape[0]

    def copies(self):
        me = self.ring.batch * self.count + self.ring.me
        for step in range(1, self.total):
            flat = lax.rem(me + step, self.total)
            yield pltpu.make_async_remote_copy(
                src_ref=self.src.at[flat // self.shared],
                dst_ref=self.came.at[step],
                send_sem=self.send.at[step],
                recv_sem=self.recv.at[step],
                device_id=(flat // self.count, lax.rem(flat, self.count)),
                device_id_type=MESH,
            )

    def start(self):
        for go in self.copies():
            go.start()
        me = self.ring.batch * self.count + self.ring.me
        self.came[0] = self.src[me // self.shared]

    def finish(self):
        total = self.came[0]
        for step, go in enumerate(self.copies(), 1):
            go.wait()
            total = total + self.came[step]
        return total

    @staticmethod
    def scratch(total):
        return [pltpu.SemaphoreType.DMA((total,)) for _ in range(2)]


class GroupSum:
    def __init__(self, ring, groups, sent, came, sems, out):
        self.ring, self.groups, self.sent, self.came, self.out = ring, groups, sent, came, out
        self.send, self.recv = sems
        self.tiles, self.each = D // ROWS, D // ROWS // groups

    def group(self, tile):
        return lax.rem(self.ring.batch + 1 + tile // self.each, self.groups)

    def column(self, tile):
        return (self.group(tile) * self.each + lax.rem(tile, self.each)) * ROWS

    def copy(self, tile):
        return pltpu.make_async_remote_copy(
            src_ref=self.sent.at[tile],
            dst_ref=self.came.at[tile],
            send_sem=self.send.at[tile],
            recv_sem=self.recv.at[tile],
            device_id=(self.group(tile), self.ring.me),
            device_id_type=MESH,
        )

    def put(self, tile, values):
        away = self.tiles - self.each

        @pl.when(tile < away)
        def _():
            self.sent[tile] = values.astype(BF)
            self.copy(tile).start()

        @pl.when(tile >= away)
        def _():
            self.out[tile - away] = values.astype(BF)

    def finish(self):
        @pl.loop(0, self.each)
        def _(tile):
            total = self.out[tile].astype(F32)
            for shift in range(self.groups - 1):
                self.copy(shift * self.each + tile).wait_recv()
                total = total + self.came[shift * self.each + tile].astype(F32)
            self.out[tile] = total.astype(BF)

        @pl.loop(0, self.tiles - self.each)
        def _(tile):
            self.copy(tile).wait_send()

    @staticmethod
    def scratch(groups, width):
        away = D // ROWS - D // ROWS // groups
        return [pltpu.VMEM((away, ROWS, width), BF) for _ in range(2)] + [
            pltpu.SemaphoreType.DMA((away,)) for _ in range(2)
        ]


def norm_back(normal, inverse, slope, gain):
    scaled = slope * gain
    back = inverse * (
        scaled
        - jnp.mean(scaled, axis=-1, keepdims=True)
        - normal * jnp.mean(scaled * normal, axis=-1, keepdims=True)
    )
    return back, jnp.sum(slope * normal, axis=0, keepdims=True), jnp.sum(slope, axis=0, keepdims=True)


def feed_kernel(
    count,
    groups,
    span,
    b_ref,
    cot_ref,
    feed_own_ref,
    feed_far_ref,
    w_out_ref,
    res_ref,
    cot_own_ref,
    vec_ref,
    out_ref,
    grad_ref,
    dr_ref,
    vec_sum_ref,
    do_ref,
    dr_send,
    bs,
    cs,
    stage,
    h,
    du,
    tiles,
    w_ref,
    db_ref,
    do_send,
    *rest,
):
    ring = Ring(count)
    own = out_ref.shape[0]
    sums = [
        RingSum(ring, *rest[7 * i : 7 * i + 3], rest[7 * i + 3 : 7 * i + 7], ref)
        for i, ref in enumerate((db_ref, out_ref))
    ]
    grads = GroupSum(ring, groups, rest[14], rest[15], rest[16:18], grad_ref)
    row_sem, tile_sem, w_sem = rest[18:21]
    exchange = Exchange(ring, count, do_send, do_ref, rest[21:24])
    pairs = ring.pairs

    def weights(index):
        held = (bs, cs)[index // 2 % 2].at[index % 2]
        rows = pl.ds(index * 2 * own, 2 * own)
        return pltpu.make_async_copy(w_out_ref.at[rows], held, w_sem.at[index % 4])


    def places(step):
        return ring.at(-1 - step) * own, ring.at(1 + step, 1 - ring.core) * own

    def row_loads(step):
        slot = lax.rem(step, 2)
        return [
            pltpu.make_async_copy(
                ref.at[pl.ds(pl.multiple_of(place, own), own)],
                held.at[slot, pl.ds(half * own, own)],
                row_sem.at[slot, 2 * which + half],
            )
            for which, (ref, held) in enumerate(((b_ref, bs), (cot_ref, cs)))
            for half, place in enumerate(places(step))
        ]

    def tile_loads(tile):
        slot = lax.rem(tile, 2)
        cols = pl.ds(pl.multiple_of(grads.column(tile), ROWS), ROWS)
        return [
            pltpu.make_async_copy(ref.at[:, cols], tiles.at[slot, which], tile_sem.at[slot, which])
            for which, ref in enumerate((b_ref, cot_ref))
        ]

    def feed_rows(shift):
        part = D // groups
        begin = lax.rem(ring.batch - shift + groups, groups) * part
        src = feed_own_ref if shift == 0 else feed_far_ref.at[shift - 1]
        return pltpu.make_async_copy(
            src, w_ref.at[pl.ds(pl.multiple_of(begin, part), part)], rest[24].at[shift]
        )

    for go in row_loads(0):
        go.start()
    for shift in range(groups):
        feed_rows(shift).start()
    ring.greet_all(count)
    for shift in range(groups):
        feed_rows(shift).wait()

    def feed(step):
        slot = lax.rem(step, 2)

        @pl.when(step + 1 < pairs)
        def _():
            for go in row_loads(step + 1):
                go.start()

        for go in row_loads(step):
            go.wait()
        gate = nn(bs[slot], w_ref[:, :span])
        up = nn(bs[slot], w_ref[:, span : 2 * span])
        slope = nn(cs[slot], w_ref[:, 2 * span :])
        coef = math.sqrt(2.0 / math.pi)
        square = gate * gate
        tanh = jnp.tanh(coef * gate * (1.0 + 0.044715 * square))
        half = 0.5 * (1.0 + tanh)
        gelu = gate * half
        gelu_slope = half + 0.5 * gate * (1.0 - tanh * tanh) * (coef * (1.0 + 3 * 0.044715 * square))
        hidden = (gelu * up).astype(BF)
        both = jnp.concatenate([slope * up * gelu_slope, slope * gelu], axis=1).astype(BF)
        for part, place in enumerate(places(step)):
            rows = pl.ds(pl.multiple_of(place, own), own)
            h[rows, :] = hidden[part * own : (part + 1) * own]
            du[rows, :] = both[part * own : (part + 1) * own]

        @pl.when(step >= 2)
        def _():
            for which, each in enumerate(sums):
                each.given(step - 2, stage.at[slot, which]).wait_send()

        wide = 512
        for which, (each, left, low, high) in enumerate(
            ((sums[0], both, 0, 2 * span), (sums[1], hidden, 2 * span, 3 * span))
        ):
            for at in range(0, D, wide):
                terms = nt(left, w_ref[at : at + wide, low:high]).astype(BF)
                each.own[step, :, at : at + wide] = terms[:own]
                stage[slot, which, :, at : at + wide] = terms[own:]
            each.given(step, stage.at[slot, which]).start()

    @pl.loop(0, pairs)
    def _(step):
        feed(step)

        @pl.when(lax.rem(step, 2) == 0)
        def _():
            sums[0].advance(step // 2)

    for go in tile_loads(0):
        go.start()
    for index in range(4):
        weights(index).start()

    @pl.loop(0, grads.tiles)
    def _(tile):
        slot = lax.rem(tile, 2)

        @pl.when(tile + 1 < grads.tiles)
        def _():
            for go in tile_loads(tile + 1):
                go.start()

        for go in tile_loads(tile):
            go.wait()
        values = jnp.concatenate([tn(tiles[slot, 0], du[...]), tn(tiles[slot, 1], h[...])], axis=1)
        grads.put(tile, values)
        later = pairs // 2 + tile // 2

        @pl.when((lax.rem(tile, 2) == 1) & (later < pairs))
        def _():
            sums[0].advance(later)

    passed = pairs // 2 + grads.tiles // 2

    @pl.loop(min(passed, pairs), pairs)
    def _(step):
        sums[0].advance(step)

    sums[1].advance(0)
    normal, inverse = norm_parts(res_ref[...])
    slope = DEEP_ALPHA * cot_own_ref[...].astype(F32) + db_ref[...]
    dr, gain_sum, bias_sum = norm_back(normal, inverse, slope, vec_ref[2:3, :])
    dr_ref[...] = dr
    vec_sum_ref[...] = jnp.concatenate([gain_sum, bias_sum], axis=0)
    dr_low = dr.astype(BF)
    for index in range(D // (2 * own)):
        weights(index).wait()
        do = nt(dr_low, (bs, cs)[index // 2 % 2][index % 2]).astype(BF)
        if (index + 4) * 2 * own < D:
            weights(index + 4).start()
        for part in range(0, 2 * own, HD):
            at = index * 2 * own + part
            do_send[at // HD] = do[:, part : part + HD]
            dr_send[at // HD] = dr_low[:, at : at + HD]
    exchange.start()

    @pl.loop(1, pairs)
    def _(step):
        sums[1].advance(step)

    exchange.finish()
    grads.finish()
    for step in (pairs - 2, pairs - 1):
        for which, each in enumerate(sums):
            each.given(step, stage.at[step % 2, which]).wait_send()
    for each in sums:
        each.finish()


def feed_forward(
    b_low, cot, feed_own, feed_far, w_out, residual, cot_own, vectors, count, groups, ident
):
    tokens, span, pairs = b_low.shape[0], feed_own.shape[1] // 3, count // 2
    own = residual.shape[0]
    inside, anywhere = pl.BlockSpec(memory_space=pltpu.VMEM), pl.BlockSpec(memory_space=pl.ANY)
    return pl.pallas_call(
        functools.partial(feed_kernel, count, groups, span),
        in_specs=[anywhere] * 5 + [inside] * 3,
        out_specs=[inside] * 4 + [anywhere, inside],
        out_shape=[
            jax.ShapeDtypeStruct((own, D), F32),
            jax.ShapeDtypeStruct((D // groups // ROWS, ROWS, 3 * span), BF),
            jax.ShapeDtypeStruct((own, D), F32),
            jax.ShapeDtypeStruct((2, D), F32),
            jax.ShapeDtypeStruct((count, own, HD), BF),
            jax.ShapeDtypeStruct((count, own, HD), BF),
        ],
        scratch_shapes=[
            pltpu.VMEM((2, 2 * own, D), BF),
            pltpu.VMEM((2, 2 * own, D), BF),
            pltpu.VMEM((2, 2, own, D), BF),
            pltpu.VMEM((tokens, span), BF),
            pltpu.VMEM((tokens, 2 * span), BF),
            pltpu.VMEM((2, 2, tokens, ROWS), BF),
            pltpu.VMEM((D, 3 * span), BF),
            pltpu.VMEM((own, D), F32),
            pltpu.VMEM((count, own, HD), BF),
        ]
        + RingSum.scratch(pairs, own) * 2
        + GroupSum.scratch(groups, 3 * span)
        + [pltpu.SemaphoreType.DMA((2, 4)), pltpu.SemaphoreType.DMA((2, 2)), pltpu.SemaphoreType.DMA((4,))]
        + Exchange.scratch(count)
        + [pltpu.SemaphoreType.DMA((groups,))],
        compiler_params=vmem(62 * 1024 * 1024, collective_id=ident, has_side_effects=True),
        cost_estimate=pl.CostEstimate(
            flops=18 * tokens * D * span, bytes_accessed=250_000_000, transcendentals=0
        ),
        name="feed_forward",
    )(b_low, cot, feed_own, feed_far, w_out, residual, cot_own, vectors)


def project_kernel(
    count,
    groups,
    dp_ref,
    w_ref,
    a_ref,
    heads_ref,
    dr_ref,
    feed_ref,
    x_ref,
    dr_own_ref,
    vec_ref,
    vec_sum_ref,
    back_ref,
    grad_ref,
    feed_out_ref,
    vec_out_ref,
    stage,
    tiles,
    da_ref,
    vec_send,
    vec_came,
    *rest,
):
    ring = Ring(count)
    own = da_ref.shape[0]
    sums = RingSum(ring, *rest[:3], rest[3:7], da_ref)
    grads = GroupSum(ring, groups, rest[7], rest[8], rest[9:11], grad_ref)
    tile_sem = rest[11]
    feed = Exchange(ring, count, feed_ref, feed_out_ref, rest[12:15])
    spread = Spread(ring, count, groups, vec_send, vec_came, rest[15:17])
    pairs, width = ring.pairs, heads_ref.shape[2]

    def places(step):
        return ring.at(-1 - step) * own, ring.at(1 + step, 1 - ring.core) * own

    def tile_loads(tile):
        slot = lax.rem(tile, 2)
        begin = pl.multiple_of(grads.column(tile), ROWS)
        loads = [
            pltpu.make_async_copy(
                a_ref.at[:, pl.ds(begin, ROWS)], tiles.at[slot, 0], tile_sem.at[slot, 0]
            )
        ]
        for part in range(ROWS // width):
            loads.append(
                pltpu.make_async_copy(
                    heads_ref.at[begin // width + part],
                    tiles.at[slot, 1, :, pl.ds(part * width, width)],
                    tile_sem.at[slot, 1 + part],
                )
            )
        return loads

    for go in tile_loads(0):
        go.start()
    ring.greet_whole(count)
    feed.start()

    def terms_of(step):
        slot = lax.rem(step, 2)

        @pl.when(step >= 2)
        def _():
            sums.given(step - 2, stage.at[slot]).wait_send()

        left = jnp.concatenate(
            [dp_ref[pl.ds(pl.multiple_of(place, own), own), :] for place in places(step)], axis=0
        )
        wide = 512
        for at in range(0, D, wide):
            terms = nt(left, w_ref[at : at + wide, :]).astype(BF)
            sums.own[step, :, at : at + wide] = terms[:own]
            stage[slot, :, at : at + wide] = terms[own:]
        sums.given(step, stage.at[slot]).start()

    terms_of(0)
    sums.advance(0)

    @pl.loop(0, grads.tiles)
    def _(tile):
        slot = lax.rem(tile, 2)

        @pl.when(tile + 1 < grads.tiles)
        def _():
            for go in tile_loads(tile + 1):
                go.start()

        for go in tile_loads(tile):
            go.wait()
        values = jnp.concatenate(
            [tn(tiles[slot, 0], dp_ref[...]), tn(tiles[slot, 1], dr_ref[...])], axis=1
        )
        grads.put(tile, values)

        @pl.when(tile + 1 < pairs)
        def _():
            terms_of(tile + 1)

        @pl.when((lax.rem(tile, 2) == 1) & (tile // 2 + 1 < pairs))
        def _():
            sums.advance(tile // 2 + 1)

    @pl.loop(1 + grads.tiles // 2, pairs)
    def _(step):
        sums.advance(step)

    normal, inverse = norm_parts(x_ref[...].astype(F32))
    slope = DEEP_ALPHA * dr_own_ref[...] + da_ref[...]
    back, gain_sum, bias_sum = norm_back(normal, inverse, slope, vec_ref[0:1, :])
    back_ref[...] = back.astype(BF)
    kinds = [gain_sum, bias_sum, vec_sum_ref[0:1, :], vec_sum_ref[1:2, :]]
    for tile in range(D // LANES):
        for kind, values in enumerate(kinds):
            vec_send[tile, kind : kind + 1, :] = values[:, tile * LANES : (tile + 1) * LANES]
    spread.start()
    grads.finish()
    for step in (pairs - 2, pairs - 1):
        sums.given(step, stage.at[step % 2]).wait_send()
    sums.finish()
    vec_out_ref[...] = spread.finish()
    feed.finish()


def project_back(
    dp, w_qkv, a_low, heads, dr_cols, grad_feed, states, dr, vectors, vec_sums, count, groups, ident
):
    tokens, pairs = dp.shape[0], count // 2
    own, width = dr.shape[0], 3 * HD + dr_cols.shape[1]
    inside, anywhere = pl.BlockSpec(memory_space=pltpu.VMEM), pl.BlockSpec(memory_space=pl.ANY)
    return pl.pallas_call(
        functools.partial(project_kernel, count, groups),
        in_specs=[inside, inside, anywhere, anywhere, inside, anywhere] + [inside] * 4,
        out_specs=[inside, inside, anywhere, inside],
        out_shape=[
            jax.ShapeDtypeStruct((own, D), BF),
            jax.ShapeDtypeStruct((D // groups // ROWS, ROWS, width), BF),
            jax.ShapeDtypeStruct(grad_feed.shape, BF),
            jax.ShapeDtypeStruct((8, LANES), F32),
        ],
        scratch_shapes=[
            pltpu.VMEM((2, own, D), BF),
            pltpu.VMEM((2, 2, tokens, ROWS), BF),
            pltpu.VMEM((own, D), F32),
            pltpu.VMEM((D // LANES, 8, LANES), F32),
            pltpu.VMEM((count * groups, 8, LANES), F32),
        ]
        + RingSum.scratch(pairs, own)
        + GroupSum.scratch(groups, width)
        + [pltpu.SemaphoreType.DMA((2, 1 + ROWS // HD))]
        + Exchange.scratch(count)
        + Spread.scratch(count * groups),
        compiler_params=vmem(collective_id=ident, has_side_effects=True),
        cost_estimate=pl.CostEstimate(
            flops=4 * tokens * D * 3 * HD, bytes_accessed=200_000_000, transcendentals=0
        ),
        name="project_back",
    )(dp, w_qkv, a_low, heads, dr_cols, grad_feed, states, dr, vectors, vec_sums)


def norm_parts(values):
    centre = values - jnp.mean(values, axis=-1, keepdims=True)
    inverse = lax.rsqrt(jnp.mean(centre * centre, axis=-1, keepdims=True) + LN_EPS)
    return centre * inverse, inverse


def qkv_kernel(x_ref, w_ref, vec_ref, cos_ref, sin_ref, a_ref, q_ref, k_ref, v_ref, kt_ref, vt_ref):
    normal, _ = norm_parts(x_ref[...].astype(F32))
    low = (normal * vec_ref[0:1, :] + vec_ref[1:2, :]).astype(BF)
    a_ref[...] = low
    projected = nn(low, w_ref[...])
    for index, ref in enumerate((q_ref, k_ref)):
        part = projected[:, index * HD : (index + 1) * HD]
        turned = part * cos_ref[...] + pltpu.roll(part, HD // 2, 1) * sin_ref[...]
        ref[...] = turned.astype(BF)
    kt_ref[...] = turned.T.astype(BF)[None]
    v_ref[...] = projected[:, 2 * HD :].astype(BF)
    vt_ref[...] = projected[:, 2 * HD :].T.astype(BF)[None]


def norm_and_project(states, w_qkv, vectors, cosine, sine):
    tokens = states.shape[0]
    whole = lambda shape: pl.BlockSpec(shape, lambda i: (0, 0))
    rows = lambda width: pl.BlockSpec((ROWS, width), lambda i: (i, 0))
    turned = pl.BlockSpec((1, HD, ROWS), lambda i: (i * ROWS // KEYS, 0, i % (KEYS // ROWS)))
    return pl.pallas_call(
        qkv_kernel,
        grid=(tokens // ROWS,),
        in_specs=[rows(D), whole((D, 3 * HD)), whole(vectors.shape), rows(HD), rows(HD)],
        out_specs=[rows(D), rows(HD), rows(HD), rows(HD), turned, turned],
        out_shape=[jax.ShapeDtypeStruct((tokens, D), BF)]
        + [jax.ShapeDtypeStruct((tokens, HD), BF) for _ in range(3)]
        + [jax.ShapeDtypeStruct((tokens // KEYS, HD, KEYS), BF) for _ in range(2)],
        compiler_params=vmem(),
        cost_estimate=pl.CostEstimate(
            flops=2 * tokens * D * 3 * HD, bytes_accessed=24_000_000, transcendentals=0
        ),
        name="norm_and_project",
    )(states, w_qkv, vectors, cosine, sine)


def masked_scores(block, query, k_ref, first_ref, last_ref, keys):
    place = block * ROWS + lax.broadcasted_iota(jnp.int32, (1, LANES), 1)
    scores = nt(k_ref[keys], query) * HD ** (-0.5)
    parts = []
    for at in range(0, ROWS, LANES):
        seen = (place + at >= first_ref[keys]) & (place + at < last_ref[keys])
        parts.append(jnp.where(seen, scores[:, at : at + LANES], NEG_LARGE))
    return jnp.concatenate(parts, axis=1)


def attend_kernel(
    low_ref, high_ref, q_ref, k_ref, vt_ref, first_ref, last_ref, o_ref, full_ref, log_ref, held
):
    block = pl.program_id(0)
    query = q_ref[...]

    def score(keys, top):
        scores = masked_scores(block, query, k_ref, first_ref, last_ref, keys)
        held[keys] = scores
        return jnp.maximum(top, jnp.max(scores, axis=0, keepdims=True))

    def add(keys, carry):
        total, out = carry
        weight = jnp.exp(held[keys] - top)
        total = total + jnp.sum(weight, axis=0, keepdims=True)
        return total, out + nn(vt_ref[keys], weight.astype(BF))

    low, high = low_ref[block], high_ref[block]
    top = lax.fori_loop(low, high, score, jnp.full((1, ROWS), NEG_LARGE, F32))
    total, out = lax.fori_loop(
        low, high, add, (jnp.zeros((1, ROWS), F32), jnp.zeros((HD, ROWS), F32))
    )
    out = out / total
    o_ref[...] = out.T.astype(BF)
    full_ref[...] = out[None]
    log_ref[...] = (top + jnp.log(total))[None]


def attend(query, key, value_t, spans):
    tokens = query.shape[0]
    blocks, span = tokens // ROWS, tokens // KEYS
    first, last, low, high = spans
    rows = pl.BlockSpec((ROWS, HD), lambda i, *_: (i, 0))
    one = lambda shape: pl.BlockSpec((1,) + shape, lambda i, *_: (i, 0, 0))
    whole = lambda shape: pl.BlockSpec(shape, lambda i, *_: (0,) * len(shape))
    return pl.pallas_call(
        attend_kernel,
        grid_spec=pltpu.PrefetchScalarGridSpec(
            num_scalar_prefetch=2,
            grid=(blocks,),
            in_specs=[
                rows,
                whole((span, KEYS, HD)),
                whole((span, HD, KEYS)),
                whole((span, KEYS, LANES)),
                whole((span, KEYS, LANES)),
            ],
            out_specs=[rows, one((HD, ROWS)), one((1, ROWS))],
            scratch_shapes=[pltpu.VMEM((span, KEYS, ROWS), F32)],
        ),
        out_shape=[
            jax.ShapeDtypeStruct((tokens, HD), BF),
            jax.ShapeDtypeStruct((blocks, HD, ROWS), F32),
            jax.ShapeDtypeStruct((blocks, 1, ROWS), F32),
        ],
        compiler_params=vmem(),
        cost_estimate=pl.CostEstimate(
            flops=2 * tokens * tokens * HD, bytes_accessed=4_000_000, transcendentals=0
        ),
        name="attend",
    )(low, high, query, key.reshape(span, KEYS, HD), value_t, first, last)


def attend_back_kernel(
    low_ref,
    high_ref,
    q_ref,
    g_ref,
    full_ref,
    log_ref,
    k_ref,
    kt_ref,
    v_ref,
    first_ref,
    last_ref,
    cos_ref,
    sin_ref,
    o_ref,
    dk_ref,
    dv_ref,
):
    block = pl.program_id(0)
    blocks = pl.num_programs(0)
    scale = HD ** (-0.5)

    @pl.when(block == 0)
    def _():
        dk_ref[...] = jnp.zeros_like(dk_ref)
        dv_ref[...] = jnp.zeros_like(dv_ref)

    query, grad = q_ref[...], g_ref[...]
    inner = jnp.sum(grad.astype(F32).T * full_ref[0], axis=0, keepdims=True)
    log = log_ref[0]

    def one(keys, total):
        scores = masked_scores(block, query, k_ref, first_ref, last_ref, keys)
        weight = jnp.exp(scores - log)
        slope = (weight * (nt(v_ref[keys], grad) - inner)).astype(BF)
        dv_ref[keys] += nn(weight.astype(BF), grad)
        dk_ref[keys] += nn(slope, query)
        return total + nn(kt_ref[keys], slope)

    total = lax.fori_loop(low_ref[block], high_ref[block], one, jnp.zeros((HD, ROWS), F32))

    def turn_back(values, cosine, sine):
        values = (values * scale).astype(BF).astype(F32)
        return (values * cosine - pltpu.roll(values, HD // 2, 1) * sine).astype(BF)

    rows = pl.ds(pl.multiple_of(block * ROWS, ROWS), ROWS)
    o_ref[rows, 0:HD] = turn_back(total.T, cos_ref[rows, :], sin_ref[rows, :])

    @pl.when(block == blocks - 1)
    def _():
        for part in range(dk_ref.shape[0]):
            there = pl.ds(part * KEYS, KEYS)
            o_ref[there, HD : 2 * HD] = turn_back(
                dk_ref[part], cos_ref[there, :], sin_ref[there, :]
            )
            o_ref[there, 2 * HD :] = dv_ref[part].astype(BF)


def attend_back(query, key, key_t, value, grad, full, log, spans, cosine, sine):
    tokens = query.shape[0]
    blocks, span = tokens // ROWS, tokens // KEYS
    first, last, low, high = spans
    rows = pl.BlockSpec((ROWS, HD), lambda i, *_: (i, 0))
    one = lambda shape: pl.BlockSpec((1,) + shape, lambda i, *_: (i, 0, 0))
    whole = lambda shape: pl.BlockSpec(shape, lambda i, *_: (0,) * len(shape))
    return pl.pallas_call(
        attend_back_kernel,
        grid_spec=pltpu.PrefetchScalarGridSpec(
            num_scalar_prefetch=2,
            grid=(blocks,),
            in_specs=[
                rows,
                rows,
                one((HD, ROWS)),
                one((1, ROWS)),
                whole((span, KEYS, HD)),
                whole((span, HD, KEYS)),
                whole((span, KEYS, HD)),
                whole((span, KEYS, LANES)),
                whole((span, KEYS, LANES)),
                whole((tokens, HD)),
                whole((tokens, HD)),
            ],
            out_specs=whole((tokens, 3 * HD)),
            scratch_shapes=[pltpu.VMEM((span, KEYS, HD), F32) for _ in range(2)],
        ),
        out_shape=jax.ShapeDtypeStruct((tokens, 3 * HD), BF),
        compiler_params=vmem(),
        cost_estimate=pl.CostEstimate(
            flops=5 * tokens * tokens * HD, bytes_accessed=6_000_000, transcendentals=0
        ),
        name="attend_back",
    )(
        low,
        high,
        query,
        grad,
        full,
        log,
        key.reshape(span, KEYS, HD),
        key_t,
        value.reshape(span, KEYS, HD),
        first,
        last,
        cosine,
        sine,
    )


def windows(at, span, count):
    total = 4 * D + 3 * FF + 4
    result = []
    for index in range(count):
        width = max(0, min(span, FF - index * span))
        begin = at + index * span
        turn = begin % LANES
        window = -(-(turn + width) // LANES) * LANES if width else 0
        window = min(window, (total - begin + turn) // LANES * LANES)
        result.append((begin - turn, window, turn, width))
    return result


FEED_AT = (4 * D, 4 * D + FF, 4 * D + 2 * FF)


def lay_out_kernel(count, span, m_ref, qkv_ref, out_ref, feed_ref):
    rows = m_ref.shape[0]
    for index in range(count):
        for part in range(3):
            at = part * D + index * HD
            qkv_ref[index, :, part * HD : (part + 1) * HD] = m_ref[:, at : at + HD].astype(BF)
    out_ref[...] = m_ref[:, 3 * D : 4 * D].astype(BF)
    column = lax.broadcasted_iota(jnp.int32, (rows, span), 1)
    for part, at in enumerate(FEED_AT):
        for index, (begin, window, turn, width) in enumerate(windows(at, span, count)):
            if width == 0:
                piece = jnp.zeros((rows, span), F32)
            else:
                piece = m_ref[:, begin : begin + window]
                if window < span:
                    piece = jnp.concatenate(
                        [piece, jnp.zeros((rows, span - window), F32)], axis=1
                    )
                if turn:
                    piece = pltpu.roll(piece, piece.shape[1] - turn, 1)
                piece = piece[:, :span]
                if width < span:
                    piece = jnp.where(column < width, piece, 0.0)
            feed_ref[index, :, part * span : (part + 1) * span] = piece.astype(BF)


def lay_out(master, count, span):
    rows = master.shape[0]
    inside = pl.BlockSpec(memory_space=pltpu.VMEM)
    return pl.pallas_call(
        functools.partial(lay_out_kernel, count, span),
        out_shape=[
            jax.ShapeDtypeStruct((count, rows, 3 * HD), BF),
            jax.ShapeDtypeStruct((rows, D), BF),
            jax.ShapeDtypeStruct((count, rows, 3 * span), BF),
        ],
        in_specs=[inside],
        out_specs=[inside] * 3,
        compiler_params=vmem(),
        cost_estimate=pl.CostEstimate(flops=0, bytes_accessed=10_000_000, transcendentals=0),
        name="lay_out",
    )(master)


STEP_COLS = 4096


def tile_of_part(ref, part, at, begin, rows, span):
    turn = at % LANES
    index = (begin - at + turn) // LANES
    tiles = span // LANES

    def piece(index):
        if index < 0 or index * LANES >= FF:
            return None
        device, inner = divmod(index, tiles)
        low = part * span + inner * LANES
        values = ref[device, :, low : low + LANES].astype(F32)
        return pltpu.roll(values, turn, 1) if turn else values

    lane = lax.broadcasted_iota(jnp.int32, (rows, LANES), 1)
    here, before = piece(index), piece(index - 1) if turn else None
    if here is None:
        return before
    return here if before is None else jnp.where(lane < turn, before, here)


def feed_tile(begin, feed_ref, vec_ref, rows, span):
    lane = lax.broadcasted_iota(jnp.int32, (rows, LANES), 1)
    total = 4 * D + 3 * FF + 4
    value = None
    for part, at in enumerate(FEED_AT):
        if at < begin + LANES and at + FF > begin:
            piece = tile_of_part(feed_ref, part, at, begin, rows, span)
            value = piece if value is None else jnp.where(lane < at - begin, value, piece)
    if begin + LANES > total - 4:
        vec = pltpu.roll(vec_ref[...], (total - 4) % LANES, 1)
        value = vec if value is None else jnp.where(lane < total - 4 - begin, value, vec)
    return value


def update_kernel(first_step, steps, tile_at, sources, *refs):
    grads, (m_ref, f_ref, s_ref, a_ref), outs = refs[:sources], refs[sources : sources + 4], refs[-4:]
    nm_ref, nf_ref, ns_ref, na_ref = outs
    rows = m_ref.shape[0]
    total = 4 * D + 3 * FF + 4

    def one(begin, cols):
        g = tile_at(begin, *grads)
        rate, decay = LR_MAT, DECAY_MAT
        if begin + LANES > total - 4:
            vector = begin + lax.broadcasted_iota(jnp.int32, (1, LANES), 1) >= total - 4
            rate, decay = jnp.where(vector, LR_VEC, LR_MAT), jnp.where(vector, 0.0, DECAY_MAT)
        new_first = BETA_ONE * f_ref[:, cols] + (1.0 - BETA_ONE) * g
        new_second = BETA_TWO * s_ref[:, cols] + (1.0 - BETA_TWO) * g * g
        nf_ref[:, cols] = new_first
        ns_ref[:, cols] = new_second
        root = jnp.sqrt(new_second * (1.0 / (1.0 - BETA_TWO**STEP))) + ADAM_EPS
        corrected = new_first * (1.0 / (1.0 - BETA_ONE**STEP)) / root
        master = m_ref[:, cols]
        new_master = master - rate * (corrected + decay * master)
        nm_ref[:, cols] = new_master
        na_ref[:, cols] = EMA_RATE * a_ref[:, cols] + (1.0 - EMA_RATE) * new_master

    for step in range(steps):

        @pl.when(pl.program_id(0) == step)
        def _():
            for at in range(0, STEP_COLS, LANES):
                begin = (first_step + step) * STEP_COLS + at
                if begin < total:
                    one(begin, slice(at, at + LANES))


def update(grads, tile_at, state, first_step, steps, done=()):
    rows, columns = state[0].shape
    whole = lambda values: pl.BlockSpec(values.shape, lambda i: (0,) * values.ndim)
    cols = pl.BlockSpec((rows, STEP_COLS), lambda i: (0, first_step + i))
    return pl.pallas_call(
        functools.partial(update_kernel, first_step, steps, tile_at, len(grads)),
        grid=(steps,),
        in_specs=[whole(g) for g in grads]
        + [cols] * 4
        + [pl.BlockSpec(memory_space=pl.ANY)] * len(done),
        out_specs=[cols] * 4,
        out_shape=[jax.ShapeDtypeStruct((rows, columns), F32) for _ in range(4)],
        input_output_aliases={len(grads) + 4 + i: i for i in range(len(done))},
        compiler_params=vmem(),
        cost_estimate=pl.CostEstimate(
            flops=0, bytes_accessed=36 * rows * steps * STEP_COLS, transcendentals=0
        ),
        name=f"update_{first_step}",
    )(*grads, *state, *done)


def chain_spans(lengths, prefix, padding, total):
    ends = jnp.cumsum(lengths, dtype=jnp.int32)
    starts = ends - lengths
    token = jnp.arange(total, dtype=jnp.int32)
    member = (token[:, None] >= starts[None, :]) & (token[:, None] < ends[None, :])
    pick = lambda values: jnp.sum(jnp.where(member, values[None, :], 0), axis=1, dtype=jnp.int32)
    start, end, pre, live = pick(starts), pick(ends), pick(prefix), pick(lengths - padding)
    place = token - start
    first = jnp.where(place < pre, start, token)
    first = jnp.where(place < live, first, 2 * total)
    low = start[::ROWS] // KEYS
    high = (end[ROWS - 1 :: ROWS] + KEYS - 1) // KEYS
    cut = lambda values: jnp.broadcast_to(values[:, None], (total, LANES)).reshape(-1, KEYS, LANES)
    return (cut(first), cut(end), low, high), place


def rotary_tables(place):
    half = HD // 2
    freq = ROPE_BASE ** (-jnp.arange(half, dtype=F32) / half)
    angles = place.astype(F32)[:, None] * freq[None, :]
    cosine, sine = jnp.cos(angles), jnp.sin(angles)
    return jnp.concatenate([cosine, cosine], axis=1), jnp.concatenate([-sine, sine], axis=1)


def to_rows(grad):
    blocks = grad.reshape(lax.axis_size("seq"), -1, grad.shape[-1])
    return lax.all_to_all(blocks, "seq", split_axis=0, concat_axis=0, tiled=True)


def on_device(hidden_in, cotangent, master, first, second, average, lengths, prefix, padding):
    groups, seq = lax.axis_size("batch"), lax.axis_size("seq")
    own = hidden_in.shape[0]
    tokens = own * seq
    rows = master.shape[0]
    span = -(-FF // (seq * LANES)) * LANES
    vec_cut = master[:, 4 * D + 3 * FF :].astype(BF).astype(F32).T
    vec_cut = jnp.pad(vec_cut, ((0, 8 - vec_cut.shape[0]), (0, LANES - rows)))[None]
    qkv_cut, out_cut, feed_cut = lay_out(master, seq, span)
    states, w_qkv, vectors = ring_gather(hidden_in, [qkv_cut, vec_cut], seq, 1)
    states = states.reshape(tokens, D)
    w_qkv = w_qkv.reshape(D, 3 * HD)
    vectors = vectors[..., :rows].transpose(2, 0, 1, 3).reshape(8, D)
    w_plane = lax.all_gather(out_cut, "seq", axis=0, tiled=True)
    feed_cut, w_plane, w_qkv = lax.optimization_barrier((feed_cut, w_plane, w_qkv))
    half = w_plane.shape[0] // 2
    half_mine = lax.dynamic_slice_in_dim(w_plane, lax.rem(lax.axis_index("seq"), 2) * half, half, 0)
    w_far = []
    for shift in range(1, groups):
        far = [(index, (index + shift) % groups) for index in range(groups)]
        w_far.append(lax.ppermute(half_mine, "batch", far))
    feed_own = lax.all_to_all(feed_cut, "seq", split_axis=0, concat_axis=0, tiled=True)
    feed_own = feed_own.reshape(D // groups, 3 * span)

    spans, place = chain_spans(lengths[0], prefix[0], padding[0], tokens)
    cosine, sine = rotary_tables(place)
    a_low, query, key, value, key_t, value_t = norm_and_project(states, w_qkv, vectors, cosine, sine)
    attended, full, log = attend(query, key, value_t, spans)
    heads, feed_far, b_low, w_out, cot_all, residual = gather_residual(
        attended, feed_own, states, vectors, cotangent, w_plane, w_far, own, seq, 2
    )
    cot_all = cot_all.reshape(tokens, D)
    out_sum, grad_feed, dr, vec_sums, do, dr_cut = feed_forward(
        b_low, cot_all, feed_own, feed_far, w_out, residual, cotangent, vectors, seq, groups, 3
    )
    dr_cols = lax.all_to_all(dr_cut, "seq", split_axis=0, concat_axis=0, tiled=True)
    normal_two, _ = norm_parts(residual)
    output = DEEP_ALPHA * (normal_two * vectors[2:3] + vectors[3:4]) + out_sum

    dp = attend_back(query, key, key_t, value, do.reshape(tokens, HD), full, log, spans, cosine, sine)
    input_grad, grad_attn, grad_feed, grad_vec = project_back(
        dp,
        w_qkv,
        a_low,
        heads,
        dr_cols.reshape(tokens, HD),
        grad_feed.reshape(seq, rows, 3 * span),
        hidden_in,
        dr,
        vectors,
        vec_sums,
        seq,
        groups,
        4,
    )
    grad_attn = to_rows(grad_attn)
    place = lax.rem(lax.axis_index("batch") * seq + lax.axis_index("seq"), LANES // rows) * rows
    grad_vec = lax.dynamic_slice_in_dim(grad_vec, place, rows, 1)[:4].T
    grad_vec = jnp.pad(grad_vec, ((0, 0), (0, LANES - 4)))

    def attn_tile(begin, ref):
        part, index = divmod(begin // HD, seq)
        return ref[index, :, part * HD : (part + 1) * HD].astype(F32)

    def other_tile(begin, feed_ref, vec_ref):
        return feed_tile(begin, feed_ref, vec_ref, rows, span)

    state = (master, first, second, average)
    steps, attn_steps = -(-master.shape[1] // STEP_COLS), 4 * D // STEP_COLS
    updated = update([grad_feed, grad_vec], other_tile, state, attn_steps, steps - attn_steps)
    updated = update([grad_attn], attn_tile, state, 0, attn_steps, updated)
    return (
        output.astype(BF),
        input_grad,
        *updated,
    )


def solution(mesh):
    spread = P(("batch", "seq"), None)
    return jax.shard_map(
        on_device,
        mesh=mesh,
        in_specs=(spread,) * 6 + (P("batch", None),) * 3,
        out_specs=(spread,) * 6,
        check_vma=False,
    )
```
